32 devices in a mesh: section: 4 (over y, x), dp: 8 (over z, core).
Axes of the slice: x: 2, y: 2, z: 4, core: 2. Of those that a mesh axis runs over, the one named last changes fastest.
Arguments:
- hidden_in: bfloat16 [128, 32, 768], P(('section', 'dp')), may hold values from -6 to 6
- lengths: int32 [128], P(('section', 'dp')), may hold values from 8 to 32, as said below
- labels: int32 [128], P(('section', 'dp')), may hold values from 0 to 31, as said below
- chosen: int32 [128, 32, 32], P(('section', 'dp')), may hold values from 0 to 4095, as said below
- slab_main: bfloat16 [4, 768, 3072], P('section'), may hold values from -1 to 1, as said below
- slab_side: bfloat16 [4, 768, 3072], P('section'), may hold values from -1 to 1, as said below
- section_gains: float32 [4, 768], P('section'), may hold values from 0.5 to 1.5
- rel_bias: float32 [32, 12], replicated, may hold values from -3 to 3
- final_gain: float32 [768], replicated, may hold values from 0.5 to 1.5
- out_proj: bfloat16 [768, 128], replicated, may hold values from -0.01953125 to 0.01953125
- doc_vectors: bfloat16 [4096, 128], P('dp'), may hold values from -3 to 3
Outputs:
- out_vectors: bfloat16 [128, 32, 128], P(('section', 'dp'))
- query_loss: float32 [128], P(('section', 'dp'))
- input_grad: float32 [128, 32, 768], P(('section', 'dp'))
- grad_main: float32 [4, 768, 3072], P('section', 'dp')
- grad_side: float32 [4, 768, 3072], P('section', 'dp')
- grad_gains: float32 [4, 768], P('section', 'dp')
- grad_bias: float32 [32, 12], replicated
- grad_final_gain: float32 [768], replicated
- grad_proj: float32 [768, 128], replicated
The draws below stay inside these ranges and needn't reach their ends.
Inputs may be any that keep to these rules, and one draw needn't show every extreme that they name: `lengths`: a query's slots at positions of at least its length are padding; its keys there are masked and its tokens there do not enter its loss. Number of the positive document of each query, among 32 documents of 128 tokens; document t holds rows t * 128 to t * 128 + 127 of doc_vectors, and index o of dp holds documents o * 4 to o * 4 + 3. Within one block of 4 queries the labels are distinct, and at most 1 of them lie on one index of dp, exactly 1 on some. `chosen`: rows of doc_vectors retrieved for each query token; every one lies in a document named by labels in the same block of 4 queries. `slab_main`: weights of order 768 ** -0.5 or smaller. `slab_side`: weights of order 768 ** -0.5 or smaller.
All inputs are finite; a program needn't handle non-finite values.
Results may differ from the reference program's by a relative error of at most 0.025.
Values may be sent and summed in bfloat16 or wider, within the bound.
A program may use at most 704 MiB of HBM per device.

```python
import jax
import jax.numpy as jnp
import numpy as np
from jax import lax

D = 768
H = 12
DH = 64
FF = 3072
BUCKETS = 32
PROJ = 128
LQ = 32
K = 32
DOC_LEN = 128
QB = 4
DOCS_DEV = 4
QUERIES = 128
DOC_TOKENS = 4096
N_SECTION = 4
N_DP = 8


def retrieval_draw(key):
    blocks = QUERIES // QB
    owner_orders = jax.vmap(lambda sub: jax.random.permutation(sub, N_DP))(jax.random.split(jax.random.fold_in(key, 101), blocks))
    position = jnp.arange(QB)
    owner_pick = owner_orders[:, position % N_DP]
    base_local = jax.random.randint(jax.random.fold_in(key, 106), (blocks, N_DP), 0, DOCS_DEV)
    local_doc = (base_local[:, position % N_DP] + position[None, :] // N_DP) % DOCS_DEV
    labels = (owner_pick * DOCS_DEV + local_doc).reshape(QUERIES)
    full_shape = (QUERIES, LQ, K)
    block_start = jnp.arange(QUERIES) // QB * QB
    partner = block_start[:, None, None] + jax.random.randint(jax.random.fold_in(key, 102), full_shape, 0, QB)
    chooser = jax.random.randint(jax.random.fold_in(key, 103), full_shape, 0, 20)
    document = jnp.where(chooser < 10, labels[:, None, None], labels[partner])
    offset = jax.random.randint(jax.random.fold_in(key, 105), full_shape, 0, DOC_LEN)
    return (labels.astype(jnp.int32), (document * DOC_LEN + offset).astype(jnp.int32))


def draw_labels(key, part):
    labels, picked = retrieval_draw(key)
    return labels


def draw_chosen(key, part):
    labels, picked = retrieval_draw(key)
    return picked


def draw_lengths(key, part):
    key = jax.random.fold_in(key, 31)
    drawn_lengths = jax.random.randint(jax.random.fold_in(key, 1), (QUERIES,), LQ // 4, LQ + 1)
    longest = jax.random.randint(jax.random.fold_in(key, 2), (), 0, QUERIES)
    return jnp.where(jnp.arange(QUERIES) == longest, LQ, drawn_lengths).astype(jnp.int32)


def draw_slab_main(key, part):
    key = jax.random.fold_in(key, 11)
    full_shape = (N_SECTION, D, FF)
    column = jnp.arange(FF)[None, None, :]
    section_id = jnp.arange(N_SECTION)[:, None, None]
    head_width = H * DH
    attention_scale = jnp.where(column < head_width, (D * DH) ** (-0.5), jnp.where(column < 3 * head_width, D ** (-0.5), (head_width / 2.0) ** (-0.5)))
    column_scale = jnp.where(section_id % 2 == 0, attention_scale, D ** (-0.5))
    raw_noise = jnp.clip(jax.random.normal(key, full_shape, jnp.float32), -3.0, 3.0)
    return (raw_noise * column_scale).astype(jnp.bfloat16)


def draw_slab_side(key, part):
    key = jax.random.fold_in(key, 12)
    full_shape = (N_SECTION, D, FF)
    section_id = jnp.arange(N_SECTION)[:, None, None]
    column_scale = jnp.where(section_id % 2 == 0, D ** (-0.5), 1.5 * FF ** (-0.5))
    raw_noise = jnp.clip(jax.random.normal(key, full_shape, jnp.float32), -3.0, 3.0)
    return (raw_noise * column_scale).astype(jnp.bfloat16)


def level_of(key, dims, shards, low, largest):
    def one(dim, parts):
        steps = jax.random.uniform(jax.random.fold_in(jax.random.fold_in(key, 6), dim), (parts,), jnp.float32, low / len(shards), largest / len(shards))
        return jnp.repeat(jnp.exp(steps), dims[dim] // parts).reshape((-1,) + (1,) * (len(dims) - dim - 1))

    factor_of = one(*shards[0])
    for cut in shards[1:]:
        factor_of = factor_of * one(*cut)
    return factor_of


def scatter_about(own_key, dims, scale, bound, cuts=(), kind=jnp.bfloat16):
    factor_of = level_of(own_key, dims, cuts, -0.22, 0.18) if cuts else 1.0
    result = jax.random.normal(own_key, dims, jnp.float32) * scale * factor_of
    return jnp.minimum(jnp.maximum(result, -bound), bound).astype(kind)


def setup_inputs(seed: int = 0) -> dict:
    key_of = jax.random.split(jax.random.key(seed), 12)
    hidden_in = scatter_about(key_of[0], (QUERIES, LQ, D), 1.0, 6.0, ((0, 32),))
    lengths = draw_lengths(jax.random.fold_in(key_of[11], 71), 0)
    labels = draw_labels(jax.random.fold_in(key_of[11], 71), 0)
    chosen = draw_chosen(jax.random.fold_in(key_of[11], 71), 0)
    slab_main = draw_slab_main(jax.random.fold_in(key_of[11], 71), 0)
    slab_side = draw_slab_side(jax.random.fold_in(key_of[11], 71), 0)
    section_gains = jnp.clip(1.0 + 0.1 * jax.random.normal(key_of[6], (N_SECTION, D), jnp.float32), 0.5, 1.5)
    rel_bias = scatter_about(key_of[7], (BUCKETS, H), 0.5, 3.0, (), jnp.float32)
    final_gain = jnp.clip(1.0 + 0.1 * jax.random.normal(key_of[8], (D,), jnp.float32), 0.5, 1.5)
    out_proj = scatter_about(key_of[9], (D, PROJ), (D * PROJ) ** -0.5, 0.01953125)
    doc_vectors = scatter_about(key_of[10], (DOC_TOKENS, PROJ), 0.5, 3.0, ((0, 8),))
    return dict(hidden_in=hidden_in, lengths=lengths, labels=labels, chosen=chosen, slab_main=slab_main, slab_side=slab_side, section_gains=section_gains, rel_bias=rel_bias, final_gain=final_gain, out_proj=out_proj, doc_vectors=doc_vectors)


EPS_NORM = 1e-06
MASK_FILL = -1000000000.0
HIGHEST = lax.Precision.HIGHEST

@jax.custom_vjp
def low(v):
    return lax.optimization_barrier(v.astype(jnp.bfloat16)).astype(jnp.float32)

@jax.custom_vjp
def low_back(v):
    return v

def low_keep(v):
    return (low(v), None)

def low_pass(kept, grad):
    return (grad,)

def back_keep(v):
    return (v, None)

def back_low(kept, grad):
    return (low(grad),)
low.defvjp(low_keep, low_pass)
low_back.defvjp(back_keep, back_low)

def bucket_onehot(query_len):
    places = np.arange(query_len)
    relative = places[None, :] - places[:, None]
    distance = np.abs(relative)
    signed_part = np.where(relative > 0, 16, 0)
    far_bucket = 8 + np.floor(np.log(np.maximum(distance, 1) / 8.0) / np.log(16.0) * 8.0).astype(np.int64)
    far_bucket = np.minimum(far_bucket, 15)
    buckets = signed_part + np.where(distance < 8, distance, far_bucket)
    return (buckets[:, :, None] == np.arange(32)[None, None, :]).astype(np.float32)

def rms_scale(values, gain_vec):
    return values * lax.rsqrt(lax.optimization_barrier(jnp.mean(values * values, axis=-1, keepdims=True)) + EPS_NORM) * gain_vec

def attention_half(states, weight_main, section_gain, bias_table, lens_now):
    batch_size = states.shape[0]
    head_width = H * DH
    normed = low(rms_scale(states, section_gain))
    projected = low(low_back(jnp.einsum('bld,de->ble', normed, weight_main[:, :3 * head_width], precision=HIGHEST)))
    queries = projected[..., :head_width].reshape(batch_size, LQ, H, DH)
    keys_part = projected[..., head_width:2 * head_width].reshape(batch_size, LQ, H, DH)
    values_part = projected[..., 2 * head_width:].reshape(batch_size, LQ, H, DH)
    raw_scores = low_back(jnp.einsum('bihd,bjhd->bhij', queries, keys_part, precision=HIGHEST))
    onehot = jnp.asarray(bucket_onehot(LQ))
    position_bias = jnp.einsum('ijc,ch->hij', onehot, bias_table, precision=HIGHEST)
    live_keys = jnp.arange(LQ)[None, :] < lens_now[:, None]
    scores = jnp.where(live_keys[:, None, None, :], raw_scores + position_bias[None], MASK_FILL)
    maximum_score = lax.optimization_barrier(jnp.max(scores, axis=-1, keepdims=True))
    exp_scores = jnp.exp(scores - maximum_score)
    soft_weights = low(exp_scores / lax.optimization_barrier(jnp.sum(exp_scores, axis=-1, keepdims=True)))
    context = jnp.einsum('bhij,bjhd->bihd', soft_weights, values_part, precision=HIGHEST).reshape(batch_size, LQ, head_width)
    context = low(low_back(context))
    branch_out = low_back(jnp.einsum('blc,dc->bld', context, weight_main[:, 3 * head_width:], precision=HIGHEST))
    return states + branch_out

def ffn_half(states, weight_main, weight_lent, weight_side, section_gain):
    normed = low(rms_scale(states, section_gain))
    gate_vals = low_back(jnp.einsum('bld,df->blf', normed, weight_main, precision=HIGHEST))
    up_vals = low_back(jnp.einsum('bld,df->blf', normed, weight_lent, precision=HIGHEST))
    hidden = low(jax.nn.gelu(gate_vals, approximate=True) * up_vals)
    branch_out = low_back(jnp.einsum('blf,df->bld', hidden, weight_side, precision=HIGHEST))
    return states + branch_out

def final_units(states, final_gain, out_proj):
    normed = low(rms_scale(states, final_gain))
    projected = low_back(jnp.einsum('bld,dp->blp', normed, out_proj, precision=HIGHEST))
    return low(projected * lax.rsqrt(lax.optimization_barrier(jnp.sum(projected * projected, axis=-1, keepdims=True)) + EPS_NORM))

def loss_from_scores(similarity, hit_table, lens_now):
    imputed = lax.optimization_barrier(jnp.mean(similarity, axis=-1))
    token_mass = jnp.exp(imputed)[..., None] + jnp.einsum('blk,blkc->blc', jnp.exp(similarity), hit_table, precision=HIGHEST)
    token_scores = jnp.log(token_mass)
    live_slots = (jnp.arange(LQ)[None, :] < lens_now[:, None]).astype(similarity.dtype)
    doc_scores = lax.optimization_barrier(jnp.sum(live_slots[:, :, None] * token_scores, axis=1)) / lens_now[:, None].astype(similarity.dtype)
    maximum_score = lax.optimization_barrier(jnp.max(doc_scores, axis=-1, keepdims=True))
    log_total = maximum_score[:, 0] + jnp.log(lax.optimization_barrier(jnp.sum(jnp.exp(doc_scores - maximum_score), axis=-1)))
    return log_total - jnp.diagonal(doc_scores)

def block_objective(hidden, weight_main, weight_side, section_gains, bias_table, final_gain, out_proj, lens_now, doc_rows, chosen_now, labels_now):
    states = hidden
    for section_id in range(N_SECTION):
        if section_id % 2 == 0:
            states = attention_half(states, weight_main[section_id], section_gains[section_id], bias_table, lens_now)
        else:
            states = ffn_half(states, weight_main[section_id], weight_side[section_id - 1], weight_side[section_id], section_gains[section_id])
        if section_id + 1 < N_SECTION:
            states = low(states)
    unit_values = final_units(states, final_gain, out_proj)
    similarity = lax.optimization_barrier(jnp.sum(unit_values[:, :, None, :] * doc_rows, axis=-1))
    hit_table = ((chosen_now // DOC_LEN)[..., None] == labels_now[None, None, None, :]).astype(similarity.dtype)
    losses = loss_from_scores(similarity, hit_table, lens_now)
    return (jnp.sum(losses), (unit_values, losses))

def reference(hidden_in, lengths, labels, chosen, slab_main, slab_side, section_gains, rel_bias, final_gain, out_proj, doc_vectors):
    blocks = QUERIES // QB
    weight_main = slab_main.astype(jnp.float32)
    weight_side = slab_side.astype(jnp.float32)
    proj_full = out_proj.astype(jnp.float32)
    docs_full = doc_vectors.astype(jnp.float32)
    inputs = (hidden_in.astype(jnp.float32).reshape(blocks, QB, LQ, D), lengths.reshape(blocks, QB), labels.reshape(blocks, QB), chosen.reshape(blocks, QB, LQ, K))

    def one_block(totals, pieces):
        hidden, lens_now, labels_now, chosen_now = pieces
        doc_rows = docs_full[chosen_now]

        def objective(hidden_arg, main_arg, side_arg, gains_arg, table_arg, fgain_arg, proj_arg):
            return block_objective(hidden_arg, main_arg, side_arg, gains_arg, table_arg, fgain_arg, proj_arg, lens_now, doc_rows, chosen_now, labels_now)
        total_loss, pullback, extras = jax.vjp(objective, hidden, weight_main, weight_side, section_gains, rel_bias, final_gain, proj_full, has_aux=True)
        gradients = pullback(jnp.ones((), total_loss.dtype))
        new_totals = tuple((running + addend for running, addend in zip(totals, gradients[1:])))
        return (new_totals, (gradients[0], extras[0], extras[1]))
    zero_start = tuple((jnp.zeros_like(member) for member in (weight_main, weight_side, section_gains, rel_bias, final_gain, proj_full)))
    totals, (in_grads, unit_values, losses) = lax.scan(one_block, zero_start, inputs)
    return (unit_values.reshape(QUERIES, LQ, PROJ).astype(jnp.bfloat16), losses.reshape(QUERIES), in_grads.reshape(QUERIES, LQ, D), totals[0], totals[1], totals[2], totals[3], totals[4], totals[5])
```

```python
import functools
import math

import jax
import jax.numpy as jnp
import numpy as np
from jax import lax
from jax.experimental import pallas as pl
from jax.experimental.pallas import tpu as pltpu
from jax.sharding import PartitionSpec as P

H = 12
DH = 64
DOC_LEN = 128
EPS_NORM = 1e-06
MASK_FILL = -1000000000.0
HIGHEST = lax.Precision.HIGHEST
MESH = pl.DeviceIdType.MESH
F32 = jnp.float32
BF16 = jnp.bfloat16
VMEM = pltpu.VMEM
GELU_C = math.sqrt(2.0 / math.pi)
GELU_A = 0.044715
FF_STEP = 512
LEND_STEP = 128


def bucket_table(query_len):
    places = np.arange(query_len)
    relative = places[None, :] - places[:, None]
    distance = np.abs(relative)
    signed_part = np.where(relative > 0, 16, 0)
    far_bucket = 8 + np.floor(np.log(np.maximum(distance, 1) / 8.0) / np.log(16.0) * 8.0).astype(
        np.int64
    )
    far_bucket = np.minimum(far_bucket, 15)
    return (signed_part + np.where(distance < 8, distance, far_bucket)).astype(np.int32)


def nn(a, b):
    return jnp.dot(a, b, preferred_element_type=F32)


def nt(a, b):
    return lax.dot_general(a, b, (((1,), (1,)), ((), ())), preferred_element_type=F32)


def tn(a, b):
    return lax.dot_general(a, b, (((0,), (0,)), ((), ())), preferred_element_type=F32)


def rms_inverse(values):
    return lax.rsqrt(jnp.mean(values * values, axis=-1, keepdims=True) + EPS_NORM)


def rms_back(scaled, inverse, gain, grad):
    inner = grad * gain
    grad_values = inverse * (inner - scaled * jnp.mean(inner * scaled, axis=-1, keepdims=True))
    return grad_values, jnp.sum(grad * scaled, axis=0, keepdims=True)


def relay_kernel(
    sections,
    dp_size,
    batch_size,
    retrieved,
    hid_ref,
    meta_ref,
    idx_ref,
    lab_ref,
    main_ref,
    side_ref,
    gain_ref,
    bias_ref,
    bucket_ref,
    fgain_ref,
    proj_ref,
    docs_ref,
    units_ref,
    loss_ref,
    dx_ref,
    l1_ref,
    r1_ref,
    l2_ref,
    l3_ref,
    r3_ref,
    dgain_ref,
    dbias_ref,
    dfgain_ref,
    dproj_ref,
    lent,
    xin,
    xout,
    dyin,
    meta_rx,
    idx_rx,
    lab_rx,
    own_docs,
    table,
    counts,
    act_b,
    n_t,
    qkv,
    probs,
    bias_sc,
    fin_rx,
    unit_tx,
    unit_rx,
    loss_tx,
    loss_rx,
    state_ss,
    state_rs,
    grad_ss,
    grad_rs,
    meta_ss,
    meta_rs,
    idx_ss,
    idx_rs,
    lab_ss,
    lab_rs,
    tab_ss,
    tab_rs,
    lend_ss,
    lend_rs,
    fin_ss,
    fin_rs,
    unit_ss,
    unit_rs,
    loss_ss,
    loss_rs,
    up_ss,
    up_rs,
    nt_ss,
    nt_rs,
):
    s = lax.axis_index("section")
    d = lax.axis_index("dp")
    rows, width = hid_ref.shape
    ff = main_ref.shape[1]
    head_width = H * DH
    doc_rows = docs_ref.shape[0]
    query_len = rows // batch_size
    last = sections - 1
    group = d - lax.rem(d, 4)
    place = lax.rem(d, 4)
    core_peer = group + place + 1 - 2 * lax.rem(place, 2)
    far_place = lax.rem(place + 2, 4)
    far_peer = group + far_place
    is_attention = lax.rem(s, 2) == 0

    def copy(src, dst, send_sem, recv_sem, section, dp):
        return pltpu.make_async_remote_copy(
            src_ref=src,
            dst_ref=dst,
            send_sem=send_sem,
            recv_sem=recv_sem,
            device_id=(section, dp),
            device_id_type=MESH,
        )

    def block(m):
        return pl.ds(pl.multiple_of(m * rows, rows), rows)

    barrier = pltpu.get_barrier_semaphore()
    for step in range(1, sections):
        pl.semaphore_signal(
            barrier, inc=1, device_id=(lax.rem(s + step, sections), d), device_id_type=MESH
        )

    def greet(step, carry):
        pl.semaphore_signal(
            barrier, inc=1, device_id=(s, lax.rem(d + step, dp_size)), device_id_type=MESH
        )
        return carry

    lax.fori_loop(1, dp_size, greet, 0)
    pl.semaphore_wait(barrier, sections - 1 + dp_size - 1)

    def lend_columns(quarter, part):
        start = quarter * (ff // 4) + part * LEND_STEP
        return pl.ds(pl.multiple_of(start, LEND_STEP), LEND_STEP)

    parts = ff // 4 // LEND_STEP

    def lend_copy(part):
        columns = lend_columns(place, part)
        return copy(
            side_ref.at[:, columns],
            lent.at[:, columns],
            lend_ss.at[0, part],
            lend_rs.at[0, part],
            lax.rem(s + 1, sections),
            d,
        )

    def lend_forward(kind, quarter, part, peer):
        columns = lend_columns(quarter, part)
        return copy(
            lent.at[:, columns],
            lent.at[:, columns],
            lend_ss.at[kind, part],
            lend_rs.at[kind, part],
            s,
            peer,
        )

    def state_copy(m):
        return copy(
            xout.at[m], xin.at[m], state_ss.at[m], state_rs.at[m], lax.rem(s + 1, sections), d
        )

    def grad_copy(m):
        return copy(
            xout.at[m],
            dyin.at[m],
            grad_ss.at[m],
            grad_rs.at[m],
            lax.rem(s + sections - 1, sections),
            d,
        )

    def up_copy(m):
        return copy(
            act_b.at[block(m), :],
            r3_ref.at[block(m), :],
            up_ss.at[m],
            up_rs.at[m],
            lax.rem(s + sections - 1, sections),
            d,
        )

    def normed_copy(m):
        return copy(
            n_t.at[:, block(m)],
            l3_ref.at[:, block(m)],
            nt_ss.at[m],
            nt_rs.at[m],
            lax.rem(s + sections - 1, sections),
            d,
        )

    def meta_copy(to, slot):
        return copy(meta_ref, meta_rx.at[slot], meta_ss.at[to], meta_rs.at[slot], to, d)

    def idx_copy(slot):
        return copy(idx_ref, idx_rx.at[slot], idx_ss, idx_rs.at[slot], last, d)

    def lab_copy(slot):
        return copy(lab_ref, lab_rx.at[slot], lab_ss, lab_rs.at[slot], last, d)

    def hid_copy(slot):
        return copy(hid_ref, xin.at[slot], state_ss.at[sections], state_rs.at[slot], 0, d)

    def unit_copy(m, to):
        return copy(unit_tx.at[m], unit_rx, unit_ss.at[m], unit_rs, to, d)

    def loss_copy(m, to):
        return copy(loss_tx.at[m], loss_rx, loss_ss.at[m], loss_rs, to, d)

    def fin_copy(m, to):
        return copy(xout.at[m], fin_rx, fin_ss.at[m], fin_rs, to, d)

    def table_rows(owner):
        return pl.ds(pl.multiple_of(owner * doc_rows, doc_rows), doc_rows)

    def table_copy(to):
        return copy(docs_ref, table.at[table_rows(d), :], tab_ss.at[to], tab_rs.at[d], s, to)

    @pl.when(s != 0)
    def _():
        hid_copy(s).start()

    @pl.when(s == 0)
    def _():
        xin[0] = hid_ref[...]

    for to in range(sections):

        @pl.when(s != to)
        def _():
            meta_copy(to, s).start()

    meta_rx[s] = meta_ref[...]

    @pl.when(s != last)
    def _():
        idx_copy(s).start()
        lab_copy(s).start()

    @pl.when(is_attention)
    def _():
        for part in range(parts):
            lend_copy(part).start()

    dgain_ref[...] = jnp.zeros_like(dgain_ref)
    dfgain_ref[...] = jnp.zeros_like(dfgain_ref)
    dproj_ref[...] = jnp.zeros_like(dproj_ref)
    dbias_ref[...] = jnp.zeros_like(dbias_ref)

    gain = gain_ref[...]

    def wait_meta(m):
        @pl.when(m != s)
        def _():
            meta_copy(0, m).wait_recv()

    def load_state(m):
        states = xin[m].astype(F32)
        inverse = rms_inverse(states)
        return states, inverse, states * inverse

    lane = lax.broadcasted_iota(jnp.int32, (1, 128), 1)
    low_half = lane < DH

    def half_of(value, upper):
        keep = jnp.logical_not(low_half) if upper else low_half
        return jnp.where(keep, value.astype(F32), 0.0).astype(BF16)

    def attention_setup():
        buckets = bucket_ref[...]
        for h in range(H):
            total = jnp.zeros(buckets.shape, F32)
            for b in range(32):
                total = jnp.where(buckets == b, bias_ref[b, h], total)
            bias_sc[h] = total

    def attention_forward(m):
        states, inverse, scaled = load_state(m)
        normed = scaled * gain
        l1_ref[:, block(m)] = normed.T.astype(BF16)
        normed_low = normed.astype(BF16)
        for start in range(0, 3 * head_width, head_width):
            qkv[block(m), start : start + head_width] = nn(
                normed_low, main_ref[:, start : start + head_width]
            ).astype(BF16)
        live = meta_rx[m, 0:1, :] > 0.5
        row_query = lax.broadcasted_iota(jnp.int32, (rows, rows), 0) // query_len
        column_query = lax.broadcasted_iota(jnp.int32, (rows, rows), 1) // query_len
        keep = jnp.logical_and(row_query == column_query, live)
        for pair in range(H // 2):
            at = pair * 128
            query = qkv[block(m), at : at + 128]
            keys = qkv[block(m), head_width + at : head_width + at + 128]
            values = qkv[block(m), 2 * head_width + at : 2 * head_width + at + 128]
            contexts = []
            for upper in (0, 1):
                h = 2 * pair + upper
                raw = nt(half_of(query, upper), keys)
                biased = raw.reshape(batch_size, query_len, rows) + bias_sc[h][None]
                scores = jnp.where(keep, biased.reshape(rows, rows), MASK_FILL)
                top = jnp.max(scores, axis=-1, keepdims=True)
                grown = jnp.exp(scores - top)
                soft = grown / jnp.sum(grown, axis=-1, keepdims=True)
                probs[m, h] = soft
                contexts.append(nn(soft.astype(BF16), values))
            r1_ref[block(m), 3 * head_width + at : 3 * head_width + at + 128] = jnp.where(
                low_half, contexts[0], contexts[1]
            ).astype(BF16)
        context = r1_ref[block(m), 3 * head_width :]
        return states + nt(context, main_ref[:, 3 * head_width :])

    def attention_backward(m):
        states, inverse, scaled = load_state(m)
        grad_low = dyin[m]
        grad = grad_low.astype(F32)
        l2_ref[:, block(m)] = grad.T.astype(BF16)
        grad_context = nn(grad_low, main_ref[:, 3 * head_width :]).astype(BF16)
        for pair in range(H // 2):
            at = pair * 128
            query = qkv[block(m), at : at + 128]
            keys = qkv[block(m), head_width + at : head_width + at + 128]
            values = qkv[block(m), 2 * head_width + at : 2 * head_width + at + 128]
            grad_pair = grad_context[:, at : at + 128]
            found = []
            for upper in (0, 1):
                h = 2 * pair + upper
                soft = probs[m, h]
                grad_soft = nt(half_of(grad_pair, upper), values)
                moved = soft * grad_soft
                grad_scores = moved - soft * jnp.sum(moved, axis=-1, keepdims=True)
                dbias_ref[h] += jnp.sum(
                    grad_scores.reshape(batch_size, query_len, rows), axis=0
                )
                scores_low = grad_scores.astype(BF16)
                found.append(
                    (
                        nn(scores_low, keys),
                        tn(scores_low, query),
                        tn(soft.astype(BF16), grad_pair),
                    )
                )
            for third in range(3):
                start = third * head_width + at
                r1_ref[block(m), start : start + 128] = jnp.where(
                    low_half, found[0][third], found[1][third]
                ).astype(BF16)
        grad_normed = nt(r1_ref[block(m), : 3 * head_width], main_ref[:, : 3 * head_width])
        grad_states, grad_gain = rms_back(scaled, inverse, gain, grad_normed)
        dgain_ref[...] += grad_gain
        return grad + grad_states

    def ffn_forward(m):
        states, inverse, scaled = load_state(m)
        normed = scaled * gain
        turned = normed.T.astype(BF16)
        l1_ref[:, block(m)] = turned
        l2_ref[:, block(m)] = turned
        n_t[:, block(m)] = turned
        normed_copy(m).start()
        normed_low = normed.astype(BF16)
        outputs = states
        for start in range(0, ff, FF_STEP):
            columns = slice(start, start + FF_STEP)
            gate = nn(normed_low, main_ref[:, columns])
            up = nn(normed_low, lent[:, columns])
            square = gate * gate
            bent = jnp.tanh(GELU_C * gate * (1.0 + GELU_A * square))
            half = 0.5 * (1.0 + bent)
            smooth = gate * half
            slope = half + 0.5 * gate * (1.0 - bent * bent) * (
                GELU_C * (1.0 + 3.0 * GELU_A * square)
            )
            hidden = (smooth * up).astype(BF16)
            r3_ref[block(m), columns] = hidden
            r1_ref[block(m), columns] = (slope * up).astype(BF16)
            act_b[block(m), columns] = smooth.astype(BF16)
            outputs = outputs + nt(hidden, side_ref[:, columns])
        return outputs

    def ffn_backward(m, grad):
        states, inverse, scaled = load_state(m)
        grad_low = grad.astype(BF16)
        l3_ref[:, block(m)] = grad.T.astype(BF16)
        grad_normed = jnp.zeros((rows, width), F32)
        for start in range(0, ff, FF_STEP):
            columns = slice(start, start + FF_STEP)
            grad_hidden = nn(grad_low, side_ref[:, columns])
            grad_gate = (grad_hidden * r1_ref[block(m), columns].astype(F32)).astype(BF16)
            grad_up = (grad_hidden * act_b[block(m), columns].astype(F32)).astype(BF16)
            r1_ref[block(m), columns] = grad_gate
            act_b[block(m), columns] = grad_up
            grad_normed = (
                grad_normed
                + nt(grad_gate, main_ref[:, columns])
                + nt(grad_up, lent[:, columns])
            )
        up_copy(m).start()
        grad_states, grad_gain = rms_back(scaled, inverse, gain, grad_normed)
        dgain_ref[...] += grad_gain
        return grad + grad_states

    def count_hits(m):
        for c in range(batch_size):
            base = lab_rx[m, c : c + 1, :] * DOC_LEN
            numbers = lax.broadcasted_iota(jnp.int32, (DOC_LEN, rows), 0) + base
            total = jnp.zeros((DOC_LEN, rows), F32)
            for k in range(retrieved):
                total = total + jnp.where(idx_rx[m, k : k + 1, :] == numbers, 1.0, 0.0)
            counts[m, c * DOC_LEN : (c + 1) * DOC_LEN, :] = total

    def pick_docs(m):
        for c in range(batch_size):
            label = lab_rx[m, c : c + 1, :]

            def pick(t, picked):
                here = table[pl.ds(pl.multiple_of(t * DOC_LEN, DOC_LEN), DOC_LEN), :].astype(F32)
                return jnp.where(label == t, here, picked)

            picked = lax.fori_loop(
                0, table.shape[0] // DOC_LEN, pick, jnp.zeros((DOC_LEN, table.shape[1]), F32)
            )
            own_docs[m, c * DOC_LEN : (c + 1) * DOC_LEN, :] = picked.astype(BF16)

    def loss_and_grad(m, unit):
        docs = own_docs[m]
        sims = nt(docs, unit)
        count = counts[m]
        imputed = jnp.sum(count * sims, axis=0, keepdims=True) / retrieved
        grown = count * jnp.exp(sims)
        imputed_mass = jnp.exp(imputed)
        mass = imputed_mass + jnp.concatenate(
            [
                jnp.sum(grown[c * DOC_LEN : (c + 1) * DOC_LEN], axis=0, keepdims=True)
                for c in range(batch_size)
            ],
            axis=0,
        )
        weighted = jnp.log(mass) * meta_rx[m, 1:2, :]
        token_query = lax.broadcasted_iota(jnp.int32, (1, rows), 1) // query_len
        candidate = lax.broadcasted_iota(jnp.int32, (batch_size, 1), 0)
        losses = jnp.zeros((1, rows), F32)
        grad_tokens = jnp.zeros((batch_size, rows), F32)
        for q in range(batch_size):
            own = token_query == q
            score = jnp.sum(jnp.where(own, weighted, 0.0), axis=1, keepdims=True)
            top = jnp.max(score, axis=0, keepdims=True)
            risen = jnp.exp(score - top)
            total = jnp.sum(risen, axis=0, keepdims=True)
            chosen_one = (candidate == q).astype(F32)
            loss = top + jnp.log(total) - jnp.sum(score * chosen_one, axis=0, keepdims=True)
            losses = losses + jnp.where(lane == q, loss, 0.0)
            grad_tokens = grad_tokens + jnp.where(own, risen / total - chosen_one, 0.0)
        grad_mass = grad_tokens * meta_rx[m, 1:2, :] / mass
        shared = jnp.sum(grad_mass, axis=0, keepdims=True) * imputed_mass / retrieved
        grad_sims = count * shared + jnp.concatenate(
            [
                grown[c * DOC_LEN : (c + 1) * DOC_LEN] * grad_mass[c : c + 1]
                for c in range(batch_size)
            ],
            axis=0,
        )
        high = grad_sims.astype(BF16)
        rest = (grad_sims - high.astype(F32)).astype(BF16)
        return losses, tn(high, docs) + tn(rest, docs)

    def finish(m, states):
        inverse = rms_inverse(states)
        scaled = states * inverse
        normed = (scaled * fgain_ref[...]).astype(BF16)
        projected = nn(normed, proj_ref[...])
        length = lax.rsqrt(jnp.sum(projected * projected, axis=-1, keepdims=True) + EPS_NORM)
        exact = projected * length
        unit = exact.astype(BF16)
        losses, grad_unit = loss_and_grad(m, unit)
        unit_tx[m] = unit
        loss_tx[m] = jnp.broadcast_to(losses, loss_tx.shape[1:])

        @pl.when(m != last)
        def _():
            unit_copy(m, m).start()
            loss_copy(m, m).start()

        @pl.when(m == last)
        def _():
            units_ref[...] = unit_tx[last]
            loss_ref[...] = loss_tx[last]

        grad_projected = (
            length * (grad_unit - exact * jnp.sum(grad_unit * exact, axis=-1, keepdims=True))
        ).astype(BF16)
        dproj_ref[...] += tn(normed, grad_projected)
        grad_normed = nt(grad_projected, proj_ref[...])
        grad_states, grad_gain = rms_back(scaled, inverse, fgain_ref[...], grad_normed)
        dfgain_ref[...] += grad_gain
        return grad_states

    def loop(body):
        def step(m, carry):
            body(m)
            return carry

        lax.fori_loop(0, sections, step, 0)

    def wait_state(m):
        @pl.when(jnp.logical_or(s != 0, m != 0))
        def _():
            state_copy(m).wait_recv()

    @pl.when(is_attention)
    def _():
        attention_setup()

        def forward(m):
            wait_meta(m)
            wait_state(m)
            xout[m] = attention_forward(m).astype(BF16)
            state_copy(m).start()

        loop(forward)
        loop(lambda m: state_copy(m).wait_send())

        def backward(m):
            grad_copy(m).wait_recv()
            result = attention_backward(m)
            xout[m] = result.astype(BF16)

            @pl.when(s != 0)
            def _():
                grad_copy(m).start()

            @pl.when(jnp.logical_and(s == 0, m != 0))
            def _():
                fin_copy(m, m).start()

            @pl.when(jnp.logical_and(s == 0, m == 0))
            def _():
                dx_ref[...] = xout[0].astype(F32)

        loop(backward)

        @pl.when(s != 0)
        def _():
            loop(lambda m: grad_copy(m).wait_send())

        @pl.when(s == 0)
        def _():
            for m in range(1, sections):
                fin_copy(m, m).wait_send()

        for part in range(parts):
            lend_copy(part).wait_send()
        loop(lambda m: normed_copy(m).wait_recv())
        loop(lambda m: up_copy(m).wait_recv())

    @pl.when(jnp.logical_not(is_attention))
    def _():
        for part in range(parts):
            lend_copy(part).wait_recv()
            lend_forward(1, place, part, core_peer).start()
            lend_forward(2, place, part, far_peer).start()

        @pl.when(s == last)
        def _():
            idx_rx[last] = idx_ref[...]
            lab_rx[last] = lab_ref[...]
            table[table_rows(d), :] = docs_ref[...]

            def send_table(step, carry):
                table_copy(lax.rem(d + step, dp_size)).start()
                return carry

            lax.fori_loop(1, dp_size, send_table, 0)

            def prepare(m):
                @pl.when(m != last)
                def _():
                    idx_copy(m).wait_recv()
                    lab_copy(m).wait_recv()

                count_hits(m)

            loop(prepare)

        for part in range(parts):
            lend_forward(2, far_place, part, far_peer).wait_recv()
            lend_forward(3, far_place, part, core_peer).start()
        for part in range(parts):
            lend_forward(1, place, part, core_peer).wait_recv()
            lend_forward(3, far_place, part, core_peer).wait_recv()

        @pl.when(s == last)
        def _():
            def take_table(step, carry):
                owner = lax.rem(d + step, dp_size)
                copy(
                    docs_ref,
                    table.at[table_rows(owner), :],
                    tab_ss.at[owner],
                    tab_rs.at[owner],
                    s,
                    owner,
                ).wait_recv()
                return carry

            lax.fori_loop(1, dp_size, take_table, 0)
            loop(pick_docs)
            loop(wait_meta)

            def both(m):
                wait_state(m)
                states = ffn_forward(m)
                grad = finish(m, states)
                xout[m] = ffn_backward(m, grad).astype(BF16)
                grad_copy(m).start()

            loop(both)
            loop(lambda m: grad_copy(m).wait_send())
            for m in range(sections - 1):
                unit_copy(m, m).wait_send()
                loss_copy(m, m).wait_send()

            def drain_table(step, carry):
                table_copy(lax.rem(d + step, dp_size)).wait_send()
                return carry

            lax.fori_loop(1, dp_size, drain_table, 0)

        @pl.when(s != last)
        def _():
            def forward(m):
                wait_state(m)
                xout[m] = ffn_forward(m).astype(BF16)
                state_copy(m).start()

            loop(forward)
            loop(lambda m: state_copy(m).wait_send())

            def backward(m):
                grad_copy(m).wait_recv()
                xout[m] = ffn_backward(m, dyin[m].astype(F32)).astype(BF16)
                grad_copy(m).start()

            loop(backward)
            loop(lambda m: grad_copy(m).wait_send())
            loop(wait_meta)

        loop(lambda m: normed_copy(m).wait_send())
        loop(lambda m: up_copy(m).wait_send())
        for part in range(parts):
            lend_forward(1, place, part, core_peer).wait_send()
            lend_forward(2, place, part, far_peer).wait_send()
            lend_forward(3, far_place, part, core_peer).wait_send()

    for to in range(sections):

        @pl.when(s != to)
        def _():
            meta_copy(to, s).wait_send()

    @pl.when(s != 0)
    def _():
        hid_copy(s).wait_send()
        fin_copy(0, s).wait_recv()
        dx_ref[...] = fin_rx[...].astype(F32)

    @pl.when(s != last)
    def _():
        idx_copy(s).wait_send()
        lab_copy(s).wait_send()
        unit_copy(0, s).wait_recv()
        loss_copy(0, s).wait_recv()
        units_ref[...] = unit_rx[...]
        loss_ref[...] = loss_rx[...]


def relay(
    sections, dp_size, batch_size, retrieved, hid, meta, idx, lab, main, side, gain, bias, buckets,
    fgain, proj, docs
):
    rows, width = hid.shape
    ff = main.shape[1]
    total = sections * rows
    vector = proj.shape[1]
    query_len = rows // batch_size
    parts = ff // 4 // LEND_STEP
    dma = pltpu.SemaphoreType.DMA
    in_vmem = pl.BlockSpec(memory_space=VMEM)
    shape = jax.ShapeDtypeStruct
    out_shape = (
        shape((rows, vector), BF16),
        shape((8, rows), F32),
        shape((rows, width), F32),
        shape((width, total), BF16),
        shape((total, ff), BF16),
        shape((width, total), BF16),
        shape((width, total), BF16),
        shape((total, ff), BF16),
        shape((1, width), F32),
        shape((H, query_len, rows), F32),
        shape((1, width), F32),
        shape((width, vector), F32),
    )
    scratch = [
        VMEM((width, ff), BF16),
        VMEM((sections, rows, width), BF16),
        VMEM((sections, rows, width), BF16),
        VMEM((sections, rows, width), BF16),
        VMEM((sections, 8, rows), F32),
        VMEM((sections, retrieved, rows), jnp.int32),
        VMEM((sections, 8, 128), jnp.int32),
        VMEM((sections, batch_size * DOC_LEN, vector), BF16),
        VMEM((dp_size * docs.shape[0], vector), BF16),
        VMEM((sections, batch_size * DOC_LEN, rows), F32),
        VMEM((total, ff), BF16),
        VMEM((width, total), BF16),
        VMEM((total, 3 * H * DH), BF16),
        VMEM((sections, H, rows, rows), F32),
        VMEM((H, query_len, rows), F32),
        VMEM((rows, width), BF16),
        VMEM((sections, rows, vector), BF16),
        VMEM((rows, vector), BF16),
        VMEM((sections, 8, rows), F32),
        VMEM((8, rows), F32),
        dma((sections + 1,)),
        dma((sections,)),
        dma((sections,)),
        dma((sections,)),
        dma((sections,)),
        dma((sections,)),
        dma,
        dma((sections,)),
        dma,
        dma((sections,)),
        dma((dp_size,)),
        dma((dp_size,)),
        dma((4, parts)),
        dma((4, parts)),
        dma((sections,)),
        dma,
        dma((sections,)),
        dma,
        dma((sections,)),
        dma,
        dma((sections,)),
        dma((sections,)),
        dma((sections,)),
        dma((sections,)),
    ]
    in_specs = [in_vmem] * 12
    in_specs[7] = pl.BlockSpec(memory_space=pltpu.SMEM)
    return pl.pallas_call(
        functools.partial(relay_kernel, sections, dp_size, batch_size, retrieved),
        out_shape=out_shape,
        in_specs=in_specs,
        out_specs=(in_vmem,) * len(out_shape),
        scratch_shapes=scratch,
        compiler_params=pltpu.CompilerParams(
            collective_id=0, has_side_effects=True, vmem_limit_bytes=62 * 2**20
        ),
        name="relay",
    )(hid, meta, idx, lab, main, side, gain, bias, buckets, fgain, proj, docs)


def per_device(
    hidden_in,
    lengths,
    labels,
    chosen,
    slab_main,
    slab_side,
    section_gains,
    rel_bias,
    final_gain,
    out_proj,
    doc_vectors,
):
    sections = lax.axis_size("section")
    dp_size = lax.axis_size("dp")
    is_attention = lax.axis_index("section") % 2 == 0
    batch_size, query_len, width = hidden_in.shape
    rows = batch_size * query_len
    retrieved = chosen.shape[2]
    head_width = H * DH

    live = (jnp.arange(query_len)[None, :] < lengths[:, None]).astype(F32)
    per_slot = live / lengths[:, None].astype(F32)
    meta = jnp.concatenate(
        [live.reshape(1, rows), per_slot.reshape(1, rows), jnp.zeros((6, rows), F32)], axis=0
    )
    idx = chosen.reshape(rows, retrieved).T
    lab = jnp.broadcast_to(jnp.pad(labels, (0, 8 - batch_size))[:, None], (8, 128))
    buckets = jnp.asarray(np.tile(bucket_table(query_len), (1, batch_size)))
    (units, loss, input_grad, l1, r1, l2, l3, r3, gain_grad, bias_grad, fgain_grad, proj_grad) = relay(
        sections,
        dp_size,
        batch_size,
        retrieved,
        hidden_in.reshape(rows, width),
        meta,
        idx,
        lab,
        slab_main[0],
        slab_side[0],
        section_gains,
        rel_bias,
        buckets,
        final_gain.reshape(1, width),
        out_proj,
        doc_vectors,
    )
    main_grad = jnp.concatenate(
        [nn(l1, r1[:, : 3 * head_width]), nn(l2, r1[:, 3 * head_width :])], axis=1
    )
    side_grad = nn(l3, r3)
    main_part = lax.psum_scatter(main_grad, "dp", scatter_dimension=0, tiled=True)
    side_part = lax.psum_scatter(side_grad, "dp", scatter_dimension=0, tiled=True)
    gain_part = lax.psum_scatter(gain_grad[0], "dp", scatter_dimension=0, tiled=True)
    onehot = jnp.asarray(
        (bucket_table(query_len)[:, :, None] == np.arange(32)[None, None, :]).astype(np.float32)
    )
    folded = jnp.sum(bias_grad.reshape(H, query_len, batch_size, query_len), axis=2)
    table_grad = jnp.einsum("hij,ijc->ch", folded, onehot, precision=HIGHEST)
    table_sum, fgain_sum, proj_sum = lax.psum(
        (table_grad, fgain_grad[0], proj_grad), ("section", "dp")
    )
    return (
        units.reshape(batch_size, query_len, -1),
        loss[0, :batch_size],
        input_grad.reshape(batch_size, query_len, width),
        main_part[None],
        side_part[None],
        gain_part[None],
        table_sum,
        fgain_sum,
        proj_sum,
    )


def solution(mesh):
    both = ("section", "dp")
    in_specs = (
        P(both, None, None),
        P(both),
        P(both),
        P(both, None, None),
        P("section", None, None),
        P("section", None, None),
        P("section", None),
        P(),
        P(),
        P(),
        P("dp", None),
    )
    out_specs = (
        P(both, None, None),
        P(both),
        P(both, None, None),
        P("section", "dp", None),
        P("section", "dp", None),
        P("section", "dp"),
        P(),
        P(),
        P(),
    )
    return jax.shard_map(
        per_device, mesh=mesh, in_specs=in_specs, out_specs=out_specs, check_vma=False
    )
```

```python
import functools
import math
import types

import jax
import jax.numpy as jnp
import numpy as np
from jax import lax
from jax.experimental import pallas as pl
from jax.experimental.pallas import tpu as pltpu
from jax.sharding import PartitionSpec as P

H = 12
DH = 64
DOC_LEN = 128
EPS_NORM = 1e-06
MASK_FILL = -1000000000.0
HIGHEST = lax.Precision.HIGHEST
MESH = pl.DeviceIdType.MESH
F32 = jnp.float32
BF16 = jnp.bfloat16
VMEM = pltpu.VMEM
GELU_C = math.sqrt(2.0 / math.pi)
GELU_A = 0.044715
FF_STEP = 512
LEND_STEP = 128


def bucket_table(query_len):
    places = np.arange(query_len)
    relative = places[None, :] - places[:, None]
    distance = np.abs(relative)
    signed_part = np.where(relative > 0, 16, 0)
    far_bucket = 8 + np.floor(np.log(np.maximum(distance, 1) / 8.0) / np.log(16.0) * 8.0).astype(
        np.int64
    )
    far_bucket = np.minimum(far_bucket, 15)
    return (signed_part + np.where(distance < 8, distance, far_bucket)).astype(np.int32)


def nn(a, b):
    return jnp.dot(a, b, preferred_element_type=F32)


def nt(a, b):
    return lax.dot_general(a, b, (((1,), (1,)), ((), ())), preferred_element_type=F32)


def tn(a, b):
    return lax.dot_general(a, b, (((0,), (0,)), ((), ())), preferred_element_type=F32)


def rms_inverse(values):
    return lax.rsqrt(jnp.mean(values * values, axis=-1, keepdims=True) + EPS_NORM)


def rms_back(scaled, inverse, gain, grad):
    inner = grad * gain
    grad_values = inverse * (inner - scaled * jnp.mean(inner * scaled, axis=-1, keepdims=True))
    return grad_values, jnp.sum(grad * scaled, axis=0, keepdims=True)


def sum_order(line):
    orders = []
    for place in range(line):
        others = [j for j in range(line) if j != place]
        others.sort(key=lambda j: (-abs(j - place), min(j, line - 1 - j)))
        orders.append(others + [place])
    return orders


class Sizes:
    def __init__(self, sections, dp_size, batch_size, query_len, retrieved, width, ff, vector, doc_rows):
        self.sections = sections
        self.dp_size = dp_size
        self.batch_size = batch_size
        self.query_len = query_len
        self.retrieved = retrieved
        self.width = width
        self.ff = ff
        self.vector = vector
        self.doc_rows = doc_rows
        self.rows = batch_size * query_len
        self.total = sections * self.rows
        self.parts = ff // 4 // LEND_STEP
        self.share = width // dp_size
        self.summed = self.share % 16 == 0 and dp_size % 2 == 0
        self.line = dp_size // 2
        self.step_columns = H * DH
        self.per_slab = ff // self.step_columns
        self.units = 2 * self.per_slab
        self.steps = self.line * self.units


def relay_kernel(z, names, *refs):
    r = types.SimpleNamespace(**dict(zip(names, refs, strict=True)))
    s = lax.axis_index("section")
    d = lax.axis_index("dp")
    sections, dp_size, rows, width, ff = z.sections, z.dp_size, z.rows, z.width, z.ff
    batch_size, query_len, parts = z.batch_size, z.query_len, z.parts
    head_width = H * DH
    last = sections - 1
    after = lax.rem(s + 1, sections)
    before = lax.rem(s + sections - 1, sections)
    group = d - lax.rem(d, 4)
    place = lax.rem(d, 4)
    core_peer = group + place + 1 - 2 * lax.rem(place, 2)
    far_place = lax.rem(place + 2, 4)
    far_peer = group + far_place
    is_attention = lax.rem(s, 2) == 0
    is_ffn = jnp.logical_not(is_attention)

    def copy(src, dst, send_sem, recv_sem, section, dp):
        return pltpu.make_async_remote_copy(
            src_ref=src,
            dst_ref=dst,
            send_sem=send_sem,
            recv_sem=recv_sem,
            device_id=(section, dp),
            device_id_type=MESH,
        )

    def block(m):
        return pl.ds(pl.multiple_of(m * rows, rows), rows)

    def peers(body):
        def step(k, carry):
            body(lax.rem(d + k, dp_size))
            return carry

        lax.fori_loop(1, dp_size, step, 0)

    def other_sections(body):
        for k in range(1, sections):
            body(lax.rem(s + k, sections))

    def main_load():
        return pltpu.make_async_copy(r.main_hbm.at[0], r.main, r.load_sem.at[0])

    def side_load():
        return pltpu.make_async_copy(r.side_hbm.at[0], r.side, r.load_sem.at[1])

    main_load().start()

    @pl.when(is_ffn)
    def _():
        side_load().start()

    barrier = pltpu.get_barrier_semaphore()
    other_sections(
        lambda to: pl.semaphore_signal(barrier, inc=1, device_id=(to, d), device_id_type=MESH)
    )
    peers(lambda to: pl.semaphore_signal(barrier, inc=1, device_id=(s, to), device_id_type=MESH))

    lane = lax.broadcasted_iota(jnp.int32, (1, rows), 1)
    token_query = lane // query_len
    token_slot = lax.rem(lane, query_len)
    length = jnp.zeros((1, rows), jnp.int32)
    for q in range(batch_size):
        length = jnp.where(token_query == q, r.lengths[q], length)
    live = jnp.where(token_slot < length, 1.0, 0.0)
    r.meta[...] = jnp.zeros_like(r.meta)
    r.meta[0:1, :] = live
    r.meta[1:2, :] = live / length.astype(F32)
    r.idx[:8, :] = jnp.zeros((8, rows), jnp.int32)
    for c in range(batch_size):
        r.idx[c : c + 1, :] = jnp.full((1, rows), r.labels[c], jnp.int32)
    r.idx[8:, :] = r.chosen[...].T

    pl.semaphore_wait(barrier, sections - 1 + dp_size - 1)

    def lend_columns(quarter, part):
        start = quarter * (ff // 4) + part * LEND_STEP
        return pl.ds(pl.multiple_of(start, LEND_STEP), LEND_STEP)

    def lend_copy(part):
        columns = lend_columns(place, part)
        return copy(
            r.side_hbm.at[0, :, columns],
            r.lent.at[:, columns],
            r.lend_ss.at[0, part],
            r.lend_rs.at[0, part],
            after,
            d,
        )

    def lend_forward(kind, quarter, part, peer):
        columns = lend_columns(quarter, part)
        return copy(
            r.lent.at[:, columns],
            r.lent.at[:, columns],
            r.lend_ss.at[kind, part],
            r.lend_rs.at[kind, part],
            s,
            peer,
        )

    def state_copy(m):
        return copy(r.xout.at[m], r.xin.at[m], r.state_ss.at[m], r.state_rs.at[m], after, d)

    def grad_copy(m):
        return copy(r.gout.at[m], r.gin.at[m], r.grad_ss.at[m], r.grad_rs.at[m], before, d)

    def meta_copy(to, slot):
        return copy(r.meta, r.meta_rx.at[slot], r.meta_ss.at[to], r.meta_rs.at[slot], to, d)

    def idx_copy(slot):
        return copy(r.idx, r.idx_rx.at[slot], r.idx_ss, r.idx_rs.at[slot], last, d)

    def hid_copy(slot):
        return copy(r.hid, r.xin.at[slot], r.state_ss.at[sections], r.state_rs.at[slot], 0, d)

    def unit_copy(m, to):
        return copy(r.unit_tx.at[m], r.unit_rx, r.unit_ss.at[m], r.unit_rs, to, d)

    def loss_copy(m, to):
        return copy(r.loss_tx.at[m], r.loss_rx, r.loss_ss.at[m], r.loss_rs, to, d)

    def fin_copy(m, to):
        return copy(r.gout.at[m], r.fin_rx, r.fin_ss.at[m], r.fin_rs, to, d)

    def table_rows(owner):
        return pl.ds(pl.multiple_of(owner * z.doc_rows, z.doc_rows), z.doc_rows)

    def table_copy(to, owner):
        return copy(
            r.docs, r.table.at[table_rows(owner), :], r.tab_ss.at[to], r.tab_rs.at[owner], s, to
        )

    @pl.when(s != 0)
    def _():
        hid_copy(s).start()

    @pl.when(s == 0)
    def _():
        r.xin[0] = r.hid[...]

    other_sections(lambda to: meta_copy(to, s).start())
    r.meta_rx[s] = r.meta[...]

    @pl.when(s != last)
    def _():
        idx_copy(s).start()

    @pl.when(is_attention)
    def _():
        for part in range(parts):
            lend_copy(part).start()

    r.small[...] = jnp.zeros_like(r.small)
    r.tab_grad[...] = jnp.zeros_like(r.tab_grad)
    r.dproj[...] = jnp.zeros_like(r.dproj)
    r.dbias[...] = jnp.zeros_like(r.dbias)
    at_gain = slice(0, width)
    at_fgain = slice(width, 2 * width)
    gain = r.gain[...]
    fgain = r.fgain[...].reshape(1, width)

    def wait_meta(m):
        @pl.when(m != s)
        def _():
            meta_copy(0, m).wait_recv()

    def load_state(m):
        states = r.xin[m].astype(F32)
        inverse = rms_inverse(states)
        return states, inverse, states * inverse

    low_half = lax.broadcasted_iota(jnp.int32, (1, 128), 1) < DH

    def half_of(value, upper):
        keep = jnp.logical_not(low_half) if upper else low_half
        return jnp.where(keep, value.astype(F32), 0.0).astype(BF16)

    def attention_setup():
        buckets = r.buckets[...]
        for h in range(H):
            total = jnp.zeros(buckets.shape, F32)
            for b in range(32):
                total = jnp.where(buckets == b, r.bias[b : b + 1, h : h + 1], total)
            r.bias_sc[h] = total

    def attention_table():
        buckets = r.buckets[...]
        head_lane = lax.broadcasted_iota(jnp.int32, (32, 128), 1)

        def head(h, carry):
            grad = r.dbias[h]
            by_bucket = jnp.concatenate(
                [
                    jnp.sum(jnp.where(buckets == b, grad, 0.0), axis=0, keepdims=True)
                    for b in range(32)
                ],
                axis=0,
            )
            column = jnp.sum(by_bucket, axis=1, keepdims=True)
            r.tab_grad[...] += jnp.where(head_lane == h, column, 0.0)
            return carry

        lax.fori_loop(0, H, head, 0)

    def attention_forward(m):
        states, inverse, scaled = load_state(m)
        normed = scaled * gain
        r.left[0, :, block(m)] = normed.T.astype(BF16)
        normed_low = normed.astype(BF16)
        for start in range(0, 3 * head_width, head_width):
            r.qkv[block(m), start : start + head_width] = nn(
                normed_low, r.main[:, start : start + head_width]
            ).astype(BF16)
        live = r.meta_rx[m, 0:1, :] > 0.5
        row_query = lax.broadcasted_iota(jnp.int32, (rows, rows), 0) // query_len
        column_query = lax.broadcasted_iota(jnp.int32, (rows, rows), 1) // query_len
        keep = jnp.logical_and(row_query == column_query, live)
        for pair in range(H // 2):
            at = pair * 128
            query = r.qkv[block(m), at : at + 128]
            keys = r.qkv[block(m), head_width + at : head_width + at + 128]
            values = r.qkv[block(m), 2 * head_width + at : 2 * head_width + at + 128]
            contexts = []
            for upper in (0, 1):
                h = 2 * pair + upper
                raw = nt(half_of(query, upper), keys)
                biased = raw.reshape(batch_size, query_len, rows) + r.bias_sc[h][None]
                scores = jnp.where(keep, biased.reshape(rows, rows), MASK_FILL)
                top = jnp.max(scores, axis=-1, keepdims=True)
                grown = jnp.exp(scores - top)
                soft = grown / jnp.sum(grown, axis=-1, keepdims=True)
                r.probs[m, h] = soft
                contexts.append(nn(soft.astype(BF16), values))
            r.right[0, block(m), 3 * head_width + at : 3 * head_width + at + 128] = jnp.where(
                low_half, contexts[0], contexts[1]
            ).astype(BF16)
        context = r.right[0, block(m), 3 * head_width :]
        return states + nt(context, r.main[:, 3 * head_width :])

    def attention_backward(m):
        states, inverse, scaled = load_state(m)
        grad_low = r.gin[m]
        grad = grad_low.astype(F32)
        r.left[1, :, block(m)] = grad.T.astype(BF16)
        grad_context = nn(grad_low, r.main[:, 3 * head_width :]).astype(BF16)
        for pair in range(H // 2):
            at = pair * 128
            query = r.qkv[block(m), at : at + 128]
            keys = r.qkv[block(m), head_width + at : head_width + at + 128]
            values = r.qkv[block(m), 2 * head_width + at : 2 * head_width + at + 128]
            grad_pair = grad_context[:, at : at + 128]
            found = []
            for upper in (0, 1):
                h = 2 * pair + upper
                soft = r.probs[m, h]
                grad_soft = nt(half_of(grad_pair, upper), values)
                moved = soft * grad_soft
                grad_scores = moved - soft * jnp.sum(moved, axis=-1, keepdims=True)
                r.dbias[h] += jnp.sum(grad_scores.reshape(batch_size, query_len, rows), axis=0)
                scores_low = grad_scores.astype(BF16)
                found.append(
                    (
                        nn(scores_low, keys),
                        tn(scores_low, query),
                        tn(soft.astype(BF16), grad_pair),
                    )
                )
            for third in range(3):
                start = third * head_width + at
                r.right[0, block(m), start : start + 128] = jnp.where(
                    low_half, found[0][third], found[1][third]
                ).astype(BF16)
        grad_normed = nt(r.right[0, block(m), : 3 * head_width], r.main[:, : 3 * head_width])
        grad_states, grad_gain = rms_back(scaled, inverse, gain, grad_normed)
        r.small[:, at_gain] += grad_gain
        return grad + grad_states

    def ffn_forward(m):
        states, inverse, scaled = load_state(m)
        normed = scaled * gain
        r.left[0, :, block(m)] = normed.T.astype(BF16)
        normed_low = normed.astype(BF16)
        outputs = states
        for start in range(0, ff, FF_STEP):
            columns = slice(start, start + FF_STEP)
            gate = nn(normed_low, r.main[:, columns])
            up = nn(normed_low, r.lent[:, columns])
            square = gate * gate
            bent = jnp.tanh(GELU_C * gate * (1.0 + GELU_A * square))
            half = 0.5 * (1.0 + bent)
            smooth = gate * half
            slope = half + 0.5 * gate * (1.0 - bent * bent) * (
                GELU_C * (1.0 + 3.0 * GELU_A * square)
            )
            hidden = (smooth * up).astype(BF16)
            r.right[1, block(m), columns] = hidden
            r.right[0, block(m), columns] = (slope * up).astype(BF16)
            r.right[2, block(m), columns] = smooth.astype(BF16)
            outputs = outputs + nt(hidden, r.side[:, columns])
        return outputs

    def ffn_backward(m, grad):
        states, inverse, scaled = load_state(m)
        grad_low = grad.astype(BF16)
        r.left[1, :, block(m)] = grad.T.astype(BF16)
        grad_normed = jnp.zeros((rows, width), F32)
        for start in range(0, ff, FF_STEP):
            columns = slice(start, start + FF_STEP)
            grad_hidden = nn(grad_low, r.side[:, columns])
            grad_gate = (grad_hidden * r.right[0, block(m), columns].astype(F32)).astype(BF16)
            grad_up = (grad_hidden * r.right[2, block(m), columns].astype(F32)).astype(BF16)
            r.right[0, block(m), columns] = grad_gate
            r.right[2, block(m), columns] = grad_up
            grad_normed = (
                grad_normed
                + nt(grad_gate, r.main[:, columns])
                + nt(grad_up, r.lent[:, columns])
            )
        grad_states, grad_gain = rms_back(scaled, inverse, gain, grad_normed)
        r.small[:, at_gain] += grad_gain
        return grad + grad_states

    def count_hits(m):
        for c in range(batch_size):
            base = r.idx_rx[m, c : c + 1, :] * DOC_LEN
            numbers = lax.broadcasted_iota(jnp.int32, (DOC_LEN, rows), 0) + base
            total = jnp.zeros((DOC_LEN, rows), F32)
            for k in range(z.retrieved):
                total = total + jnp.where(r.idx_rx[m, 8 + k : 9 + k, :] == numbers, 1.0, 0.0)
            r.counts[m, c * DOC_LEN : (c + 1) * DOC_LEN, :] = total

    def pick_docs(m):
        for c in range(batch_size):
            label = r.idx_rx[m, c : c + 1, :]

            def pick(t, picked):
                here = r.table[pl.ds(pl.multiple_of(t * DOC_LEN, DOC_LEN), DOC_LEN), :].astype(F32)
                return jnp.where(label == t, here, picked)

            picked = lax.fori_loop(
                0, dp_size * z.doc_rows // DOC_LEN, pick, jnp.zeros((DOC_LEN, z.vector), F32)
            )
            r.own_docs[m, c * DOC_LEN : (c + 1) * DOC_LEN, :] = picked.astype(BF16)

    def loss_and_grad(m, unit):
        docs = r.own_docs[m]
        sims = nt(docs, unit)
        count = r.counts[m]
        imputed = jnp.sum(count * sims, axis=0, keepdims=True) / z.retrieved
        grown = count * jnp.exp(sims)
        imputed_mass = jnp.exp(imputed)
        mass = imputed_mass + jnp.concatenate(
            [
                jnp.sum(grown[c * DOC_LEN : (c + 1) * DOC_LEN], axis=0, keepdims=True)
                for c in range(batch_size)
            ],
            axis=0,
        )
        weighted = jnp.log(mass) * r.meta_rx[m, 1:2, :]
        candidate = lax.broadcasted_iota(jnp.int32, (batch_size, 1), 0)
        losses = jnp.zeros((1, rows), F32)
        grad_tokens = jnp.zeros((batch_size, rows), F32)
        for q in range(batch_size):
            own = token_query == q
            score = jnp.sum(jnp.where(own, weighted, 0.0), axis=1, keepdims=True)
            top = jnp.max(score, axis=0, keepdims=True)
            risen = jnp.exp(score - top)
            total = jnp.sum(risen, axis=0, keepdims=True)
            chosen_one = (candidate == q).astype(F32)
            loss = top + jnp.log(total) - jnp.sum(score * chosen_one, axis=0, keepdims=True)
            losses = losses + jnp.where(lane == q, loss, 0.0)
            grad_tokens = grad_tokens + jnp.where(own, risen / total - chosen_one, 0.0)
        grad_mass = grad_tokens * r.meta_rx[m, 1:2, :] / mass
        shared = jnp.sum(grad_mass, axis=0, keepdims=True) * imputed_mass / z.retrieved
        grad_sims = count * shared + jnp.concatenate(
            [
                grown[c * DOC_LEN : (c + 1) * DOC_LEN] * grad_mass[c : c + 1]
                for c in range(batch_size)
            ],
            axis=0,
        )
        high = grad_sims.astype(BF16)
        rest = (grad_sims - high.astype(F32)).astype(BF16)
        return losses, tn(high, docs) + tn(rest, docs)

    def finish_states(m, states):
        inverse = rms_inverse(states)
        scaled = states * inverse
        normed = (scaled * fgain).astype(BF16)
        projected = nn(normed, r.proj[...])
        size = lax.rsqrt(jnp.sum(projected * projected, axis=-1, keepdims=True) + EPS_NORM)
        exact = projected * size
        unit = exact.astype(BF16)
        losses, grad_unit = loss_and_grad(m, unit)
        r.unit_tx[m] = unit
        r.loss_tx[m] = jnp.broadcast_to(losses, (8, rows))

        @pl.when(m != last)
        def _():
            unit_copy(m, m).start()
            loss_copy(m, m).start()

        grad_projected = (
            size * (grad_unit - exact * jnp.sum(grad_unit * exact, axis=-1, keepdims=True))
        ).astype(BF16)
        r.dproj[...] += tn(normed, grad_projected)
        grad_normed = nt(grad_projected, r.proj[...])
        grad_states, grad_gain = rms_back(scaled, inverse, fgain, grad_normed)
        r.small[:, at_fgain] += grad_gain
        return grad_states

    def loop(body):
        def step(m, carry):
            body(m)
            return carry

        lax.fori_loop(0, sections, step, 0)

    def wait_state(m):
        @pl.when(jnp.logical_or(s != 0, m != 0))
        def _():
            state_copy(m).wait_recv()

    @pl.when(is_attention)
    def _():
        attention_setup()
        main_load().wait()

        def forward(m):
            wait_meta(m)
            wait_state(m)
            r.xout[m] = attention_forward(m).astype(BF16)
            state_copy(m).start()

        loop(forward)

        def backward(m):
            grad_copy(m).wait_recv()
            r.gout[m] = attention_backward(m).astype(BF16)

            @pl.when(s != 0)
            def _():
                grad_copy(m).start()

            @pl.when(jnp.logical_and(s == 0, m != 0))
            def _():
                fin_copy(m, m).start()

        loop(backward)
        attention_table()

    @pl.when(is_ffn)
    def _():
        for part in range(parts):
            lend_copy(part).wait_recv()
            lend_forward(1, place, part, core_peer).start()
            lend_forward(2, place, part, far_peer).start()

        @pl.when(s == last)
        def _():
            r.idx_rx[last] = r.idx[...]
            r.table[table_rows(d), :] = r.docs[...]
            peers(lambda to: table_copy(to, d).start())

            def prepare(m):
                @pl.when(m != last)
                def _():
                    idx_copy(m).wait_recv()

                count_hits(m)

            loop(prepare)

        for part in range(parts):
            lend_forward(2, far_place, part, far_peer).wait_recv()
            lend_forward(3, far_place, part, core_peer).start()
        for part in range(parts):
            lend_forward(1, place, part, core_peer).wait_recv()
            lend_forward(3, far_place, part, core_peer).wait_recv()
        main_load().wait()
        side_load().wait()

        @pl.when(s == last)
        def _():
            peers(lambda owner: table_copy(owner, owner).wait_recv())
            loop(pick_docs)
            loop(wait_meta)

            def both(m):
                wait_state(m)
                states = ffn_forward(m)
                grad = finish_states(m, states)
                r.gout[m] = ffn_backward(m, grad).astype(BF16)
                grad_copy(m).start()

            loop(both)

        @pl.when(s != last)
        def _():
            def forward(m):
                wait_state(m)
                r.xout[m] = ffn_forward(m).astype(BF16)
                state_copy(m).start()

            loop(forward)

            def backward(m):
                grad_copy(m).wait_recv()
                r.gout[m] = ffn_backward(m, r.gin[m].astype(F32)).astype(BF16)
                grad_copy(m).start()

            loop(backward)
            loop(wait_meta)

        for part in range(parts):
            lend_forward(1, place, part, core_peer).wait_send()
            lend_forward(2, place, part, far_peer).wait_send()
            lend_forward(3, far_place, part, core_peer).wait_send()

    if z.summed:
        sum_gradients(z, r, s, d, copy, peers, other_sections, is_attention)

    other_sections(lambda to: meta_copy(to, s).wait_send())

    @pl.when(s != 0)
    def _():
        hid_copy(s).wait_send()
        fin_copy(0, s).wait_recv()
        r.dx[...] = r.fin_rx[...].astype(F32).reshape(batch_size, query_len, width)
        loop(lambda m: grad_copy(m).wait_send())

    @pl.when(s == 0)
    def _():
        r.dx[...] = r.gout[0].astype(F32).reshape(batch_size, query_len, width)
        for m in range(1, sections):
            fin_copy(m, m).wait_send()

    @pl.when(is_attention)
    def _():
        for part in range(parts):
            lend_copy(part).wait_send()

    def write_own(unit, losses):
        r.units[...] = unit.reshape(batch_size, query_len, z.vector)
        r.loss[...] = losses

    @pl.when(s != last)
    def _():
        idx_copy(s).wait_send()
        loop(lambda m: state_copy(m).wait_send())
        unit_copy(0, s).wait_recv()
        loss_copy(0, s).wait_recv()
        write_own(r.unit_rx[...], r.loss_rx[...])

    @pl.when(s == last)
    def _():
        peers(lambda to: table_copy(to, d).wait_send())
        for m in range(sections - 1):
            unit_copy(m, m).wait_send()
            loss_copy(m, m).wait_send()
        write_own(r.unit_tx[last], r.loss_tx[last])


def sum_gradients(z, r, s, d, copy, peers, other_sections, is_attention):
    sections, dp_size, width, ff, share, line = z.sections, z.dp_size, z.width, z.ff, z.share, z.line
    step_columns, per_slab, units, steps = z.step_columns, z.per_slab, z.units, z.steps
    place = d // 2
    core = lax.rem(d, 2)
    peer = d + 1 - 2 * core
    last = sections - 1
    before = lax.rem(s + sections - 1, sections)
    is_ffn = jnp.logical_not(is_attention)
    orders = sum_order(line)

    def piece_rows(owner):
        return pl.ds(pl.multiple_of(owner * share, share), share)

    def small_copies(to, slot):
        return (
            copy(r.small, r.small_rx.at[slot], r.small_ss.at[0, to], r.small_rs.at[0, slot], s, to),
            copy(r.tab_grad, r.tab_rx.at[slot], r.small_ss.at[1, to], r.small_rs.at[1, slot], s, to),
        )

    def proj_copy(to, slot):
        return copy(
            r.dproj.at[piece_rows(to), :],
            r.proj_rx.at[slot],
            r.proj_ss.at[to],
            r.proj_rs.at[slot],
            s,
            to,
        )

    def column_copies(to, slot):
        return (
            copy(
                r.small_tx, r.small_cx.at[slot], r.column_ss.at[0, to], r.column_rs.at[0, slot], to, d
            ),
            copy(r.tab_tx, r.tab_cx.at[slot], r.column_ss.at[1, to], r.column_rs.at[1, slot], to, d),
        )

    def piece_copy(to):
        rows = piece_rows(d)
        return copy(
            r.proj_out.at[rows, :], r.proj_out.at[rows, :], r.piece_ss.at[to], r.piece_rs, to, d
        )

    def spread_copy(to, owner):
        rows = piece_rows(owner)
        return copy(
            r.proj_out.at[rows, :],
            r.proj_out.at[rows, :],
            r.spread_ss.at[to],
            r.spread_rs.at[owner],
            s,
            to,
        )

    def each(copies, action):
        for one in copies:
            getattr(one, action)()

    def total_of(ref, count):
        total = ref[0]
        for k in range(1, count):
            total = total + ref[k]
        return total

    def small_first():
        peers(lambda to: each(small_copies(to, d), "start"))
        r.small_rx[d] = r.small[...]
        r.tab_rx[d] = r.tab_grad[...]

        @pl.when(s == last)
        def _():
            peers(lambda to: proj_copy(to, d).start())
            r.proj_rx[d] = r.dproj[piece_rows(d), :]

    def small_second():
        peers(lambda owner: each(small_copies(owner, owner), "wait_recv"))
        r.small_tx[...] = total_of(r.small_rx, dp_size)
        r.tab_tx[...] = total_of(r.tab_rx, dp_size)
        r.small_cx[s] = r.small_tx[...]
        r.tab_cx[s] = r.tab_tx[...]
        other_sections(lambda to: each(column_copies(to, s), "start"))

        @pl.when(s == last)
        def _():
            peers(lambda owner: proj_copy(owner, owner).wait_recv())
            r.proj_out[piece_rows(d), :] = total_of(r.proj_rx, dp_size)
            for to in range(sections - 1):
                piece_copy(to).start()
            peers(lambda to: spread_copy(to, d).start())

    def small_third():
        other_sections(lambda to: each(column_copies(to, to), "wait_recv"))
        r.fgain_out[...] = total_of(r.small_cx, sections)[:, width:]
        r.table_out[...] = total_of(r.tab_cx, sections)[:, :H]
        r.gain_out[...] = pltpu.roll(
            jnp.broadcast_to(r.small_tx[:, :width], (8, width)), width - d * share, 1
        )[0:1, :share]

        @pl.when(s != last)
        def _():
            piece_copy(0).wait_recv()
            peers(lambda to: spread_copy(to, d).start())

    def small_last():
        peers(lambda owner: spread_copy(owner, owner).wait_recv())
        peers(lambda to: spread_copy(to, d).wait_send())
        peers(lambda to: each(small_copies(to, d), "wait_send"))
        other_sections(lambda to: each(column_copies(to, s), "wait_send"))

        @pl.when(s == last)
        def _():
            peers(lambda to: proj_copy(to, d).wait_send())
            for to in range(sections - 1):
                piece_copy(to).wait_send()

    def target(i):
        found = jnp.int32(0)
        for k in range(line):
            found = jnp.where(place == k, orders[k][i], found)
        return found

    targets = [target(i) for i in range(line)]

    def parts_of(t):
        i, u = t // units, lax.rem(t, units)
        j = targets[0]
        for k in range(1, line):
            j = jnp.where(i == k, targets[k], j)
        slab, column = lax.rem(u, 2), u // 2
        columns = pl.ds(pl.multiple_of(column * step_columns, step_columns), step_columns)
        return j, u, slab, column, columns

    def core_copy(t):
        return copy(
            r.core_tx.at[lax.rem(t, 4)], r.core_rx.at[t], r.core_ss.at[t], r.core_rs.at[t], s, peer
        )

    def up_core_copy(k):
        return copy(
            r.up_core_tx.at[lax.rem(k, 4)], r.up_rx.at[k], r.up_core_ss.at[k], r.up_rs.at[k], s, peer
        )

    def up_copy(k):
        return copy(
            r.up_tx.at[lax.rem(k, 4)], r.up_rx.at[k], r.up_ss.at[k], r.up_rs.at[k], before, d
        )

    def line_view(t):
        row = pl.ds(pl.multiple_of(lax.rem(t, dp_size) * share, share), share)
        column = pl.ds(pl.multiple_of(t // dp_size * step_columns, step_columns), step_columns)
        return r.lent.at[row, column]

    def line_copy(t, way, j, u, to):
        slot = j - 1 + way
        return copy(
            line_view(t),
            r.line_rx.at[way, slot, u],
            r.line_ss.at[t],
            r.line_rs.at[way, slot, u],
            s,
            to * 2 + core,
        )

    def theirs(j):
        return pl.ds(pl.multiple_of((j * 2 + 1 - core) * share, share), share)

    def ours(j):
        return pl.ds(pl.multiple_of((j * 2 + core) * share, share), share)

    def begin(t):
        j, u, slab, column, columns = parts_of(t)
        k = t // 2
        mixed = jnp.logical_and(is_attention, column == per_slab - 1)
        which = jnp.where(jnp.logical_or(slab == 1, mixed), 1, 0)

        @pl.when(jnp.logical_or(is_ffn, slab == 0))
        def _():
            right = r.right[slab, :, columns]

            @pl.when(t >= 4)
            def _():
                core_copy(t - 4).wait_send()

            r.core_tx[lax.rem(t, 4)] = nn(r.left[which, theirs(j), :], right).astype(BF16)
            core_copy(t).start()
            r.mine[lax.rem(t, 2)] = nn(r.left[which, ours(j), :], right)

        @pl.when(jnp.logical_and(is_ffn, slab == 1))
        def _():
            right = r.right[2, :, columns]

            @pl.when(k >= 4)
            def _():
                up_core_copy(k - 4).wait_send()

            r.up_core_tx[lax.rem(k, 4)] = nn(r.left[0, theirs(j), :], right).astype(BF16)
            up_core_copy(k).start()
            r.up_mine[...] = nn(r.left[0, ours(j), :], right)

    def finish(t):
        j, u, slab, column, columns = parts_of(t)
        k = t // 2
        total = r.mine.at[lax.rem(t, 2)]

        @pl.when(jnp.logical_or(is_ffn, slab == 0))
        def _():
            core_copy(t).wait_recv()
            total[...] += r.core_rx[t].astype(F32)

        @pl.when(jnp.logical_and(is_attention, slab == 1))
        def _():
            up_copy(k).wait_recv()
            total[...] = r.up_rx[k].astype(F32)

        @pl.when(jnp.logical_and(is_ffn, slab == 1))
        def _():
            up_core_copy(k).wait_recv()

            @pl.when(k >= 4)
            def _():
                up_copy(k - 4).wait_send()

            r.up_tx[lax.rem(k, 4)] = (r.up_mine[...] + r.up_rx[k].astype(F32)).astype(BF16)
            up_copy(k).start()

        way = jnp.where(j < place, 1, 0)

        @pl.when(jnp.logical_and(place > 0, j >= place))
        def _():
            line_copy(t, 0, j, u, place).wait_recv()
            total[...] += r.line_rx[0, j - 1, u].astype(F32)

        @pl.when(jnp.logical_and(place < line - 1, j <= place))
        def _():
            line_copy(t, 1, j, u, place).wait_recv()
            total[...] += r.line_rx[1, j, u].astype(F32)

        @pl.when(jnp.logical_and(j == place, slab == 0))
        def _():
            r.main_out[0, :, columns] = total[...]

        @pl.when(jnp.logical_and(j == place, slab == 1))
        def _():
            r.side_out[0, :, columns] = total[...]

        @pl.when(j != place)
        def _():
            line_view(t)[...] = total[...].astype(BF16)
            line_copy(t, way, j, u, place + 1 - 2 * way).start()

    small_first()
    begin(jnp.int32(0))

    def step(t, carry):
        @pl.when(t < steps)
        def _():
            begin(t)

        finish(t - 1)

        @pl.when(t == units)
        def _():
            small_second()

        @pl.when(t == steps - units)
        def _():
            small_third()

        return carry

    lax.fori_loop(1, steps + 1, step, 0)
    small_last()

    def drain(t, carry):
        line_copy(t, 0, 1, 0, place).wait_send()
        return carry

    lax.fori_loop(0, steps - units, drain, 0)

    def drain_core(t, carry):
        slab = lax.rem(t, 2)

        @pl.when(jnp.logical_or(is_ffn, slab == 0))
        def _():
            core_copy(t).wait_send()

        return carry

    lax.fori_loop(steps - 4, steps, drain_core, 0)

    @pl.when(is_ffn)
    def _():
        for k in range(steps // 2 - 4, steps // 2):
            up_core_copy(k).wait_send()
            up_copy(k).wait_send()


def relay(z, hid, lengths, labels, chosen, main, side, gain, bias, buckets, fgain, proj, docs):
    dma = pltpu.SemaphoreType.DMA
    shape = jax.ShapeDtypeStruct
    sections, rows, width, ff, dp_size = z.sections, z.rows, z.width, z.ff, z.dp_size
    share, steps, units = z.share, z.steps, z.units
    piece = (share, z.step_columns)
    vmem = pl.BlockSpec(memory_space=VMEM)
    smem = pl.BlockSpec(memory_space=pltpu.SMEM)
    anywhere = pl.BlockSpec(memory_space=pl.ANY)
    inputs = dict(
        hid=(hid, vmem),
        lengths=(lengths, smem),
        labels=(labels, smem),
        chosen=(chosen, vmem),
        main_hbm=(main, anywhere),
        side_hbm=(side, anywhere),
        gain=(gain, vmem),
        bias=(bias, vmem),
        buckets=(buckets, vmem),
        fgain=(fgain, vmem),
        proj=(proj, vmem),
        docs=(docs, vmem),
    )
    outputs = dict(
        units=shape((z.batch_size, z.query_len, z.vector), BF16),
        loss=shape((8, rows), F32),
        dx=shape((z.batch_size, z.query_len, width), F32),
    )
    scratch = dict(
        main=VMEM((width, ff), BF16),
        side=VMEM((width, ff), BF16),
        lent=VMEM((width, ff), BF16),
        xin=VMEM((sections, rows, width), BF16),
        xout=VMEM((sections, rows, width), BF16),
        gin=VMEM((sections, rows, width), BF16),
        gout=VMEM((sections, rows, width), BF16),
        meta=VMEM((8, rows), F32),
        meta_rx=VMEM((sections, 8, rows), F32),
        idx=VMEM((8 + z.retrieved, rows), jnp.int32),
        idx_rx=VMEM((sections, 8 + z.retrieved, rows), jnp.int32),
        own_docs=VMEM((sections, z.batch_size * DOC_LEN, z.vector), BF16),
        table=VMEM((dp_size * z.doc_rows, z.vector), BF16),
        counts=VMEM((sections, z.batch_size * DOC_LEN, rows), F32),
        qkv=VMEM((z.total, 3 * H * DH), BF16),
        probs=VMEM((sections, H, rows, rows), F32),
        bias_sc=VMEM((H, z.query_len, rows), F32),
        dbias=VMEM((H, z.query_len, rows), F32),
        fin_rx=VMEM((rows, width), BF16),
        unit_tx=VMEM((sections, rows, z.vector), BF16),
        unit_rx=VMEM((rows, z.vector), BF16),
        loss_tx=VMEM((sections, 8, rows), F32),
        loss_rx=VMEM((8, rows), F32),
        load_sem=dma((2,)),
        state_ss=dma((sections + 1,)),
        state_rs=dma((sections,)),
        grad_ss=dma((sections,)),
        grad_rs=dma((sections,)),
        meta_ss=dma((sections,)),
        meta_rs=dma((sections,)),
        idx_ss=dma,
        idx_rs=dma((sections,)),
        tab_ss=dma((dp_size,)),
        tab_rs=dma((dp_size,)),
        lend_ss=dma((4, z.parts)),
        lend_rs=dma((4, z.parts)),
        fin_ss=dma((sections,)),
        fin_rs=dma,
        unit_ss=dma((sections,)),
        unit_rs=dma,
        loss_ss=dma((sections,)),
        loss_rs=dma,
    )
    factors = dict(left=((2, width, z.total), BF16), right=((3, z.total, ff), BF16))
    partials = dict(
        small=((1, 2 * width), F32), tab_grad=((32, 128), F32), dproj=((width, z.vector), F32)
    )
    if z.summed:
        outputs |= dict(
            main_out=shape((1, share, ff), F32),
            side_out=shape((1, share, ff), F32),
            gain_out=shape((1, share), F32),
            table_out=shape((32, H), F32),
            fgain_out=shape((1, width), F32),
            proj_out=shape((width, z.vector), F32),
        )
        scratch |= {name: VMEM(*kind) for name, kind in (factors | partials).items()}
        scratch |= dict(
            mine=VMEM((2,) + piece, F32),
            up_mine=VMEM(piece, F32),
            core_tx=VMEM((4,) + piece, BF16),
            core_rx=VMEM((steps,) + piece, BF16),
            up_core_tx=VMEM((4,) + piece, BF16),
            up_tx=VMEM((4,) + piece, BF16),
            up_rx=VMEM((steps // 2,) + piece, BF16),
            line_rx=VMEM((2, z.line - 1, units) + piece, BF16),
            small_rx=VMEM((dp_size, 1, 2 * width), F32),
            small_tx=VMEM((1, 2 * width), F32),
            small_cx=VMEM((sections, 1, 2 * width), F32),
            tab_rx=VMEM((dp_size, 32, 128), F32),
            tab_tx=VMEM((32, 128), F32),
            tab_cx=VMEM((sections, 32, 128), F32),
            proj_rx=VMEM((dp_size, share, z.vector), F32),
            core_ss=dma((steps,)),
            core_rs=dma((steps,)),
            up_core_ss=dma((steps // 2,)),
            up_ss=dma((steps // 2,)),
            up_rs=dma((steps // 2,)),
            line_ss=dma((steps,)),
            line_rs=dma((2, z.line - 1, units)),
            small_ss=dma((2, dp_size)),
            small_rs=dma((2, dp_size)),
            column_ss=dma((2, sections)),
            column_rs=dma((2, sections)),
            proj_ss=dma((dp_size,)),
            proj_rs=dma((dp_size,)),
            piece_ss=dma((sections,)),
            piece_rs=dma,
            spread_ss=dma((dp_size,)),
            spread_rs=dma((dp_size,)),
        )
    else:
        outputs |= {name: shape(*kind) for name, kind in (factors | partials).items()}
    results = pl.pallas_call(
        functools.partial(relay_kernel, z, (*inputs, *outputs, *scratch)),
        out_shape=tuple(outputs.values()),
        in_specs=[spec for _, spec in inputs.values()],
        out_specs=(vmem,) * len(outputs),
        scratch_shapes=list(scratch.values()),
        compiler_params=pltpu.CompilerParams(
            collective_id=0, has_side_effects=True, vmem_limit_bytes=62 * 2**20
        ),
        name="relay",
    )(*[value for value, _ in inputs.values()])
    return types.SimpleNamespace(**dict(zip(outputs, results, strict=True)))


def sums_outside(z, out):
    head_width = H * DH
    section = lax.axis_index("section")
    is_attention = section % 2 == 0
    left, right = out.left, out.right
    second = jnp.where(is_attention, left[1], left[0])
    main_grad = jnp.concatenate(
        [nn(left[0], right[0, :, : 3 * head_width]), nn(second, right[0, :, 3 * head_width :])],
        axis=1,
    )
    up_grad = lax.ppermute(
        nn(left[0], right[2]).astype(BF16),
        "section",
        [(k, k - 1) for k in range(1, z.sections)],
    )
    side_grad = jnp.where(is_attention, up_grad.astype(F32), nn(left[1], right[1]))
    scatter = functools.partial(
        lax.psum_scatter, axis_name="dp", scatter_dimension=0, tiled=True
    )
    table, fgain, proj = lax.psum(
        (out.tab_grad[:, :H], out.small[0, z.width :], out.dproj), ("section", "dp")
    )
    return (
        scatter(main_grad)[None],
        scatter(side_grad)[None],
        scatter(out.small[0, : z.width])[None],
        table,
        fgain,
        proj,
    )


def per_device(
    hidden_in,
    lengths,
    labels,
    chosen,
    slab_main,
    slab_side,
    section_gains,
    rel_bias,
    final_gain,
    out_proj,
    doc_vectors,
):
    batch_size, query_len, width = hidden_in.shape
    rows = batch_size * query_len
    retrieved = chosen.shape[2]
    z = Sizes(
        lax.axis_size("section"),
        lax.axis_size("dp"),
        batch_size,
        query_len,
        retrieved,
        width,
        slab_main.shape[2],
        out_proj.shape[1],
        doc_vectors.shape[0],
    )
    buckets = jnp.asarray(np.tile(bucket_table(query_len), (1, batch_size)))
    out = relay(
        z,
        hidden_in.reshape(rows, width),
        lengths,
        labels,
        chosen.reshape(rows, retrieved),
        slab_main,
        slab_side,
        section_gains,
        rel_bias,
        buckets,
        final_gain,
        out_proj,
        doc_vectors,
    )
    if z.summed:
        sums = (
            out.main_out,
            out.side_out,
            out.gain_out,
            out.table_out,
            out.fgain_out[0],
            out.proj_out,
        )
    else:
        sums = sums_outside(z, out)
    return (out.units, out.loss[0, :batch_size], out.dx) + sums


def solution(mesh):
    both = ("section", "dp")
    in_specs = (
        P(both, None, None),
        P(both),
        P(both),
        P(both, None, None),
        P("section", None, None),
        P("section", None, None),
        P("section", None),
        P(),
        P(),
        P(),
        P("dp", None),
    )
    out_specs = (
        P(both, None, None),
        P(both),
        P(both, None, None),
        P("section", "dp", None),
        P("section", "dp", None),
        P("section", "dp"),
        P(),
        P(),
        P(),
    )
    return jax.shard_map(
        per_device, mesh=mesh, in_specs=in_specs, out_specs=out_specs, check_vma=False
    )
```

```python
import functools
import math
import types

import jax
import jax.numpy as jnp
import numpy as np
from jax import lax
from jax.experimental import pallas as pl
from jax.experimental.pallas import tpu as pltpu
from jax.sharding import PartitionSpec as P

H = 12
DH = 64
DOC_LEN = 128
EPS_NORM = 1e-06
MASK_FILL = -1000000000.0
HIGHEST = lax.Precision.HIGHEST
MESH = pl.DeviceIdType.MESH
F32 = jnp.float32
BF16 = jnp.bfloat16
VMEM = pltpu.VMEM
GELU_C = math.sqrt(2.0 / math.pi)
GELU_A = 0.044715
FF_STEP = 768
LEND_STEP = 128


def bucket_table(query_len):
    places = np.arange(query_len)
    relative = places[None, :] - places[:, None]
    distance = np.abs(relative)
    signed_part = np.where(relative > 0, 16, 0)
    far_bucket = 8 + np.floor(np.log(np.maximum(distance, 1) / 8.0) / np.log(16.0) * 8.0).astype(
        np.int64
    )
    far_bucket = np.minimum(far_bucket, 15)
    return (signed_part + np.where(distance < 8, distance, far_bucket)).astype(np.int32)


def nn(a, b):
    return jnp.dot(a, b, preferred_element_type=F32)


def nt(a, b):
    return lax.dot_general(a, b, (((1,), (1,)), ((), ())), preferred_element_type=F32)


def tn(a, b):
    return lax.dot_general(a, b, (((0,), (0,)), ((), ())), preferred_element_type=F32)


def rms_inverse(values):
    return lax.rsqrt(jnp.mean(values * values, axis=-1, keepdims=True) + EPS_NORM)


def rms_back(scaled, inverse, gain, grad):
    inner = grad * gain
    grad_values = inverse * (inner - scaled * jnp.mean(inner * scaled, axis=-1, keepdims=True))
    return grad_values, jnp.sum(grad * scaled, axis=0, keepdims=True)


def sum_order(line):
    orders = []
    for place in range(line):
        others = [j for j in range(line) if j != place]
        others.sort(key=lambda j: (-abs(j - place), min(j, line - 1 - j)))
        orders.append(others + [place])
    return orders


class Sizes:
    def __init__(self, sections, dp_size, batch_size, query_len, retrieved, width, ff, vector, doc_rows):
        self.sections = sections
        self.dp_size = dp_size
        self.batch_size = batch_size
        self.query_len = query_len
        self.retrieved = retrieved
        self.width = width
        self.ff = ff
        self.vector = vector
        self.doc_rows = doc_rows
        self.rows = batch_size * query_len
        self.total = sections * self.rows
        self.parts = ff // 4 // LEND_STEP
        self.share = width // dp_size
        self.summed = self.share % 16 == 0 and dp_size % 2 == 0
        self.line = dp_size // 2
        self.step_columns = H * DH
        self.per_slab = ff // self.step_columns
        self.units = 2 * self.per_slab
        self.steps = self.line * self.units
        self.chunk = self.share if self.summed else H * 8
        self.slab_chunks = ff // self.chunk
        arriving = self.steps + 2 * (self.line - 1) * self.units
        self.pool = max(3 * self.slab_chunks, arriving if self.summed else 0)


def relay_kernel(z, names, *refs):
    r = types.SimpleNamespace(**dict(zip(names, refs, strict=True)))
    s = lax.axis_index("section")
    d = lax.axis_index("dp")
    sections, dp_size, rows, width, ff = z.sections, z.dp_size, z.rows, z.width, z.ff
    batch_size, query_len, parts = z.batch_size, z.query_len, z.parts
    head_width = H * DH
    last = sections - 1
    after = lax.rem(s + 1, sections)
    before = lax.rem(s + sections - 1, sections)
    group = d - lax.rem(d, 4)
    place = lax.rem(d, 4)
    core_peer = group + place + 1 - 2 * lax.rem(place, 2)
    far_place = lax.rem(place + 2, 4)
    far_peer = group + far_place
    is_attention = lax.rem(s, 2) == 0
    is_ffn = jnp.logical_not(is_attention)

    def copy(src, dst, send_sem, recv_sem, section, dp):
        return pltpu.make_async_remote_copy(
            src_ref=src,
            dst_ref=dst,
            send_sem=send_sem,
            recv_sem=recv_sem,
            device_id=(section, dp),
            device_id_type=MESH,
        )

    def block(m):
        return pl.ds(pl.multiple_of(m * rows, rows), rows)

    def peers(body):
        def step(k, carry):
            body(lax.rem(d + k, dp_size))
            return carry

        lax.fori_loop(1, dp_size, step, 0)

    def other_sections(body):
        for k in range(1, sections):
            body(lax.rem(s + k, sections))

    def main_load():
        return pltpu.make_async_copy(r.main_hbm.at[0], r.main, r.load_sem.at[0])

    def side_load():
        return pltpu.make_async_copy(r.side_hbm.at[0], r.side, r.load_sem.at[1])

    main_load().start()

    @pl.when(is_ffn)
    def _():
        side_load().start()

    barrier = pltpu.get_barrier_semaphore()
    other_sections(
        lambda to: pl.semaphore_signal(barrier, inc=1, device_id=(to, d), device_id_type=MESH)
    )
    peers(lambda to: pl.semaphore_signal(barrier, inc=1, device_id=(s, to), device_id_type=MESH))

    lane = lax.broadcasted_iota(jnp.int32, (1, rows), 1)
    token_query = lane // query_len
    token_slot = lax.rem(lane, query_len)
    length = jnp.zeros((1, rows), jnp.int32)
    for q in range(batch_size):
        length = jnp.where(token_query == q, r.lengths[q], length)
    live = jnp.where(token_slot < length, 1.0, 0.0)
    r.meta[...] = jnp.zeros_like(r.meta)
    r.meta[0:1, :] = live
    r.meta[1:2, :] = live / length.astype(F32)
    r.idx[:8, :] = jnp.zeros((8, rows), jnp.int32)
    for c in range(batch_size):
        r.idx[c : c + 1, :] = jnp.full((1, rows), r.labels[c], jnp.int32)
    r.idx[8:, :] = r.chosen[...].T

    pl.semaphore_wait(barrier, sections - 1 + dp_size - 1)

    def lend_columns(quarter, part):
        start = quarter * (ff // 4) + part * LEND_STEP
        return pl.ds(pl.multiple_of(start, LEND_STEP), LEND_STEP)

    def lend_copy(part):
        columns = lend_columns(place, part)
        return copy(
            r.side_hbm.at[0, :, columns],
            r.lent.at[:, columns],
            r.lend_ss.at[0, part],
            r.lend_rs.at[0, part],
            after,
            d,
        )

    def lend_forward(kind, quarter, part, peer):
        columns = lend_columns(quarter, part)
        return copy(
            r.lent.at[:, columns],
            r.lent.at[:, columns],
            r.lend_ss.at[kind, part],
            r.lend_rs.at[kind, part],
            s,
            peer,
        )

    def state_copy(m):
        return copy(r.xout.at[m], r.xin.at[m], r.state_ss.at[m], r.state_rs.at[m], after, d)

    def grad_copy(m):
        return copy(r.gout.at[m], r.gin.at[m], r.grad_ss.at[m], r.grad_rs.at[m], before, d)

    def meta_copy(to, slot):
        return copy(r.meta, r.meta_rx.at[slot], r.meta_ss.at[to], r.meta_rs.at[slot], to, d)

    def idx_copy(slot):
        return copy(r.idx, r.idx_rx.at[slot], r.idx_ss, r.idx_rs.at[slot], last, d)

    def hid_copy(slot):
        return copy(r.hid, r.xin.at[slot], r.state_ss.at[sections], r.state_rs.at[slot], 0, d)

    def unit_copy(m, to):
        return copy(r.unit_tx.at[m], r.unit_rx, r.unit_ss.at[m], r.unit_rs, to, d)

    def loss_copy(m, to):
        return copy(r.loss_tx.at[m], r.loss_rx, r.loss_ss.at[m], r.loss_rs, to, d)

    def fin_copy(m, to):
        return copy(r.gout.at[m], r.fin_rx, r.fin_ss.at[m], r.fin_rs, to, d)

    def table_rows(owner):
        return pl.ds(pl.multiple_of(owner * z.doc_rows, z.doc_rows), z.doc_rows)

    def table_copy(to, owner):
        return copy(
            r.docs, r.table.at[table_rows(owner), :], r.tab_ss.at[to], r.tab_rs.at[owner], s, to
        )

    @pl.when(s != 0)
    def _():
        hid_copy(s).start()

    @pl.when(s == 0)
    def _():
        r.xin[0] = r.hid[...]

    other_sections(lambda to: meta_copy(to, s).start())
    r.meta_rx[s] = r.meta[...]

    @pl.when(s != last)
    def _():
        idx_copy(s).start()

    @pl.when(is_attention)
    def _():
        for part in range(parts):
            lend_copy(part).start()

    r.gain_grad[...] = jnp.zeros_like(r.gain_grad)
    r.fgain_grad[...] = jnp.zeros_like(r.fgain_grad)

    if not z.summed:

        @pl.when(is_ffn)
        def _():
            r.tab_grad[...] = jnp.zeros_like(r.tab_grad)


    if not z.summed:

        @pl.when(s != last)
        def _():
            r.dproj[...] = jnp.zeros_like(r.dproj)

    r.dbias[...] = jnp.zeros_like(r.dbias)
    gain = r.gain[...]
    fgain = r.fgain[...].reshape(1, width)

    def wait_meta(m):
        @pl.when(m != s)
        def _():
            meta_copy(0, m).wait_recv()

    def load_state(m):
        states = r.xin[m].astype(F32)
        inverse = rms_inverse(states)
        return states, inverse, states * inverse

    low_half = lax.broadcasted_iota(jnp.int32, (1, 128), 1) < DH

    def half_of(value, upper):
        keep = jnp.logical_not(low_half) if upper else low_half
        return jnp.where(keep, value.astype(F32), 0.0).astype(BF16)

    def attention_setup():
        buckets = r.buckets[...]
        for h in range(H):
            total = jnp.zeros(buckets.shape, F32)
            for b in range(32):
                total = jnp.where(buckets == b, r.bias[h : h + 1, b : b + 1], total)
            r.bias_sc[h] = total

    def attention_table():
        buckets = r.buckets[...]
        ones = jnp.ones((16, 128), BF16)
        head_row = lax.broadcasted_iota(jnp.int32, (16, 32), 0)

        def head(h, carry):
            grad = r.dbias[h]
            rest = jnp.concatenate(
                [
                    jnp.sum(jnp.where(buckets == b, grad, 0.0), axis=0, keepdims=True)
                    for b in range(32)
                ],
                axis=0,
            )
            total = jnp.zeros((16, 32), F32)
            for _ in range(3):
                part = rest.astype(BF16)
                total = total + nt(ones, part)
                rest = rest - part.astype(F32)
            return carry + jnp.where(head_row == h, total, 0.0)

        r.tab_grad[...] = lax.fori_loop(0, H, head, jnp.zeros((16, 32), F32))

    def turn(source, slab, start):
        size = FF_STEP // z.chunk
        first = slab * z.slab_chunks + start // z.chunk
        r.pool[first : first + size] = source[:, start : start + FF_STEP].T.reshape(
            size, z.chunk, width
        )

    def turned(slab, start, stop):
        first = slab * z.slab_chunks
        return r.pool[first + start // z.chunk : first + stop // z.chunk].reshape(
            stop - start, width
        )

    def attention_forward(m):
        states, inverse, scaled = load_state(m)
        normed = scaled * gain
        r.left[0, :, block(m)] = normed.T.astype(BF16)
        normed_low = normed.astype(BF16)
        for start in range(0, 3 * head_width, head_width):
            r.qkv[block(m), start : start + head_width] = nn(
                normed_low, r.main[:, start : start + head_width]
            ).astype(BF16)
        live = r.meta_rx[m, 0:1, :] > 0.5
        row_query = lax.broadcasted_iota(jnp.int32, (rows, rows), 0) // query_len
        column_query = lax.broadcasted_iota(jnp.int32, (rows, rows), 1) // query_len
        keep = jnp.logical_and(row_query == column_query, live)
        for pair in range(H // 2):
            at = pair * 128
            query = r.qkv[block(m), at : at + 128]
            keys = r.qkv[block(m), head_width + at : head_width + at + 128]
            values = r.qkv[block(m), 2 * head_width + at : 2 * head_width + at + 128]
            contexts = []
            for upper in (0, 1):
                h = 2 * pair + upper
                raw = nt(half_of(query, upper), keys)
                biased = raw.reshape(batch_size, query_len, rows) + r.bias_sc[h][None]
                scores = jnp.where(keep, biased.reshape(rows, rows), MASK_FILL)
                top = jnp.max(scores, axis=-1, keepdims=True)
                grown = jnp.exp(scores - top)
                soft = grown / jnp.sum(grown, axis=-1, keepdims=True)
                r.probs[m, h] = soft
                contexts.append(nn(soft.astype(BF16), values))
            r.right[0, block(m), 3 * head_width + at : 3 * head_width + at + 128] = jnp.where(
                low_half, contexts[0], contexts[1]
            ).astype(BF16)
        context = r.right[0, block(m), 3 * head_width :]
        return states + nt(context, r.main[:, 3 * head_width :])

    def attention_backward(m):
        states, inverse, scaled = load_state(m)
        grad_low = r.gin[m]
        grad = grad_low.astype(F32)
        r.left[1, :, block(m)] = grad.T.astype(BF16)
        grad_context = nn(grad_low, r.main[:, 3 * head_width :]).astype(BF16)
        for pair in range(H // 2):
            at = pair * 128
            query = r.qkv[block(m), at : at + 128]
            keys = r.qkv[block(m), head_width + at : head_width + at + 128]
            values = r.qkv[block(m), 2 * head_width + at : 2 * head_width + at + 128]
            grad_pair = grad_context[:, at : at + 128]
            found = []
            for upper in (0, 1):
                h = 2 * pair + upper
                soft = r.probs[m, h]
                grad_soft = nt(half_of(grad_pair, upper), values)
                moved = soft * grad_soft
                grad_scores = moved - soft * jnp.sum(moved, axis=-1, keepdims=True)
                r.dbias[h] += jnp.sum(grad_scores.reshape(batch_size, query_len, rows), axis=0)
                scores_low = grad_scores.astype(BF16)
                found.append(
                    (
                        nn(scores_low, keys),
                        tn(scores_low, query),
                        tn(soft.astype(BF16), grad_pair),
                    )
                )
            for third in range(3):
                start = third * head_width + at
                r.right[0, block(m), start : start + 128] = jnp.where(
                    low_half, found[0][third], found[1][third]
                ).astype(BF16)
        grad_normed = nn(r.right[0, block(m), : 3 * head_width], turned(0, 0, 3 * head_width))
        grad_states, grad_gain = rms_back(scaled, inverse, gain, grad_normed)
        r.gain_grad[...] += grad_gain
        return grad + grad_states

    def ffn_forward(m):
        states, inverse, scaled = load_state(m)
        normed = scaled * gain
        r.left[0, :, block(m)] = normed.T.astype(BF16)
        normed_low = normed.astype(BF16)
        outputs = states
        for start in range(0, ff, FF_STEP):
            columns = slice(start, start + FF_STEP)
            gate = nn(normed_low, r.main[:, columns])
            up = nn(normed_low, r.lent[:, columns])
            square = gate * gate
            bent = jnp.tanh(GELU_C * gate * (1.0 + GELU_A * square))
            half = 0.5 * (1.0 + bent)
            smooth = gate * half
            slope = half + 0.5 * gate * (1.0 - bent * bent) * (
                GELU_C * (1.0 + 3.0 * GELU_A * square)
            )
            hidden = (smooth * up).astype(BF16)
            r.right[1, block(m), columns] = hidden
            r.right[0, block(m), columns] = (slope * up).astype(BF16)
            r.right[2, block(m), columns] = smooth.astype(BF16)
            outputs = outputs + nn(hidden, turned(1, start, start + FF_STEP))
        return outputs

    def ffn_backward(m, grad):
        states, inverse, scaled = load_state(m)
        grad_low = grad.astype(BF16)
        r.left[1, :, block(m)] = grad.T.astype(BF16)
        grad_normed = jnp.zeros((rows, width), F32)
        for start in range(0, ff, FF_STEP):
            columns = slice(start, start + FF_STEP)
            grad_hidden = nn(grad_low, r.side[:, columns])
            grad_gate = (grad_hidden * r.right[0, block(m), columns].astype(F32)).astype(BF16)
            grad_up = (grad_hidden * r.right[2, block(m), columns].astype(F32)).astype(BF16)
            r.right[0, block(m), columns] = grad_gate
            r.right[2, block(m), columns] = grad_up
            grad_normed = (
                grad_normed
                + nn(grad_gate, turned(0, start, start + FF_STEP))
                + nn(grad_up, turned(2, start, start + FF_STEP))
            )
        grad_states, grad_gain = rms_back(scaled, inverse, gain, grad_normed)
        r.gain_grad[...] += grad_gain
        return grad + grad_states

    def count_hits(m):
        for c in range(batch_size):
            base = r.idx_rx[m, c : c + 1, :] * DOC_LEN
            numbers = lax.broadcasted_iota(jnp.int32, (DOC_LEN, rows), 0) + base
            total = jnp.zeros((DOC_LEN, rows), F32)
            for k in range(z.retrieved):
                total = total + jnp.where(r.idx_rx[m, 8 + k : 9 + k, :] == numbers, 1.0, 0.0)
            r.counts[m, c * DOC_LEN : (c + 1) * DOC_LEN, :] = total.astype(BF16)

    def pick_docs(m):
        for c in range(batch_size):
            label = r.idx_rx[m, c : c + 1, :]

            def pick(t, picked):
                here = r.table[pl.ds(pl.multiple_of(t * DOC_LEN, DOC_LEN), DOC_LEN), :].astype(F32)
                return jnp.where(label == t, here, picked)

            picked = lax.fori_loop(
                0, dp_size * z.doc_rows // DOC_LEN, pick, jnp.zeros((DOC_LEN, z.vector), F32)
            )
            r.own_docs[m, c * DOC_LEN : (c + 1) * DOC_LEN, :] = picked.astype(BF16)

    def loss_and_grad(m, unit):
        docs = r.own_docs[m]
        sims = nt(docs, unit)
        count = r.counts[m].astype(F32)
        imputed = jnp.sum(count * sims, axis=0, keepdims=True) / z.retrieved
        grown = count * jnp.exp(sims)
        imputed_mass = jnp.exp(imputed)
        mass = imputed_mass + jnp.concatenate(
            [
                jnp.sum(grown[c * DOC_LEN : (c + 1) * DOC_LEN], axis=0, keepdims=True)
                for c in range(batch_size)
            ],
            axis=0,
        )
        weighted = jnp.log(mass) * r.meta_rx[m, 1:2, :]
        candidate = lax.broadcasted_iota(jnp.int32, (batch_size, 1), 0)
        losses = jnp.zeros((1, rows), F32)
        grad_tokens = jnp.zeros((batch_size, rows), F32)
        for q in range(batch_size):
            own = token_query == q
            score = jnp.sum(jnp.where(own, weighted, 0.0), axis=1, keepdims=True)
            top = jnp.max(score, axis=0, keepdims=True)
            risen = jnp.exp(score - top)
            total = jnp.sum(risen, axis=0, keepdims=True)
            chosen_one = (candidate == q).astype(F32)
            loss = top + jnp.log(total) - jnp.sum(score * chosen_one, axis=0, keepdims=True)
            losses = losses + jnp.where(lane == q, loss, 0.0)
            grad_tokens = grad_tokens + jnp.where(own, risen / total - chosen_one, 0.0)
        grad_mass = grad_tokens * r.meta_rx[m, 1:2, :] / mass
        shared = jnp.sum(grad_mass, axis=0, keepdims=True) * imputed_mass / z.retrieved
        grad_sims = count * shared + jnp.concatenate(
            [
                grown[c * DOC_LEN : (c + 1) * DOC_LEN] * grad_mass[c : c + 1]
                for c in range(batch_size)
            ],
            axis=0,
        )
        high = grad_sims.astype(BF16)
        rest = (grad_sims - high.astype(F32)).astype(BF16)
        return losses, tn(high, docs) + tn(rest, docs)

    def finish_states(m, states):
        inverse = rms_inverse(states)
        scaled = states * inverse
        normed = (scaled * fgain).astype(BF16)
        projected = nn(normed, r.proj[...])
        size = lax.rsqrt(jnp.sum(projected * projected, axis=-1, keepdims=True) + EPS_NORM)
        exact = projected * size
        unit = exact.astype(BF16)
        losses, grad_unit = loss_and_grad(m, unit)
        r.unit_tx[m] = unit
        r.loss_tx[m] = jnp.broadcast_to(losses, (8, rows))

        @pl.when(m != last)
        def _():
            unit_copy(m, m).start()
            loss_copy(m, m).start()

        grad_projected = (
            size * (grad_unit - exact * jnp.sum(grad_unit * exact, axis=-1, keepdims=True))
        ).astype(BF16)
        r.xout[m] = normed
        r.final_right[block(m), :] = grad_projected
        grad_normed = nt(grad_projected, r.proj[...])
        grad_states, grad_gain = rms_back(scaled, inverse, fgain, grad_normed)
        r.fgain_grad[...] += grad_gain
        return grad_states

    def loop(body):
        def step(m, carry):
            body(m)
            return carry

        lax.fori_loop(0, sections, step, 0)

    def wait_state(m):
        @pl.when(jnp.logical_or(s != 0, m != 0))
        def _():
            state_copy(m).wait_recv()

    @pl.when(is_attention)
    def _():
        attention_setup()
        main_load().wait()

        def forward(m):
            wait_meta(m)
            wait_state(m)
            r.xout[m] = attention_forward(m).astype(BF16)
            state_copy(m).start()

        loop(forward)
        for start in range(0, ff, FF_STEP):
            turn(r.main, 0, start)

        def backward(m):
            grad_copy(m).wait_recv()
            r.gout[m] = attention_backward(m).astype(BF16)

            @pl.when(s != 0)
            def _():
                grad_copy(m).start()

            @pl.when(jnp.logical_and(s == 0, m != 0))
            def _():
                fin_copy(m, m).start()

        loop(backward)
        if not z.summed:
            attention_table()

    @pl.when(is_ffn)
    def _():
        turns = [(r.main, 0, start) for start in range(0, ff, FF_STEP)]
        turns += [(r.side, 1, start) for start in range(0, ff, FF_STEP)]
        main_load().wait()
        side_load().wait()
        for part in range(parts):
            lend_copy(part).wait_recv()
            lend_forward(1, place, part, core_peer).start()
            lend_forward(2, place, part, far_peer).start()
            for one in turns[part :: parts]:
                turn(*one)

        @pl.when(s == last)
        def _():
            r.idx_rx[last] = r.idx[...]
            r.table[table_rows(d), :] = r.docs[...]
            peers(lambda to: table_copy(to, d).start())

            def prepare(m):
                @pl.when(m != last)
                def _():
                    idx_copy(m).wait_recv()

                count_hits(m)

            loop(prepare)

        for part in range(parts):
            lend_forward(2, far_place, part, far_peer).wait_recv()
            lend_forward(3, far_place, part, core_peer).start()
        for part in range(parts):
            lend_forward(1, place, part, core_peer).wait_recv()
            lend_forward(3, far_place, part, core_peer).wait_recv()

        def turn_lent():
            for start in range(0, ff, FF_STEP):
                turn(r.lent, 2, start)

        @pl.when(s == last)
        def _():
            peers(lambda owner: table_copy(owner, owner).wait_recv())
            loop(pick_docs)
            turn_lent()
            loop(wait_meta)

            def both(m):
                wait_state(m)
                states = ffn_forward(m)
                grad = finish_states(m, states)
                r.gout[m] = ffn_backward(m, grad).astype(BF16)
                grad_copy(m).start()

            loop(both)
            r.dproj[...] = tn(r.xout[...].reshape(z.total, width), r.final_right[...])

        @pl.when(s != last)
        def _():
            def forward(m):
                wait_state(m)
                r.xout[m] = ffn_forward(m).astype(BF16)
                state_copy(m).start()

            loop(forward)
            turn_lent()

            def backward(m):
                grad_copy(m).wait_recv()
                r.gout[m] = ffn_backward(m, r.gin[m].astype(F32)).astype(BF16)
                grad_copy(m).start()

            loop(backward)
            loop(wait_meta)

        for part in range(parts):
            lend_forward(1, place, part, core_peer).wait_send()
            lend_forward(2, place, part, far_peer).wait_send()
            lend_forward(3, far_place, part, core_peer).wait_send()

    if z.summed:
        sum_gradients(z, r, s, d, copy, peers, other_sections, is_attention, attention_table)

    other_sections(lambda to: meta_copy(to, s).wait_send())

    @pl.when(s != 0)
    def _():
        hid_copy(s).wait_send()
        fin_copy(0, s).wait_recv()
        r.dx[...] = r.fin_rx[...].astype(F32).reshape(batch_size, query_len, width)
        loop(lambda m: grad_copy(m).wait_send())

    @pl.when(s == 0)
    def _():
        r.dx[...] = r.gout[0].astype(F32).reshape(batch_size, query_len, width)
        for m in range(1, sections):
            fin_copy(m, m).wait_send()

    @pl.when(is_attention)
    def _():
        for part in range(parts):
            lend_copy(part).wait_send()

    def write_own(unit, losses):
        r.units[...] = unit.reshape(batch_size, query_len, z.vector)
        r.loss[...] = losses

    @pl.when(s != last)
    def _():
        idx_copy(s).wait_send()
        loop(lambda m: state_copy(m).wait_send())
        unit_copy(0, s).wait_recv()
        loss_copy(0, s).wait_recv()
        write_own(r.unit_rx[...], r.loss_rx[...])

    @pl.when(s == last)
    def _():
        peers(lambda to: table_copy(to, d).wait_send())
        for m in range(sections - 1):
            unit_copy(m, m).wait_send()
            loss_copy(m, m).wait_send()
        write_own(r.unit_tx[last], r.loss_tx[last])


def sum_gradients(z, r, s, d, copy, peers, other_sections, is_attention, attention_table):
    sections, dp_size, width, ff, share, line = z.sections, z.dp_size, z.width, z.ff, z.share, z.line
    step_columns, per_slab, units, steps = z.step_columns, z.per_slab, z.units, z.steps
    place = d // 2
    core = lax.rem(d, 2)
    peer = d + 1 - 2 * core
    last = sections - 1
    before = lax.rem(s + sections - 1, sections)
    is_ffn = jnp.logical_not(is_attention)
    orders = sum_order(line)

    def piece_rows(owner):
        return pl.ds(pl.multiple_of(owner * share, share), share)

    def gain_copy(to, slot):
        return copy(r.gain_grad, r.gain_rx.at[slot], r.gain_ss.at[to], r.gain_rs.at[slot], s, to)

    def table_copy(to, slot):
        return copy(r.tab_grad, r.tab_rx.at[slot], r.tabs_ss.at[to], r.tabs_rs.at[slot], s, to)

    def fgain_copy(to, slot):
        return copy(r.fgain_grad, r.fgain_rx.at[slot], r.fg_ss.at[to], r.fg_rs.at[slot], s, to)

    def proj_copy(to, slot):
        return copy(
            r.dproj.at[piece_rows(to), :],
            r.proj_rx.at[slot],
            r.proj_ss.at[to],
            r.proj_rs.at[slot],
            s,
            to,
        )

    def spread_copy(to, owner):
        rows = piece_rows(owner)
        return copy(
            r.proj_sum.at[rows, :],
            r.proj_sum.at[rows, :],
            r.spread_ss.at[to],
            r.spread_rs.at[owner],
            s,
            to,
        )

    def table_across(to, slot):
        return copy(r.tab_tx, r.tab_cx.at[slot], r.across_ss.at[0, to], r.across_rs.at[slot], to, d)

    def fgain_across(to):
        return copy(
            r.fgain_tx, r.fgain_sum, r.across_ss.at[1, to], r.across_rs.at[sections], to, d
        )

    def proj_across(to):
        return copy(
            r.proj_sum, r.proj_sum, r.across_ss.at[2, to], r.across_rs.at[sections + 1], to, d
        )

    def total_of(ref, count):
        total = ref[0]
        for k in range(1, count):
            total = total + ref[k]
        return total

    def to_others(body):
        for to in range(sections):

            @pl.when(s != to)
            def _():
                body(to)

    def small_first():
        peers(lambda to: gain_copy(to, d).start())
        r.gain_rx[d] = r.gain_grad[...]

        @pl.when(is_attention)
        def _():
            attention_table()
            peers(lambda to: table_copy(to, d).start())
            r.tab_rx[d] = r.tab_grad[...]

    def proj_first():
        peers(lambda to: proj_copy(to, d).start())
        peers(lambda to: fgain_copy(to, d).start())
        r.proj_rx[d] = r.dproj[piece_rows(d), :]
        r.fgain_rx[d] = r.fgain_grad[...]

    def proj_second():
        peers(lambda owner: proj_copy(owner, owner).wait_recv())
        peers(lambda owner: fgain_copy(owner, owner).wait_recv())
        r.proj_sum[piece_rows(d), :] = total_of(r.proj_rx, dp_size)
        r.fgain_tx[...] = total_of(r.fgain_rx, dp_size)
        r.fgain_sum[...] = r.fgain_tx[...]
        peers(lambda to: spread_copy(to, d).start())
        to_others(lambda to: fgain_across(to).start())

    def proj_third():
        peers(lambda owner: spread_copy(owner, owner).wait_recv())
        to_others(lambda to: proj_across(to).start())

    def small_second():
        peers(lambda owner: gain_copy(owner, owner).wait_recv())
        gain_sum = jnp.broadcast_to(total_of(r.gain_rx, dp_size), (8, width))
        r.gain_out[...] = pltpu.roll(gain_sum, width - d * share, 1)[0:1, :share]

        @pl.when(is_attention)
        def _():
            peers(lambda owner: table_copy(owner, owner).wait_recv())
            r.tab_tx[...] = total_of(r.tab_rx, dp_size)
            r.tab_cx[s // 2] = r.tab_tx[...]
            to_others(lambda to: table_across(to, s // 2).start())

    def small_last():
        for source in range(0, sections, 2):

            @pl.when(s != source)
            def _():
                table_across(source, source // 2).wait_recv()

        r.table_out[...] = total_of(r.tab_cx, (sections + 1) // 2)[:H]

        @pl.when(s != last)
        def _():
            fgain_across(last).wait_recv()
            proj_across(last).wait_recv()

        r.fgain_out[...] = r.fgain_sum[...].reshape(width)
        r.proj_out[...] = r.proj_sum[...]
        peers(lambda to: gain_copy(to, d).wait_send())

        @pl.when(is_attention)
        def _():
            peers(lambda to: table_copy(to, d).wait_send())
            to_others(lambda to: table_across(to, s // 2).wait_send())

        @pl.when(s == last)
        def _():
            peers(lambda to: proj_copy(to, d).wait_send())
            peers(lambda to: fgain_copy(to, d).wait_send())
            peers(lambda to: spread_copy(to, d).wait_send())
            to_others(lambda to: fgain_across(to).wait_send())
            to_others(lambda to: proj_across(to).wait_send())

    def target(i):
        found = jnp.int32(0)
        for k in range(line):
            found = jnp.where(place == k, orders[k][i], found)
        return found

    targets = [target(i) for i in range(line)]

    def parts_of(t):
        i, u = t // units, lax.rem(t, units)
        j = targets[0]
        for k in range(1, line):
            j = jnp.where(i == k, targets[k], j)
        slab, column = lax.rem(u, 2), u // 2
        columns = pl.ds(pl.multiple_of(column * step_columns, step_columns), step_columns)
        return j, u, slab, column, columns

    def core_copy(t):
        return copy(
            r.core_tx.at[lax.rem(t, 4)], r.pool.at[t], r.core_ss.at[t], r.core_rs.at[t], s, peer
        )

    def up_core_copy(k):
        return copy(
            r.up_core_tx.at[lax.rem(k, 4)], r.up_rx.at[k], r.up_core_ss.at[k], r.up_rs.at[k], s, peer
        )

    def up_copy(k):
        return copy(
            r.up_tx.at[lax.rem(k, 4)], r.up_rx.at[k], r.up_ss.at[k], r.up_rs.at[k], before, d
        )

    def line_view(t):
        row = pl.ds(pl.multiple_of(lax.rem(t, dp_size) * share, share), share)
        column = pl.ds(pl.multiple_of(t // dp_size * step_columns, step_columns), step_columns)
        return r.lent.at[row, column]

    def line_slot(way, j, u):
        return steps + (way * (line - 1) + j - 1 + way) * units + u

    def line_copy(t, way, j, u, to):
        slot = j - 1 + way
        return copy(
            line_view(t),
            r.pool.at[line_slot(way, j, u)],
            r.line_ss.at[t],
            r.line_rs.at[way, slot, u],
            s,
            to * 2 + core,
        )

    def theirs(j):
        return pl.ds(pl.multiple_of((j * 2 + 1 - core) * share, share), share)

    def ours(j):
        return pl.ds(pl.multiple_of((j * 2 + core) * share, share), share)

    def begin(t):
        j, u, slab, column, columns = parts_of(t)
        k = t // 2
        mixed = jnp.logical_and(is_attention, column == per_slab - 1)
        which = jnp.where(jnp.logical_or(slab == 1, mixed), 1, 0)

        @pl.when(jnp.logical_or(is_ffn, slab == 0))
        def _():
            right = r.right[slab, :, columns]

            @pl.when(t >= 4)
            def _():
                core_copy(t - 4).wait_send()

            r.core_tx[lax.rem(t, 4)] = nn(r.left[which, theirs(j), :], right).astype(BF16)
            core_copy(t).start()
            r.mine[lax.rem(t, 2)] = nn(r.left[which, ours(j), :], right)

        @pl.when(jnp.logical_and(is_ffn, slab == 1))
        def _():
            right = r.right[2, :, columns]

            @pl.when(k >= 4)
            def _():
                up_core_copy(k - 4).wait_send()

            r.up_core_tx[lax.rem(k, 4)] = nn(r.left[0, theirs(j), :], right).astype(BF16)
            up_core_copy(k).start()
            r.up_mine[...] = nn(r.left[0, ours(j), :], right)

    def finish(t):
        j, u, slab, column, columns = parts_of(t)
        k = t // 2
        total = r.mine.at[lax.rem(t, 2)]

        @pl.when(jnp.logical_or(is_ffn, slab == 0))
        def _():
            core_copy(t).wait_recv()
            total[...] += r.pool[t].astype(F32)

        @pl.when(jnp.logical_and(is_attention, slab == 1))
        def _():
            up_copy(k).wait_recv()
            total[...] = r.up_rx[k].astype(F32)

        @pl.when(jnp.logical_and(is_ffn, slab == 1))
        def _():
            up_core_copy(k).wait_recv()

            @pl.when(k >= 4)
            def _():
                up_copy(k - 4).wait_send()

            r.up_tx[lax.rem(k, 4)] = (r.up_mine[...] + r.up_rx[k].astype(F32)).astype(BF16)
            up_copy(k).start()

        way = jnp.where(j < place, 1, 0)

        @pl.when(jnp.logical_and(place > 0, j >= place))
        def _():
            line_copy(t, 0, j, u, place).wait_recv()
            total[...] += r.pool[line_slot(0, j, u)].astype(F32)

        @pl.when(jnp.logical_and(place < line - 1, j <= place))
        def _():
            line_copy(t, 1, j, u, place).wait_recv()
            total[...] += r.pool[line_slot(1, j, u)].astype(F32)

        @pl.when(jnp.logical_and(j == place, slab == 0))
        def _():
            r.main_out[0, :, columns] = total[...]

        @pl.when(jnp.logical_and(j == place, slab == 1))
        def _():
            r.side_out[0, :, columns] = total[...]

        @pl.when(j != place)
        def _():
            line_view(t)[...] = total[...].astype(BF16)
            line_copy(t, way, j, u, place + 1 - 2 * way).start()

    pl.semaphore_signal(r.core_ready, inc=1, device_id=(s, peer), device_id_type=MESH)

    @pl.when(place > 0)
    def _():
        pl.semaphore_signal(r.line_ready, inc=1, device_id=(s, d - 2), device_id_type=MESH)

    @pl.when(place < line - 1)
    def _():
        pl.semaphore_signal(r.line_ready, inc=1, device_id=(s, d + 2), device_id_type=MESH)

    @pl.when(s == last)
    def _():
        proj_first()

    pl.semaphore_wait(r.core_ready, 1)
    begin(jnp.int32(0))
    neighbours = jnp.where(place > 0, 1, 0) + jnp.where(place < line - 1, 1, 0)
    pl.semaphore_wait(r.line_ready, neighbours)

    def step(t, carry):
        @pl.when(t < steps)
        def _():
            begin(t)

        finish(t - 1)

        @pl.when(jnp.logical_and(s == last, t == 2))
        def _():
            proj_second()

        @pl.when(t == 4)
        def _():
            small_first()

        @pl.when(jnp.logical_and(s == last, t == 6))
        def _():
            proj_third()

        @pl.when(t == units + 4)
        def _():
            small_second()

        return carry

    lax.fori_loop(1, steps + 1, step, 0)
    small_last()

    def drain(t, carry):
        line_copy(t, 0, 1, 0, place).wait_send()
        return carry

    lax.fori_loop(0, steps - units, drain, 0)

    def drain_core(t, carry):
        slab = lax.rem(t, 2)

        @pl.when(jnp.logical_or(is_ffn, slab == 0))
        def _():
            core_copy(t).wait_send()

        return carry

    lax.fori_loop(steps - 4, steps, drain_core, 0)

    @pl.when(is_ffn)
    def _():
        for k in range(steps // 2 - 4, steps // 2):
            up_core_copy(k).wait_send()
            up_copy(k).wait_send()


def relay(z, hid, lengths, labels, chosen, main, side, gain, bias, buckets, fgain, proj, docs):
    dma = pltpu.SemaphoreType.DMA
    shape = jax.ShapeDtypeStruct
    sections, rows, width, ff, dp_size = z.sections, z.rows, z.width, z.ff, z.dp_size
    share, steps, units = z.share, z.steps, z.units
    piece = (share, z.step_columns)
    vmem = pl.BlockSpec(memory_space=VMEM)
    smem = pl.BlockSpec(memory_space=pltpu.SMEM)
    anywhere = pl.BlockSpec(memory_space=pl.ANY)
    inputs = dict(
        hid=(hid, vmem),
        lengths=(lengths, smem),
        labels=(labels, smem),
        chosen=(chosen, vmem),
        main_hbm=(main, anywhere),
        side_hbm=(side, anywhere),
        gain=(gain, vmem),
        bias=(bias, vmem),
        buckets=(buckets, vmem),
        fgain=(fgain, vmem),
        proj=(proj, vmem),
        docs=(docs, vmem),
    )
    outputs = dict(
        units=shape((z.batch_size, z.query_len, z.vector), BF16),
        loss=shape((8, rows), F32),
        dx=shape((z.batch_size, z.query_len, width), F32),
    )
    scratch = dict(
        main=VMEM((width, ff), BF16),
        side=VMEM((width, ff), BF16),
        lent=VMEM((width, ff), BF16),
        xin=VMEM((sections, rows, width), BF16),
        xout=VMEM((sections, rows, width), BF16),
        gin=VMEM((sections, rows, width), BF16),
        gout=VMEM((sections, rows, width), BF16),
        meta=VMEM((8, rows), F32),
        meta_rx=VMEM((sections, 8, rows), F32),
        idx=VMEM((8 + z.retrieved, rows), jnp.int32),
        idx_rx=VMEM((sections, 8 + z.retrieved, rows), jnp.int32),
        own_docs=VMEM((sections, z.batch_size * DOC_LEN, z.vector), BF16),
        table=VMEM((dp_size * z.doc_rows, z.vector), BF16),
        counts=VMEM((sections, z.batch_size * DOC_LEN, rows), BF16),
        pool=VMEM((z.pool, z.chunk, width), BF16),
        final_right=VMEM((z.total, z.vector), BF16),
        qkv=VMEM((z.total, 3 * H * DH), BF16),
        probs=VMEM((sections, H, rows, rows), F32),
        bias_sc=VMEM((H, z.query_len, rows), F32),
        dbias=VMEM((H, z.query_len, rows), F32),
        fin_rx=VMEM((rows, width), BF16),
        unit_tx=VMEM((sections, rows, z.vector), BF16),
        unit_rx=VMEM((rows, z.vector), BF16),
        loss_tx=VMEM((sections, 8, rows), F32),
        loss_rx=VMEM((8, rows), F32),
        load_sem=dma((2,)),
        state_ss=dma((sections + 1,)),
        state_rs=dma((sections,)),
        grad_ss=dma((sections,)),
        grad_rs=dma((sections,)),
        meta_ss=dma((sections,)),
        meta_rs=dma((sections,)),
        idx_ss=dma,
        idx_rs=dma((sections,)),
        tab_ss=dma((dp_size,)),
        tab_rs=dma((dp_size,)),
        lend_ss=dma((4, z.parts)),
        lend_rs=dma((4, z.parts)),
        fin_ss=dma((sections,)),
        fin_rs=dma,
        unit_ss=dma((sections,)),
        unit_rs=dma,
        loss_ss=dma((sections,)),
        loss_rs=dma,
    )
    factors = dict(left=((2, width, z.total), BF16), right=((3, z.total, ff), BF16))
    partials = dict(
        gain_grad=((1, width), F32),
        fgain_grad=((1, width), F32),
        tab_grad=((16, 32), F32),
        dproj=((width, z.vector), F32),
    )
    if z.summed:
        outputs |= dict(
            main_out=shape((1, share, ff), F32),
            side_out=shape((1, share, ff), F32),
            gain_out=shape((1, share), F32),
            table_out=shape((H, 32), F32),
            fgain_out=shape((width,), F32),
            proj_out=shape((width, z.vector), F32),
        )
        scratch |= {name: VMEM(*kind) for name, kind in (factors | partials).items()}
        scratch |= dict(
            mine=VMEM((2,) + piece, F32),
            up_mine=VMEM(piece, F32),
            core_tx=VMEM((4,) + piece, BF16),
            up_core_tx=VMEM((4,) + piece, BF16),
            up_tx=VMEM((4,) + piece, BF16),
            up_rx=VMEM((steps // 2,) + piece, BF16),
            gain_rx=VMEM((dp_size, 1, width), F32),
            tab_rx=VMEM((dp_size, 16, 32), F32),
            tab_tx=VMEM((16, 32), F32),
            tab_cx=VMEM(((sections + 1) // 2, 16, 32), F32),
            fgain_rx=VMEM((dp_size, 1, width), F32),
            fgain_tx=VMEM((1, width), F32),
            fgain_sum=VMEM((1, width), F32),
            proj_sum=VMEM((width, z.vector), F32),
            proj_rx=VMEM((dp_size, share, z.vector), F32),
            core_ss=dma((steps,)),
            core_rs=dma((steps,)),
            up_core_ss=dma((steps // 2,)),
            up_ss=dma((steps // 2,)),
            up_rs=dma((steps // 2,)),
            line_ss=dma((steps,)),
            line_rs=dma((2, z.line - 1, units)),
            core_ready=pltpu.SemaphoreType.REGULAR,
            line_ready=pltpu.SemaphoreType.REGULAR,
            gain_ss=dma((dp_size,)),
            gain_rs=dma((dp_size,)),
            tabs_ss=dma((dp_size,)),
            tabs_rs=dma((dp_size,)),
            fg_ss=dma((dp_size,)),
            fg_rs=dma((dp_size,)),
            across_ss=dma((3, sections)),
            across_rs=dma((sections + 2,)),
            proj_ss=dma((dp_size,)),
            proj_rs=dma((dp_size,)),
            spread_ss=dma((dp_size,)),
            spread_rs=dma((dp_size,)),
        )
    else:
        outputs |= {name: shape(*kind) for name, kind in (factors | partials).items()}
    results = pl.pallas_call(
        functools.partial(relay_kernel, z, (*inputs, *outputs, *scratch)),
        out_shape=tuple(outputs.values()),
        in_specs=[spec for _, spec in inputs.values()],
        out_specs=(vmem,) * len(outputs),
        scratch_shapes=list(scratch.values()),
        compiler_params=pltpu.CompilerParams(
            collective_id=0, has_side_effects=True, vmem_limit_bytes=62 * 2**20
        ),
        name="relay",
    )(*[value for value, _ in inputs.values()])
    return types.SimpleNamespace(**dict(zip(outputs, results, strict=True)))


def deliver_kernel(count, *refs):
    for k in range(count):
        refs[count + 1 + k][...] = refs[k][...]
    losses, out = refs[count], refs[-1]
    out[...] = losses[0:1, : out.shape[0]].reshape(out.shape)


def deliver(values, losses, queries):
    count = len(values)
    vmem = pl.BlockSpec(memory_space=VMEM)
    return pl.pallas_call(
        functools.partial(deliver_kernel, count),
        out_shape=tuple(jax.ShapeDtypeStruct(v.shape, v.dtype) for v in values)
        + (jax.ShapeDtypeStruct((queries,), F32),),
        in_specs=[vmem] * (count + 1),
        out_specs=(vmem,) * (count + 1),
        name="deliver",
    )(*values, losses)


def sums_outside(z, out):
    head_width = H * DH
    section = lax.axis_index("section")
    is_attention = section % 2 == 0
    left, right = out.left, out.right
    second = jnp.where(is_attention, left[1], left[0])
    main_grad = jnp.concatenate(
        [nn(left[0], right[0, :, : 3 * head_width]), nn(second, right[0, :, 3 * head_width :])],
        axis=1,
    )
    up_grad = lax.ppermute(
        nn(left[0], right[2]).astype(BF16),
        "section",
        [(k, k - 1) for k in range(1, z.sections)],
    )
    side_grad = jnp.where(is_attention, up_grad.astype(F32), nn(left[1], right[1]))
    scatter = functools.partial(
        lax.psum_scatter, axis_name="dp", scatter_dimension=0, tiled=True
    )
    table, fgain, proj = lax.psum(
        (out.tab_grad[:H], out.fgain_grad[0], out.dproj), ("section", "dp")
    )
    return (
        scatter(main_grad)[None],
        scatter(side_grad)[None],
        scatter(out.gain_grad[0])[None],
        table.T,
        fgain,
        proj,
    )


def per_device(
    hidden_in,
    lengths,
    labels,
    chosen,
    slab_main,
    slab_side,
    section_gains,
    rel_bias,
    final_gain,
    out_proj,
    doc_vectors,
):
    batch_size, query_len, width = hidden_in.shape
    rows = batch_size * query_len
    retrieved = chosen.shape[2]
    z = Sizes(
        lax.axis_size("section"),
        lax.axis_size("dp"),
        batch_size,
        query_len,
        retrieved,
        width,
        slab_main.shape[2],
        out_proj.shape[1],
        doc_vectors.shape[0],
    )
    buckets = jnp.asarray(np.tile(bucket_table(query_len), (1, batch_size)))
    out = relay(
        z,
        hidden_in.reshape(rows, width),
        lengths,
        labels,
        chosen.reshape(rows, retrieved),
        slab_main,
        slab_side,
        section_gains,
        rel_bias.T,
        buckets,
        final_gain,
        out_proj,
        doc_vectors,
    )
    if not z.summed:
        return (out.units, out.loss[0, :batch_size], out.dx) + sums_outside(z, out)
    names = ("units", "dx", "main_out", "side_out", "gain_out", "table_out", "fgain_out", "proj_out")
    units, dx, main, side, gain, table, fgain, proj, losses = deliver(
        [getattr(out, n) for n in names], out.loss, batch_size
    )
    return units, losses, dx, main, side, gain, table.T, fgain, proj


def solution(mesh):
    both = ("section", "dp")
    in_specs = (
        P(both, None, None),
        P(both),
        P(both),
        P(both, None, None),
        P("section", None, None),
        P("section", None, None),
        P("section", None),
        P(),
        P(),
        P(),
        P("dp", None),
    )
    out_specs = (
        P(both, None, None),
        P(both),
        P(both, None, None),
        P("section", "dp", None),
        P("section", "dp", None),
        P("section", "dp"),
        P(),
        P(),
        P(),
    )
    return jax.shard_map(
        per_device, mesh=mesh, in_specs=in_specs, out_specs=out_specs, check_vma=False
    )
```

```python
import functools
import math
import types

import jax
import jax.numpy as jnp
import numpy as np
from jax import lax
from jax.experimental import pallas as pl
from jax.experimental.pallas import tpu as pltpu
from jax.sharding import PartitionSpec as P

H = 12
DH = 64
DOC_LEN = 128
EPS_NORM = 1e-06
MASK_FILL = -1000000000.0
HIGHEST = lax.Precision.HIGHEST
MESH = pl.DeviceIdType.MESH
F32 = jnp.float32
BF16 = jnp.bfloat16
VMEM = pltpu.VMEM
GELU_C = math.sqrt(2.0 / math.pi)
GELU_A = 0.044715
FF_STEP = 768
LEND_STEP = 128


def bucket_table(query_len):
    places = np.arange(query_len)
    relative = places[None, :] - places[:, None]
    distance = np.abs(relative)
    signed_part = np.where(relative > 0, 16, 0)
    far_bucket = 8 + np.floor(np.log(np.maximum(distance, 1) / 8.0) / np.log(16.0) * 8.0).astype(
        np.int64
    )
    far_bucket = np.minimum(far_bucket, 15)
    return (signed_part + np.where(distance < 8, distance, far_bucket)).astype(np.int32)


def nn(a, b):
    return jnp.dot(a, b, preferred_element_type=F32)


def nt(a, b):
    return lax.dot_general(a, b, (((1,), (1,)), ((), ())), preferred_element_type=F32)


def tn(a, b):
    return lax.dot_general(a, b, (((0,), (0,)), ((), ())), preferred_element_type=F32)


def rms_inverse(values):
    return lax.rsqrt(jnp.mean(values * values, axis=-1, keepdims=True) + EPS_NORM)


def rms_back(scaled, inverse, gain, grad):
    inner = grad * gain
    grad_values = inverse * (inner - scaled * jnp.mean(inner * scaled, axis=-1, keepdims=True))
    return grad_values, jnp.sum(grad * scaled, axis=0, keepdims=True)


def sum_order(line):
    orders = []
    for place in range(line):
        others = [j for j in range(line) if j != place]
        others.sort(key=lambda j: (-abs(j - place), min(j, line - 1 - j)))
        orders.append(others + [place])
    return orders


class Sizes:
    def __init__(self, sections, dp_size, batch_size, query_len, retrieved, width, ff, vector, doc_rows):
        self.sections = sections
        self.dp_size = dp_size
        self.batch_size = batch_size
        self.query_len = query_len
        self.retrieved = retrieved
        self.width = width
        self.ff = ff
        self.vector = vector
        self.doc_rows = doc_rows
        self.rows = batch_size * query_len
        self.total = sections * self.rows
        self.parts = ff // 4 // LEND_STEP
        self.share = width // dp_size
        self.summed = self.share % 16 == 0 and dp_size % 2 == 0
        self.line = dp_size // 2
        self.step_columns = H * DH
        self.per_slab = ff // self.step_columns
        self.units = 2 * self.per_slab
        self.steps = self.line * self.units
        self.chunk = self.share if self.summed else H * 8
        self.slab_chunks = ff // self.chunk
        arriving = self.steps + 2 * (self.line - 1) * self.units
        self.pool = max(3 * self.slab_chunks, arriving if self.summed else 0)


def relay_kernel(z, names, *refs):
    r = types.SimpleNamespace(**dict(zip(names, refs, strict=True)))
    s = lax.axis_index("section")
    d = lax.axis_index("dp")
    sections, dp_size, rows, width, ff = z.sections, z.dp_size, z.rows, z.width, z.ff
    batch_size, query_len, parts = z.batch_size, z.query_len, z.parts
    head_width = H * DH
    last = sections - 1
    after = lax.rem(s + 1, sections)
    before = lax.rem(s + sections - 1, sections)
    group = d - lax.rem(d, 4)
    place = lax.rem(d, 4)
    core_peer = group + place + 1 - 2 * lax.rem(place, 2)
    far_place = lax.rem(place + 2, 4)
    far_peer = group + far_place
    is_attention = lax.rem(s, 2) == 0
    is_ffn = jnp.logical_not(is_attention)

    def copy(src, dst, send_sem, recv_sem, section, dp):
        return pltpu.make_async_remote_copy(
            src_ref=src,
            dst_ref=dst,
            send_sem=send_sem,
            recv_sem=recv_sem,
            device_id=(section, dp),
            device_id_type=MESH,
        )

    def block(m):
        return pl.ds(pl.multiple_of(m * rows, rows), rows)

    def peers(body):
        def step(k, carry):
            body(lax.rem(d + k, dp_size))
            return carry

        lax.fori_loop(1, dp_size, step, 0)

    def other_sections(body):
        for k in range(1, sections):
            body(lax.rem(s + k, sections))

    def main_load():
        return pltpu.make_async_copy(r.main_hbm.at[0], r.main, r.load_sem.at[0])

    def side_load():
        return pltpu.make_async_copy(r.side_hbm.at[0], r.side, r.load_sem.at[1])

    small_loads = [
        pltpu.make_async_copy(getattr(r, name + "_hbm"), getattr(r, name), r.small_sem.at[k])
        for k, name in enumerate(("chosen", "bias", "buckets", "gain", "fgain", "proj"))
    ]
    for one in small_loads:
        one.start()

    def hid_load():
        return pltpu.make_async_copy(r.hid_hbm, r.xin.at[0], r.load_sem.at[2])

    def docs_load():
        return pltpu.make_async_copy(r.docs_hbm, r.table.at[table_rows(d), :], r.load_sem.at[2])

    def table_rows(owner):
        return pl.ds(pl.multiple_of(owner * z.doc_rows, z.doc_rows), z.doc_rows)

    @pl.when(s == 0)
    def _():
        hid_load().start()

    main_load().start()

    @pl.when(is_ffn)
    def _():
        side_load().start()

    @pl.when(s == last)
    def _():
        docs_load().start()

    barrier = pltpu.get_barrier_semaphore()
    other_sections(
        lambda to: pl.semaphore_signal(barrier, inc=1, device_id=(to, d), device_id_type=MESH)
    )
    peers(lambda to: pl.semaphore_signal(barrier, inc=1, device_id=(s, to), device_id_type=MESH))

    lane = lax.broadcasted_iota(jnp.int32, (1, rows), 1)
    token_query = lane // query_len
    token_slot = lax.rem(lane, query_len)
    length = jnp.zeros((1, rows), jnp.int32)
    for q in range(batch_size):
        length = jnp.where(token_query == q, r.lengths[q], length)
    live = jnp.where(token_slot < length, 1.0, 0.0)
    r.meta[...] = jnp.zeros_like(r.meta)
    r.meta[0:1, :] = live
    r.meta[1:2, :] = live / length.astype(F32)
    r.idx[:8, :] = jnp.zeros((8, rows), jnp.int32)
    for c in range(batch_size):
        r.idx[c : c + 1, :] = jnp.full((1, rows), r.labels[c], jnp.int32)
    for one in small_loads:
        one.wait()
    r.idx[8:, :] = r.chosen[...].T

    pl.semaphore_wait(barrier, sections - 1 + dp_size - 1)

    def lend_columns(quarter, part):
        start = quarter * (ff // 4) + part * LEND_STEP
        return pl.ds(pl.multiple_of(start, LEND_STEP), LEND_STEP)

    def lend_copy(part, half):
        columns = lend_columns(place, part)
        depth = slice(half * (width // 2), (half + 1) * (width // 2))
        return copy(
            r.side_hbm.at[0, depth, columns],
            r.lent.at[depth, columns],
            r.lend_ss.at[0, part, half],
            r.lend_rs.at[0, part, half],
            after,
            d,
        )

    def lend_forward(kind, quarter, part, half, peer):
        columns = lend_columns(quarter, part)
        depth = slice(half * (width // 2), (half + 1) * (width // 2))
        return copy(
            r.lent.at[depth, columns],
            r.lent.at[depth, columns],
            r.lend_ss.at[kind, part, half],
            r.lend_rs.at[kind, part, half],
            s,
            peer,
        )

    pieces = [(part, half) for part in range(parts) for half in range(2)]

    def state_copy(m):
        return copy(r.xout.at[m], r.xin.at[m], r.state_ss.at[m], r.state_rs.at[m], after, d)

    def grad_copy(m):
        return copy(r.gout.at[m], r.gin.at[m], r.grad_ss.at[m], r.grad_rs.at[m], before, d)

    def meta_copy(to, slot):
        return copy(r.meta, r.meta_rx.at[slot], r.meta_ss.at[to], r.meta_rs.at[slot], to, d)

    def idx_copy(slot):
        return copy(r.idx, r.idx_rx.at[slot], r.idx_ss, r.idx_rs.at[slot], last, d)

    def hid_copy(slot):
        return copy(r.hid_hbm, r.xin.at[slot], r.state_ss.at[sections], r.state_rs.at[slot], 0, d)

    def unit_copy(m, to):
        return copy(r.unit_tx.at[m], r.unit_rx, r.unit_ss.at[m], r.unit_rs, to, d)

    def loss_copy(m, to):
        return copy(r.loss_tx.at[m], r.loss_rx, r.loss_ss.at[m], r.loss_rs, to, d)

    def fin_copy(m, to):
        return copy(r.gout.at[m], r.fin_rx, r.fin_ss.at[m], r.fin_rs, to, d)

    def table_copy(to, owner):
        return copy(
            r.docs_hbm, r.table.at[table_rows(owner), :], r.tab_ss.at[to], r.tab_rs.at[owner], s, to
        )

    def table_near(owner):
        return copy(
            r.docs_hbm,
            r.table.at[table_rows(owner), :],
            r.tab_ss.at[core_peer],
            r.tab_rs.at[owner],
            s,
            core_peer,
        )

    def table_forward(owner):
        rows = table_rows(owner)
        return copy(
            r.table.at[rows, :], r.table.at[rows, :], r.tabf_ss.at[owner], r.tab_rs.at[owner], s, core_peer
        )

    def far_owners(body):
        def step(k, carry):
            body(lax.rem(d + 2 * k, dp_size))
            return carry

        lax.fori_loop(1, dp_size // 2, step, 0)

    @pl.when(s != 0)
    def _():
        hid_copy(s).start()

    @pl.when(s == last)
    def _():
        table_near(d).start()
        far_owners(lambda to: table_copy(to, d).start())

    @pl.when(is_attention)
    def _():
        for part in range(parts):
            for half in range(2):
                lend_copy(part, half).start()

    other_sections(lambda to: meta_copy(to, s).start())
    r.meta_rx[s] = r.meta[...]

    @pl.when(s != last)
    def _():
        idx_copy(s).start()

    r.gain_grad[...] = jnp.zeros_like(r.gain_grad)
    r.fgain_grad[...] = jnp.zeros_like(r.fgain_grad)

    if not z.summed:

        @pl.when(is_ffn)
        def _():
            r.tab_grad[...] = jnp.zeros_like(r.tab_grad)


    if not z.summed:

        @pl.when(s != last)
        def _():
            r.dproj[...] = jnp.zeros_like(r.dproj)

    r.dbias[...] = jnp.zeros_like(r.dbias)
    gain = r.gain[...]
    fgain = r.fgain[...].reshape(1, width)

    def wait_meta(m):
        @pl.when(m != s)
        def _():
            meta_copy(0, m).wait_recv()

    def load_state(m):
        states = r.xin[m].astype(F32)
        inverse = rms_inverse(states)
        return states, inverse, states * inverse

    low_half = lax.broadcasted_iota(jnp.int32, (1, 128), 1) < DH

    def half_of(value, upper):
        keep = jnp.logical_not(low_half) if upper else low_half
        return jnp.where(keep, value.astype(F32), 0.0).astype(BF16)

    def attention_setup():
        buckets = r.buckets[...]
        for h in range(H):
            total = jnp.zeros(buckets.shape, F32)
            for b in range(32):
                total = jnp.where(buckets == b, r.bias[h : h + 1, b : b + 1], total)
            r.bias_sc[h] = total

    def attention_table():
        buckets = r.buckets[...]
        ones = jnp.ones((16, 128), BF16)
        head_row = lax.broadcasted_iota(jnp.int32, (16, 32), 0)

        def head(h, carry):
            grad = r.dbias[h]
            rest = jnp.concatenate(
                [
                    jnp.sum(jnp.where(buckets == b, grad, 0.0), axis=0, keepdims=True)
                    for b in range(32)
                ],
                axis=0,
            )
            total = jnp.zeros((16, 32), F32)
            for _ in range(3):
                part = rest.astype(BF16)
                total = total + nt(ones, part)
                rest = rest - part.astype(F32)
            return carry + jnp.where(head_row == h, total, 0.0)

        r.tab_grad[...] = lax.fori_loop(0, H, head, jnp.zeros((16, 32), F32))

    def turn(source, slab, start):
        size = FF_STEP // z.chunk
        first = slab * z.slab_chunks + start // z.chunk
        r.pool[first : first + size] = source[:, start : start + FF_STEP].T.reshape(
            size, z.chunk, width
        )

    def turned(slab, start, stop):
        first = slab * z.slab_chunks
        return r.pool[first + start // z.chunk : first + stop // z.chunk].reshape(
            stop - start, width
        )

    def attention_forward(m):
        states, inverse, scaled = load_state(m)
        normed = scaled * gain
        r.left[0, :, block(m)] = normed.T.astype(BF16)
        normed_low = normed.astype(BF16)
        for start in range(0, 3 * head_width, head_width):
            r.qkv[block(m), start : start + head_width] = nn(
                normed_low, r.main[:, start : start + head_width]
            ).astype(BF16)
        live = r.meta_rx[m, 0:1, :] > 0.5
        row_query = lax.broadcasted_iota(jnp.int32, (rows, rows), 0) // query_len
        column_query = lax.broadcasted_iota(jnp.int32, (rows, rows), 1) // query_len
        keep = jnp.logical_and(row_query == column_query, live)
        for pair in range(H // 2):
            at = pair * 128
            query = r.qkv[block(m), at : at + 128]
            keys = r.qkv[block(m), head_width + at : head_width + at + 128]
            values = r.qkv[block(m), 2 * head_width + at : 2 * head_width + at + 128]
            contexts = []
            for upper in (0, 1):
                h = 2 * pair + upper
                raw = nt(half_of(query, upper), keys)
                biased = raw.reshape(batch_size, query_len, rows) + r.bias_sc[h][None]
                scores = jnp.where(keep, biased.reshape(rows, rows), MASK_FILL)
                top = jnp.max(scores, axis=-1, keepdims=True)
                grown = jnp.exp(scores - top)
                soft = grown / jnp.sum(grown, axis=-1, keepdims=True)
                r.probs[m, h] = soft
                contexts.append(nn(soft.astype(BF16), values))
            r.right[0, block(m), 3 * head_width + at : 3 * head_width + at + 128] = jnp.where(
                low_half, contexts[0], contexts[1]
            ).astype(BF16)
        context = r.right[0, block(m), 3 * head_width :]
        return states + nt(context, r.main[:, 3 * head_width :])

    def attention_backward(m):
        states, inverse, scaled = load_state(m)
        grad_low = r.gin[m]
        grad = grad_low.astype(F32)
        r.left[1, :, block(m)] = grad.T.astype(BF16)
        grad_context = nn(grad_low, r.main[:, 3 * head_width :]).astype(BF16)
        for pair in range(H // 2):
            at = pair * 128
            query = r.qkv[block(m), at : at + 128]
            keys = r.qkv[block(m), head_width + at : head_width + at + 128]
            values = r.qkv[block(m), 2 * head_width + at : 2 * head_width + at + 128]
            grad_pair = grad_context[:, at : at + 128]
            found = []
            for upper in (0, 1):
                h = 2 * pair + upper
                soft = r.probs[m, h]
                grad_soft = nt(half_of(grad_pair, upper), values)
                moved = soft * grad_soft
                grad_scores = moved - soft * jnp.sum(moved, axis=-1, keepdims=True)
                r.dbias[h] += jnp.sum(grad_scores.reshape(batch_size, query_len, rows), axis=0)
                scores_low = grad_scores.astype(BF16)
                found.append(
                    (
                        nn(scores_low, keys),
                        tn(scores_low, query),
                        tn(soft.astype(BF16), grad_pair),
                    )
                )
            for third in range(3):
                start = third * head_width + at
                r.right[0, block(m), start : start + 128] = jnp.where(
                    low_half, found[0][third], found[1][third]
                ).astype(BF16)
        grad_normed = nn(r.right[0, block(m), : 3 * head_width], turned(0, 0, 3 * head_width))
        grad_states, grad_gain = rms_back(scaled, inverse, gain, grad_normed)
        r.gain_grad[...] += grad_gain
        return grad + grad_states

    def ffn_forward(m):
        states, inverse, scaled = load_state(m)
        normed = scaled * gain
        r.left[0, :, block(m)] = normed.T.astype(BF16)
        normed_low = normed.astype(BF16)
        outputs = states
        for start in range(0, ff, FF_STEP):
            columns = slice(start, start + FF_STEP)
            gate = nn(normed_low, r.main[:, columns])
            up = nn(normed_low, r.lent[:, columns])
            square = gate * gate
            bent = jnp.tanh(GELU_C * gate * (1.0 + GELU_A * square))
            half = 0.5 * (1.0 + bent)
            smooth = gate * half
            slope = half + 0.5 * gate * (1.0 - bent * bent) * (
                GELU_C * (1.0 + 3.0 * GELU_A * square)
            )
            hidden = (smooth * up).astype(BF16)
            r.right[1, block(m), columns] = hidden
            r.right[0, block(m), columns] = (slope * up).astype(BF16)
            r.right[2, block(m), columns] = smooth.astype(BF16)
            outputs = outputs + nn(hidden, turned(1, start, start + FF_STEP))
        return outputs

    def ffn_backward(m, grad):
        states, inverse, scaled = load_state(m)
        grad_low = grad.astype(BF16)
        r.left[1, :, block(m)] = grad.T.astype(BF16)
        grad_normed = jnp.zeros((rows, width), F32)
        for start in range(0, ff, FF_STEP):
            columns = slice(start, start + FF_STEP)
            grad_hidden = nn(grad_low, r.side[:, columns])
            grad_gate = (grad_hidden * r.right[0, block(m), columns].astype(F32)).astype(BF16)
            grad_up = (grad_hidden * r.right[2, block(m), columns].astype(F32)).astype(BF16)
            r.right[0, block(m), columns] = grad_gate
            r.right[2, block(m), columns] = grad_up
            grad_normed = (
                grad_normed
                + nn(grad_gate, turned(0, start, start + FF_STEP))
                + nn(grad_up, turned(2, start, start + FF_STEP))
            )
        grad_states, grad_gain = rms_back(scaled, inverse, gain, grad_normed)
        r.gain_grad[...] += grad_gain
        return grad + grad_states

    def count_hits(m):
        for c in range(batch_size):
            base = r.idx_rx[m, c : c + 1, :] * DOC_LEN
            numbers = lax.broadcasted_iota(jnp.int32, (DOC_LEN, rows), 0) + base
            total = jnp.zeros((DOC_LEN, rows), F32)
            for k in range(z.retrieved):
                total = total + jnp.where(r.idx_rx[m, 8 + k : 9 + k, :] == numbers, 1.0, 0.0)
            r.counts[m, c * DOC_LEN : (c + 1) * DOC_LEN, :] = total.astype(BF16)

    def pick_docs(m):
        for c in range(batch_size):
            label = r.idx_rx[m, c : c + 1, :]

            def pick(t, picked):
                here = r.table[pl.ds(pl.multiple_of(t * DOC_LEN, DOC_LEN), DOC_LEN), :].astype(F32)
                return jnp.where(label == t, here, picked)

            picked = lax.fori_loop(
                0, dp_size * z.doc_rows // DOC_LEN, pick, jnp.zeros((DOC_LEN, z.vector), F32)
            )
            r.own_docs[m, c * DOC_LEN : (c + 1) * DOC_LEN, :] = picked.astype(BF16)

    def loss_and_grad(m, unit):
        docs = r.own_docs[m]
        sims = nt(docs, unit)
        count = r.counts[m].astype(F32)
        imputed = jnp.sum(count * sims, axis=0, keepdims=True) / z.retrieved
        grown = count * jnp.exp(sims)
        imputed_mass = jnp.exp(imputed)
        mass = imputed_mass + jnp.concatenate(
            [
                jnp.sum(grown[c * DOC_LEN : (c + 1) * DOC_LEN], axis=0, keepdims=True)
                for c in range(batch_size)
            ],
            axis=0,
        )
        weighted = jnp.log(mass) * r.meta_rx[m, 1:2, :]
        candidate = lax.broadcasted_iota(jnp.int32, (batch_size, 1), 0)
        losses = jnp.zeros((1, rows), F32)
        grad_tokens = jnp.zeros((batch_size, rows), F32)
        for q in range(batch_size):
            own = token_query == q
            score = jnp.sum(jnp.where(own, weighted, 0.0), axis=1, keepdims=True)
            top = jnp.max(score, axis=0, keepdims=True)
            risen = jnp.exp(score - top)
            total = jnp.sum(risen, axis=0, keepdims=True)
            chosen_one = (candidate == q).astype(F32)
            loss = top + jnp.log(total) - jnp.sum(score * chosen_one, axis=0, keepdims=True)
            losses = losses + jnp.where(lane == q, loss, 0.0)
            grad_tokens = grad_tokens + jnp.where(own, risen / total - chosen_one, 0.0)
        grad_mass = grad_tokens * r.meta_rx[m, 1:2, :] / mass
        shared = jnp.sum(grad_mass, axis=0, keepdims=True) * imputed_mass / z.retrieved
        grad_sims = count * shared + jnp.concatenate(
            [
                grown[c * DOC_LEN : (c + 1) * DOC_LEN] * grad_mass[c : c + 1]
                for c in range(batch_size)
            ],
            axis=0,
        )
        high = grad_sims.astype(BF16)
        rest = (grad_sims - high.astype(F32)).astype(BF16)
        return losses, tn(high, docs) + tn(rest, docs)

    def finish_states(m, states):
        inverse = rms_inverse(states)
        scaled = states * inverse
        normed = (scaled * fgain).astype(BF16)
        projected = nn(normed, r.proj[...])
        size = lax.rsqrt(jnp.sum(projected * projected, axis=-1, keepdims=True) + EPS_NORM)
        exact = projected * size
        unit = exact.astype(BF16)
        losses, grad_unit = loss_and_grad(m, unit)
        r.unit_tx[m] = unit
        r.loss_tx[m] = jnp.broadcast_to(losses, (8, rows))

        @pl.when(m != last)
        def _():
            unit_copy(m, m).start()
            loss_copy(m, m).start()

        grad_projected = (
            size * (grad_unit - exact * jnp.sum(grad_unit * exact, axis=-1, keepdims=True))
        ).astype(BF16)
        r.xout[m] = normed
        r.final_right[block(m), :] = grad_projected
        grad_normed = nt(grad_projected, r.proj[...])
        grad_states, grad_gain = rms_back(scaled, inverse, fgain, grad_normed)
        r.fgain_grad[...] += grad_gain
        return grad_states

    def loop(body):
        def step(m, carry):
            body(m)
            return carry

        lax.fori_loop(0, sections, step, 0)

    def wait_state(m):
        @pl.when(jnp.logical_or(s != 0, m != 0))
        def _():
            state_copy(m).wait_recv()

    @pl.when(is_attention)
    def _():
        attention_setup()
        main_load().wait()

        def forward(m):
            wait_meta(m)
            wait_state(m)

            @pl.when(jnp.logical_and(s == 0, m == 0))
            def _():
                hid_load().wait()

            r.xout[m] = attention_forward(m).astype(BF16)
            state_copy(m).start()

        loop(forward)
        for start in range(0, ff, FF_STEP):
            turn(r.main, 0, start)

        def backward(m):
            grad_copy(m).wait_recv()
            r.gout[m] = attention_backward(m).astype(BF16)

            @pl.when(s != 0)
            def _():
                grad_copy(m).start()

            @pl.when(jnp.logical_and(s == 0, m != 0))
            def _():
                fin_copy(m, m).start()

        loop(backward)
        if not z.summed:
            attention_table()

    @pl.when(is_ffn)
    def _():
        turns = [(r.main, 0, start) for start in range(0, ff, FF_STEP)]
        turns += [(r.side, 1, start) for start in range(0, ff, FF_STEP)]
        main_load().wait()
        side_load().wait()
        def far_arrived(piece):
            lend_forward(2, far_place, *piece, far_peer).wait_recv()
            lend_forward(3, far_place, *piece, core_peer).start()

        lag = 2
        for k, piece in enumerate(pieces):
            lend_copy(*piece).wait_recv()
            lend_forward(2, place, *piece, far_peer).start()
            lend_forward(1, place, *piece, core_peer).start()
            if k >= lag:
                far_arrived(pieces[k - lag])
            for one in turns[k :: len(pieces)]:
                turn(*one)

        @pl.when(s == last)
        def _():
            r.idx_rx[last] = r.idx[...]

            def pass_on(owner):
                table_copy(owner, owner).wait_recv()
                table_forward(owner).start()

            far_owners(pass_on)

            def prepare(m):
                @pl.when(m != last)
                def _():
                    idx_copy(m).wait_recv()

                count_hits(m)

            loop(prepare)

        for piece in pieces[-lag:]:
            far_arrived(piece)
        for piece in pieces:
            lend_forward(1, place, *piece, core_peer).wait_recv()
            lend_forward(3, far_place, *piece, core_peer).wait_recv()

        def turn_lent():
            for start in range(0, ff, FF_STEP):
                turn(r.lent, 2, start)

        @pl.when(s == last)
        def _():
            docs_load().wait()
            table_near(core_peer).wait_recv()

            def take(owner):
                table_forward(owner + core_peer - d).wait_recv()

            far_owners(take)
            loop(pick_docs)
            turn_lent()
            loop(wait_meta)

            def both(m):
                wait_state(m)
                states = ffn_forward(m)
                grad = finish_states(m, states)
                r.gout[m] = ffn_backward(m, grad).astype(BF16)
                grad_copy(m).start()

            loop(both)
            r.dproj[...] = tn(r.xout[...].reshape(z.total, width), r.final_right[...])

        @pl.when(s != last)
        def _():
            def forward(m):
                wait_state(m)
                r.xout[m] = ffn_forward(m).astype(BF16)
                state_copy(m).start()

            loop(forward)
            turn_lent()

            def backward(m):
                grad_copy(m).wait_recv()
                r.gout[m] = ffn_backward(m, r.gin[m].astype(F32)).astype(BF16)
                grad_copy(m).start()

            loop(backward)
            loop(wait_meta)

        for piece in pieces:
            lend_forward(1, place, *piece, core_peer).wait_send()
            lend_forward(2, place, *piece, far_peer).wait_send()
            lend_forward(3, far_place, *piece, core_peer).wait_send()

    def put(k, name):
        return pltpu.make_async_copy(getattr(r, name + "_v"), getattr(r, name), r.put_sem.at[k])

    homes = [put(k, name) for k, name in enumerate(("units", "loss", "dx"))]

    def come_home():
        @pl.when(s != 0)
        def _():
            fin_copy(0, s).wait_recv()
            r.dx_v[...] = r.fin_rx[...].astype(F32).reshape(batch_size, query_len, width)

        @pl.when(s == 0)
        def _():
            r.dx_v[...] = r.gout[0].astype(F32).reshape(batch_size, query_len, width)

        def write_own(unit, losses):
            r.units_v[...] = unit.reshape(batch_size, query_len, z.vector)
            r.loss_v[...] = losses

        @pl.when(s != last)
        def _():
            unit_copy(0, s).wait_recv()
            loss_copy(0, s).wait_recv()
            write_own(r.unit_rx[...], r.loss_rx[...])

        @pl.when(s == last)
        def _():
            write_own(r.unit_tx[last], r.loss_tx[last])

        for one in homes:
            one.start()

    if z.summed:
        sum_gradients(
            z, r, s, d, copy, peers, other_sections, is_attention, attention_table, come_home
        )
    else:
        come_home()

    for one in homes:
        one.wait()
    other_sections(lambda to: meta_copy(to, s).wait_send())

    @pl.when(s != 0)
    def _():
        hid_copy(s).wait_send()
        loop(lambda m: grad_copy(m).wait_send())

    @pl.when(s == 0)
    def _():
        for m in range(1, sections):
            fin_copy(m, m).wait_send()

    @pl.when(is_attention)
    def _():
        for piece in pieces:
            lend_copy(*piece).wait_send()

    @pl.when(s != last)
    def _():
        idx_copy(s).wait_send()
        loop(lambda m: state_copy(m).wait_send())

    @pl.when(s == last)
    def _():
        table_near(d).wait_send()
        far_owners(lambda to: table_copy(to, d).wait_send())
        far_owners(lambda owner: table_forward(owner).wait_send())
        for m in range(sections - 1):
            unit_copy(m, m).wait_send()
            loss_copy(m, m).wait_send()


def sum_gradients(
    z, r, s, d, copy, peers, other_sections, is_attention, attention_table, come_home
):
    sections, dp_size, width, ff, share, line = z.sections, z.dp_size, z.width, z.ff, z.share, z.line
    step_columns, per_slab, units, steps = z.step_columns, z.per_slab, z.units, z.steps
    place = d // 2
    core = lax.rem(d, 2)
    peer = d + 1 - 2 * core
    last = sections - 1
    before = lax.rem(s + sections - 1, sections)
    is_ffn = jnp.logical_not(is_attention)
    orders = sum_order(line)

    def piece_rows(owner):
        return pl.ds(pl.multiple_of(owner * share, share), share)

    def gain_copy(to, slot):
        return copy(r.gain_grad, r.gain_rx.at[slot], r.gain_ss.at[to], r.gain_rs.at[slot], s, to)

    def table_copy(to, slot):
        return copy(r.tab_grad, r.tab_rx.at[slot], r.tabs_ss.at[to], r.tabs_rs.at[slot], s, to)

    def fgain_copy(to, slot):
        return copy(r.fgain_grad, r.fgain_rx.at[slot], r.fg_ss.at[to], r.fg_rs.at[slot], s, to)

    def proj_copy(to, slot):
        return copy(
            r.dproj.at[piece_rows(to), :],
            r.proj_rx.at[slot],
            r.proj_ss.at[to],
            r.proj_rs.at[slot],
            s,
            to,
        )

    def spread_copy(to, owner):
        rows = piece_rows(owner)
        return copy(
            r.proj_sum.at[rows, :],
            r.proj_sum.at[rows, :],
            r.spread_ss.at[to],
            r.spread_rs.at[owner],
            s,
            to,
        )

    def table_across(to, slot):
        return copy(r.tab_tx, r.tab_cx.at[slot], r.across_ss.at[0, to], r.across_rs.at[slot], to, d)

    def fgain_across(to):
        return copy(
            r.fgain_tx, r.fgain_sum, r.across_ss.at[1, to], r.across_rs.at[sections], to, d
        )

    def proj_across(to):
        return copy(
            r.proj_sum, r.proj_sum, r.across_ss.at[2, to], r.across_rs.at[sections + 1], to, d
        )

    small_puts = [
        pltpu.make_async_copy(source, target, r.put_sem.at[3 + k])
        for k, (source, target) in enumerate(
            (
                (r.gain_out_v, r.gain_out),
                (r.table_out_v, r.table_out),
                (r.fgain_out_v, r.fgain_out),
                (r.proj_sum, r.proj_out),
            )
        )
    ]

    def slab_put(slab, column, columns):
        source, target = ((r.main_v, r.main_out), (r.side_v, r.side_out))[slab]
        return pltpu.make_async_copy(
            source.at[:, columns], target.at[0, :, columns], r.slab_sem.at[slab, column]
        )

    def total_of(ref, count):
        total = ref[0]
        for k in range(1, count):
            total = total + ref[k]
        return total

    def to_others(body):
        for to in range(sections):

            @pl.when(s != to)
            def _():
                body(to)

    def small_first():
        peers(lambda to: gain_copy(to, d).start())
        r.gain_rx[d] = r.gain_grad[...]

        @pl.when(is_attention)
        def _():
            attention_table()
            peers(lambda to: table_copy(to, d).start())
            r.tab_rx[d] = r.tab_grad[...]

    def proj_first():
        peers(lambda to: proj_copy(to, d).start())
        peers(lambda to: fgain_copy(to, d).start())
        r.proj_rx[d] = r.dproj[piece_rows(d), :]
        r.fgain_rx[d] = r.fgain_grad[...]

    def proj_second():
        peers(lambda owner: proj_copy(owner, owner).wait_recv())
        peers(lambda owner: fgain_copy(owner, owner).wait_recv())
        r.proj_sum[piece_rows(d), :] = total_of(r.proj_rx, dp_size)
        r.fgain_tx[...] = total_of(r.fgain_rx, dp_size)
        r.fgain_sum[...] = r.fgain_tx[...]
        peers(lambda to: spread_copy(to, d).start())
        to_others(lambda to: fgain_across(to).start())

    def proj_third():
        peers(lambda owner: spread_copy(owner, owner).wait_recv())
        to_others(lambda to: proj_across(to).start())

    def small_second():
        peers(lambda owner: gain_copy(owner, owner).wait_recv())
        gain_sum = jnp.broadcast_to(total_of(r.gain_rx, dp_size), (8, width))
        r.gain_out_v[...] = pltpu.roll(gain_sum, width - d * share, 1)[0:1, :share]

        @pl.when(is_attention)
        def _():
            peers(lambda owner: table_copy(owner, owner).wait_recv())
            r.tab_tx[...] = total_of(r.tab_rx, dp_size)
            r.tab_cx[s // 2] = r.tab_tx[...]
            to_others(lambda to: table_across(to, s // 2).start())

    def small_last():
        for source in range(0, sections, 2):

            @pl.when(s != source)
            def _():
                table_across(source, source // 2).wait_recv()

        r.table_out_v[...] = total_of(r.tab_cx, (sections + 1) // 2)[:H]

        @pl.when(s != last)
        def _():
            fgain_across(last).wait_recv()
            proj_across(last).wait_recv()

        r.fgain_out_v[...] = r.fgain_sum[...].reshape(width)
        for one in small_puts:
            one.start()
        peers(lambda to: gain_copy(to, d).wait_send())

        @pl.when(is_attention)
        def _():
            peers(lambda to: table_copy(to, d).wait_send())
            to_others(lambda to: table_across(to, s // 2).wait_send())

        @pl.when(s == last)
        def _():
            peers(lambda to: proj_copy(to, d).wait_send())
            peers(lambda to: fgain_copy(to, d).wait_send())
            peers(lambda to: spread_copy(to, d).wait_send())
            to_others(lambda to: fgain_across(to).wait_send())
            to_others(lambda to: proj_across(to).wait_send())

    def target(i):
        found = jnp.int32(0)
        for k in range(line):
            found = jnp.where(place == k, orders[k][i], found)
        return found

    targets = [target(i) for i in range(line)]

    def target_of(i):
        j = targets[0]
        for k in range(1, line):
            j = jnp.where(i == k, targets[k], j)
        return j

    def parts_of(t):
        i, u = t // units, lax.rem(t, units)
        j = target_of(i)
        slab, column = lax.rem(u, 2), u // 2
        columns = pl.ds(pl.multiple_of(column * step_columns, step_columns), step_columns)
        return j, u, slab, column, columns

    def core_copy(t):
        return copy(
            r.core_tx.at[lax.rem(t, 4)], r.pool.at[t], r.core_ss.at[t], r.core_rs.at[t], s, peer
        )

    def up_core_copy(k):
        return copy(
            r.up_core_tx.at[lax.rem(k, 4)], r.up_rx.at[k], r.up_core_ss.at[k], r.up_rs.at[k], s, peer
        )

    def up_copy(k):
        return copy(
            r.up_tx.at[lax.rem(k, 4)], r.up_rx.at[k], r.up_ss.at[k], r.up_rs.at[k], before, d
        )

    def line_view(t):
        row = pl.ds(pl.multiple_of(lax.rem(t, dp_size) * share, share), share)
        column = pl.ds(pl.multiple_of(t // dp_size * step_columns, step_columns), step_columns)
        return r.lent.at[row, column]

    def line_slot(way, j, u):
        return steps + (way * (line - 1) + j - 1 + way) * units + u

    def line_copy(t, way, j, u, to):
        slot = j - 1 + way
        return copy(
            line_view(t),
            r.pool.at[line_slot(way, j, u)],
            r.line_ss.at[t],
            r.line_rs.at[way, slot, u],
            s,
            to * 2 + core,
        )

    def theirs(j):
        return pl.ds(pl.multiple_of((j * 2 + 1 - core) * share, share), share)

    def ours(j):
        return pl.ds(pl.multiple_of((j * 2 + core) * share, share), share)

    def begin(t):
        j, u, slab, column, columns = parts_of(t)
        mixed = jnp.logical_and(is_attention, column == per_slab - 1)
        which = jnp.where(jnp.logical_or(slab == 1, mixed), 1, 0)

        @pl.when(jnp.logical_or(is_ffn, slab == 0))
        def _():
            right = r.right[slab, :, columns]

            @pl.when(t >= 4)
            def _():
                core_copy(t - 4).wait_send()

            r.core_tx[lax.rem(t, 4)] = nn(r.left[which, theirs(j), :], right).astype(BF16)
            core_copy(t).start()
            r.mine[lax.rem(t, 2)] = nn(r.left[which, ours(j), :], right)

    def up_parts(k):
        i, column = k // per_slab, lax.rem(k, per_slab)
        columns = pl.ds(pl.multiple_of(column * step_columns, step_columns), step_columns)
        return target_of(i), columns

    def begin_up(k):
        j, columns = up_parts(k)
        right = r.right[2, :, columns]

        @pl.when(k >= 4)
        def _():
            up_core_copy(k - 4).wait_send()

        r.up_core_tx[lax.rem(k, 4)] = nn(r.left[0, theirs(j), :], right).astype(BF16)
        up_core_copy(k).start()
        r.up_mine[lax.rem(k, 2)] = nn(r.left[0, ours(j), :], right)

    def finish_up(k):
        up_core_copy(k).wait_recv()

        @pl.when(k >= 4)
        def _():
            up_copy(k - 4).wait_send()

        r.up_tx[lax.rem(k, 4)] = (r.up_mine[lax.rem(k, 2)] + r.up_rx[k].astype(F32)).astype(BF16)
        up_copy(k).start()

    def finish(t):
        j, u, slab, column, columns = parts_of(t)
        k = t // 2
        total = r.mine.at[lax.rem(t, 2)]

        @pl.when(jnp.logical_or(is_ffn, slab == 0))
        def _():
            core_copy(t).wait_recv()
            total[...] += r.pool[t].astype(F32)

        @pl.when(jnp.logical_and(is_attention, slab == 1))
        def _():
            up_copy(k).wait_recv()
            total[...] = r.up_rx[k].astype(F32)

        way = jnp.where(j < place, 1, 0)

        @pl.when(jnp.logical_and(place > 0, j >= place))
        def _():
            line_copy(t, 0, j, u, place).wait_recv()
            total[...] += r.pool[line_slot(0, j, u)].astype(F32)

        @pl.when(jnp.logical_and(place < line - 1, j <= place))
        def _():
            line_copy(t, 1, j, u, place).wait_recv()
            total[...] += r.pool[line_slot(1, j, u)].astype(F32)

        @pl.when(jnp.logical_and(j == place, slab == 0))
        def _():
            r.main_v[:, columns] = total[...]
            slab_put(0, column, columns).start()

        @pl.when(jnp.logical_and(j == place, slab == 1))
        def _():
            r.side_v[:, columns] = total[...]
            slab_put(1, column, columns).start()

        @pl.when(j != place)
        def _():
            line_view(t)[...] = total[...].astype(BF16)
            line_copy(t, way, j, u, place + 1 - 2 * way).start()

    pl.semaphore_signal(r.core_ready, inc=1, device_id=(s, peer), device_id_type=MESH)

    @pl.when(place > 0)
    def _():
        pl.semaphore_signal(r.line_ready, inc=1, device_id=(s, d - 2), device_id_type=MESH)

    @pl.when(place < line - 1)
    def _():
        pl.semaphore_signal(r.line_ready, inc=1, device_id=(s, d + 2), device_id_type=MESH)

    @pl.when(s == last)
    def _():
        proj_first()

    ups = steps // 2
    pl.semaphore_wait(r.core_ready, 1)
    begin(jnp.int32(0))

    @pl.when(is_ffn)
    def _():
        begin_up(jnp.int32(0))

    neighbours = jnp.where(place > 0, 1, 0) + jnp.where(place < line - 1, 1, 0)
    pl.semaphore_wait(r.line_ready, neighbours)

    def step(t, carry):
        @pl.when(t < steps)
        def _():
            begin(t)

        @pl.when(jnp.logical_and(is_ffn, t < ups))
        def _():
            begin_up(t)

        finish(t - 1)

        @pl.when(jnp.logical_and(is_ffn, t <= ups))
        def _():
            finish_up(t - 1)

        @pl.when(jnp.logical_and(s == last, t == 2))
        def _():
            proj_second()

        @pl.when(t == 4)
        def _():
            small_first()

        @pl.when(jnp.logical_and(s == last, t == 6))
        def _():
            proj_third()

        @pl.when(t == units + 4)
        def _():
            small_second()

        @pl.when(t == steps - units)
        def _():
            come_home()

        return carry

    lax.fori_loop(1, steps + 1, step, 0)
    small_last()
    for slab in range(2):
        for column in range(per_slab):
            slab_put(
                slab, column, slice(column * step_columns, (column + 1) * step_columns)
            ).wait()
    for one in small_puts:
        one.wait()

    def drain(t, carry):
        line_copy(t, 0, 1, 0, place).wait_send()
        return carry

    lax.fori_loop(0, steps - units, drain, 0)

    def drain_core(t, carry):
        slab = lax.rem(t, 2)

        @pl.when(jnp.logical_or(is_ffn, slab == 0))
        def _():
            core_copy(t).wait_send()

        return carry

    lax.fori_loop(steps - 4, steps, drain_core, 0)

    @pl.when(is_ffn)
    def _():
        for k in range(steps // 2 - 4, steps // 2):
            up_core_copy(k).wait_send()
            up_copy(k).wait_send()


def relay(z, hid, lengths, labels, chosen, main, side, gain, bias, buckets, fgain, proj, docs):
    dma = pltpu.SemaphoreType.DMA
    shape = jax.ShapeDtypeStruct
    sections, rows, width, ff, dp_size = z.sections, z.rows, z.width, z.ff, z.dp_size
    share, steps, units = z.share, z.steps, z.units
    piece = (share, z.step_columns)
    vmem = pl.BlockSpec(memory_space=VMEM)
    smem = pl.BlockSpec(memory_space=pltpu.SMEM)
    anywhere = pl.BlockSpec(memory_space=pl.ANY)
    inputs = dict(
        hid_hbm=(hid, anywhere),
        lengths=(lengths, smem),
        labels=(labels, smem),
        chosen_hbm=(chosen, anywhere),
        main_hbm=(main, anywhere),
        side_hbm=(side, anywhere),
        gain_hbm=(gain, anywhere),
        bias_hbm=(bias, anywhere),
        buckets_hbm=(buckets, anywhere),
        fgain_hbm=(fgain, anywhere),
        proj_hbm=(proj, anywhere),
        docs_hbm=(docs, anywhere),
    )
    outputs = dict(
        units=shape((z.batch_size, z.query_len, z.vector), BF16),
        loss=shape((8, rows), F32),
        dx=shape((z.batch_size, z.query_len, width), F32),
    )
    def like(value):
        return VMEM(value.shape, value.dtype)

    scratch = {name + "_v": like(value) for name, value in outputs.items()}
    scratch |= dict(
        chosen=like(chosen),
        bias=like(bias),
        buckets=like(buckets),
        gain=like(gain),
        fgain=like(fgain),
        proj=like(proj),
        main=VMEM((width, ff), BF16),
        side=VMEM((width, ff), BF16),
        lent=VMEM((width, ff), BF16),
        xin=VMEM((sections, rows, width), BF16),
        xout=VMEM((sections, rows, width), BF16),
        gin=VMEM((sections, rows, width), BF16),
        gout=VMEM((sections, rows, width), BF16),
        meta=VMEM((8, rows), F32),
        meta_rx=VMEM((sections, 8, rows), F32),
        idx=VMEM((8 + z.retrieved, rows), jnp.int32),
        idx_rx=VMEM((sections, 8 + z.retrieved, rows), jnp.int32),
        own_docs=VMEM((sections, z.batch_size * DOC_LEN, z.vector), BF16),
        table=VMEM((dp_size * z.doc_rows, z.vector), BF16),
        counts=VMEM((sections, z.batch_size * DOC_LEN, rows), BF16),
        pool=VMEM((z.pool, z.chunk, width), BF16),
        final_right=VMEM((z.total, z.vector), BF16),
        qkv=VMEM((z.total, 3 * H * DH), BF16),
        probs=VMEM((sections, H, rows, rows), F32),
        bias_sc=VMEM((H, z.query_len, rows), F32),
        dbias=VMEM((H, z.query_len, rows), F32),
        fin_rx=VMEM((rows, width), BF16),
        unit_tx=VMEM((sections, rows, z.vector), BF16),
        unit_rx=VMEM((rows, z.vector), BF16),
        loss_tx=VMEM((sections, 8, rows), F32),
        loss_rx=VMEM((8, rows), F32),
        small_sem=dma((6,)),
        load_sem=dma((3,)),
        put_sem=dma((7,)),
        state_ss=dma((sections + 1,)),
        state_rs=dma((sections,)),
        grad_ss=dma((sections,)),
        grad_rs=dma((sections,)),
        meta_ss=dma((sections,)),
        meta_rs=dma((sections,)),
        idx_ss=dma,
        idx_rs=dma((sections,)),
        tab_ss=dma((dp_size,)),
        tab_rs=dma((dp_size,)),
        tabf_ss=dma((dp_size,)),
        lend_ss=dma((4, z.parts, 2)),
        lend_rs=dma((4, z.parts, 2)),
        fin_ss=dma((sections,)),
        fin_rs=dma,
        unit_ss=dma((sections,)),
        unit_rs=dma,
        loss_ss=dma((sections,)),
        loss_rs=dma,
    )
    factors = dict(left=((2, width, z.total), BF16), right=((3, z.total, ff), BF16))
    partials = dict(
        gain_grad=((1, width), F32),
        fgain_grad=((1, width), F32),
        tab_grad=((16, 32), F32),
        dproj=((width, z.vector), F32),
    )
    if z.summed:
        outputs |= dict(
            main_out=shape((1, share, ff), F32),
            side_out=shape((1, share, ff), F32),
            gain_out=shape((1, share), F32),
            table_out=shape((H, 32), F32),
            fgain_out=shape((width,), F32),
            proj_out=shape((width, z.vector), F32),
        )
        scratch |= {name: VMEM(*kind) for name, kind in (factors | partials).items()}
        scratch |= dict(
            gain_out_v=VMEM((1, share), F32),
            table_out_v=VMEM((H, 32), F32),
            fgain_out_v=VMEM((width,), F32),
            main_v=VMEM((share, ff), F32),
            side_v=VMEM((share, ff), F32),
            slab_sem=dma((2, z.per_slab)),
            mine=VMEM((2,) + piece, F32),
            up_mine=VMEM((2,) + piece, F32),
            core_tx=VMEM((4,) + piece, BF16),
            up_core_tx=VMEM((4,) + piece, BF16),
            up_tx=VMEM((4,) + piece, BF16),
            up_rx=VMEM((steps // 2,) + piece, BF16),
            gain_rx=VMEM((dp_size, 1, width), F32),
            tab_rx=VMEM((dp_size, 16, 32), F32),
            tab_tx=VMEM((16, 32), F32),
            tab_cx=VMEM(((sections + 1) // 2, 16, 32), F32),
            fgain_rx=VMEM((dp_size, 1, width), F32),
            fgain_tx=VMEM((1, width), F32),
            fgain_sum=VMEM((1, width), F32),
            proj_sum=VMEM((width, z.vector), F32),
            proj_rx=VMEM((dp_size, share, z.vector), F32),
            core_ss=dma((steps,)),
            core_rs=dma((steps,)),
            up_core_ss=dma((steps // 2,)),
            up_ss=dma((steps // 2,)),
            up_rs=dma((steps // 2,)),
            line_ss=dma((steps,)),
            line_rs=dma((2, z.line - 1, units)),
            core_ready=pltpu.SemaphoreType.REGULAR,
            line_ready=pltpu.SemaphoreType.REGULAR,
            gain_ss=dma((dp_size,)),
            gain_rs=dma((dp_size,)),
            tabs_ss=dma((dp_size,)),
            tabs_rs=dma((dp_size,)),
            fg_ss=dma((dp_size,)),
            fg_rs=dma((dp_size,)),
            across_ss=dma((3, sections)),
            across_rs=dma((sections + 2,)),
            proj_ss=dma((dp_size,)),
            proj_rs=dma((dp_size,)),
            spread_ss=dma((dp_size,)),
            spread_rs=dma((dp_size,)),
        )
    else:
        outputs |= {name: shape(*kind) for name, kind in (factors | partials).items()}
    results = pl.pallas_call(
        functools.partial(relay_kernel, z, (*inputs, *outputs, *scratch)),
        out_shape=tuple(outputs.values()),
        in_specs=[spec for _, spec in inputs.values()],
        out_specs=tuple(vmem if name in factors or name in partials else anywhere for name in outputs),
        scratch_shapes=list(scratch.values()),
        compiler_params=pltpu.CompilerParams(
            collective_id=0, has_side_effects=True, vmem_limit_bytes=62 * 2**20
        ),
        name="relay",
    )(*[value for value, _ in inputs.values()])
    return types.SimpleNamespace(**dict(zip(outputs, results, strict=True)))


def deliver_kernel(count, *refs):
    for k in range(count):
        refs[count + 1 + k][...] = refs[k][...]
    losses, out = refs[count], refs[-1]
    out[...] = losses[0:1, : out.shape[0]].reshape(out.shape)


def deliver(values, losses, queries):
    count = len(values)
    vmem = pl.BlockSpec(memory_space=VMEM)
    return pl.pallas_call(
        functools.partial(deliver_kernel, count),
        out_shape=tuple(jax.ShapeDtypeStruct(v.shape, v.dtype) for v in values)
        + (jax.ShapeDtypeStruct((queries,), F32),),
        in_specs=[vmem] * (count + 1),
        out_specs=(vmem,) * (count + 1),
        name="deliver",
    )(*values, losses)


def sums_outside(z, out):
    head_width = H * DH
    section = lax.axis_index("section")
    is_attention = section % 2 == 0
    left, right = out.left, out.right
    second = jnp.where(is_attention, left[1], left[0])
    main_grad = jnp.concatenate(
        [nn(left[0], right[0, :, : 3 * head_width]), nn(second, right[0, :, 3 * head_width :])],
        axis=1,
    )
    up_grad = lax.ppermute(
        nn(left[0], right[2]).astype(BF16),
        "section",
        [(k, k - 1) for k in range(1, z.sections)],
    )
    side_grad = jnp.where(is_attention, up_grad.astype(F32), nn(left[1], right[1]))
    scatter = functools.partial(
        lax.psum_scatter, axis_name="dp", scatter_dimension=0, tiled=True
    )
    table, fgain, proj = lax.psum(
        (out.tab_grad[:H], out.fgain_grad[0], out.dproj), ("section", "dp")
    )
    return (
        scatter(main_grad)[None],
        scatter(side_grad)[None],
        scatter(out.gain_grad[0])[None],
        table.T,
        fgain,
        proj,
    )


def per_device(
    hidden_in,
    lengths,
    labels,
    chosen,
    slab_main,
    slab_side,
    section_gains,
    rel_bias,
    final_gain,
    out_proj,
    doc_vectors,
):
    batch_size, query_len, width = hidden_in.shape
    rows = batch_size * query_len
    retrieved = chosen.shape[2]
    z = Sizes(
        lax.axis_size("section"),
        lax.axis_size("dp"),
        batch_size,
        query_len,
        retrieved,
        width,
        slab_main.shape[2],
        out_proj.shape[1],
        doc_vectors.shape[0],
    )
    buckets = jnp.asarray(np.tile(bucket_table(query_len), (1, batch_size)))
    out = relay(
        z,
        hidden_in.reshape(rows, width),
        lengths,
        labels,
        chosen.reshape(rows, retrieved),
        slab_main,
        slab_side,
        section_gains,
        rel_bias.T,
        buckets,
        final_gain,
        out_proj,
        doc_vectors,
    )
    if not z.summed:
        return (out.units, out.loss[0, :batch_size], out.dx) + sums_outside(z, out)
    names = ("units", "dx", "main_out", "side_out", "gain_out", "table_out", "fgain_out", "proj_out")
    units, dx, main, side, gain, table, fgain, proj, losses = deliver(
        [getattr(out, n) for n in names], out.loss, batch_size
    )
    return units, losses, dx, main, side, gain, table.T, fgain, proj


def solution(mesh):
    both = ("section", "dp")
    in_specs = (
        P(both, None, None),
        P(both),
        P(both),
        P(both, None, None),
        P("section", None, None),
        P("section", None, None),
        P("section", None),
        P(),
        P(),
        P(),
        P("dp", None),
    )
    out_specs = (
        P(both, None, None),
        P(both),
        P(both, None, None),
        P("section", "dp", None),
        P("section", "dp", None),
        P("section", "dp"),
        P(),
        P(),
        P(),
    )
    return jax.shard_map(
        per_device, mesh=mesh, in_specs=in_specs, out_specs=out_specs, check_vma=False
    )
```

```python
import functools
import math
import types

import jax
import jax.numpy as jnp
import numpy as np
from jax import lax
from jax.experimental import pallas as pl
from jax.experimental.pallas import tpu as pltpu
from jax.sharding import PartitionSpec as P

H = 12
DH = 64
DOC_LEN = 128
EPS_NORM = 1e-06
MASK_FILL = -1000000000.0
HIGHEST = lax.Precision.HIGHEST
MESH = pl.DeviceIdType.MESH
F32 = jnp.float32
BF16 = jnp.bfloat16
VMEM = pltpu.VMEM
GELU_C = math.sqrt(2.0 / math.pi)
GELU_A = 0.044715
FF_STEP = 768
LEND_STEP = 128


def bucket_table(query_len):
    places = np.arange(query_len)
    relative = places[None, :] - places[:, None]
    distance = np.abs(relative)
    signed_part = np.where(relative > 0, 16, 0)
    far_bucket = 8 + np.floor(np.log(np.maximum(distance, 1) / 8.0) / np.log(16.0) * 8.0).astype(
        np.int64
    )
    far_bucket = np.minimum(far_bucket, 15)
    return (signed_part + np.where(distance < 8, distance, far_bucket)).astype(np.int32)


def nn(a, b):
    return jnp.dot(a, b, preferred_element_type=F32)


def nt(a, b):
    return lax.dot_general(a, b, (((1,), (1,)), ((), ())), preferred_element_type=F32)


def tn(a, b):
    return lax.dot_general(a, b, (((0,), (0,)), ((), ())), preferred_element_type=F32)


def rms_inverse(values):
    return lax.rsqrt(jnp.mean(values * values, axis=-1, keepdims=True) + EPS_NORM)


def rms_back(scaled, inverse, gain, grad):
    inner = grad * gain
    grad_values = inverse * (inner - scaled * jnp.mean(inner * scaled, axis=-1, keepdims=True))
    return grad_values, jnp.sum(grad * scaled, axis=0, keepdims=True)


def sum_order(line):
    orders = []
    for place in range(line):
        others = [j for j in range(line) if j != place]
        others.sort(key=lambda j: (-abs(j - place), min(j, line - 1 - j)))
        orders.append(others + [place])
    return orders


class Sizes:
    def __init__(self, sections, dp_size, batch_size, query_len, retrieved, width, ff, vector, doc_rows):
        self.sections = sections
        self.dp_size = dp_size
        self.batch_size = batch_size
        self.query_len = query_len
        self.retrieved = retrieved
        self.width = width
        self.ff = ff
        self.vector = vector
        self.doc_rows = doc_rows
        self.rows = batch_size * query_len
        self.total = sections * self.rows
        self.parts = ff // 4 // LEND_STEP
        self.share = width // dp_size
        self.summed = self.share % 16 == 0 and dp_size % 2 == 0
        self.line = dp_size // 2
        self.step_columns = H * DH
        self.per_slab = ff // self.step_columns
        self.units = 2 * self.per_slab
        self.steps = self.line * self.units
        self.chunk = self.share if self.summed else H * 8
        self.slab_chunks = ff // self.chunk
        self.windows = self.total // self.chunk
        self.handed = self.summed and sections == 4 and 3 * self.line - 2 <= 3 * self.windows
        arriving = self.steps + 2 * (self.line - 1) * self.units
        self.pool = max(3 * self.slab_chunks, arriving if self.summed else 0)


def relay_kernel(z, names, *refs):
    r = types.SimpleNamespace(**dict(zip(names, refs, strict=True)))
    s = lax.axis_index("section")
    d = lax.axis_index("dp")
    sections, dp_size, rows, width, ff = z.sections, z.dp_size, z.rows, z.width, z.ff
    batch_size, query_len, parts = z.batch_size, z.query_len, z.parts
    head_width = H * DH
    last = sections - 1
    after = lax.rem(s + 1, sections)
    before = lax.rem(s + sections - 1, sections)
    group = d - lax.rem(d, 4)
    place = lax.rem(d, 4)
    core_peer = group + place + 1 - 2 * lax.rem(place, 2)
    far_place = lax.rem(place + 2, 4)
    far_peer = group + far_place
    is_attention = lax.rem(s, 2) == 0
    is_ffn = jnp.logical_not(is_attention)

    def copy(src, dst, send_sem, recv_sem, section, dp):
        return pltpu.make_async_remote_copy(
            src_ref=src,
            dst_ref=dst,
            send_sem=send_sem,
            recv_sem=recv_sem,
            device_id=(section, dp),
            device_id_type=MESH,
        )

    def block(m):
        return pl.ds(pl.multiple_of(m * rows, rows), rows)

    def peers(body):
        def step(k, carry):
            body(lax.rem(d + k, dp_size))
            return carry

        lax.fori_loop(1, dp_size, step, 0)

    def other_sections(body):
        for k in range(1, sections):
            body(lax.rem(s + k, sections))

    def main_load():
        return pltpu.make_async_copy(r.main_hbm.at[0], r.main, r.load_sem.at[0])

    def side_load():
        return pltpu.make_async_copy(r.side_hbm.at[0], r.side, r.load_sem.at[1])

    small_loads = [
        pltpu.make_async_copy(getattr(r, name + "_hbm"), getattr(r, name), r.small_sem.at[k])
        for k, name in enumerate(("chosen", "bias", "buckets", "gain", "fgain", "proj"))
    ]
    for one in small_loads:
        one.start()

    def hid_load():
        return pltpu.make_async_copy(r.hid_hbm, r.xin.at[0], r.load_sem.at[2])

    def docs_load():
        return pltpu.make_async_copy(r.docs_hbm, r.table.at[table_rows(d), :], r.load_sem.at[2])

    def table_rows(owner):
        return pl.ds(pl.multiple_of(owner * z.doc_rows, z.doc_rows), z.doc_rows)

    @pl.when(s == 0)
    def _():
        hid_load().start()

    main_load().start()

    @pl.when(is_ffn)
    def _():
        side_load().start()

    @pl.when(s == last)
    def _():
        docs_load().start()

    barrier = pltpu.get_barrier_semaphore()
    other_sections(
        lambda to: pl.semaphore_signal(barrier, inc=1, device_id=(to, d), device_id_type=MESH)
    )
    peers(lambda to: pl.semaphore_signal(barrier, inc=1, device_id=(s, to), device_id_type=MESH))

    lane = lax.broadcasted_iota(jnp.int32, (1, rows), 1)
    token_query = lane // query_len
    token_slot = lax.rem(lane, query_len)
    length = jnp.zeros((1, rows), jnp.int32)
    for q in range(batch_size):
        length = jnp.where(token_query == q, r.lengths[q], length)
    live = jnp.where(token_slot < length, 1.0, 0.0)
    r.meta[...] = jnp.zeros_like(r.meta)
    r.meta[0:1, :] = live
    r.meta[1:2, :] = live / length.astype(F32)
    r.idx[:8, :] = jnp.zeros((8, rows), jnp.int32)
    for c in range(batch_size):
        r.idx[c : c + 1, :] = jnp.full((1, rows), r.labels[c], jnp.int32)
    for one in small_loads:
        one.wait()
    r.idx[8:, :] = r.chosen[...].T

    pl.semaphore_wait(barrier, sections - 1 + dp_size - 1)

    def lend_columns(quarter, part):
        start = quarter * (ff // 4) + part * LEND_STEP
        return pl.ds(pl.multiple_of(start, LEND_STEP), LEND_STEP)

    def lend_copy(part, half):
        columns = lend_columns(place, part)
        depth = slice(half * (width // 2), (half + 1) * (width // 2))
        return copy(
            r.side_hbm.at[0, depth, columns],
            r.lent.at[depth, columns],
            r.lend_ss.at[0, part, half],
            r.lend_rs.at[0, part, half],
            after,
            d,
        )

    def lend_forward(kind, quarter, part, half, peer):
        columns = lend_columns(quarter, part)
        depth = slice(half * (width // 2), (half + 1) * (width // 2))
        return copy(
            r.lent.at[depth, columns],
            r.lent.at[depth, columns],
            r.lend_ss.at[kind, part, half],
            r.lend_rs.at[kind, part, half],
            s,
            peer,
        )

    pieces = [(part, half) for part in range(parts) for half in range(2)]

    def state_copy(m):
        return copy(r.xout.at[m], r.xin.at[m], r.state_ss.at[m], r.state_rs.at[m], after, d)

    def grad_copy(m):
        return copy(r.gout.at[m], r.gin.at[m], r.grad_ss.at[m], r.grad_rs.at[m], before, d)

    def meta_copy(to, slot):
        return copy(r.meta, r.meta_rx.at[slot], r.meta_ss.at[to], r.meta_rs.at[slot], to, d)

    def idx_copy(slot):
        return copy(r.idx, r.idx_rx.at[slot], r.idx_ss, r.idx_rs.at[slot], last, d)

    def hid_copy(slot):
        return copy(r.hid_hbm, r.xin.at[slot], r.state_ss.at[sections], r.state_rs.at[slot], 0, d)

    def unit_copy(m, to):
        return copy(r.unit_tx.at[m], r.unit_rx, r.unit_ss.at[m], r.unit_rs, to, d)

    def loss_copy(m, to):
        return copy(r.loss_tx.at[m], r.loss_rx, r.loss_ss.at[m], r.loss_rs, to, d)

    def fin_copy(m, to):
        return copy(r.gout.at[m], r.fin_rx, r.fin_ss.at[m], r.fin_rs, to, d)

    def table_copy(to, owner):
        return copy(
            r.docs_hbm, r.table.at[table_rows(owner), :], r.tab_ss.at[to], r.tab_rs.at[owner], s, to
        )

    def table_near(owner):
        return copy(
            r.docs_hbm,
            r.table.at[table_rows(owner), :],
            r.tab_ss.at[core_peer],
            r.tab_rs.at[owner],
            s,
            core_peer,
        )

    def table_forward(owner):
        rows = table_rows(owner)
        return copy(
            r.table.at[rows, :], r.table.at[rows, :], r.tabf_ss.at[owner], r.tab_rs.at[owner], s, core_peer
        )

    def far_owners(body):
        def step(k, carry):
            body(lax.rem(d + 2 * k, dp_size))
            return carry

        lax.fori_loop(1, dp_size // 2, step, 0)

    @pl.when(s != 0)
    def _():
        hid_copy(s).start()

    @pl.when(s == last)
    def _():
        table_near(d).start()
        far_owners(lambda to: table_copy(to, d).start())

    @pl.when(is_attention)
    def _():
        for part in range(parts):
            for half in range(2):
                lend_copy(part, half).start()

    other_sections(lambda to: meta_copy(to, s).start())
    r.meta_rx[s] = r.meta[...]

    @pl.when(s != last)
    def _():
        idx_copy(s).start()

    r.gain_grad[...] = jnp.zeros_like(r.gain_grad)
    r.fgain_grad[...] = jnp.zeros_like(r.fgain_grad)

    if not z.summed:

        @pl.when(is_ffn)
        def _():
            r.tab_grad[...] = jnp.zeros_like(r.tab_grad)


    if not z.summed:

        @pl.when(s != last)
        def _():
            r.dproj[...] = jnp.zeros_like(r.dproj)

    r.dbias[...] = jnp.zeros_like(r.dbias)
    gain = r.gain[...]
    fgain = r.fgain[...].reshape(1, width)

    def wait_meta(m):
        @pl.when(m != s)
        def _():
            meta_copy(0, m).wait_recv()

    def load_state(m):
        states = r.xin[m].astype(F32)
        inverse = rms_inverse(states)
        return states, inverse, states * inverse

    low_half = lax.broadcasted_iota(jnp.int32, (1, 128), 1) < DH

    def half_of(value, upper):
        keep = jnp.logical_not(low_half) if upper else low_half
        return jnp.where(keep, value.astype(F32), 0.0).astype(BF16)

    def attention_setup():
        buckets = r.buckets[...]
        for h in range(H):
            total = jnp.zeros(buckets.shape, F32)
            for b in range(32):
                total = jnp.where(buckets == b, r.bias[h : h + 1, b : b + 1], total)
            r.bias_sc[h] = total

    def attention_table():
        buckets = r.buckets[...]
        ones = jnp.ones((16, 128), BF16)
        head_row = lax.broadcasted_iota(jnp.int32, (16, 32), 0)

        def head(h, carry):
            grad = r.dbias[h]
            rest = jnp.concatenate(
                [
                    jnp.sum(jnp.where(buckets == b, grad, 0.0), axis=0, keepdims=True)
                    for b in range(32)
                ],
                axis=0,
            )
            total = jnp.zeros((16, 32), F32)
            for _ in range(3):
                part = rest.astype(BF16)
                total = total + nt(ones, part)
                rest = rest - part.astype(F32)
            return carry + jnp.where(head_row == h, total, 0.0)

        r.tab_grad[...] = lax.fori_loop(0, H, head, jnp.zeros((16, 32), F32))

    def turn(source, slab, start):
        size = FF_STEP // z.chunk
        first = slab * z.slab_chunks + start // z.chunk
        r.pool[first : first + size] = source[:, start : start + FF_STEP].T.reshape(
            size, z.chunk, width
        )

    def turned(slab, start, stop):
        first = slab * z.slab_chunks
        return r.pool[first + start // z.chunk : first + stop // z.chunk].reshape(
            stop - start, width
        )

    def attention_forward(m):
        states, inverse, scaled = load_state(m)
        normed = scaled * gain
        r.left[0, :, block(m)] = normed.T.astype(BF16)
        normed_low = normed.astype(BF16)
        for start in range(0, 3 * head_width, head_width):
            r.qkv[block(m), start : start + head_width] = nn(
                normed_low, r.main[:, start : start + head_width]
            ).astype(BF16)
        live = r.meta_rx[m, 0:1, :] > 0.5
        row_query = lax.broadcasted_iota(jnp.int32, (rows, rows), 0) // query_len
        column_query = lax.broadcasted_iota(jnp.int32, (rows, rows), 1) // query_len
        keep = jnp.logical_and(row_query == column_query, live)
        for pair in range(H // 2):
            at = pair * 128
            query = r.qkv[block(m), at : at + 128]
            keys = r.qkv[block(m), head_width + at : head_width + at + 128]
            values = r.qkv[block(m), 2 * head_width + at : 2 * head_width + at + 128]
            contexts = []
            for upper in (0, 1):
                h = 2 * pair + upper
                raw = nt(half_of(query, upper), keys)
                biased = raw.reshape(batch_size, query_len, rows) + r.bias_sc[h][None]
                scores = jnp.where(keep, biased.reshape(rows, rows), MASK_FILL)
                top = jnp.max(scores, axis=-1, keepdims=True)
                grown = jnp.exp(scores - top)
                soft = grown / jnp.sum(grown, axis=-1, keepdims=True)
                r.probs[m, h] = soft
                contexts.append(nn(soft.astype(BF16), values))
            r.right[0, block(m), 3 * head_width + at : 3 * head_width + at + 128] = jnp.where(
                low_half, contexts[0], contexts[1]
            ).astype(BF16)
        context = r.right[0, block(m), 3 * head_width :]
        return states + nt(context, r.main[:, 3 * head_width :])

    def attention_backward(m):
        states, inverse, scaled = load_state(m)
        grad_low = r.gin[m]
        grad = grad_low.astype(F32)
        r.left[1, :, block(m)] = grad.T.astype(BF16)
        grad_context = nn(grad_low, r.main[:, 3 * head_width :]).astype(BF16)
        for pair in range(H // 2):
            at = pair * 128
            query = r.qkv[block(m), at : at + 128]
            keys = r.qkv[block(m), head_width + at : head_width + at + 128]
            values = r.qkv[block(m), 2 * head_width + at : 2 * head_width + at + 128]
            grad_pair = grad_context[:, at : at + 128]
            found = []
            for upper in (0, 1):
                h = 2 * pair + upper
                soft = r.probs[m, h]
                grad_soft = nt(half_of(grad_pair, upper), values)
                moved = soft * grad_soft
                grad_scores = moved - soft * jnp.sum(moved, axis=-1, keepdims=True)
                r.dbias[h] += jnp.sum(grad_scores.reshape(batch_size, query_len, rows), axis=0)
                scores_low = grad_scores.astype(BF16)
                found.append(
                    (
                        nn(scores_low, keys),
                        tn(scores_low, query),
                        tn(soft.astype(BF16), grad_pair),
                    )
                )
            for third in range(3):
                start = third * head_width + at
                r.right[0, block(m), start : start + 128] = jnp.where(
                    low_half, found[0][third], found[1][third]
                ).astype(BF16)
        grad_normed = nn(r.right[0, block(m), : 3 * head_width], turned(0, 0, 3 * head_width))
        grad_states, grad_gain = rms_back(scaled, inverse, gain, grad_normed)
        r.gain_grad[...] += grad_gain
        return grad + grad_states

    def ffn_forward(m):
        states, inverse, scaled = load_state(m)
        normed = scaled * gain
        r.left[0, :, block(m)] = normed.T.astype(BF16)
        normed_low = normed.astype(BF16)
        outputs = states
        for start in range(0, ff, FF_STEP):
            columns = slice(start, start + FF_STEP)
            gate = nn(normed_low, r.main[:, columns])
            up = nn(normed_low, r.lent[:, columns])
            square = gate * gate
            bent = jnp.tanh(GELU_C * gate * (1.0 + GELU_A * square))
            half = 0.5 * (1.0 + bent)
            smooth = gate * half
            slope = half + 0.5 * gate * (1.0 - bent * bent) * (
                GELU_C * (1.0 + 3.0 * GELU_A * square)
            )
            hidden = (smooth * up).astype(BF16)
            r.right[1, block(m), columns] = hidden
            r.right[0, block(m), columns] = (slope * up).astype(BF16)
            r.right[2, block(m), columns] = smooth.astype(BF16)
            outputs = outputs + nn(hidden, turned(1, start, start + FF_STEP))
        return outputs

    def ffn_backward(m, grad):
        states, inverse, scaled = load_state(m)
        grad_low = grad.astype(BF16)
        r.left[1, :, block(m)] = grad.T.astype(BF16)
        grad_normed = jnp.zeros((rows, width), F32)
        for start in range(0, ff, FF_STEP):
            columns = slice(start, start + FF_STEP)
            grad_hidden = nn(grad_low, r.side[:, columns])
            grad_gate = (grad_hidden * r.right[0, block(m), columns].astype(F32)).astype(BF16)
            grad_up = (grad_hidden * r.right[2, block(m), columns].astype(F32)).astype(BF16)
            r.right[0, block(m), columns] = grad_gate
            r.right[2, block(m), columns] = grad_up
            grad_normed = (
                grad_normed
                + nn(grad_gate, turned(0, start, start + FF_STEP))
                + nn(grad_up, turned(2, start, start + FF_STEP))
            )
        grad_states, grad_gain = rms_back(scaled, inverse, gain, grad_normed)
        r.gain_grad[...] += grad_gain
        return grad + grad_states

    def count_hits(m):
        for c in range(batch_size):
            base = r.idx_rx[m, c : c + 1, :] * DOC_LEN
            numbers = lax.broadcasted_iota(jnp.int32, (DOC_LEN, rows), 0) + base
            total = jnp.zeros((DOC_LEN, rows), F32)
            for k in range(z.retrieved):
                total = total + jnp.where(r.idx_rx[m, 8 + k : 9 + k, :] == numbers, 1.0, 0.0)
            r.counts[m, c * DOC_LEN : (c + 1) * DOC_LEN, :] = total.astype(BF16)

    def pick_docs(m):
        for c in range(batch_size):
            label = r.idx_rx[m, c : c + 1, :]

            def pick(t, picked):
                here = r.table[pl.ds(pl.multiple_of(t * DOC_LEN, DOC_LEN), DOC_LEN), :].astype(F32)
                return jnp.where(label == t, here, picked)

            picked = lax.fori_loop(
                0, dp_size * z.doc_rows // DOC_LEN, pick, jnp.zeros((DOC_LEN, z.vector), F32)
            )
            r.own_docs[m, c * DOC_LEN : (c + 1) * DOC_LEN, :] = picked.astype(BF16)

    def loss_and_grad(m, unit):
        docs = r.own_docs[m]
        sims = nt(docs, unit)
        count = r.counts[m].astype(F32)
        imputed = jnp.sum(count * sims, axis=0, keepdims=True) / z.retrieved
        grown = count * jnp.exp(sims)
        imputed_mass = jnp.exp(imputed)
        mass = imputed_mass + jnp.concatenate(
            [
                jnp.sum(grown[c * DOC_LEN : (c + 1) * DOC_LEN], axis=0, keepdims=True)
                for c in range(batch_size)
            ],
            axis=0,
        )
        weighted = jnp.log(mass) * r.meta_rx[m, 1:2, :]
        candidate = lax.broadcasted_iota(jnp.int32, (batch_size, 1), 0)
        losses = jnp.zeros((1, rows), F32)
        grad_tokens = jnp.zeros((batch_size, rows), F32)
        for q in range(batch_size):
            own = token_query == q
            score = jnp.sum(jnp.where(own, weighted, 0.0), axis=1, keepdims=True)
            top = jnp.max(score, axis=0, keepdims=True)
            risen = jnp.exp(score - top)
            total = jnp.sum(risen, axis=0, keepdims=True)
            chosen_one = (candidate == q).astype(F32)
            loss = top + jnp.log(total) - jnp.sum(score * chosen_one, axis=0, keepdims=True)
            losses = losses + jnp.where(lane == q, loss, 0.0)
            grad_tokens = grad_tokens + jnp.where(own, risen / total - chosen_one, 0.0)
        grad_mass = grad_tokens * r.meta_rx[m, 1:2, :] / mass
        shared = jnp.sum(grad_mass, axis=0, keepdims=True) * imputed_mass / z.retrieved
        grad_sims = count * shared + jnp.concatenate(
            [
                grown[c * DOC_LEN : (c + 1) * DOC_LEN] * grad_mass[c : c + 1]
                for c in range(batch_size)
            ],
            axis=0,
        )
        high = grad_sims.astype(BF16)
        rest = (grad_sims - high.astype(F32)).astype(BF16)
        return losses, tn(high, docs) + tn(rest, docs)

    def finish_states(m, states):
        inverse = rms_inverse(states)
        scaled = states * inverse
        normed = (scaled * fgain).astype(BF16)
        projected = nn(normed, r.proj[...])
        size = lax.rsqrt(jnp.sum(projected * projected, axis=-1, keepdims=True) + EPS_NORM)
        exact = projected * size
        unit = exact.astype(BF16)
        losses, grad_unit = loss_and_grad(m, unit)
        r.unit_tx[m] = unit
        r.loss_tx[m] = jnp.broadcast_to(losses, (8, rows))

        @pl.when(m != last)
        def _():
            unit_copy(m, m).start()
            loss_copy(m, m).start()

        grad_projected = (
            size * (grad_unit - exact * jnp.sum(grad_unit * exact, axis=-1, keepdims=True))
        ).astype(BF16)
        r.xout[m] = normed
        r.final_right[block(m), :] = grad_projected
        grad_normed = nt(grad_projected, r.proj[...])
        grad_states, grad_gain = rms_back(scaled, inverse, fgain, grad_normed)
        r.fgain_grad[...] += grad_gain
        return grad_states

    def loop(body):
        def step(m, carry):
            body(m)
            return carry

        lax.fori_loop(0, sections, step, 0)

    def wait_state(m):
        @pl.when(jnp.logical_or(s != 0, m != 0))
        def _():
            state_copy(m).wait_recv()

    @pl.when(is_attention)
    def _():
        attention_setup()
        main_load().wait()

        def forward(m):
            wait_meta(m)
            wait_state(m)

            @pl.when(jnp.logical_and(s == 0, m == 0))
            def _():
                hid_load().wait()

            r.xout[m] = attention_forward(m).astype(BF16)
            state_copy(m).start()

        loop(forward)
        for start in range(0, ff, FF_STEP):
            turn(r.main, 0, start)

        def backward(m):
            grad_copy(m).wait_recv()
            r.gout[m] = attention_backward(m).astype(BF16)

            @pl.when(s != 0)
            def _():
                grad_copy(m).start()

            @pl.when(jnp.logical_and(s == 0, m != 0))
            def _():
                fin_copy(m, m).start()

        loop(backward)
        if not z.summed:
            attention_table()

    @pl.when(is_ffn)
    def _():
        turns = [(r.main, 0, start) for start in range(0, ff, FF_STEP)]
        turns += [(r.side, 1, start) for start in range(0, ff, FF_STEP)]
        main_load().wait()
        side_load().wait()
        def far_arrived(piece):
            lend_forward(2, far_place, *piece, far_peer).wait_recv()
            lend_forward(3, far_place, *piece, core_peer).start()

        lag = 2
        for k, piece in enumerate(pieces):
            lend_copy(*piece).wait_recv()
            lend_forward(2, place, *piece, far_peer).start()
            lend_forward(1, place, *piece, core_peer).start()
            if k >= lag:
                far_arrived(pieces[k - lag])
            for one in turns[k :: len(pieces)]:
                turn(*one)

        @pl.when(s == last)
        def _():
            r.idx_rx[last] = r.idx[...]

            def pass_on(owner):
                table_copy(owner, owner).wait_recv()
                table_forward(owner).start()

            far_owners(pass_on)

            def prepare(m):
                @pl.when(m != last)
                def _():
                    idx_copy(m).wait_recv()

                count_hits(m)

            loop(prepare)

        for piece in pieces[-lag:]:
            far_arrived(piece)
        for piece in pieces:
            lend_forward(1, place, *piece, core_peer).wait_recv()
            lend_forward(3, far_place, *piece, core_peer).wait_recv()

        def turn_lent():
            for start in range(0, ff, FF_STEP):
                turn(r.lent, 2, start)

        @pl.when(s == last)
        def _():
            docs_load().wait()
            table_near(core_peer).wait_recv()

            def take(owner):
                table_forward(owner + core_peer - d).wait_recv()

            far_owners(take)
            loop(pick_docs)
            turn_lent()
            loop(wait_meta)

            def both(m):
                wait_state(m)
                states = ffn_forward(m)
                grad = finish_states(m, states)
                r.gout[m] = ffn_backward(m, grad).astype(BF16)
                grad_copy(m).start()

            loop(both)
            r.dproj[...] = tn(r.xout[...].reshape(z.total, width), r.final_right[...]).astype(
                r.dproj.dtype
            )

        @pl.when(s != last)
        def _():
            def forward(m):
                wait_state(m)
                r.xout[m] = ffn_forward(m).astype(BF16)
                state_copy(m).start()

            loop(forward)
            turn_lent()

            def backward(m):
                grad_copy(m).wait_recv()
                r.gout[m] = ffn_backward(m, r.gin[m].astype(F32)).astype(BF16)
                grad_copy(m).start()

            loop(backward)
            loop(wait_meta)

        for piece in pieces:
            lend_forward(1, place, *piece, core_peer).wait_send()
            lend_forward(2, place, *piece, far_peer).wait_send()
            lend_forward(3, far_place, *piece, core_peer).wait_send()

    def put(k, name):
        return pltpu.make_async_copy(getattr(r, name + "_v"), getattr(r, name), r.put_sem.at[k])

    homes = [put(k, name) for k, name in enumerate(("units", "loss", "dx"))]

    def come_home():
        @pl.when(s != 0)
        def _():
            fin_copy(0, s).wait_recv()
            r.dx_v[...] = r.fin_rx[...].astype(F32).reshape(batch_size, query_len, width)

        @pl.when(s == 0)
        def _():
            r.dx_v[...] = r.gout[0].astype(F32).reshape(batch_size, query_len, width)

        def write_own(unit, losses):
            r.units_v[...] = unit.reshape(batch_size, query_len, z.vector)
            r.loss_v[...] = losses

        @pl.when(s != last)
        def _():
            unit_copy(0, s).wait_recv()
            loss_copy(0, s).wait_recv()
            write_own(r.unit_rx[...], r.loss_rx[...])

        @pl.when(s == last)
        def _():
            write_own(r.unit_tx[last], r.loss_tx[last])

        for one in homes:
            one.start()

    if z.summed:
        sum_gradients(
            z, r, s, d, copy, peers, other_sections, is_attention, attention_table, come_home
        )
    else:
        come_home()

    for one in homes:
        one.wait()
    other_sections(lambda to: meta_copy(to, s).wait_send())

    @pl.when(s != 0)
    def _():
        hid_copy(s).wait_send()
        loop(lambda m: grad_copy(m).wait_send())

    @pl.when(s == 0)
    def _():
        for m in range(1, sections):
            fin_copy(m, m).wait_send()

    @pl.when(is_attention)
    def _():
        for piece in pieces:
            lend_copy(*piece).wait_send()

    @pl.when(s != last)
    def _():
        idx_copy(s).wait_send()
        loop(lambda m: state_copy(m).wait_send())

    @pl.when(s == last)
    def _():
        table_near(d).wait_send()
        far_owners(lambda to: table_copy(to, d).wait_send())
        far_owners(lambda owner: table_forward(owner).wait_send())
        for m in range(sections - 1):
            unit_copy(m, m).wait_send()
            loss_copy(m, m).wait_send()


def sum_gradients(
    z, r, s, d, copy, peers, other_sections, is_attention, attention_table, come_home
):
    sections, dp_size, width, ff, share, line = z.sections, z.dp_size, z.width, z.ff, z.share, z.line
    step_columns, per_slab, units, steps = z.step_columns, z.per_slab, z.units, z.steps
    place = d // 2
    core = lax.rem(d, 2)
    peer = d + 1 - 2 * core
    last = sections - 1
    before = lax.rem(s + sections - 1, sections)
    is_ffn = jnp.logical_not(is_attention)
    orders = sum_order(line)

    def piece_rows(owner):
        return pl.ds(pl.multiple_of(owner * share, share), share)

    def gain_copy(to, slot):
        return copy(r.gain_grad, r.gain_rx.at[slot], r.gain_ss.at[to], r.gain_rs.at[slot], s, to)

    def table_copy(to, slot):
        return copy(r.tab_grad, r.tab_rx.at[slot], r.tabs_ss.at[to], r.tabs_rs.at[slot], s, to)

    def fgain_copy(to, slot):
        return copy(r.fgain_grad, r.fgain_rx.at[slot], r.fg_ss.at[to], r.fg_rs.at[slot], s, to)

    def proj_copy(to, slot):
        return copy(
            r.dproj.at[piece_rows(to), :],
            r.proj_rx.at[slot],
            r.proj_ss.at[to],
            r.proj_rs.at[slot],
            s,
            to,
        )

    def spread_copy(to, owner):
        rows = piece_rows(owner)
        return copy(
            r.proj_sum.at[rows, :],
            r.proj_sum.at[rows, :],
            r.spread_ss.at[to],
            r.spread_rs.at[owner],
            s,
            to,
        )

    def table_across(to, slot):
        return copy(r.tab_tx, r.tab_cx.at[slot], r.across_ss.at[0, to], r.across_rs.at[slot], to, d)

    def fgain_across(to):
        return copy(
            r.fgain_tx, r.fgain_sum, r.across_ss.at[1, to], r.across_rs.at[sections], to, d
        )

    def proj_across(to):
        return copy(
            r.proj_sum, r.proj_sum, r.across_ss.at[2, to], r.across_rs.at[sections + 1], to, d
        )

    small_puts = [
        pltpu.make_async_copy(source, target, r.put_sem.at[3 + k])
        for k, (source, target) in enumerate(
            (
                (r.gain_out_v, r.gain_out),
                (r.table_out_v, r.table_out),
                (r.fgain_out_v, r.fgain_out),
                (r.proj_v, r.proj_out),
            )
        )
    ]

    def slab_put(slab, column, columns):
        source, target = ((r.main_v, r.main_out), (r.side_v, r.side_out))[slab]
        return pltpu.make_async_copy(
            source.at[:, columns], target.at[0, :, columns], r.slab_sem.at[slab, column]
        )

    def total_of(ref, count):
        total = ref[0].astype(F32)
        for k in range(1, count):
            total = total + ref[k].astype(F32)
        return total

    def to_others(body):
        for to in range(sections):

            @pl.when(s != to)
            def _():
                body(to)

    def small_first():
        peers(lambda to: gain_copy(to, d).start())
        r.gain_rx[d] = r.gain_grad[...]

        @pl.when(is_attention)
        def _():
            attention_table()
            peers(lambda to: table_copy(to, d).start())
            r.tab_rx[d] = r.tab_grad[...]

    def proj_first():
        peers(lambda to: proj_copy(to, d).start())
        peers(lambda to: fgain_copy(to, d).start())
        r.proj_rx[d] = r.dproj[piece_rows(d), :]
        r.fgain_rx[d] = r.fgain_grad[...]

    def proj_second():
        peers(lambda owner: proj_copy(owner, owner).wait_recv())
        peers(lambda owner: fgain_copy(owner, owner).wait_recv())
        r.proj_sum[piece_rows(d), :] = total_of(r.proj_rx, dp_size).astype(BF16)
        r.fgain_tx[...] = total_of(r.fgain_rx, dp_size)
        r.fgain_sum[...] = r.fgain_tx[...]
        peers(lambda to: spread_copy(to, d).start())
        to_others(lambda to: fgain_across(to).start())

    def proj_third():
        peers(lambda owner: spread_copy(owner, owner).wait_recv())
        to_others(lambda to: proj_across(to).start())

    def small_second():
        peers(lambda owner: gain_copy(owner, owner).wait_recv())
        gain_sum = jnp.broadcast_to(total_of(r.gain_rx, dp_size), (8, width))
        r.gain_out_v[...] = pltpu.roll(gain_sum, width - d * share, 1)[0:1, :share]

        @pl.when(is_attention)
        def _():
            peers(lambda owner: table_copy(owner, owner).wait_recv())
            r.tab_tx[...] = total_of(r.tab_rx, dp_size)
            r.tab_cx[s // 2] = r.tab_tx[...]
            to_others(lambda to: table_across(to, s // 2).start())

    def small_last():
        for source in range(0, sections, 2):

            @pl.when(s != source)
            def _():
                table_across(source, source // 2).wait_recv()

        r.table_out_v[...] = total_of(r.tab_cx, (sections + 1) // 2)[:H]

        @pl.when(s != last)
        def _():
            fgain_across(last).wait_recv()
            proj_across(last).wait_recv()

        r.fgain_out_v[...] = r.fgain_sum[...].reshape(width)
        r.proj_v[...] = r.proj_sum[...].astype(F32)
        for one in small_puts:
            one.start()
        peers(lambda to: gain_copy(to, d).wait_send())

        @pl.when(is_attention)
        def _():
            peers(lambda to: table_copy(to, d).wait_send())
            to_others(lambda to: table_across(to, s // 2).wait_send())

        @pl.when(s == last)
        def _():
            peers(lambda to: proj_copy(to, d).wait_send())
            peers(lambda to: fgain_copy(to, d).wait_send())
            peers(lambda to: spread_copy(to, d).wait_send())
            to_others(lambda to: fgain_across(to).wait_send())
            to_others(lambda to: proj_across(to).wait_send())

    def target(i):
        found = jnp.int32(0)
        for k in range(line):
            found = jnp.where(place == k, orders[k][i], found)
        return found

    targets = [target(i) for i in range(line)]

    def target_of(i):
        j = targets[0]
        for k in range(1, line):
            j = jnp.where(i == k, targets[k], j)
        return j

    def parts_of(t):
        i, u = t // units, lax.rem(t, units)
        j = target_of(i)
        slab, column = lax.rem(u, 2), u // 2
        columns = pl.ds(pl.multiple_of(column * step_columns, step_columns), step_columns)
        return j, u, slab, column, columns

    def core_copy(t):
        return copy(
            r.core_tx.at[lax.rem(t, 4)], r.pool.at[t], r.core_ss.at[t], r.core_rs.at[t], s, peer
        )

    def up_core_copy(k):
        return copy(
            r.up_core_tx.at[lax.rem(k, 4)], r.up_rx.at[k], r.up_core_ss.at[k], r.up_rs.at[k], s, peer
        )

    def up_copy(k):
        return copy(
            r.up_tx.at[lax.rem(k, 4)], r.up_rx.at[k], r.up_ss.at[k], r.up_rs.at[k], before, d
        )

    hand_column = per_slab - 1
    hand_columns = slice(hand_column * step_columns, ff)

    def window(n):
        row = pl.ds(pl.multiple_of(lax.rem(n, z.windows) * share, share), share)
        column = pl.ds(pl.multiple_of(n // z.windows * step_columns, step_columns), step_columns)
        return r.qkv.at[row, column]

    def hand_copy(k):
        i = k // per_slab
        return copy(r.up_tx.at[lax.rem(k, 4)], window(i), r.up_ss.at[k], r.hand_rs.at[i], last, d)

    def hand_line(i, way, j, to):
        slot = way * (line - 1) + j - 1 + way
        return copy(
            line_view(steps - units + i),
            window(line + slot),
            r.line_ss.at[steps - units + i],
            r.hand_rs.at[line + slot],
            s,
            to * 2 + core,
        )

    def hand_home():
        return copy(
            r.up_mine.at[0], r.side_v.at[:, hand_columns], r.home_ss, r.home_rs, 0, d
        )

    def extra(i):
        j = target_of(i)
        total = r.up_mine.at[0]
        hand_copy(i * per_slab).wait_recv()
        total[...] = window(i)[...].astype(F32)
        way = jnp.where(j < place, 1, 0)

        @pl.when(jnp.logical_and(place > 0, j >= place))
        def _():
            hand_line(i, 0, j, place).wait_recv()
            total[...] += window(line + j - 1)[...].astype(F32)

        @pl.when(jnp.logical_and(place < line - 1, j <= place))
        def _():
            hand_line(i, 1, j, place).wait_recv()
            total[...] += window(line + line - 1 + j)[...].astype(F32)

        @pl.when(j == place)
        def _():
            hand_home().start()

        @pl.when(j != place)
        def _():
            line_view(steps - units + i)[...] = total[...].astype(BF16)
            hand_line(i, way, j, place + 1 - 2 * way).start()

    def line_view(t):
        row = pl.ds(pl.multiple_of(lax.rem(t, dp_size) * share, share), share)
        column = pl.ds(pl.multiple_of(t // dp_size * step_columns, step_columns), step_columns)
        return r.lent.at[row, column]

    def line_slot(way, j, u):
        return steps + (way * (line - 1) + j - 1 + way) * units + u

    def line_copy(t, way, j, u, to):
        slot = j - 1 + way
        return copy(
            line_view(t),
            r.pool.at[line_slot(way, j, u)],
            r.line_ss.at[t],
            r.line_rs.at[way, slot, u],
            s,
            to * 2 + core,
        )

    def theirs(j):
        return pl.ds(pl.multiple_of((j * 2 + 1 - core) * share, share), share)

    def ours(j):
        return pl.ds(pl.multiple_of((j * 2 + core) * share, share), share)

    def begin(t):
        j, u, slab, column, columns = parts_of(t)
        mixed = jnp.logical_and(is_attention, column == per_slab - 1)
        which = jnp.where(jnp.logical_or(slab == 1, mixed), 1, 0)

        @pl.when(jnp.logical_or(is_ffn, slab == 0))
        def _():
            right = r.right[slab, :, columns]

            @pl.when(t >= 4)
            def _():
                core_copy(t - 4).wait_send()

            r.core_tx[lax.rem(t, 4)] = nn(r.left[which, theirs(j), :], right).astype(BF16)
            core_copy(t).start()
            r.mine[lax.rem(t, 2)] = nn(r.left[which, ours(j), :], right)

    def up_parts(k):
        i, column = k // per_slab, lax.rem(k, per_slab)
        columns = pl.ds(pl.multiple_of(column * step_columns, step_columns), step_columns)
        return target_of(i), columns

    def begin_up(k):
        j, columns = up_parts(k)
        right = r.right[2, :, columns]

        @pl.when(k >= 4)
        def _():
            up_core_copy(k - 4).wait_send()

        r.up_core_tx[lax.rem(k, 4)] = nn(r.left[0, theirs(j), :], right).astype(BF16)
        up_core_copy(k).start()
        r.up_mine[lax.rem(k, 2)] = nn(r.left[0, ours(j), :], right)

    def finish_up(k):
        up_core_copy(k).wait_recv()

        @pl.when(k >= 4)
        def _():
            up_copy(k - 4).wait_send()

        r.up_tx[lax.rem(k, 4)] = (r.up_mine[lax.rem(k, 2)] + r.up_rx[k].astype(F32)).astype(BF16)
        if z.handed:
            handed = jnp.logical_and(s == 1, lax.rem(k, per_slab) == hand_column)

            @pl.when(handed)
            def _():
                hand_copy(k).start()

            @pl.when(jnp.logical_not(handed))
            def _():
                up_copy(k).start()
        else:
            up_copy(k).start()

    def gone(t):
        return jnp.logical_and(s == 0, lax.rem(t, units) == units - 1) if z.handed else False

    def finish(t):
        @pl.when(jnp.logical_not(gone(t)))
        def _():
            finish_here(t)

    def finish_here(t):
        j, u, slab, column, columns = parts_of(t)
        k = t // 2
        total = r.mine.at[lax.rem(t, 2)]

        @pl.when(jnp.logical_or(is_ffn, slab == 0))
        def _():
            core_copy(t).wait_recv()
            total[...] += r.pool[t].astype(F32)

        @pl.when(jnp.logical_and(is_attention, slab == 1))
        def _():
            up_copy(k).wait_recv()
            total[...] = r.up_rx[k].astype(F32)

        way = jnp.where(j < place, 1, 0)

        @pl.when(jnp.logical_and(place > 0, j >= place))
        def _():
            line_copy(t, 0, j, u, place).wait_recv()
            total[...] += r.pool[line_slot(0, j, u)].astype(F32)

        @pl.when(jnp.logical_and(place < line - 1, j <= place))
        def _():
            line_copy(t, 1, j, u, place).wait_recv()
            total[...] += r.pool[line_slot(1, j, u)].astype(F32)

        @pl.when(jnp.logical_and(j == place, slab == 0))
        def _():
            r.main_v[:, columns] = total[...]
            slab_put(0, column, columns).start()

        @pl.when(jnp.logical_and(j == place, slab == 1))
        def _():
            r.side_v[:, columns] = total[...]
            slab_put(1, column, columns).start()

        @pl.when(j != place)
        def _():
            line_view(t)[...] = total[...].astype(BF16)
            line_copy(t, way, j, u, place + 1 - 2 * way).start()

    pl.semaphore_signal(r.core_ready, inc=1, device_id=(s, peer), device_id_type=MESH)

    @pl.when(place > 0)
    def _():
        pl.semaphore_signal(r.line_ready, inc=1, device_id=(s, d - 2), device_id_type=MESH)

    @pl.when(place < line - 1)
    def _():
        pl.semaphore_signal(r.line_ready, inc=1, device_id=(s, d + 2), device_id_type=MESH)

    @pl.when(s == last)
    def _():
        proj_first()

    ups = steps // 2
    pl.semaphore_wait(r.core_ready, 1)
    begin(jnp.int32(0))

    @pl.when(is_ffn)
    def _():
        begin_up(jnp.int32(0))

    neighbours = jnp.where(place > 0, 1, 0) + jnp.where(place < line - 1, 1, 0)
    pl.semaphore_wait(r.line_ready, neighbours)

    def step(t, carry):
        @pl.when(t < steps)
        def _():
            begin(t)

        @pl.when(jnp.logical_and(is_ffn, t < ups))
        def _():
            begin_up(t)

        finish(t - 1)

        @pl.when(jnp.logical_and(is_ffn, t <= ups))
        def _():
            finish_up(t - 1)

        if z.handed:

            @pl.when(jnp.logical_and(s == last, jnp.logical_and(t >= 2 * units, t < 2 * units + line)))
            def _():
                extra(t - 2 * units)

        @pl.when(jnp.logical_and(s == last, t == 2))
        def _():
            proj_second()

        @pl.when(t == 4)
        def _():
            small_first()

        @pl.when(jnp.logical_and(s == last, t == 6))
        def _():
            proj_third()

        @pl.when(t == units + 4)
        def _():
            small_second()

        @pl.when(t == steps - units)
        def _():
            come_home()

        return carry

    lax.fori_loop(1, steps + 1, step, 0)
    small_last()
    if z.handed:

        @pl.when(s == 0)
        def _():
            hand_home().wait_recv()
            slab_put(1, hand_column, hand_columns).start()

        @pl.when(s == last)
        def _():
            hand_home().wait_send()
            for i in range(line - 1):
                hand_line(i, 0, 1, place).wait_send()

    for slab in range(2):
        for column in range(per_slab):
            slab_put(
                slab, column, slice(column * step_columns, (column + 1) * step_columns)
            ).wait()
    for one in small_puts:
        one.wait()

    def drain(t, carry):
        @pl.when(jnp.logical_not(gone(t)))
        def _():
            line_copy(t, 0, 1, 0, place).wait_send()

        return carry

    lax.fori_loop(0, steps - units, drain, 0)

    def drain_core(t, carry):
        slab = lax.rem(t, 2)

        @pl.when(jnp.logical_or(is_ffn, slab == 0))
        def _():
            core_copy(t).wait_send()

        return carry

    lax.fori_loop(steps - 4, steps, drain_core, 0)

    @pl.when(is_ffn)
    def _():
        for k in range(steps // 2 - 4, steps // 2):
            up_core_copy(k).wait_send()
            up_copy(k).wait_send()


def relay(z, hid, lengths, labels, chosen, main, side, gain, bias, buckets, fgain, proj, docs):
    dma = pltpu.SemaphoreType.DMA
    shape = jax.ShapeDtypeStruct
    sections, rows, width, ff, dp_size = z.sections, z.rows, z.width, z.ff, z.dp_size
    share, steps, units = z.share, z.steps, z.units
    piece = (share, z.step_columns)
    vmem = pl.BlockSpec(memory_space=VMEM)
    smem = pl.BlockSpec(memory_space=pltpu.SMEM)
    anywhere = pl.BlockSpec(memory_space=pl.ANY)
    inputs = dict(
        hid_hbm=(hid, anywhere),
        lengths=(lengths, smem),
        labels=(labels, smem),
        chosen_hbm=(chosen, anywhere),
        main_hbm=(main, anywhere),
        side_hbm=(side, anywhere),
        gain_hbm=(gain, anywhere),
        bias_hbm=(bias, anywhere),
        buckets_hbm=(buckets, anywhere),
        fgain_hbm=(fgain, anywhere),
        proj_hbm=(proj, anywhere),
        docs_hbm=(docs, anywhere),
    )
    outputs = dict(
        units=shape((z.batch_size, z.query_len, z.vector), BF16),
        loss=shape((8, rows), F32),
        dx=shape((z.batch_size, z.query_len, width), F32),
    )
    def like(value):
        return VMEM(value.shape, value.dtype)

    scratch = {name + "_v": like(value) for name, value in outputs.items()}
    scratch |= dict(
        chosen=like(chosen),
        bias=like(bias),
        buckets=like(buckets),
        gain=like(gain),
        fgain=like(fgain),
        proj=like(proj),
        main=VMEM((width, ff), BF16),
        side=VMEM((width, ff), BF16),
        lent=VMEM((width, ff), BF16),
        xin=VMEM((sections, rows, width), BF16),
        xout=VMEM((sections, rows, width), BF16),
        gin=VMEM((sections, rows, width), BF16),
        gout=VMEM((sections, rows, width), BF16),
        meta=VMEM((8, rows), F32),
        meta_rx=VMEM((sections, 8, rows), F32),
        idx=VMEM((8 + z.retrieved, rows), jnp.int32),
        idx_rx=VMEM((sections, 8 + z.retrieved, rows), jnp.int32),
        own_docs=VMEM((sections, z.batch_size * DOC_LEN, z.vector), BF16),
        table=VMEM((dp_size * z.doc_rows, z.vector), BF16),
        counts=VMEM((sections, z.batch_size * DOC_LEN, rows), BF16),
        pool=VMEM((z.pool, z.chunk, width), BF16),
        final_right=VMEM((z.total, z.vector), BF16),
        qkv=VMEM((z.total, 3 * H * DH), BF16),
        probs=VMEM((sections, H, rows, rows), F32),
        bias_sc=VMEM((H, z.query_len, rows), F32),
        dbias=VMEM((H, z.query_len, rows), F32),
        fin_rx=VMEM((rows, width), BF16),
        unit_tx=VMEM((sections, rows, z.vector), BF16),
        unit_rx=VMEM((rows, z.vector), BF16),
        loss_tx=VMEM((sections, 8, rows), F32),
        loss_rx=VMEM((8, rows), F32),
        small_sem=dma((6,)),
        load_sem=dma((3,)),
        put_sem=dma((7,)),
        state_ss=dma((sections + 1,)),
        state_rs=dma((sections,)),
        grad_ss=dma((sections,)),
        grad_rs=dma((sections,)),
        meta_ss=dma((sections,)),
        meta_rs=dma((sections,)),
        idx_ss=dma,
        idx_rs=dma((sections,)),
        tab_ss=dma((dp_size,)),
        tab_rs=dma((dp_size,)),
        tabf_ss=dma((dp_size,)),
        lend_ss=dma((4, z.parts, 2)),
        lend_rs=dma((4, z.parts, 2)),
        fin_ss=dma((sections,)),
        fin_rs=dma,
        unit_ss=dma((sections,)),
        unit_rs=dma,
        loss_ss=dma((sections,)),
        loss_rs=dma,
    )
    factors = dict(left=((2, width, z.total), BF16), right=((3, z.total, ff), BF16))
    partials = dict(
        gain_grad=((1, width), F32),
        fgain_grad=((1, width), F32),
        tab_grad=((16, 32), F32),
        dproj=((width, z.vector), BF16 if z.summed else F32),
    )
    if z.summed:
        outputs |= dict(
            main_out=shape((1, share, ff), F32),
            side_out=shape((1, share, ff), F32),
            gain_out=shape((1, share), F32),
            table_out=shape((H, 32), F32),
            fgain_out=shape((width,), F32),
            proj_out=shape((width, z.vector), F32),
        )
        scratch |= {name: VMEM(*kind) for name, kind in (factors | partials).items()}
        scratch |= dict(
            gain_out_v=VMEM((1, share), F32),
            table_out_v=VMEM((H, 32), F32),
            fgain_out_v=VMEM((width,), F32),
            main_v=VMEM((share, ff), F32),
            side_v=VMEM((share, ff), F32),
            slab_sem=dma((2, z.per_slab)),
            mine=VMEM((2,) + piece, F32),
            up_mine=VMEM((2,) + piece, F32),
            core_tx=VMEM((4,) + piece, BF16),
            up_core_tx=VMEM((4,) + piece, BF16),
            up_tx=VMEM((4,) + piece, BF16),
            up_rx=VMEM((steps // 2,) + piece, BF16),
            gain_rx=VMEM((dp_size, 1, width), F32),
            tab_rx=VMEM((dp_size, 16, 32), F32),
            tab_tx=VMEM((16, 32), F32),
            tab_cx=VMEM(((sections + 1) // 2, 16, 32), F32),
            fgain_rx=VMEM((dp_size, 1, width), F32),
            fgain_tx=VMEM((1, width), F32),
            fgain_sum=VMEM((1, width), F32),
            proj_sum=VMEM((width, z.vector), BF16),
            proj_v=VMEM((width, z.vector), F32),
            proj_rx=VMEM((dp_size, share, z.vector), BF16),
            core_ss=dma((steps,)),
            core_rs=dma((steps,)),
            up_core_ss=dma((steps // 2,)),
            up_ss=dma((steps // 2,)),
            up_rs=dma((steps // 2,)),
            hand_rs=dma((3 * z.line - 2,)),
            home_ss=dma,
            home_rs=dma,
            line_ss=dma((steps,)),
            line_rs=dma((2, z.line - 1, units)),
            core_ready=pltpu.SemaphoreType.REGULAR,
            line_ready=pltpu.SemaphoreType.REGULAR,
            gain_ss=dma((dp_size,)),
            gain_rs=dma((dp_size,)),
            tabs_ss=dma((dp_size,)),
            tabs_rs=dma((dp_size,)),
            fg_ss=dma((dp_size,)),
            fg_rs=dma((dp_size,)),
            across_ss=dma((3, sections)),
            across_rs=dma((sections + 2,)),
            proj_ss=dma((dp_size,)),
            proj_rs=dma((dp_size,)),
            spread_ss=dma((dp_size,)),
            spread_rs=dma((dp_size,)),
        )
    else:
        outputs |= {name: shape(*kind) for name, kind in (factors | partials).items()}
    results = pl.pallas_call(
        functools.partial(relay_kernel, z, (*inputs, *outputs, *scratch)),
        out_shape=tuple(outputs.values()),
        in_specs=[spec for _, spec in inputs.values()],
        out_specs=tuple(vmem if name in factors or name in partials else anywhere for name in outputs),
        scratch_shapes=list(scratch.values()),
        compiler_params=pltpu.CompilerParams(
            collective_id=0, has_side_effects=True, vmem_limit_bytes=62 * 2**20
        ),
        name="relay",
    )(*[value for value, _ in inputs.values()])
    return types.SimpleNamespace(**dict(zip(outputs, results, strict=True)))


def deliver_kernel(count, *refs):
    for k in range(count):
        refs[count + 1 + k][...] = refs[k][...]
    losses, out = refs[count], refs[-1]
    out[...] = losses[0:1, : out.shape[0]].reshape(out.shape)


def deliver(values, losses, queries):
    count = len(values)
    vmem = pl.BlockSpec(memory_space=VMEM)
    return pl.pallas_call(
        functools.partial(deliver_kernel, count),
        out_shape=tuple(jax.ShapeDtypeStruct(v.shape, v.dtype) for v in values)
        + (jax.ShapeDtypeStruct((queries,), F32),),
        in_specs=[vmem] * (count + 1),
        out_specs=(vmem,) * (count + 1),
        name="deliver",
    )(*values, losses)


def sums_outside(z, out):
    head_width = H * DH
    section = lax.axis_index("section")
    is_attention = section % 2 == 0
    left, right = out.left, out.right
    second = jnp.where(is_attention, left[1], left[0])
    main_grad = jnp.concatenate(
        [nn(left[0], right[0, :, : 3 * head_width]), nn(second, right[0, :, 3 * head_width :])],
        axis=1,
    )
    up_grad = lax.ppermute(
        nn(left[0], right[2]).astype(BF16),
        "section",
        [(k, k - 1) for k in range(1, z.sections)],
    )
    side_grad = jnp.where(is_attention, up_grad.astype(F32), nn(left[1], right[1]))
    scatter = functools.partial(
        lax.psum_scatter, axis_name="dp", scatter_dimension=0, tiled=True
    )
    table, fgain, proj = lax.psum(
        (out.tab_grad[:H], out.fgain_grad[0], out.dproj), ("section", "dp")
    )
    return (
        scatter(main_grad)[None],
        scatter(side_grad)[None],
        scatter(out.gain_grad[0])[None],
        table.T,
        fgain,
        proj,
    )


def per_device(
    hidden_in,
    lengths,
    labels,
    chosen,
    slab_main,
    slab_side,
    section_gains,
    rel_bias,
    final_gain,
    out_proj,
    doc_vectors,
):
    batch_size, query_len, width = hidden_in.shape
    rows = batch_size * query_len
    retrieved = chosen.shape[2]
    z = Sizes(
        lax.axis_size("section"),
        lax.axis_size("dp"),
        batch_size,
        query_len,
        retrieved,
        width,
        slab_main.shape[2],
        out_proj.shape[1],
        doc_vectors.shape[0],
    )
    buckets = jnp.asarray(np.tile(bucket_table(query_len), (1, batch_size)))
    out = relay(
        z,
        hidden_in.reshape(rows, width),
        lengths,
        labels,
        chosen.reshape(rows, retrieved),
        slab_main,
        slab_side,
        section_gains,
        rel_bias.T,
        buckets,
        final_gain,
        out_proj,
        doc_vectors,
    )
    if not z.summed:
        return (out.units, out.loss[0, :batch_size], out.dx) + sums_outside(z, out)
    names = ("units", "dx", "main_out", "side_out", "gain_out", "table_out", "fgain_out", "proj_out")
    units, dx, main, side, gain, table, fgain, proj, losses = deliver(
        [getattr(out, n) for n in names], out.loss, batch_size
    )
    return units, losses, dx, main, side, gain, table.T, fgain, proj


def solution(mesh):
    both = ("section", "dp")
    in_specs = (
        P(both, None, None),
        P(both),
        P(both),
        P(both, None, None),
        P("section", None, None),
        P("section", None, None),
        P("section", None),
        P(),
        P(),
        P(),
        P("dp", None),
    )
    out_specs = (
        P(both, None, None),
        P(both),
        P(both, None, None),
        P("section", "dp", None),
        P("section", "dp", None),
        P("section", "dp"),
        P(),
        P(),
        P(),
    )
    return jax.shard_map(
        per_device, mesh=mesh, in_specs=in_specs, out_specs=out_specs, check_vma=False
    )
```

```python
import functools
import math
import types

import jax
import jax.numpy as jnp
import numpy as np
from jax import lax
from jax.experimental import pallas as pl
from jax.experimental.pallas import tpu as pltpu
from jax.sharding import PartitionSpec as P

H = 12
DH = 64
DOC_LEN = 128
EPS_NORM = 1e-06
MASK_FILL = -1000000000.0
HIGHEST = lax.Precision.HIGHEST
MESH = pl.DeviceIdType.MESH
F32 = jnp.float32
BF16 = jnp.bfloat16
VMEM = pltpu.VMEM
GELU_C = math.sqrt(2.0 / math.pi)
GELU_A = 0.044715
FF_STEP = 768
LEND_STEP = 128


def bucket_table(query_len):
    places = np.arange(query_len)
    relative = places[None, :] - places[:, None]
    distance = np.abs(relative)
    signed_part = np.where(relative > 0, 16, 0)
    far_bucket = 8 + np.floor(np.log(np.maximum(distance, 1) / 8.0) / np.log(16.0) * 8.0).astype(
        np.int64
    )
    far_bucket = np.minimum(far_bucket, 15)
    return (signed_part + np.where(distance < 8, distance, far_bucket)).astype(np.int32)


def nn(a, b):
    return jnp.dot(a, b, preferred_element_type=F32)


def nt(a, b):
    return lax.dot_general(a, b, (((1,), (1,)), ((), ())), preferred_element_type=F32)


def tn(a, b):
    return lax.dot_general(a, b, (((0,), (0,)), ((), ())), preferred_element_type=F32)


def rms_inverse(values):
    return lax.rsqrt(jnp.mean(values * values, axis=-1, keepdims=True) + EPS_NORM)


def rms_back(scaled, inverse, gain, grad):
    inner = grad * gain
    grad_values = inverse * (inner - scaled * jnp.mean(inner * scaled, axis=-1, keepdims=True))
    return grad_values, jnp.sum(grad * scaled, axis=0, keepdims=True)


def sum_order(line):
    orders = []
    for place in range(line):
        others = [j for j in range(line) if j != place]
        others.sort(key=lambda j: (-abs(j - place), min(j, line - 1 - j)))
        orders.append(others + [place])
    return orders


class Sizes:
    def __init__(self, sections, dp_size, batch_size, query_len, retrieved, width, ff, vector, doc_rows):
        self.sections = sections
        self.dp_size = dp_size
        self.batch_size = batch_size
        self.query_len = query_len
        self.retrieved = retrieved
        self.width = width
        self.ff = ff
        self.vector = vector
        self.doc_rows = doc_rows
        self.rows = batch_size * query_len
        self.total = sections * self.rows
        self.parts = ff // 4 // LEND_STEP
        self.share = width // dp_size
        self.summed = self.share % 16 == 0 and dp_size % 2 == 0
        self.line = dp_size // 2
        self.step_columns = H * DH
        self.per_slab = ff // self.step_columns
        self.units = 2 * self.per_slab
        self.steps = self.line * self.units
        self.chunk = self.share if self.summed else H * 8
        self.slab_chunks = ff // self.chunk
        self.windows = self.total // self.chunk
        self.handed = self.summed and sections == 4 and 3 * self.line - 2 <= 3 * self.windows
        arriving = self.steps + 2 * (self.line - 1) * self.units
        self.pool = max(3 * self.slab_chunks, arriving if self.summed else 0)


def relay_kernel(z, names, *refs):
    r = types.SimpleNamespace(**dict(zip(names, refs, strict=True)))
    s = lax.axis_index("section")
    d = lax.axis_index("dp")
    sections, dp_size, rows, width, ff = z.sections, z.dp_size, z.rows, z.width, z.ff
    batch_size, query_len, parts = z.batch_size, z.query_len, z.parts
    head_width = H * DH
    last = sections - 1
    after = lax.rem(s + 1, sections)
    before = lax.rem(s + sections - 1, sections)
    group = d - lax.rem(d, 4)
    place = lax.rem(d, 4)
    core_peer = group + place + 1 - 2 * lax.rem(place, 2)
    far_place = lax.rem(place + 2, 4)
    far_peer = group + far_place
    is_attention = lax.rem(s, 2) == 0
    is_ffn = jnp.logical_not(is_attention)

    def copy(src, dst, send_sem, recv_sem, section, dp):
        return pltpu.make_async_remote_copy(
            src_ref=src,
            dst_ref=dst,
            send_sem=send_sem,
            recv_sem=recv_sem,
            device_id=(section, dp),
            device_id_type=MESH,
        )

    def block(m):
        return pl.ds(pl.multiple_of(m * rows, rows), rows)

    def peers(body):
        def step(k, carry):
            body(lax.rem(d + k, dp_size))
            return carry

        lax.fori_loop(1, dp_size, step, 0)

    def other_sections(body):
        for k in range(1, sections):
            body(lax.rem(s + k, sections))

    def main_load():
        return pltpu.make_async_copy(r.main_hbm.at[0], r.main, r.load_sem.at[0])

    def side_load():
        return pltpu.make_async_copy(r.side_hbm.at[0], r.side, r.load_sem.at[1])

    small_loads = [
        pltpu.make_async_copy(getattr(r, name + "_hbm"), getattr(r, name), r.small_sem.at[k])
        for k, name in enumerate(("chosen", "bias", "buckets", "gain", "fgain", "proj"))
    ]
    for one in small_loads:
        one.start()

    def hid_load():
        return pltpu.make_async_copy(r.hid_hbm, r.xin.at[0], r.load_sem.at[2])

    def docs_load():
        return pltpu.make_async_copy(r.docs_hbm, r.table.at[table_rows(d), :], r.load_sem.at[2])

    def table_rows(owner):
        return pl.ds(pl.multiple_of(owner * z.doc_rows, z.doc_rows), z.doc_rows)

    @pl.when(s == 0)
    def _():
        hid_load().start()

    main_load().start()

    @pl.when(is_ffn)
    def _():
        side_load().start()

    @pl.when(s == last)
    def _():
        docs_load().start()

    barrier = pltpu.get_barrier_semaphore()
    other_sections(
        lambda to: pl.semaphore_signal(barrier, inc=1, device_id=(to, d), device_id_type=MESH)
    )
    peers(lambda to: pl.semaphore_signal(barrier, inc=1, device_id=(s, to), device_id_type=MESH))

    lane = lax.broadcasted_iota(jnp.int32, (1, rows), 1)
    token_query = lane // query_len
    token_slot = lax.rem(lane, query_len)
    length = jnp.zeros((1, rows), jnp.int32)
    for q in range(batch_size):
        length = jnp.where(token_query == q, r.lengths[q], length)
    live = jnp.where(token_slot < length, 1.0, 0.0)
    r.meta[...] = jnp.zeros_like(r.meta)
    r.meta[0:1, :] = live
    r.meta[1:2, :] = live / length.astype(F32)
    r.idx[:8, :] = jnp.zeros((8, rows), jnp.int32)
    for c in range(batch_size):
        r.idx[c : c + 1, :] = jnp.full((1, rows), r.labels[c], jnp.int32)
    for one in small_loads:
        one.wait()
    r.idx[8:, :] = r.chosen[...].T

    pl.semaphore_wait(barrier, sections - 1 + dp_size - 1)

    def lend_columns(quarter, part):
        start = quarter * (ff // 4) + part * LEND_STEP
        return pl.ds(pl.multiple_of(start, LEND_STEP), LEND_STEP)

    def lend_copy(part, half):
        columns = lend_columns(place, part)
        depth = slice(half * (width // 2), (half + 1) * (width // 2))
        return copy(
            r.side_hbm.at[0, depth, columns],
            r.lent.at[depth, columns],
            r.lend_ss.at[0, part, half],
            r.lend_rs.at[0, part, half],
            after,
            d,
        )

    def lend_forward(kind, quarter, part, half, peer):
        columns = lend_columns(quarter, part)
        depth = slice(half * (width // 2), (half + 1) * (width // 2))
        return copy(
            r.lent.at[depth, columns],
            r.lent.at[depth, columns],
            r.lend_ss.at[kind, part, half],
            r.lend_rs.at[kind, part, half],
            s,
            peer,
        )

    pieces = [(part, half) for part in range(parts) for half in range(2)]

    def state_copy(m):
        return copy(r.xout.at[m], r.xin.at[m], r.state_ss.at[m], r.state_rs.at[m], after, d)

    def grad_copy(m):
        return copy(r.gout.at[m], r.gin.at[m], r.grad_ss.at[m], r.grad_rs.at[m], before, d)

    def meta_copy(to, slot):
        return copy(r.meta, r.meta_rx.at[slot], r.meta_ss.at[to], r.meta_rs.at[slot], to, d)

    def idx_copy(slot):
        return copy(r.idx, r.idx_rx.at[slot], r.idx_ss, r.idx_rs.at[slot], last, d)

    def hid_copy(slot):
        return copy(r.hid_hbm, r.xin.at[slot], r.state_ss.at[sections], r.state_rs.at[slot], 0, d)

    def unit_copy(m, to):
        return copy(r.unit_tx.at[m], r.unit_rx, r.unit_ss.at[m], r.unit_rs, to, d)

    def loss_copy(m, to):
        return copy(r.loss_tx.at[m], r.loss_rx, r.loss_ss.at[m], r.loss_rs, to, d)

    def fin_copy(m, to):
        return copy(r.gout.at[m], r.fin_rx, r.fin_ss.at[m], r.fin_rs, to, d)

    def table_copy(to, owner):
        return copy(
            r.docs_hbm, r.table.at[table_rows(owner), :], r.tab_ss.at[to], r.tab_rs.at[owner], s, to
        )

    def table_near(owner):
        return copy(
            r.docs_hbm,
            r.table.at[table_rows(owner), :],
            r.tab_ss.at[core_peer],
            r.tab_rs.at[owner],
            s,
            core_peer,
        )

    def table_forward(owner):
        rows = table_rows(owner)
        return copy(
            r.table.at[rows, :], r.table.at[rows, :], r.tabf_ss.at[owner], r.tab_rs.at[owner], s, core_peer
        )

    def far_owners(body):
        def step(k, carry):
            body(lax.rem(d + 2 * k, dp_size))
            return carry

        lax.fori_loop(1, dp_size // 2, step, 0)

    @pl.when(s != 0)
    def _():
        hid_copy(s).start()

    @pl.when(s == last)
    def _():
        table_near(d).start()
        far_owners(lambda to: table_copy(to, d).start())

    @pl.when(is_attention)
    def _():
        for part in range(parts):
            for half in range(2):
                lend_copy(part, half).start()

    other_sections(lambda to: meta_copy(to, s).start())
    r.meta_rx[s] = r.meta[...]

    @pl.when(s != last)
    def _():
        idx_copy(s).start()

    r.gain_grad[...] = jnp.zeros_like(r.gain_grad)
    r.fgain_grad[...] = jnp.zeros_like(r.fgain_grad)

    if not z.summed:

        @pl.when(is_ffn)
        def _():
            r.tab_grad[...] = jnp.zeros_like(r.tab_grad)


    if not z.summed:

        @pl.when(s != last)
        def _():
            r.dproj[...] = jnp.zeros_like(r.dproj)

    r.dbias[...] = jnp.zeros_like(r.dbias)
    gain = r.gain[...]
    fgain = r.fgain[...].reshape(1, width)

    def wait_meta(m):
        @pl.when(m != s)
        def _():
            meta_copy(0, m).wait_recv()

    def load_state(m):
        states = r.xin[m].astype(F32)
        inverse = rms_inverse(states)
        return states, inverse, states * inverse

    low_half = lax.broadcasted_iota(jnp.int32, (1, 128), 1) < DH

    def split_heads(value):
        wide = value.astype(F32)
        return jnp.concatenate(
            [jnp.where(low_half, wide, 0.0), jnp.where(low_half, 0.0, wide)], axis=0
        ).astype(BF16)

    def join_heads(value):
        return jnp.where(low_half, value[:rows], value[rows:]).astype(BF16)

    def attention_setup():
        buckets = r.buckets[...]
        for h in range(H):
            total = jnp.zeros(buckets.shape, F32)
            for b in range(32):
                total = jnp.where(buckets == b, r.bias[h : h + 1, b : b + 1], total)
            r.bias_sc[h // 2, h % 2] = total

    def attention_table():
        buckets = r.buckets[...]
        ones = jnp.ones((16, 128), BF16)
        head_row = lax.broadcasted_iota(jnp.int32, (16, 32), 0)

        def head(h, carry):
            grad = r.dbias[h // 2, lax.rem(h, 2)]
            rest = jnp.concatenate(
                [
                    jnp.sum(jnp.where(buckets == b, grad, 0.0), axis=0, keepdims=True)
                    for b in range(32)
                ],
                axis=0,
            )
            total = jnp.zeros((16, 32), F32)
            for _ in range(3):
                part = rest.astype(BF16)
                total = total + nt(ones, part)
                rest = rest - part.astype(F32)
            return carry + jnp.where(head_row == h, total, 0.0)

        r.tab_grad[...] = lax.fori_loop(0, H, head, jnp.zeros((16, 32), F32))

    def turn(source, slab, start):
        size = FF_STEP // z.chunk
        first = slab * z.slab_chunks + start // z.chunk
        r.pool[first : first + size] = source[:, start : start + FF_STEP].T.reshape(
            size, z.chunk, width
        )

    def turned(slab, start, stop):
        first = slab * z.slab_chunks
        return r.pool[first + start // z.chunk : first + stop // z.chunk].reshape(
            stop - start, width
        )

    def attention_forward(m):
        states, inverse, scaled = load_state(m)
        normed = scaled * gain
        r.left[0, :, block(m)] = normed.T.astype(BF16)
        normed_low = normed.astype(BF16)
        for start in range(0, 3 * head_width, head_width):
            r.qkv[block(m), start : start + head_width] = nn(
                normed_low, r.main[:, start : start + head_width]
            ).astype(BF16)
        live = jnp.broadcast_to(r.meta_rx[m, 0:1, :], (rows, rows)).T > 0.5
        row_query = lax.broadcasted_iota(jnp.int32, (rows, rows), 0) // query_len
        column_query = lax.broadcasted_iota(jnp.int32, (rows, rows), 1) // query_len
        keep = jnp.logical_and(row_query == column_query, live)
        for pair in range(H // 2):
            at = pair * 128
            query = r.qkv[block(m), at : at + 128]
            keys = r.qkv[block(m), head_width + at : head_width + at + 128]
            values = r.qkv[block(m), 2 * head_width + at : 2 * head_width + at + 128]
            raw = nt(split_heads(keys), query)
            biased = raw.reshape(2, batch_size, query_len, rows) + r.bias_sc[pair][:, None]
            scores = jnp.where(keep[None], biased.reshape(2, rows, rows), MASK_FILL)
            top = jnp.max(scores, axis=1, keepdims=True)
            grown = jnp.exp(scores - top)
            soft = (grown / jnp.sum(grown, axis=1, keepdims=True)).reshape(2 * rows, rows)
            r.probs[m, pair] = soft
            r.right[0, block(m), 3 * head_width + at : 3 * head_width + at + 128] = tn(
                soft.astype(BF16), split_heads(values)
            ).astype(BF16)
        context = r.right[0, block(m), 3 * head_width :]
        return states + nt(context, r.main[:, 3 * head_width :])

    def attention_backward(m):
        states, inverse, scaled = load_state(m)
        grad_low = r.gin[m]
        grad = grad_low.astype(F32)
        r.left[1, :, block(m)] = grad.T.astype(BF16)
        grad_context = nn(grad_low, r.main[:, 3 * head_width :]).astype(BF16)
        for pair in range(H // 2):
            at = pair * 128
            query = r.qkv[block(m), at : at + 128]
            keys = r.qkv[block(m), head_width + at : head_width + at + 128]
            values = r.qkv[block(m), 2 * head_width + at : 2 * head_width + at + 128]
            grad_pair = grad_context[:, at : at + 128]
            soft = r.probs[m, pair]
            grad_soft = nt(split_heads(values), grad_pair)
            moved = (soft * grad_soft).reshape(2, rows, rows)
            grad_scores = moved - soft.reshape(2, rows, rows) * jnp.sum(
                moved, axis=1, keepdims=True
            )
            r.dbias[pair] += jnp.sum(
                grad_scores.reshape(2, batch_size, query_len, rows), axis=1
            )
            scores_low = grad_scores.reshape(2 * rows, rows).astype(BF16)
            found = (
                tn(scores_low, split_heads(keys)).astype(BF16),
                join_heads(nn(scores_low, query)),
                join_heads(nn(soft.astype(BF16), grad_pair)),
            )
            for third in range(3):
                start = third * head_width + at
                r.right[0, block(m), start : start + 128] = found[third]
        grad_normed = nn(r.right[0, block(m), : 3 * head_width], turned(0, 0, 3 * head_width))
        grad_states, grad_gain = rms_back(scaled, inverse, gain, grad_normed)
        r.gain_grad[...] += grad_gain
        return grad + grad_states

    def ffn_forward(m):
        states, inverse, scaled = load_state(m)
        normed = scaled * gain
        r.left[0, :, block(m)] = normed.T.astype(BF16)
        normed_low = normed.astype(BF16)
        outputs = states
        for start in range(0, ff, FF_STEP):
            columns = slice(start, start + FF_STEP)
            gate = nn(normed_low, r.main[:, columns])
            up = nn(normed_low, r.lent[:, columns])
            square = gate * gate
            bent = jnp.tanh(GELU_C * gate * (1.0 + GELU_A * square))
            half = 0.5 * (1.0 + bent)
            smooth = gate * half
            slope = half + 0.5 * gate * (1.0 - bent * bent) * (
                GELU_C * (1.0 + 3.0 * GELU_A * square)
            )
            hidden = (smooth * up).astype(BF16)
            r.right[1, block(m), columns] = hidden
            r.right[0, block(m), columns] = (slope * up).astype(BF16)
            r.right[2, block(m), columns] = smooth.astype(BF16)
            outputs = outputs + nn(hidden, turned(1, start, start + FF_STEP))
        return outputs

    def ffn_backward(m, grad):
        states, inverse, scaled = load_state(m)
        grad_low = grad.astype(BF16)
        r.left[1, :, block(m)] = grad.T.astype(BF16)
        grad_normed = jnp.zeros((rows, width), F32)
        for start in range(0, ff, FF_STEP):
            columns = slice(start, start + FF_STEP)
            grad_hidden = nn(grad_low, r.side[:, columns])
            grad_gate = (grad_hidden * r.right[0, block(m), columns].astype(F32)).astype(BF16)
            grad_up = (grad_hidden * r.right[2, block(m), columns].astype(F32)).astype(BF16)
            r.right[0, block(m), columns] = grad_gate
            r.right[2, block(m), columns] = grad_up
            grad_normed = (
                grad_normed
                + nn(grad_gate, turned(0, start, start + FF_STEP))
                + nn(grad_up, turned(2, start, start + FF_STEP))
            )
        grad_states, grad_gain = rms_back(scaled, inverse, gain, grad_normed)
        r.gain_grad[...] += grad_gain
        return grad + grad_states

    def count_hits(m):
        for c in range(batch_size):
            base = r.idx_rx[m, c : c + 1, :] * DOC_LEN
            numbers = lax.broadcasted_iota(jnp.int32, (DOC_LEN, rows), 0) + base
            total = jnp.zeros((DOC_LEN, rows), F32)
            for k in range(z.retrieved):
                total = total + jnp.where(r.idx_rx[m, 8 + k : 9 + k, :] == numbers, 1.0, 0.0)
            r.counts[m, c * DOC_LEN : (c + 1) * DOC_LEN, :] = total.astype(BF16)

    def pick_docs(m):
        for c in range(batch_size):
            label = r.idx_rx[m, c : c + 1, :]

            def pick(t, picked):
                here = r.table[pl.ds(pl.multiple_of(t * DOC_LEN, DOC_LEN), DOC_LEN), :].astype(F32)
                return jnp.where(label == t, here, picked)

            picked = lax.fori_loop(
                0, dp_size * z.doc_rows // DOC_LEN, pick, jnp.zeros((DOC_LEN, z.vector), F32)
            )
            r.own_docs[m, c * DOC_LEN : (c + 1) * DOC_LEN, :] = picked.astype(BF16)

    def loss_and_grad(m, unit):
        docs = r.own_docs[m]
        sims = nt(docs, unit)
        count = r.counts[m].astype(F32)
        imputed = jnp.sum(count * sims, axis=0, keepdims=True) / z.retrieved
        grown = count * jnp.exp(sims)
        imputed_mass = jnp.exp(imputed)
        mass = imputed_mass + jnp.concatenate(
            [
                jnp.sum(grown[c * DOC_LEN : (c + 1) * DOC_LEN], axis=0, keepdims=True)
                for c in range(batch_size)
            ],
            axis=0,
        )
        weighted = jnp.log(mass) * r.meta_rx[m, 1:2, :]
        candidate = lax.broadcasted_iota(jnp.int32, (batch_size, 1), 0)
        losses = jnp.zeros((1, rows), F32)
        grad_tokens = jnp.zeros((batch_size, rows), F32)
        for q in range(batch_size):
            own = token_query == q
            score = jnp.sum(jnp.where(own, weighted, 0.0), axis=1, keepdims=True)
            top = jnp.max(score, axis=0, keepdims=True)
            risen = jnp.exp(score - top)
            total = jnp.sum(risen, axis=0, keepdims=True)
            chosen_one = (candidate == q).astype(F32)
            loss = top + jnp.log(total) - jnp.sum(score * chosen_one, axis=0, keepdims=True)
            losses = losses + jnp.where(lane == q, loss, 0.0)
            grad_tokens = grad_tokens + jnp.where(own, risen / total - chosen_one, 0.0)
        grad_mass = grad_tokens * r.meta_rx[m, 1:2, :] / mass
        shared = jnp.sum(grad_mass, axis=0, keepdims=True) * imputed_mass / z.retrieved
        grad_sims = count * shared + jnp.concatenate(
            [
                grown[c * DOC_LEN : (c + 1) * DOC_LEN] * grad_mass[c : c + 1]
                for c in range(batch_size)
            ],
            axis=0,
        )
        high = grad_sims.astype(BF16)
        rest = (grad_sims - high.astype(F32)).astype(BF16)
        return losses, tn(high, docs) + tn(rest, docs)

    def finish_states(m, states):
        inverse = rms_inverse(states)
        scaled = states * inverse
        normed = (scaled * fgain).astype(BF16)
        projected = nn(normed, r.proj[...])
        size = lax.rsqrt(jnp.sum(projected * projected, axis=-1, keepdims=True) + EPS_NORM)
        exact = projected * size
        unit = exact.astype(BF16)
        losses, grad_unit = loss_and_grad(m, unit)
        r.unit_tx[m] = unit
        r.loss_tx[m] = jnp.broadcast_to(losses, (8, rows))

        @pl.when(m != last)
        def _():
            unit_copy(m, m).start()
            loss_copy(m, m).start()

        grad_projected = (
            size * (grad_unit - exact * jnp.sum(grad_unit * exact, axis=-1, keepdims=True))
        ).astype(BF16)
        r.xout[m] = normed
        r.final_right[block(m), :] = grad_projected
        grad_normed = nt(grad_projected, r.proj[...])
        grad_states, grad_gain = rms_back(scaled, inverse, fgain, grad_normed)
        r.fgain_grad[...] += grad_gain
        return grad_states

    def loop(body):
        def step(m, carry):
            body(m)
            return carry

        lax.fori_loop(0, sections, step, 0)

    def wait_state(m):
        @pl.when(jnp.logical_or(s != 0, m != 0))
        def _():
            state_copy(m).wait_recv()

    @pl.when(is_attention)
    def _():
        attention_setup()
        main_load().wait()

        def forward(m):
            wait_meta(m)
            wait_state(m)

            @pl.when(jnp.logical_and(s == 0, m == 0))
            def _():
                hid_load().wait()

            r.xout[m] = attention_forward(m).astype(BF16)
            state_copy(m).start()

        loop(forward)
        for start in range(0, ff, FF_STEP):
            turn(r.main, 0, start)

        def backward(m):
            grad_copy(m).wait_recv()
            r.gout[m] = attention_backward(m).astype(BF16)

            @pl.when(s != 0)
            def _():
                grad_copy(m).start()

            @pl.when(jnp.logical_and(s == 0, m != 0))
            def _():
                fin_copy(m, m).start()

        loop(backward)
        if not z.summed:
            attention_table()

    @pl.when(is_ffn)
    def _():
        turns = [(r.main, 0, start) for start in range(0, ff, FF_STEP)]
        turns += [(r.side, 1, start) for start in range(0, ff, FF_STEP)]
        main_load().wait()
        side_load().wait()
        def far_arrived(piece):
            lend_forward(2, far_place, *piece, far_peer).wait_recv()
            lend_forward(3, far_place, *piece, core_peer).start()

        lag = 2
        for k, piece in enumerate(pieces):
            lend_copy(*piece).wait_recv()
            lend_forward(2, place, *piece, far_peer).start()
            lend_forward(1, place, *piece, core_peer).start()
            if k >= lag:
                far_arrived(pieces[k - lag])
            for one in turns[k :: len(pieces)]:
                turn(*one)

        @pl.when(s == last)
        def _():
            r.idx_rx[last] = r.idx[...]

            def pass_on(owner):
                table_copy(owner, owner).wait_recv()
                table_forward(owner).start()

            far_owners(pass_on)

            def prepare(m):
                @pl.when(m != last)
                def _():
                    idx_copy(m).wait_recv()

                count_hits(m)

            loop(prepare)

        for piece in pieces[-lag:]:
            far_arrived(piece)
        for piece in pieces:
            lend_forward(1, place, *piece, core_peer).wait_recv()
            lend_forward(3, far_place, *piece, core_peer).wait_recv()

        def turn_lent():
            for start in range(0, ff, FF_STEP):
                turn(r.lent, 2, start)

        @pl.when(s == last)
        def _():
            docs_load().wait()
            table_near(core_peer).wait_recv()

            def take(owner):
                table_forward(owner + core_peer - d).wait_recv()

            far_owners(take)
            loop(pick_docs)
            turn_lent()
            loop(wait_meta)

            def both(m):
                wait_state(m)
                states = ffn_forward(m)
                grad = finish_states(m, states)
                r.gout[m] = ffn_backward(m, grad).astype(BF16)
                grad_copy(m).start()

            loop(both)
            r.dproj[...] = tn(r.xout[...].reshape(z.total, width), r.final_right[...]).astype(
                r.dproj.dtype
            )

        @pl.when(s != last)
        def _():
            def forward(m):
                wait_state(m)
                r.xout[m] = ffn_forward(m).astype(BF16)
                state_copy(m).start()

            loop(forward)
            turn_lent()

            def backward(m):
                grad_copy(m).wait_recv()
                r.gout[m] = ffn_backward(m, r.gin[m].astype(F32)).astype(BF16)
                grad_copy(m).start()

            loop(backward)
            loop(wait_meta)

        for piece in pieces:
            lend_forward(1, place, *piece, core_peer).wait_send()
            lend_forward(2, place, *piece, far_peer).wait_send()
            lend_forward(3, far_place, *piece, core_peer).wait_send()

    def put(k, name):
        return pltpu.make_async_copy(getattr(r, name + "_v"), getattr(r, name), r.put_sem.at[k])

    homes = [put(k, name) for k, name in enumerate(("units", "loss", "dx"))]

    def come_home():
        @pl.when(s != 0)
        def _():
            fin_copy(0, s).wait_recv()
            r.dx_v[...] = r.fin_rx[...].astype(F32).reshape(batch_size, query_len, width)

        @pl.when(s == 0)
        def _():
            r.dx_v[...] = r.gout[0].astype(F32).reshape(batch_size, query_len, width)

        def write_own(unit, losses):
            r.units_v[...] = unit.reshape(batch_size, query_len, z.vector)
            r.loss_v[...] = losses

        @pl.when(s != last)
        def _():
            unit_copy(0, s).wait_recv()
            loss_copy(0, s).wait_recv()
            write_own(r.unit_rx[...], r.loss_rx[...])

        @pl.when(s == last)
        def _():
            write_own(r.unit_tx[last], r.loss_tx[last])

        for one in homes:
            one.start()

    if z.summed:
        sum_gradients(
            z, r, s, d, copy, peers, other_sections, is_attention, attention_table, come_home
        )
    else:
        come_home()

    for one in homes:
        one.wait()
    other_sections(lambda to: meta_copy(to, s).wait_send())

    @pl.when(s != 0)
    def _():
        hid_copy(s).wait_send()
        loop(lambda m: grad_copy(m).wait_send())

    @pl.when(s == 0)
    def _():
        for m in range(1, sections):
            fin_copy(m, m).wait_send()

    @pl.when(is_attention)
    def _():
        for piece in pieces:
            lend_copy(*piece).wait_send()

    @pl.when(s != last)
    def _():
        idx_copy(s).wait_send()
        loop(lambda m: state_copy(m).wait_send())

    @pl.when(s == last)
    def _():
        table_near(d).wait_send()
        far_owners(lambda to: table_copy(to, d).wait_send())
        far_owners(lambda owner: table_forward(owner).wait_send())
        for m in range(sections - 1):
            unit_copy(m, m).wait_send()
            loss_copy(m, m).wait_send()


def sum_gradients(
    z, r, s, d, copy, peers, other_sections, is_attention, attention_table, come_home
):
    sections, dp_size, width, ff, share, line = z.sections, z.dp_size, z.width, z.ff, z.share, z.line
    step_columns, per_slab, units, steps = z.step_columns, z.per_slab, z.units, z.steps
    place = d // 2
    core = lax.rem(d, 2)
    peer = d + 1 - 2 * core
    last = sections - 1
    before = lax.rem(s + sections - 1, sections)
    is_ffn = jnp.logical_not(is_attention)
    orders = sum_order(line)

    def piece_rows(owner):
        return pl.ds(pl.multiple_of(owner * share, share), share)

    def gain_copy(to, slot):
        return copy(r.gain_grad, r.gain_rx.at[slot], r.gain_ss.at[to], r.gain_rs.at[slot], s, to)

    def table_copy(to, slot):
        return copy(r.tab_grad, r.tab_rx.at[slot], r.tabs_ss.at[to], r.tabs_rs.at[slot], s, to)

    def fgain_copy(to, slot):
        return copy(r.fgain_grad, r.fgain_rx.at[slot], r.fg_ss.at[to], r.fg_rs.at[slot], s, to)

    def proj_copy(to, slot):
        return copy(
            r.dproj.at[piece_rows(to), :],
            r.proj_rx.at[slot],
            r.proj_ss.at[to],
            r.proj_rs.at[slot],
            s,
            to,
        )

    def spread_copy(to, owner):
        rows = piece_rows(owner)
        return copy(
            r.proj_sum.at[rows, :],
            r.proj_sum.at[rows, :],
            r.spread_ss.at[to],
            r.spread_rs.at[owner],
            s,
            to,
        )

    def table_across(to, slot):
        return copy(r.tab_tx, r.tab_cx.at[slot], r.across_ss.at[0, to], r.across_rs.at[slot], to, d)

    def fgain_across(to):
        return copy(
            r.fgain_tx, r.fgain_sum, r.across_ss.at[1, to], r.across_rs.at[sections], to, d
        )

    def proj_across(to):
        return copy(
            r.proj_sum, r.proj_sum, r.across_ss.at[2, to], r.across_rs.at[sections + 1], to, d
        )

    small_puts = [
        pltpu.make_async_copy(source, target, r.put_sem.at[3 + k])
        for k, (source, target) in enumerate(
            (
                (r.gain_out_v, r.gain_out),
                (r.table_out_v, r.table_out),
                (r.fgain_out_v, r.fgain_out),
                (r.proj_v, r.proj_out),
            )
        )
    ]

    def slab_put(slab, column, columns):
        source, target = ((r.main_v, r.main_out), (r.side_v, r.side_out))[slab]
        return pltpu.make_async_copy(
            source.at[:, columns], target.at[0, :, columns], r.slab_sem.at[slab, column]
        )

    def total_of(ref, count):
        total = ref[0].astype(F32)
        for k in range(1, count):
            total = total + ref[k].astype(F32)
        return total

    def to_others(body):
        for to in range(sections):

            @pl.when(s != to)
            def _():
                body(to)

    def small_first():
        peers(lambda to: gain_copy(to, d).start())
        r.gain_rx[d] = r.gain_grad[...]

        @pl.when(is_attention)
        def _():
            attention_table()
            peers(lambda to: table_copy(to, d).start())
            r.tab_rx[d] = r.tab_grad[...]

    def proj_first():
        peers(lambda to: proj_copy(to, d).start())
        peers(lambda to: fgain_copy(to, d).start())
        r.proj_rx[d] = r.dproj[piece_rows(d), :]
        r.fgain_rx[d] = r.fgain_grad[...]

    def proj_second():
        peers(lambda owner: proj_copy(owner, owner).wait_recv())
        peers(lambda owner: fgain_copy(owner, owner).wait_recv())
        r.proj_sum[piece_rows(d), :] = total_of(r.proj_rx, dp_size).astype(BF16)
        r.fgain_tx[...] = total_of(r.fgain_rx, dp_size)
        r.fgain_sum[...] = r.fgain_tx[...]
        peers(lambda to: spread_copy(to, d).start())
        to_others(lambda to: fgain_across(to).start())

    def proj_third():
        peers(lambda owner: spread_copy(owner, owner).wait_recv())
        to_others(lambda to: proj_across(to).start())

    def small_second():
        peers(lambda owner: gain_copy(owner, owner).wait_recv())
        gain_sum = jnp.broadcast_to(total_of(r.gain_rx, dp_size), (8, width))
        r.gain_out_v[...] = pltpu.roll(gain_sum, width - d * share, 1)[0:1, :share]

        @pl.when(is_attention)
        def _():
            peers(lambda owner: table_copy(owner, owner).wait_recv())
            r.tab_tx[...] = total_of(r.tab_rx, dp_size)
            r.tab_cx[s // 2] = r.tab_tx[...]
            to_others(lambda to: table_across(to, s // 2).start())

    def small_last():
        for source in range(0, sections, 2):

            @pl.when(s != source)
            def _():
                table_across(source, source // 2).wait_recv()

        r.table_out_v[...] = total_of(r.tab_cx, (sections + 1) // 2)[:H]

        @pl.when(s != last)
        def _():
            fgain_across(last).wait_recv()
            proj_across(last).wait_recv()

        r.fgain_out_v[...] = r.fgain_sum[...].reshape(width)
        r.proj_v[...] = r.proj_sum[...].astype(F32)
        for one in small_puts:
            one.start()
        peers(lambda to: gain_copy(to, d).wait_send())

        @pl.when(is_attention)
        def _():
            peers(lambda to: table_copy(to, d).wait_send())
            to_others(lambda to: table_across(to, s // 2).wait_send())

        @pl.when(s == last)
        def _():
            peers(lambda to: proj_copy(to, d).wait_send())
            peers(lambda to: fgain_copy(to, d).wait_send())
            peers(lambda to: spread_copy(to, d).wait_send())
            to_others(lambda to: fgain_across(to).wait_send())
            to_others(lambda to: proj_across(to).wait_send())

    def target(i):
        found = jnp.int32(0)
        for k in range(line):
            found = jnp.where(place == k, orders[k][i], found)
        return found

    targets = [target(i) for i in range(line)]

    def target_of(i):
        j = targets[0]
        for k in range(1, line):
            j = jnp.where(i == k, targets[k], j)
        return j

    def parts_of(t):
        i, u = t // units, lax.rem(t, units)
        j = target_of(i)
        slab, column = lax.rem(u, 2), u // 2
        columns = pl.ds(pl.multiple_of(column * step_columns, step_columns), step_columns)
        return j, u, slab, column, columns

    def core_copy(t):
        return copy(
            r.core_tx.at[lax.rem(t, 4)], r.pool.at[t], r.core_ss.at[t], r.core_rs.at[t], s, peer
        )

    def up_core_copy(k):
        return copy(
            r.up_core_tx.at[lax.rem(k, 4)], r.up_rx.at[k], r.up_core_ss.at[k], r.up_rs.at[k], s, peer
        )

    def up_copy(k):
        return copy(
            r.up_tx.at[lax.rem(k, 4)], r.up_rx.at[k], r.up_ss.at[k], r.up_rs.at[k], before, d
        )

    hand_column = per_slab - 1
    hand_columns = slice(hand_column * step_columns, ff)

    def window(n):
        row = pl.ds(pl.multiple_of(lax.rem(n, z.windows) * share, share), share)
        column = pl.ds(pl.multiple_of(n // z.windows * step_columns, step_columns), step_columns)
        return r.qkv.at[row, column]

    def hand_copy(k):
        i = k // per_slab
        return copy(r.up_tx.at[lax.rem(k, 4)], window(i), r.up_ss.at[k], r.hand_rs.at[i], last, d)

    def hand_line(i, way, j, to):
        slot = way * (line - 1) + j - 1 + way
        return copy(
            line_view(steps - units + i),
            window(line + slot),
            r.line_ss.at[steps - units + i],
            r.hand_rs.at[line + slot],
            s,
            to * 2 + core,
        )

    def hand_home():
        return copy(
            r.up_mine.at[0], r.side_v.at[:, hand_columns], r.home_ss, r.home_rs, 0, d
        )

    def extra(i):
        j = target_of(i)
        total = r.up_mine.at[0]
        hand_copy(i * per_slab).wait_recv()
        total[...] = window(i)[...].astype(F32)
        way = jnp.where(j < place, 1, 0)

        @pl.when(jnp.logical_and(place > 0, j >= place))
        def _():
            hand_line(i, 0, j, place).wait_recv()
            total[...] += window(line + j - 1)[...].astype(F32)

        @pl.when(jnp.logical_and(place < line - 1, j <= place))
        def _():
            hand_line(i, 1, j, place).wait_recv()
            total[...] += window(line + line - 1 + j)[...].astype(F32)

        @pl.when(j == place)
        def _():
            hand_home().start()

        @pl.when(j != place)
        def _():
            line_view(steps - units + i)[...] = total[...].astype(BF16)
            hand_line(i, way, j, place + 1 - 2 * way).start()

    def line_view(t):
        row = pl.ds(pl.multiple_of(lax.rem(t, dp_size) * share, share), share)
        column = pl.ds(pl.multiple_of(t // dp_size * step_columns, step_columns), step_columns)
        return r.lent.at[row, column]

    def line_slot(way, j, u):
        return steps + (way * (line - 1) + j - 1 + way) * units + u

    def line_copy(t, way, j, u, to):
        slot = j - 1 + way
        return copy(
            line_view(t),
            r.pool.at[line_slot(way, j, u)],
            r.line_ss.at[t],
            r.line_rs.at[way, slot, u],
            s,
            to * 2 + core,
        )

    def theirs(j):
        return pl.ds(pl.multiple_of((j * 2 + 1 - core) * share, share), share)

    def ours(j):
        return pl.ds(pl.multiple_of((j * 2 + core) * share, share), share)

    def begin(t):
        j, u, slab, column, columns = parts_of(t)
        mixed = jnp.logical_and(is_attention, column == per_slab - 1)
        which = jnp.where(jnp.logical_or(slab == 1, mixed), 1, 0)

        @pl.when(jnp.logical_or(is_ffn, slab == 0))
        def _():
            right = r.right[slab, :, columns]

            @pl.when(t >= 4)
            def _():
                core_copy(t - 4).wait_send()

            r.core_tx[lax.rem(t, 4)] = nn(r.left[which, theirs(j), :], right).astype(BF16)
            core_copy(t).start()
            r.mine[lax.rem(t, 2)] = nn(r.left[which, ours(j), :], right)

    def up_parts(k):
        i, column = k // per_slab, lax.rem(k, per_slab)
        columns = pl.ds(pl.multiple_of(column * step_columns, step_columns), step_columns)
        return target_of(i), columns

    def begin_up(k):
        j, columns = up_parts(k)
        right = r.right[2, :, columns]

        @pl.when(k >= 4)
        def _():
            up_core_copy(k - 4).wait_send()

        r.up_core_tx[lax.rem(k, 4)] = nn(r.left[0, theirs(j), :], right).astype(BF16)
        up_core_copy(k).start()
        r.up_mine[lax.rem(k, 2)] = nn(r.left[0, ours(j), :], right)

    def finish_up(k):
        up_core_copy(k).wait_recv()

        @pl.when(k >= 4)
        def _():
            up_copy(k - 4).wait_send()

        r.up_tx[lax.rem(k, 4)] = (r.up_mine[lax.rem(k, 2)] + r.up_rx[k].astype(F32)).astype(BF16)
        if z.handed:
            handed = jnp.logical_and(s == 1, lax.rem(k, per_slab) == hand_column)

            @pl.when(handed)
            def _():
                hand_copy(k).start()

            @pl.when(jnp.logical_not(handed))
            def _():
                up_copy(k).start()
        else:
            up_copy(k).start()

    def gone(t):
        return jnp.logical_and(s == 0, lax.rem(t, units) == units - 1) if z.handed else False

    def finish(t):
        @pl.when(jnp.logical_not(gone(t)))
        def _():
            finish_here(t)

    def finish_here(t):
        j, u, slab, column, columns = parts_of(t)
        k = t // 2
        total = r.mine.at[lax.rem(t, 2)]

        @pl.when(jnp.logical_or(is_ffn, slab == 0))
        def _():
            core_copy(t).wait_recv()
            total[...] += r.pool[t].astype(F32)

        @pl.when(jnp.logical_and(is_attention, slab == 1))
        def _():
            up_copy(k).wait_recv()
            total[...] = r.up_rx[k].astype(F32)

        way = jnp.where(j < place, 1, 0)

        @pl.when(jnp.logical_and(place > 0, j >= place))
        def _():
            line_copy(t, 0, j, u, place).wait_recv()
            total[...] += r.pool[line_slot(0, j, u)].astype(F32)

        @pl.when(jnp.logical_and(place < line - 1, j <= place))
        def _():
            line_copy(t, 1, j, u, place).wait_recv()
            total[...] += r.pool[line_slot(1, j, u)].astype(F32)

        @pl.when(jnp.logical_and(j == place, slab == 0))
        def _():
            r.main_v[:, columns] = total[...]
            slab_put(0, column, columns).start()

        @pl.when(jnp.logical_and(j == place, slab == 1))
        def _():
            r.side_v[:, columns] = total[...]
            slab_put(1, column, columns).start()

        @pl.when(j != place)
        def _():
            line_view(t)[...] = total[...].astype(BF16)
            line_copy(t, way, j, u, place + 1 - 2 * way).start()

    pl.semaphore_signal(r.core_ready, inc=1, device_id=(s, peer), device_id_type=MESH)

    @pl.when(place > 0)
    def _():
        pl.semaphore_signal(r.line_ready, inc=1, device_id=(s, d - 2), device_id_type=MESH)

    @pl.when(place < line - 1)
    def _():
        pl.semaphore_signal(r.line_ready, inc=1, device_id=(s, d + 2), device_id_type=MESH)

    @pl.when(s == last)
    def _():
        proj_first()

    ups = steps // 2
    pl.semaphore_wait(r.core_ready, 1)
    begin(jnp.int32(0))

    @pl.when(is_ffn)
    def _():
        begin_up(jnp.int32(0))

    neighbours = jnp.where(place > 0, 1, 0) + jnp.where(place < line - 1, 1, 0)
    pl.semaphore_wait(r.line_ready, neighbours)

    def step(t, carry):
        @pl.when(t < steps)
        def _():
            begin(t)

        @pl.when(jnp.logical_and(is_ffn, t < ups))
        def _():
            begin_up(t)

        finish(t - 1)

        @pl.when(jnp.logical_and(is_ffn, t <= ups))
        def _():
            finish_up(t - 1)

        if z.handed:

            @pl.when(jnp.logical_and(s == last, jnp.logical_and(t >= 2 * units, t < 2 * units + line)))
            def _():
                extra(t - 2 * units)

        @pl.when(jnp.logical_and(s == last, t == 2))
        def _():
            proj_second()

        @pl.when(t == 4)
        def _():
            small_first()

        @pl.when(jnp.logical_and(s == last, t == 6))
        def _():
            proj_third()

        @pl.when(t == units + 4)
        def _():
            small_second()

        @pl.when(t == steps - units)
        def _():
            come_home()

        return carry

    lax.fori_loop(1, steps + 1, step, 0)
    small_last()
    if z.handed:

        @pl.when(s == 0)
        def _():
            hand_home().wait_recv()
            slab_put(1, hand_column, hand_columns).start()

        @pl.when(s == last)
        def _():
            hand_home().wait_send()
            for i in range(line - 1):
                hand_line(i, 0, 1, place).wait_send()

    for slab in range(2):
        for column in range(per_slab):
            slab_put(
                slab, column, slice(column * step_columns, (column + 1) * step_columns)
            ).wait()
    for one in small_puts:
        one.wait()

    def drain(t, carry):
        @pl.when(jnp.logical_not(gone(t)))
        def _():
            line_copy(t, 0, 1, 0, place).wait_send()

        return carry

    lax.fori_loop(0, steps - units, drain, 0)

    def drain_core(t, carry):
        slab = lax.rem(t, 2)

        @pl.when(jnp.logical_or(is_ffn, slab == 0))
        def _():
            core_copy(t).wait_send()

        return carry

    lax.fori_loop(steps - 4, steps, drain_core, 0)

    @pl.when(is_ffn)
    def _():
        for k in range(steps // 2 - 4, steps // 2):
            up_core_copy(k).wait_send()
            up_copy(k).wait_send()


def relay(z, hid, lengths, labels, chosen, main, side, gain, bias, buckets, fgain, proj, docs):
    dma = pltpu.SemaphoreType.DMA
    shape = jax.ShapeDtypeStruct
    sections, rows, width, ff, dp_size = z.sections, z.rows, z.width, z.ff, z.dp_size
    share, steps, units = z.share, z.steps, z.units
    piece = (share, z.step_columns)
    vmem = pl.BlockSpec(memory_space=VMEM)
    smem = pl.BlockSpec(memory_space=pltpu.SMEM)
    anywhere = pl.BlockSpec(memory_space=pl.ANY)
    inputs = dict(
        hid_hbm=(hid, anywhere),
        lengths=(lengths, smem),
        labels=(labels, smem),
        chosen_hbm=(chosen, anywhere),
        main_hbm=(main, anywhere),
        side_hbm=(side, anywhere),
        gain_hbm=(gain, anywhere),
        bias_hbm=(bias, anywhere),
        buckets_hbm=(buckets, anywhere),
        fgain_hbm=(fgain, anywhere),
        proj_hbm=(proj, anywhere),
        docs_hbm=(docs, anywhere),
    )
    outputs = dict(
        units=shape((z.batch_size, z.query_len, z.vector), BF16),
        loss=shape((8, rows), F32),
        dx=shape((z.batch_size, z.query_len, width), F32),
    )
    def like(value):
        return VMEM(value.shape, value.dtype)

    scratch = {name + "_v": like(value) for name, value in outputs.items()}
    scratch |= dict(
        chosen=like(chosen),
        bias=like(bias),
        buckets=like(buckets),
        gain=like(gain),
        fgain=like(fgain),
        proj=like(proj),
        main=VMEM((width, ff), BF16),
        side=VMEM((width, ff), BF16),
        lent=VMEM((width, ff), BF16),
        xin=VMEM((sections, rows, width), BF16),
        xout=VMEM((sections, rows, width), BF16),
        gin=VMEM((sections, rows, width), BF16),
        gout=VMEM((sections, rows, width), BF16),
        meta=VMEM((8, rows), F32),
        meta_rx=VMEM((sections, 8, rows), F32),
        idx=VMEM((8 + z.retrieved, rows), jnp.int32),
        idx_rx=VMEM((sections, 8 + z.retrieved, rows), jnp.int32),
        own_docs=VMEM((sections, z.batch_size * DOC_LEN, z.vector), BF16),
        table=VMEM((dp_size * z.doc_rows, z.vector), BF16),
        counts=VMEM((sections, z.batch_size * DOC_LEN, rows), BF16),
        pool=VMEM((z.pool, z.chunk, width), BF16),
        final_right=VMEM((z.total, z.vector), BF16),
        qkv=VMEM((z.total, 3 * H * DH), BF16),
        probs=VMEM((sections, H // 2, 2 * rows, rows), F32),
        bias_sc=VMEM((H // 2, 2, z.query_len, rows), F32),
        dbias=VMEM((H // 2, 2, z.query_len, rows), F32),
        fin_rx=VMEM((rows, width), BF16),
        unit_tx=VMEM((sections, rows, z.vector), BF16),
        unit_rx=VMEM((rows, z.vector), BF16),
        loss_tx=VMEM((sections, 8, rows), F32),
        loss_rx=VMEM((8, rows), F32),
        small_sem=dma((6,)),
        load_sem=dma((3,)),
        put_sem=dma((7,)),
        state_ss=dma((sections + 1,)),
        state_rs=dma((sections,)),
        grad_ss=dma((sections,)),
        grad_rs=dma((sections,)),
        meta_ss=dma((sections,)),
        meta_rs=dma((sections,)),
        idx_ss=dma,
        idx_rs=dma((sections,)),
        tab_ss=dma((dp_size,)),
        tab_rs=dma((dp_size,)),
        tabf_ss=dma((dp_size,)),
        lend_ss=dma((4, z.parts, 2)),
        lend_rs=dma((4, z.parts, 2)),
        fin_ss=dma((sections,)),
        fin_rs=dma,
        unit_ss=dma((sections,)),
        unit_rs=dma,
        loss_ss=dma((sections,)),
        loss_rs=dma,
    )
    factors = dict(left=((2, width, z.total), BF16), right=((3, z.total, ff), BF16))
    partials = dict(
        gain_grad=((1, width), F32),
        fgain_grad=((1, width), F32),
        tab_grad=((16, 32), F32),
        dproj=((width, z.vector), BF16 if z.summed else F32),
    )
    if z.summed:
        outputs |= dict(
            main_out=shape((1, share, ff), F32),
            side_out=shape((1, share, ff), F32),
            gain_out=shape((1, share), F32),
            table_out=shape((H, 32), F32),
            fgain_out=shape((width,), F32),
            proj_out=shape((width, z.vector), F32),
        )
        scratch |= {name: VMEM(*kind) for name, kind in (factors | partials).items()}
        scratch |= dict(
            gain_out_v=VMEM((1, share), F32),
            table_out_v=VMEM((H, 32), F32),
            fgain_out_v=VMEM((width,), F32),
            main_v=VMEM((share, ff), F32),
            side_v=VMEM((share, ff), F32),
            slab_sem=dma((2, z.per_slab)),
            mine=VMEM((2,) + piece, F32),
            up_mine=VMEM((2,) + piece, F32),
            core_tx=VMEM((4,) + piece, BF16),
            up_core_tx=VMEM((4,) + piece, BF16),
            up_tx=VMEM((4,) + piece, BF16),
            up_rx=VMEM((steps // 2,) + piece, BF16),
            gain_rx=VMEM((dp_size, 1, width), F32),
            tab_rx=VMEM((dp_size, 16, 32), F32),
            tab_tx=VMEM((16, 32), F32),
            tab_cx=VMEM(((sections + 1) // 2, 16, 32), F32),
            fgain_rx=VMEM((dp_size, 1, width), F32),
            fgain_tx=VMEM((1, width), F32),
            fgain_sum=VMEM((1, width), F32),
            proj_sum=VMEM((width, z.vector), BF16),
            proj_v=VMEM((width, z.vector), F32),
            proj_rx=VMEM((dp_size, share, z.vector), BF16),
            core_ss=dma((steps,)),
            core_rs=dma((steps,)),
            up_core_ss=dma((steps // 2,)),
            up_ss=dma((steps // 2,)),
            up_rs=dma((steps // 2,)),
            hand_rs=dma((3 * z.line - 2,)),
            home_ss=dma,
            home_rs=dma,
            line_ss=dma((steps,)),
            line_rs=dma((2, z.line - 1, units)),
            core_ready=pltpu.SemaphoreType.REGULAR,
            line_ready=pltpu.SemaphoreType.REGULAR,
            gain_ss=dma((dp_size,)),
            gain_rs=dma((dp_size,)),
            tabs_ss=dma((dp_size,)),
            tabs_rs=dma((dp_size,)),
            fg_ss=dma((dp_size,)),
            fg_rs=dma((dp_size,)),
            across_ss=dma((3, sections)),
            across_rs=dma((sections + 2,)),
            proj_ss=dma((dp_size,)),
            proj_rs=dma((dp_size,)),
            spread_ss=dma((dp_size,)),
            spread_rs=dma((dp_size,)),
        )
    else:
        outputs |= {name: shape(*kind) for name, kind in (factors | partials).items()}
    results = pl.pallas_call(
        functools.partial(relay_kernel, z, (*inputs, *outputs, *scratch)),
        out_shape=tuple(outputs.values()),
        in_specs=[spec for _, spec in inputs.values()],
        out_specs=tuple(vmem if name in factors or name in partials else anywhere for name in outputs),
        scratch_shapes=list(scratch.values()),
        compiler_params=pltpu.CompilerParams(
            collective_id=0, has_side_effects=True, vmem_limit_bytes=62 * 2**20
        ),
        name="relay",
    )(*[value for value, _ in inputs.values()])
    return types.SimpleNamespace(**dict(zip(outputs, results, strict=True)))


def deliver_kernel(count, *refs):
    for k in range(count):
        refs[count + 1 + k][...] = refs[k][...]
    losses, out = refs[count], refs[-1]
    out[...] = losses[0:1, : out.shape[0]].reshape(out.shape)


def deliver(values, losses, queries):
    count = len(values)
    vmem = pl.BlockSpec(memory_space=VMEM)
    return pl.pallas_call(
        functools.partial(deliver_kernel, count),
        out_shape=tuple(jax.ShapeDtypeStruct(v.shape, v.dtype) for v in values)
        + (jax.ShapeDtypeStruct((queries,), F32),),
        in_specs=[vmem] * (count + 1),
        out_specs=(vmem,) * (count + 1),
        name="deliver",
    )(*values, losses)


def sums_outside(z, out):
    head_width = H * DH
    section = lax.axis_index("section")
    is_attention = section % 2 == 0
    left, right = out.left, out.right
    second = jnp.where(is_attention, left[1], left[0])
    main_grad = jnp.concatenate(
        [nn(left[0], right[0, :, : 3 * head_width]), nn(second, right[0, :, 3 * head_width :])],
        axis=1,
    )
    up_grad = lax.ppermute(
        nn(left[0], right[2]).astype(BF16),
        "section",
        [(k, k - 1) for k in range(1, z.sections)],
    )
    side_grad = jnp.where(is_attention, up_grad.astype(F32), nn(left[1], right[1]))
    scatter = functools.partial(
        lax.psum_scatter, axis_name="dp", scatter_dimension=0, tiled=True
    )
    table, fgain, proj = lax.psum(
        (out.tab_grad[:H], out.fgain_grad[0], out.dproj), ("section", "dp")
    )
    return (
        scatter(main_grad)[None],
        scatter(side_grad)[None],
        scatter(out.gain_grad[0])[None],
        table.T,
        fgain,
        proj,
    )


def per_device(
    hidden_in,
    lengths,
    labels,
    chosen,
    slab_main,
    slab_side,
    section_gains,
    rel_bias,
    final_gain,
    out_proj,
    doc_vectors,
):
    batch_size, query_len, width = hidden_in.shape
    rows = batch_size * query_len
    retrieved = chosen.shape[2]
    z = Sizes(
        lax.axis_size("section"),
        lax.axis_size("dp"),
        batch_size,
        query_len,
        retrieved,
        width,
        slab_main.shape[2],
        out_proj.shape[1],
        doc_vectors.shape[0],
    )
    buckets = jnp.asarray(np.tile(bucket_table(query_len).T, (1, batch_size)))
    out = relay(
        z,
        hidden_in.reshape(rows, width),
        lengths,
        labels,
        chosen.reshape(rows, retrieved),
        slab_main,
        slab_side,
        section_gains,
        rel_bias.T,
        buckets,
        final_gain,
        out_proj,
        doc_vectors,
    )
    if not z.summed:
        return (out.units, out.loss[0, :batch_size], out.dx) + sums_outside(z, out)
    names = ("units", "dx", "main_out", "side_out", "gain_out", "table_out", "fgain_out", "proj_out")
    units, dx, main, side, gain, table, fgain, proj, losses = deliver(
        [getattr(out, n) for n in names], out.loss, batch_size
    )
    return units, losses, dx, main, side, gain, table.T, fgain, proj


def solution(mesh):
    both = ("section", "dp")
    in_specs = (
        P(both, None, None),
        P(both),
        P(both),
        P(both, None, None),
        P("section", None, None),
        P("section", None, None),
        P("section", None),
        P(),
        P(),
        P(),
        P("dp", None),
    )
    out_specs = (
        P(both, None, None),
        P(both),
        P(both, None, None),
        P("section", "dp", None),
        P("section", "dp", None),
        P("section", "dp"),
        P(),
        P(),
        P(),
    )
    return jax.shard_map(
        per_device, mesh=mesh, in_specs=in_specs, out_specs=out_specs, check_vma=False
    )
```

```python
import functools
import math
import types

import jax
import jax.numpy as jnp
import numpy as np
from jax import lax
from jax.experimental import pallas as pl
from jax.experimental.pallas import tpu as pltpu
from jax.sharding import PartitionSpec as P

H = 12
DH = 64
DOC_LEN = 128
EPS_NORM = 1e-06
MASK_FILL = -1000000000.0
HIGHEST = lax.Precision.HIGHEST
MESH = pl.DeviceIdType.MESH
F32 = jnp.float32
BF16 = jnp.bfloat16
VMEM = pltpu.VMEM
GELU_C = math.sqrt(2.0 / math.pi)
GELU_A = 0.044715
FF_STEP = 768
LEND_STEP = 128
LEND_CUTS = 2


def bucket_table(query_len):
    places = np.arange(query_len)
    relative = places[None, :] - places[:, None]
    distance = np.abs(relative)
    signed_part = np.where(relative > 0, 16, 0)
    far_bucket = 8 + np.floor(np.log(np.maximum(distance, 1) / 8.0) / np.log(16.0) * 8.0).astype(
        np.int64
    )
    far_bucket = np.minimum(far_bucket, 15)
    return (signed_part + np.where(distance < 8, distance, far_bucket)).astype(np.int32)


def nn(a, b):
    return jnp.dot(a, b, preferred_element_type=F32)


def nt(a, b):
    return lax.dot_general(a, b, (((1,), (1,)), ((), ())), preferred_element_type=F32)


def tn(a, b):
    return lax.dot_general(a, b, (((0,), (0,)), ((), ())), preferred_element_type=F32)


def rms_inverse(values):
    return lax.rsqrt(jnp.mean(values * values, axis=-1, keepdims=True) + EPS_NORM)


def rms_back(scaled, inverse, gain, grad):
    inner = grad * gain
    grad_values = inverse * (inner - scaled * jnp.mean(inner * scaled, axis=-1, keepdims=True))
    return grad_values, jnp.sum(grad * scaled, axis=0, keepdims=True)


def sum_order(line):
    orders = []
    for place in range(line):
        others = [j for j in range(line) if j != place]
        others.sort(key=lambda j: (-abs(j - place), min(j, line - 1 - j)))
        orders.append(others + [place])
    return orders


class Sizes:
    def __init__(self, sections, dp_size, batch_size, query_len, retrieved, width, ff, vector, doc_rows):
        self.sections = sections
        self.dp_size = dp_size
        self.batch_size = batch_size
        self.query_len = query_len
        self.retrieved = retrieved
        self.width = width
        self.ff = ff
        self.vector = vector
        self.doc_rows = doc_rows
        self.rows = batch_size * query_len
        self.total = sections * self.rows
        self.parts = ff // 4 // LEND_STEP
        self.share = width // dp_size
        self.summed = self.share % 16 == 0 and dp_size % 2 == 0
        self.line = dp_size // 2
        self.step_columns = H * DH
        self.per_slab = ff // self.step_columns
        self.units = 2 * self.per_slab
        self.steps = self.line * self.units
        self.chunk = self.share if self.summed else H * 8
        self.slab_chunks = ff // self.chunk
        self.windows = self.total // self.chunk
        self.handed = self.summed and sections == 4 and 3 * self.line - 2 <= 3 * self.windows
        arriving = self.steps + 2 * (self.line - 1) * self.units
        self.pool = max(3 * self.slab_chunks, arriving if self.summed else 0)


def relay_kernel(z, names, *refs):
    r = types.SimpleNamespace(**dict(zip(names, refs, strict=True)))
    s = lax.axis_index("section")
    d = lax.axis_index("dp")
    sections, dp_size, rows, width, ff = z.sections, z.dp_size, z.rows, z.width, z.ff
    batch_size, query_len, parts = z.batch_size, z.query_len, z.parts
    head_width = H * DH
    last = sections - 1
    after = lax.rem(s + 1, sections)
    before = lax.rem(s + sections - 1, sections)
    group = d - lax.rem(d, 4)
    place = lax.rem(d, 4)
    core_peer = group + place + 1 - 2 * lax.rem(place, 2)
    far_place = lax.rem(place + 2, 4)
    far_peer = group + far_place
    is_attention = lax.rem(s, 2) == 0
    is_ffn = jnp.logical_not(is_attention)

    def copy(src, dst, send_sem, recv_sem, section, dp):
        return pltpu.make_async_remote_copy(
            src_ref=src,
            dst_ref=dst,
            send_sem=send_sem,
            recv_sem=recv_sem,
            device_id=(section, dp),
            device_id_type=MESH,
        )

    def block(m):
        return pl.ds(pl.multiple_of(m * rows, rows), rows)

    def peers(body):
        def step(k, carry):
            body(lax.rem(d + k, dp_size))
            return carry

        lax.fori_loop(1, dp_size, step, 0)

    def other_sections(body):
        for k in range(1, sections):
            body(lax.rem(s + k, sections))

    def main_load():
        return pltpu.make_async_copy(r.main_hbm.at[0], r.main, r.load_sem.at[0])

    def side_load():
        return pltpu.make_async_copy(r.side_hbm.at[0], r.side, r.load_sem.at[1])

    small_loads = [
        pltpu.make_async_copy(getattr(r, name + "_hbm"), getattr(r, name), r.small_sem.at[k])
        for k, name in enumerate(("chosen", "bias", "buckets", "gain", "fgain", "proj"))
    ]
    for one in small_loads:
        one.start()

    def hid_load():
        return pltpu.make_async_copy(r.hid_hbm, r.xin.at[0], r.load_sem.at[2])

    def docs_load():
        return pltpu.make_async_copy(r.docs_hbm, r.table.at[table_rows(d), :], r.load_sem.at[2])

    def table_rows(owner):
        return pl.ds(pl.multiple_of(owner * z.doc_rows, z.doc_rows), z.doc_rows)

    @pl.when(s == 0)
    def _():
        hid_load().start()

    main_load().start()

    @pl.when(is_ffn)
    def _():
        side_load().start()

    @pl.when(s == last)
    def _():
        docs_load().start()

    barrier = pltpu.get_barrier_semaphore()
    other_sections(
        lambda to: pl.semaphore_signal(barrier, inc=1, device_id=(to, d), device_id_type=MESH)
    )
    peers(lambda to: pl.semaphore_signal(barrier, inc=1, device_id=(s, to), device_id_type=MESH))

    lane = lax.broadcasted_iota(jnp.int32, (1, rows), 1)
    token_query = lane // query_len
    token_slot = lax.rem(lane, query_len)
    length = jnp.zeros((1, rows), jnp.int32)
    for q in range(batch_size):
        length = jnp.where(token_query == q, r.lengths[q], length)
    live = jnp.where(token_slot < length, 1.0, 0.0)
    r.meta[...] = jnp.zeros_like(r.meta)
    r.meta[0:1, :] = live
    r.meta[1:2, :] = live / length.astype(F32)
    r.idx[:8, :] = jnp.zeros((8, rows), jnp.int32)
    for c in range(batch_size):
        r.idx[c : c + 1, :] = jnp.full((1, rows), r.labels[c], jnp.int32)
    for one in small_loads:
        one.wait()
    r.idx[8:, :] = r.chosen[...].T

    pl.semaphore_wait(barrier, sections - 1 + dp_size - 1)

    def lend_columns(quarter, part):
        start = quarter * (ff // 4) + part * LEND_STEP
        return pl.ds(pl.multiple_of(start, LEND_STEP), LEND_STEP)

    def lend_copy(part, half):
        columns = lend_columns(place, part)
        depth = slice(half * (width // LEND_CUTS), (half + 1) * (width // LEND_CUTS))
        return copy(
            r.side_hbm.at[0, depth, columns],
            r.lent.at[depth, columns],
            r.lend_ss.at[0, part, half],
            r.lend_rs.at[0, part, half],
            after,
            d,
        )

    def lend_forward(kind, quarter, part, half, peer):
        columns = lend_columns(quarter, part)
        depth = slice(half * (width // LEND_CUTS), (half + 1) * (width // LEND_CUTS))
        return copy(
            r.lent.at[depth, columns],
            r.lent.at[depth, columns],
            r.lend_ss.at[kind, part, half],
            r.lend_rs.at[kind, part, half],
            s,
            peer,
        )

    pieces = [(part, half) for part in range(parts) for half in range(LEND_CUTS)]

    def state_copy(m):
        return copy(r.xout.at[m], r.xin.at[m], r.state_ss.at[m], r.state_rs.at[m], after, d)

    def grad_copy(m):
        return copy(r.gout.at[m], r.gin.at[m], r.grad_ss.at[m], r.grad_rs.at[m], before, d)

    def meta_copy(to, slot):
        return copy(r.meta, r.meta_rx.at[slot], r.meta_ss.at[to], r.meta_rs.at[slot], to, d)

    def idx_copy(slot):
        return copy(r.idx, r.idx_rx.at[slot], r.idx_ss, r.idx_rs.at[slot], last, d)

    def hid_copy(slot):
        return copy(r.hid_hbm, r.xin.at[slot], r.state_ss.at[sections], r.state_rs.at[slot], 0, d)

    def unit_copy(m, to):
        return copy(r.unit_tx.at[m], r.unit_rx, r.unit_ss.at[m], r.unit_rs, to, d)

    def loss_copy(m, to):
        return copy(r.loss_tx.at[m], r.loss_rx, r.loss_ss.at[m], r.loss_rs, to, d)

    def fin_copy(m, to):
        return copy(r.gout.at[m], r.fin_rx, r.fin_ss.at[m], r.fin_rs, to, d)

    def table_copy(to, owner):
        return copy(
            r.docs_hbm, r.table.at[table_rows(owner), :], r.tab_ss.at[to], r.tab_rs.at[owner], s, to
        )

    def table_near(owner):
        return copy(
            r.docs_hbm,
            r.table.at[table_rows(owner), :],
            r.tab_ss.at[core_peer],
            r.tab_rs.at[owner],
            s,
            core_peer,
        )

    def table_forward(owner):
        rows = table_rows(owner)
        return copy(
            r.table.at[rows, :], r.table.at[rows, :], r.tabf_ss.at[owner], r.tab_rs.at[owner], s, core_peer
        )

    def far_owners(body):
        def step(k, carry):
            body(lax.rem(d + 2 * k, dp_size))
            return carry

        lax.fori_loop(1, dp_size // 2, step, 0)

    @pl.when(s != 0)
    def _():
        hid_copy(s).start()

    @pl.when(s == last)
    def _():
        table_near(d).start()
        far_owners(lambda to: table_copy(to, d).start())

    @pl.when(is_attention)
    def _():
        for part in range(parts):
            for half in range(LEND_CUTS):
                lend_copy(part, half).start()

    other_sections(lambda to: meta_copy(to, s).start())
    r.meta_rx[s] = r.meta[...]

    @pl.when(s != last)
    def _():
        idx_copy(s).start()

    r.gain_grad[...] = jnp.zeros_like(r.gain_grad)
    r.fgain_grad[...] = jnp.zeros_like(r.fgain_grad)

    if not z.summed:

        @pl.when(is_ffn)
        def _():
            r.tab_grad[...] = jnp.zeros_like(r.tab_grad)


    if not z.summed:

        @pl.when(s != last)
        def _():
            r.dproj[...] = jnp.zeros_like(r.dproj)

    r.dbias[...] = jnp.zeros_like(r.dbias)
    gain = r.gain[...]
    fgain = r.fgain[...].reshape(1, width)

    def wait_meta(m):
        @pl.when(m != s)
        def _():
            meta_copy(0, m).wait_recv()

    def load_state(m):
        states = r.xin[m].astype(F32)
        inverse = rms_inverse(states)
        return states, inverse, states * inverse

    low_half = lax.broadcasted_iota(jnp.int32, (1, 128), 1) < DH

    low_lanes = jnp.where(low_half, 1.0, 0.0).astype(BF16)
    high_lanes = jnp.where(low_half, 0.0, 1.0).astype(BF16)

    def split_heads(value):
        return jnp.concatenate([value * low_lanes, value * high_lanes], axis=0)

    def join_heads(value):
        return jnp.where(low_half, value[:rows], value[rows:]).astype(BF16)

    def attention_setup():
        buckets = r.buckets[...]
        for h in range(H):
            total = jnp.zeros(buckets.shape, F32)
            for b in range(32):
                total = jnp.where(buckets == b, r.bias[h : h + 1, b : b + 1], total)
            r.bias_sc[h // 2, h % 2] = total

    def attention_table():
        buckets = r.buckets[...]
        ones = jnp.ones((16, 128), BF16)
        head_row = lax.broadcasted_iota(jnp.int32, (16, 32), 0)

        def head(h, carry):
            grad = r.dbias[h // 2, lax.rem(h, 2)]
            rest = jnp.concatenate(
                [
                    jnp.sum(jnp.where(buckets == b, grad, 0.0), axis=0, keepdims=True)
                    for b in range(32)
                ],
                axis=0,
            )
            total = jnp.zeros((16, 32), F32)
            for _ in range(3):
                part = rest.astype(BF16)
                total = total + nt(ones, part)
                rest = rest - part.astype(F32)
            return carry + jnp.where(head_row == h, total, 0.0)

        r.tab_grad[...] = lax.fori_loop(0, H, head, jnp.zeros((16, 32), F32))

    def turn(source, slab, start):
        size = FF_STEP // z.chunk
        first = slab * z.slab_chunks + start // z.chunk
        r.pool[first : first + size] = source[:, start : start + FF_STEP].T.reshape(
            size, z.chunk, width
        )

    def turned(slab, start, stop):
        first = slab * z.slab_chunks
        return r.pool[first + start // z.chunk : first + stop // z.chunk].reshape(
            stop - start, width
        )

    def attention_forward(m):
        states, inverse, scaled = load_state(m)
        normed = scaled * gain
        r.left[0, :, block(m)] = normed.T.astype(BF16)
        normed_low = normed.astype(BF16)
        for start in range(0, 3 * head_width, head_width):
            r.qkv[block(m), start : start + head_width] = nn(
                normed_low, r.main[:, start : start + head_width]
            ).astype(BF16)
        live = jnp.broadcast_to(r.meta_rx[m, 0:1, :], (rows, rows)).T > 0.5
        row_query = lax.broadcasted_iota(jnp.int32, (rows, rows), 0) // query_len
        column_query = lax.broadcasted_iota(jnp.int32, (rows, rows), 1) // query_len
        keep = jnp.logical_and(row_query == column_query, live)
        for pair in range(H // 2):
            at = pair * 128
            query = r.qkv[block(m), at : at + 128]
            keys = r.qkv[block(m), head_width + at : head_width + at + 128]
            values = r.qkv[block(m), 2 * head_width + at : 2 * head_width + at + 128]
            raw = nt(split_heads(keys), query)
            biased = raw.reshape(2, batch_size, query_len, rows) + r.bias_sc[pair][:, None]
            scores = jnp.where(keep[None], biased.reshape(2, rows, rows), MASK_FILL)
            top = jnp.max(scores, axis=1, keepdims=True)
            grown = jnp.exp(scores - top)
            soft = grown * (1.0 / jnp.sum(grown, axis=1, keepdims=True))
            soft = soft.reshape(2 * rows, rows)
            r.probs[m, pair] = soft
            r.right[0, block(m), 3 * head_width + at : 3 * head_width + at + 128] = tn(
                soft.astype(BF16), split_heads(values)
            ).astype(BF16)
        context = r.right[0, block(m), 3 * head_width :]
        return states + nn(context, turned(0, 3 * head_width, ff))

    def attention_backward(m):
        states, inverse, scaled = load_state(m)
        grad_low = r.gin[m]
        grad = grad_low.astype(F32)
        r.left[1, :, block(m)] = grad.T.astype(BF16)
        grad_context = nn(grad_low, r.main[:, 3 * head_width :]).astype(BF16)
        for pair in range(H // 2):
            at = pair * 128
            query = r.qkv[block(m), at : at + 128]
            keys = r.qkv[block(m), head_width + at : head_width + at + 128]
            values = r.qkv[block(m), 2 * head_width + at : 2 * head_width + at + 128]
            grad_pair = grad_context[:, at : at + 128]
            soft = r.probs[m, pair]
            grad_soft = nt(split_heads(values), grad_pair)
            moved = (soft * grad_soft).reshape(2, rows, rows)
            grad_scores = moved - soft.reshape(2, rows, rows) * jnp.sum(
                moved, axis=1, keepdims=True
            )
            r.dbias[pair] += jnp.sum(
                grad_scores.reshape(2, batch_size, query_len, rows), axis=1
            )
            scores_low = grad_scores.reshape(2 * rows, rows).astype(BF16)
            found = (
                tn(scores_low, split_heads(keys)).astype(BF16),
                join_heads(nn(scores_low, query)),
                join_heads(nn(soft.astype(BF16), grad_pair)),
            )
            for third in range(3):
                start = third * head_width + at
                r.right[0, block(m), start : start + 128] = found[third]
        grad_normed = nn(r.right[0, block(m), : 3 * head_width], turned(0, 0, 3 * head_width))
        grad_states, grad_gain = rms_back(scaled, inverse, gain, grad_normed)
        r.gain_grad[...] += grad_gain
        return grad + grad_states

    def ffn_forward(m):
        states, inverse, scaled = load_state(m)
        normed = scaled * gain
        r.left[0, :, block(m)] = normed.T.astype(BF16)
        normed_low = normed.astype(BF16)
        outputs = states
        for start in range(0, ff, FF_STEP):
            columns = slice(start, start + FF_STEP)
            gate = nn(normed_low, r.main[:, columns])
            up = nn(normed_low, r.lent[:, columns])
            square = gate * gate
            bent = jnp.tanh(GELU_C * gate * (1.0 + GELU_A * square))
            half = 0.5 * (1.0 + bent)
            smooth = gate * half
            slope = half + 0.5 * gate * (1.0 - bent * bent) * (
                GELU_C * (1.0 + 3.0 * GELU_A * square)
            )
            hidden = (smooth * up).astype(BF16)
            r.right[1, block(m), columns] = hidden
            r.right[0, block(m), columns] = (slope * up).astype(BF16)
            r.right[2, block(m), columns] = smooth.astype(BF16)
            outputs = outputs + nn(hidden, turned(1, start, start + FF_STEP))
        return outputs

    def ffn_backward(m, grad):
        states, inverse, scaled = load_state(m)
        grad_low = grad.astype(BF16)
        r.left[1, :, block(m)] = grad.T.astype(BF16)
        grad_normed = jnp.zeros((rows, width), F32)
        for start in range(0, ff, FF_STEP):
            columns = slice(start, start + FF_STEP)
            grad_hidden = nn(grad_low, r.side[:, columns])
            grad_gate = (grad_hidden * r.right[0, block(m), columns].astype(F32)).astype(BF16)
            grad_up = (grad_hidden * r.right[2, block(m), columns].astype(F32)).astype(BF16)
            r.right[0, block(m), columns] = grad_gate
            r.right[2, block(m), columns] = grad_up
            grad_normed = (
                grad_normed
                + nn(grad_gate, turned(0, start, start + FF_STEP))
                + nn(grad_up, turned(2, start, start + FF_STEP))
            )
        grad_states, grad_gain = rms_back(scaled, inverse, gain, grad_normed)
        r.gain_grad[...] += grad_gain
        return grad + grad_states

    def count_hits(m):
        for c in range(batch_size):
            base = r.idx_rx[m, c : c + 1, :] * DOC_LEN
            numbers = lax.broadcasted_iota(jnp.int32, (DOC_LEN, rows), 0) + base
            total = jnp.zeros((DOC_LEN, rows), F32)
            for k in range(z.retrieved):
                total = total + jnp.where(r.idx_rx[m, 8 + k : 9 + k, :] == numbers, 1.0, 0.0)
            r.counts[m, c * DOC_LEN : (c + 1) * DOC_LEN, :] = total.astype(BF16)

    def pick_docs(m):
        for c in range(batch_size):
            label = r.idx_rx[m, c : c + 1, :]

            def pick(t, picked):
                here = r.table[pl.ds(pl.multiple_of(t * DOC_LEN, DOC_LEN), DOC_LEN), :].astype(F32)
                return jnp.where(label == t, here, picked)

            picked = lax.fori_loop(
                0, dp_size * z.doc_rows // DOC_LEN, pick, jnp.zeros((DOC_LEN, z.vector), F32)
            )
            r.own_docs[m, c * DOC_LEN : (c + 1) * DOC_LEN, :] = picked.astype(BF16)

    def loss_and_grad(m, unit):
        docs = r.own_docs[m]
        sims = nt(docs, unit)
        count = r.counts[m].astype(F32)
        imputed = jnp.sum(count * sims, axis=0, keepdims=True) / z.retrieved
        grown = count * jnp.exp(sims)
        imputed_mass = jnp.exp(imputed)
        mass = imputed_mass + jnp.concatenate(
            [
                jnp.sum(grown[c * DOC_LEN : (c + 1) * DOC_LEN], axis=0, keepdims=True)
                for c in range(batch_size)
            ],
            axis=0,
        )
        weighted = jnp.log(mass) * r.meta_rx[m, 1:2, :]
        candidate = lax.broadcasted_iota(jnp.int32, (batch_size, 1), 0)
        losses = jnp.zeros((1, rows), F32)
        grad_tokens = jnp.zeros((batch_size, rows), F32)
        for q in range(batch_size):
            own = token_query == q
            score = jnp.sum(jnp.where(own, weighted, 0.0), axis=1, keepdims=True)
            top = jnp.max(score, axis=0, keepdims=True)
            risen = jnp.exp(score - top)
            total = jnp.sum(risen, axis=0, keepdims=True)
            chosen_one = (candidate == q).astype(F32)
            loss = top + jnp.log(total) - jnp.sum(score * chosen_one, axis=0, keepdims=True)
            losses = losses + jnp.where(lane == q, loss, 0.0)
            grad_tokens = grad_tokens + jnp.where(own, risen / total - chosen_one, 0.0)
        grad_mass = grad_tokens * r.meta_rx[m, 1:2, :] / mass
        shared = jnp.sum(grad_mass, axis=0, keepdims=True) * imputed_mass / z.retrieved
        grad_sims = count * shared + jnp.concatenate(
            [
                grown[c * DOC_LEN : (c + 1) * DOC_LEN] * grad_mass[c : c + 1]
                for c in range(batch_size)
            ],
            axis=0,
        )
        high = grad_sims.astype(BF16)
        rest = (grad_sims - high.astype(F32)).astype(BF16)
        return losses, tn(high, docs) + tn(rest, docs)

    def finish_states(m, states):
        inverse = rms_inverse(states)
        scaled = states * inverse
        normed = (scaled * fgain).astype(BF16)
        projected = nn(normed, r.proj[...])
        size = lax.rsqrt(jnp.sum(projected * projected, axis=-1, keepdims=True) + EPS_NORM)
        exact = projected * size
        unit = exact.astype(BF16)
        losses, grad_unit = loss_and_grad(m, unit)
        r.unit_tx[m] = unit
        r.loss_tx[m] = jnp.broadcast_to(losses, (8, rows))

        @pl.when(m != last)
        def _():
            unit_copy(m, m).start()
            loss_copy(m, m).start()

        grad_projected = (
            size * (grad_unit - exact * jnp.sum(grad_unit * exact, axis=-1, keepdims=True))
        ).astype(BF16)
        r.xout[m] = normed
        r.final_right[block(m), :] = grad_projected
        grad_normed = nt(grad_projected, r.proj[...])
        grad_states, grad_gain = rms_back(scaled, inverse, fgain, grad_normed)
        r.fgain_grad[...] += grad_gain
        return grad_states

    def loop(body):
        def step(m, carry):
            body(m)
            return carry

        lax.fori_loop(0, sections, step, 0)

    def wait_state(m):
        @pl.when(jnp.logical_or(s != 0, m != 0))
        def _():
            state_copy(m).wait_recv()

    @pl.when(is_attention)
    def _():
        attention_setup()
        main_load().wait()
        for start in range(0, ff, FF_STEP):
            turn(r.main, 0, start)

        def forward(m):
            wait_meta(m)
            wait_state(m)

            @pl.when(jnp.logical_and(s == 0, m == 0))
            def _():
                hid_load().wait()

            r.xout[m] = attention_forward(m).astype(BF16)
            state_copy(m).start()

        loop(forward)

        def backward(m):
            grad_copy(m).wait_recv()
            r.gout[m] = attention_backward(m).astype(BF16)

            @pl.when(s != 0)
            def _():
                grad_copy(m).start()

            @pl.when(jnp.logical_and(s == 0, m != 0))
            def _():
                fin_copy(m, m).start()

        loop(backward)
        if not z.summed:
            attention_table()

    @pl.when(is_ffn)
    def _():
        turns = [(r.main, 0, start) for start in range(0, ff, FF_STEP)]
        turns += [(r.side, 1, start) for start in range(0, ff, FF_STEP)]
        main_load().wait()
        side_load().wait()
        def far_arrived(piece):
            lend_forward(2, far_place, *piece, far_peer).wait_recv()
            lend_forward(3, far_place, *piece, core_peer).start()

        lag = LEND_CUTS
        for k, piece in enumerate(pieces):
            lend_copy(*piece).wait_recv()
            lend_forward(2, place, *piece, far_peer).start()
            lend_forward(1, place, *piece, core_peer).start()
            if k >= lag:
                far_arrived(pieces[k - lag])
            for one in turns[k :: len(pieces)]:
                turn(*one)

        @pl.when(s == last)
        def _():
            r.idx_rx[last] = r.idx[...]

            def pass_on(owner):
                table_copy(owner, owner).wait_recv()
                table_forward(owner).start()

            far_owners(pass_on)

            def prepare(m):
                @pl.when(m != last)
                def _():
                    idx_copy(m).wait_recv()

                count_hits(m)

            loop(prepare)

        for piece in pieces[-lag:]:
            far_arrived(piece)
        for piece in pieces:
            lend_forward(1, place, *piece, core_peer).wait_recv()
            lend_forward(3, far_place, *piece, core_peer).wait_recv()

        def turn_lent():
            for start in range(0, ff, FF_STEP):
                turn(r.lent, 2, start)

        def lend_sent():
            for piece in pieces:
                lend_forward(1, place, *piece, core_peer).wait_send()
                lend_forward(2, place, *piece, far_peer).wait_send()
                lend_forward(3, far_place, *piece, core_peer).wait_send()

        @pl.when(s == last)
        def _():
            docs_load().wait()
            table_near(core_peer).wait_recv()

            def take(owner):
                table_forward(owner + core_peer - d).wait_recv()

            far_owners(take)
            loop(pick_docs)
            turn_lent()
            loop(wait_meta)
            lend_sent()

            def both(m):
                wait_state(m)
                states = ffn_forward(m)
                grad = finish_states(m, states)
                r.gout[m] = ffn_backward(m, grad).astype(BF16)
                grad_copy(m).start()

            loop(both)
            r.dproj[...] = tn(r.xout[...].reshape(z.total, width), r.final_right[...]).astype(
                r.dproj.dtype
            )

        @pl.when(s != last)
        def _():
            def forward(m):
                wait_state(m)
                r.xout[m] = ffn_forward(m).astype(BF16)
                state_copy(m).start()

            loop(forward)
            turn_lent()
            loop(wait_meta)
            lend_sent()

            def backward(m):
                grad_copy(m).wait_recv()
                r.gout[m] = ffn_backward(m, r.gin[m].astype(F32)).astype(BF16)
                grad_copy(m).start()

            loop(backward)

    def put(k, name):
        return pltpu.make_async_copy(getattr(r, name + "_v"), getattr(r, name), r.put_sem.at[k])

    homes = [put(k, name) for k, name in enumerate(("units", "loss", "dx"))]

    def come_home():
        @pl.when(s != 0)
        def _():
            fin_copy(0, s).wait_recv()
            r.dx_v[...] = r.fin_rx[...].astype(F32).reshape(batch_size, query_len, width)

        @pl.when(s == 0)
        def _():
            r.dx_v[...] = r.gout[0].astype(F32).reshape(batch_size, query_len, width)

        def write_own(unit, losses):
            r.units_v[...] = unit.reshape(batch_size, query_len, z.vector)
            r.loss_v[...] = losses

        @pl.when(s != last)
        def _():
            unit_copy(0, s).wait_recv()
            loss_copy(0, s).wait_recv()
            write_own(r.unit_rx[...], r.loss_rx[...])

        @pl.when(s == last)
        def _():
            write_own(r.unit_tx[last], r.loss_tx[last])

        for one in homes:
            one.start()

    if z.summed:
        sum_gradients(
            z, r, s, d, copy, peers, other_sections, is_attention, attention_table, come_home
        )
    else:
        come_home()

    for one in homes:
        one.wait()
    other_sections(lambda to: meta_copy(to, s).wait_send())

    @pl.when(s != 0)
    def _():
        hid_copy(s).wait_send()
        loop(lambda m: grad_copy(m).wait_send())

    @pl.when(s == 0)
    def _():
        for m in range(1, sections):
            fin_copy(m, m).wait_send()

    @pl.when(is_attention)
    def _():
        for piece in pieces:
            lend_copy(*piece).wait_send()

    @pl.when(s != last)
    def _():
        idx_copy(s).wait_send()
        loop(lambda m: state_copy(m).wait_send())

    @pl.when(s == last)
    def _():
        table_near(d).wait_send()
        far_owners(lambda to: table_copy(to, d).wait_send())
        far_owners(lambda owner: table_forward(owner).wait_send())
        for m in range(sections - 1):
            unit_copy(m, m).wait_send()
            loss_copy(m, m).wait_send()


def sum_gradients(
    z, r, s, d, copy, peers, other_sections, is_attention, attention_table, come_home
):
    sections, dp_size, width, ff, share, line = z.sections, z.dp_size, z.width, z.ff, z.share, z.line
    step_columns, per_slab, units, steps = z.step_columns, z.per_slab, z.units, z.steps
    place = d // 2
    core = lax.rem(d, 2)
    peer = d + 1 - 2 * core
    last = sections - 1
    before = lax.rem(s + sections - 1, sections)
    is_ffn = jnp.logical_not(is_attention)
    orders = sum_order(line)

    def piece_rows(owner):
        return pl.ds(pl.multiple_of(owner * share, share), share)

    def gain_copy(to, slot):
        return copy(r.gain_grad, r.gain_rx.at[slot], r.gain_ss.at[to], r.gain_rs.at[slot], s, to)

    def table_copy(to, slot):
        return copy(r.tab_grad, r.tab_rx.at[slot], r.tabs_ss.at[to], r.tabs_rs.at[slot], s, to)

    def fgain_copy(to, slot):
        return copy(r.fgain_grad, r.fgain_rx.at[slot], r.fg_ss.at[to], r.fg_rs.at[slot], s, to)

    def proj_copy(to, slot):
        return copy(
            r.dproj.at[piece_rows(to), :],
            r.proj_rx.at[slot],
            r.proj_ss.at[to],
            r.proj_rs.at[slot],
            s,
            to,
        )

    def spread_copy(to, owner):
        rows = piece_rows(owner)
        return copy(
            r.proj_sum.at[rows, :],
            r.proj_sum.at[rows, :],
            r.spread_ss.at[to],
            r.spread_rs.at[owner],
            s,
            to,
        )

    def table_across(to, slot):
        return copy(r.tab_tx, r.tab_cx.at[slot], r.across_ss.at[0, to], r.across_rs.at[slot], to, d)

    def fgain_across(to):
        return copy(
            r.fgain_tx, r.fgain_sum, r.across_ss.at[1, to], r.across_rs.at[sections], to, d
        )

    def proj_across(to):
        return copy(
            r.proj_sum, r.proj_sum, r.across_ss.at[2, to], r.across_rs.at[sections + 1], to, d
        )

    small_puts = [
        pltpu.make_async_copy(source, target, r.put_sem.at[3 + k])
        for k, (source, target) in enumerate(
            (
                (r.gain_out_v, r.gain_out),
                (r.table_out_v, r.table_out),
                (r.fgain_out_v, r.fgain_out),
                (r.proj_v, r.proj_out),
            )
        )
    ]

    def slab_put(slab, column, columns):
        source, target = ((r.main_v, r.main_out), (r.side_v, r.side_out))[slab]
        return pltpu.make_async_copy(
            source.at[:, columns], target.at[0, :, columns], r.slab_sem.at[slab, column]
        )

    def total_of(ref, count):
        total = ref[0].astype(F32)
        for k in range(1, count):
            total = total + ref[k].astype(F32)
        return total

    def to_others(body):
        for to in range(sections):

            @pl.when(s != to)
            def _():
                body(to)

    def small_first():
        peers(lambda to: gain_copy(to, d).start())
        r.gain_rx[d] = r.gain_grad[...]

        @pl.when(is_attention)
        def _():
            attention_table()
            peers(lambda to: table_copy(to, d).start())
            r.tab_rx[d] = r.tab_grad[...]

    def proj_first():
        peers(lambda to: proj_copy(to, d).start())
        peers(lambda to: fgain_copy(to, d).start())
        r.proj_rx[d] = r.dproj[piece_rows(d), :]
        r.fgain_rx[d] = r.fgain_grad[...]

    def proj_second():
        peers(lambda owner: proj_copy(owner, owner).wait_recv())
        peers(lambda owner: fgain_copy(owner, owner).wait_recv())
        r.proj_sum[piece_rows(d), :] = total_of(r.proj_rx, dp_size).astype(BF16)
        r.fgain_tx[...] = total_of(r.fgain_rx, dp_size)
        r.fgain_sum[...] = r.fgain_tx[...]
        peers(lambda to: spread_copy(to, d).start())
        to_others(lambda to: fgain_across(to).start())

    def proj_third():
        peers(lambda owner: spread_copy(owner, owner).wait_recv())
        to_others(lambda to: proj_across(to).start())

    def small_second():
        peers(lambda owner: gain_copy(owner, owner).wait_recv())
        gain_sum = jnp.broadcast_to(total_of(r.gain_rx, dp_size), (8, width))
        r.gain_out_v[...] = pltpu.roll(gain_sum, width - d * share, 1)[0:1, :share]

        @pl.when(is_attention)
        def _():
            peers(lambda owner: table_copy(owner, owner).wait_recv())
            r.tab_tx[...] = total_of(r.tab_rx, dp_size)
            r.tab_cx[s // 2] = r.tab_tx[...]
            to_others(lambda to: table_across(to, s // 2).start())

    def small_last():
        for source in range(0, sections, 2):

            @pl.when(s != source)
            def _():
                table_across(source, source // 2).wait_recv()

        r.table_out_v[...] = total_of(r.tab_cx, (sections + 1) // 2)[:H]

        @pl.when(s != last)
        def _():
            fgain_across(last).wait_recv()
            proj_across(last).wait_recv()

        r.fgain_out_v[...] = r.fgain_sum[...].reshape(width)
        r.proj_v[...] = r.proj_sum[...].astype(F32)
        for one in small_puts:
            one.start()
        peers(lambda to: gain_copy(to, d).wait_send())

        @pl.when(is_attention)
        def _():
            peers(lambda to: table_copy(to, d).wait_send())
            to_others(lambda to: table_across(to, s // 2).wait_send())

        @pl.when(s == last)
        def _():
            peers(lambda to: proj_copy(to, d).wait_send())
            peers(lambda to: fgain_copy(to, d).wait_send())
            peers(lambda to: spread_copy(to, d).wait_send())
            to_others(lambda to: fgain_across(to).wait_send())
            to_others(lambda to: proj_across(to).wait_send())

    def target(i):
        found = jnp.int32(0)
        for k in range(line):
            found = jnp.where(place == k, orders[k][i], found)
        return found

    targets = [target(i) for i in range(line)]

    def target_of(i):
        j = targets[0]
        for k in range(1, line):
            j = jnp.where(i == k, targets[k], j)
        return j

    def parts_of(t):
        i, u = t // units, lax.rem(t, units)
        j = target_of(i)
        slab, column = 1 - lax.rem(u, 2), u // 2
        columns = pl.ds(pl.multiple_of(column * step_columns, step_columns), step_columns)
        return j, u, slab, column, columns

    def core_copy(t):
        return copy(
            r.core_tx.at[lax.rem(t, 4)], r.pool.at[t], r.core_ss.at[t], r.core_rs.at[t], s, peer
        )

    def up_core_copy(k):
        return copy(
            r.up_core_tx.at[lax.rem(k, 4)], r.up_rx.at[k], r.up_core_ss.at[k], r.up_rs.at[k], s, peer
        )

    def up_copy(k):
        return copy(
            r.up_tx.at[lax.rem(k, 4)], r.up_rx.at[k], r.up_ss.at[k], r.up_rs.at[k], before, d
        )

    hand_column = per_slab - 1
    hand_columns = slice(hand_column * step_columns, ff)

    def window(n):
        row = pl.ds(pl.multiple_of(lax.rem(n, z.windows) * share, share), share)
        column = pl.ds(pl.multiple_of(n // z.windows * step_columns, step_columns), step_columns)
        return r.qkv.at[row, column]

    def hand_copy(k):
        i = k // per_slab
        return copy(r.up_tx.at[lax.rem(k, 4)], window(i), r.up_ss.at[k], r.hand_rs.at[i], last, d)

    def hand_line(i, way, j, to):
        slot = way * (line - 1) + j - 1 + way
        return copy(
            line_view(steps - units + i),
            window(line + slot),
            r.line_ss.at[steps - units + i],
            r.hand_rs.at[line + slot],
            s,
            to * 2 + core,
        )

    def hand_home():
        return copy(
            r.up_mine.at[0], r.side_v.at[:, hand_columns], r.home_ss, r.home_rs, 0, d
        )

    def extra(i):
        j = target_of(i)
        total = r.up_mine.at[0]
        hand_copy(i * per_slab).wait_recv()
        total[...] = window(i)[...].astype(F32)
        way = jnp.where(j < place, 1, 0)

        @pl.when(jnp.logical_and(place > 0, j >= place))
        def _():
            hand_line(i, 0, j, place).wait_recv()
            total[...] += window(line + j - 1)[...].astype(F32)

        @pl.when(jnp.logical_and(place < line - 1, j <= place))
        def _():
            hand_line(i, 1, j, place).wait_recv()
            total[...] += window(line + line - 1 + j)[...].astype(F32)

        @pl.when(j == place)
        def _():
            hand_home().start()

        @pl.when(j != place)
        def _():
            line_view(steps - units + i)[...] = total[...].astype(BF16)
            hand_line(i, way, j, place + 1 - 2 * way).start()

    def line_view(t):
        row = pl.ds(pl.multiple_of(lax.rem(t, dp_size) * share, share), share)
        column = pl.ds(pl.multiple_of(t // dp_size * step_columns, step_columns), step_columns)
        return r.lent.at[row, column]

    def line_slot(way, j, u):
        return steps + (way * (line - 1) + j - 1 + way) * units + u

    def line_copy(t, way, j, u, to):
        slot = j - 1 + way
        return copy(
            line_view(t),
            r.pool.at[line_slot(way, j, u)],
            r.line_ss.at[t],
            r.line_rs.at[way, slot, u],
            s,
            to * 2 + core,
        )

    def theirs(j):
        return pl.ds(pl.multiple_of((j * 2 + 1 - core) * share, share), share)

    def ours(j):
        return pl.ds(pl.multiple_of((j * 2 + core) * share, share), share)

    def begin(t):
        j, u, slab, column, columns = parts_of(t)
        mixed = jnp.logical_and(is_attention, column == per_slab - 1)
        which = jnp.where(jnp.logical_or(slab == 1, mixed), 1, 0)

        @pl.when(jnp.logical_or(is_ffn, slab == 0))
        def _():
            right = r.right[slab, :, columns]

            @pl.when(t >= 4)
            def _():
                core_copy(t - 4).wait_send()

            r.core_tx[lax.rem(t, 4)] = nn(r.left[which, theirs(j), :], right).astype(BF16)
            core_copy(t).start()
            r.mine[lax.rem(t, 2)] = nn(r.left[which, ours(j), :], right)

    def up_parts(k):
        i, column = k // per_slab, lax.rem(k, per_slab)
        columns = pl.ds(pl.multiple_of(column * step_columns, step_columns), step_columns)
        return target_of(i), columns

    def begin_up(k):
        j, columns = up_parts(k)
        right = r.right[2, :, columns]

        @pl.when(k >= 4)
        def _():
            up_core_copy(k - 4).wait_send()

        r.up_core_tx[lax.rem(k, 4)] = nn(r.left[0, theirs(j), :], right).astype(BF16)
        up_core_copy(k).start()
        r.up_mine[lax.rem(k, 2)] = nn(r.left[0, ours(j), :], right)

    def finish_up(k):
        up_core_copy(k).wait_recv()

        @pl.when(k >= 4)
        def _():
            up_copy(k - 4).wait_send()

        r.up_tx[lax.rem(k, 4)] = (r.up_mine[lax.rem(k, 2)] + r.up_rx[k].astype(F32)).astype(BF16)
        if z.handed:
            handed = jnp.logical_and(s == 1, lax.rem(k, per_slab) == hand_column)

            @pl.when(handed)
            def _():
                hand_copy(k).start()

            @pl.when(jnp.logical_not(handed))
            def _():
                up_copy(k).start()
        else:
            up_copy(k).start()

    def gone(t):
        return jnp.logical_and(s == 0, lax.rem(t, units) == units - 2) if z.handed else False

    def finish(t):
        @pl.when(jnp.logical_not(gone(t)))
        def _():
            finish_here(t)

    def finish_here(t):
        j, u, slab, column, columns = parts_of(t)
        k = t // 2
        total = r.mine.at[lax.rem(t, 2)]

        @pl.when(jnp.logical_or(is_ffn, slab == 0))
        def _():
            core_copy(t).wait_recv()
            total[...] += r.pool[t].astype(F32)

        @pl.when(jnp.logical_and(is_attention, slab == 1))
        def _():
            up_copy(k).wait_recv()
            total[...] = r.up_rx[k].astype(F32)

        way = jnp.where(j < place, 1, 0)

        @pl.when(jnp.logical_and(place > 0, j >= place))
        def _():
            line_copy(t, 0, j, u, place).wait_recv()
            total[...] += r.pool[line_slot(0, j, u)].astype(F32)

        @pl.when(jnp.logical_and(place < line - 1, j <= place))
        def _():
            line_copy(t, 1, j, u, place).wait_recv()
            total[...] += r.pool[line_slot(1, j, u)].astype(F32)

        @pl.when(jnp.logical_and(j == place, slab == 0))
        def _():
            r.main_v[:, columns] = total[...]
            slab_put(0, column, columns).start()

        @pl.when(jnp.logical_and(j == place, slab == 1))
        def _():
            r.side_v[:, columns] = total[...]
            slab_put(1, column, columns).start()

        @pl.when(j != place)
        def _():
            line_view(t)[...] = total[...].astype(BF16)
            line_copy(t, way, j, u, place + 1 - 2 * way).start()

    pl.semaphore_signal(r.core_ready, inc=1, device_id=(s, peer), device_id_type=MESH)

    @pl.when(place > 0)
    def _():
        pl.semaphore_signal(r.line_ready, inc=1, device_id=(s, d - 2), device_id_type=MESH)

    @pl.when(place < line - 1)
    def _():
        pl.semaphore_signal(r.line_ready, inc=1, device_id=(s, d + 2), device_id_type=MESH)

    @pl.when(s == last)
    def _():
        proj_first()

    ups = steps // 2
    pl.semaphore_wait(r.core_ready, 1)
    begin(jnp.int32(0))

    @pl.when(is_ffn)
    def _():
        begin_up(jnp.int32(0))

    neighbours = jnp.where(place > 0, 1, 0) + jnp.where(place < line - 1, 1, 0)
    pl.semaphore_wait(r.line_ready, neighbours)

    def step(t, carry):
        @pl.when(t < steps)
        def _():
            begin(t)

        @pl.when(jnp.logical_and(is_ffn, t < ups))
        def _():
            begin_up(t)

        finish(t - 1)

        @pl.when(jnp.logical_and(is_ffn, t <= ups))
        def _():
            finish_up(t - 1)

        if z.handed:

            @pl.when(jnp.logical_and(s == last, jnp.logical_and(t >= 2 * units, t < 2 * units + line)))
            def _():
                extra(t - 2 * units)

        @pl.when(jnp.logical_and(s == last, t == 2))
        def _():
            proj_second()

        @pl.when(t == 4)
        def _():
            small_first()

        @pl.when(jnp.logical_and(s == last, t == 6))
        def _():
            proj_third()

        @pl.when(t == units + 4)
        def _():
            small_second()

        @pl.when(t == steps - units)
        def _():
            come_home()

        return carry

    lax.fori_loop(1, steps + 1, step, 0)
    small_last()
    if z.handed:

        @pl.when(s == 0)
        def _():
            hand_home().wait_recv()
            slab_put(1, hand_column, hand_columns).start()

        @pl.when(s == last)
        def _():
            hand_home().wait_send()
            for i in range(line - 1):
                hand_line(i, 0, 1, place).wait_send()

    for slab in range(2):
        for column in range(per_slab):
            slab_put(
                slab, column, slice(column * step_columns, (column + 1) * step_columns)
            ).wait()
    for one in small_puts:
        one.wait()

    def drain(t, carry):
        @pl.when(jnp.logical_not(gone(t)))
        def _():
            line_copy(t, 0, 1, 0, place).wait_send()

        return carry

    lax.fori_loop(0, steps - units, drain, 0)

    def drain_core(t, carry):
        slab = 1 - lax.rem(t, 2)

        @pl.when(jnp.logical_or(is_ffn, slab == 0))
        def _():
            core_copy(t).wait_send()

        return carry

    lax.fori_loop(steps - 4, steps, drain_core, 0)

    @pl.when(is_ffn)
    def _():
        for k in range(steps // 2 - 4, steps // 2):
            up_core_copy(k).wait_send()
            up_copy(k).wait_send()


def relay(z, hid, lengths, labels, chosen, main, side, gain, bias, buckets, fgain, proj, docs):
    dma = pltpu.SemaphoreType.DMA
    shape = jax.ShapeDtypeStruct
    sections, rows, width, ff, dp_size = z.sections, z.rows, z.width, z.ff, z.dp_size
    share, steps, units = z.share, z.steps, z.units
    piece = (share, z.step_columns)
    vmem = pl.BlockSpec(memory_space=VMEM)
    smem = pl.BlockSpec(memory_space=pltpu.SMEM)
    anywhere = pl.BlockSpec(memory_space=pl.ANY)
    inputs = dict(
        hid_hbm=(hid, anywhere),
        lengths=(lengths, smem),
        labels=(labels, smem),
        chosen_hbm=(chosen, anywhere),
        main_hbm=(main, anywhere),
        side_hbm=(side, anywhere),
        gain_hbm=(gain, anywhere),
        bias_hbm=(bias, anywhere),
        buckets_hbm=(buckets, anywhere),
        fgain_hbm=(fgain, anywhere),
        proj_hbm=(proj, anywhere),
        docs_hbm=(docs, anywhere),
    )
    outputs = dict(
        units=shape((z.batch_size, z.query_len, z.vector), BF16),
        loss=shape((8, rows), F32),
        dx=shape((z.batch_size, z.query_len, width), F32),
    )
    def like(value):
        return VMEM(value.shape, value.dtype)

    scratch = {name + "_v": like(value) for name, value in outputs.items()}
    scratch |= dict(
        chosen=like(chosen),
        bias=like(bias),
        buckets=like(buckets),
        gain=like(gain),
        fgain=like(fgain),
        proj=like(proj),
        main=VMEM((width, ff), BF16),
        side=VMEM((width, ff), BF16),
        lent=VMEM((width, ff), BF16),
        xin=VMEM((sections, rows, width), BF16),
        xout=VMEM((sections, rows, width), BF16),
        gin=VMEM((sections, rows, width), BF16),
        gout=VMEM((sections, rows, width), BF16),
        meta=VMEM((8, rows), F32),
        meta_rx=VMEM((sections, 8, rows), F32),
        idx=VMEM((8 + z.retrieved, rows), jnp.int32),
        idx_rx=VMEM((sections, 8 + z.retrieved, rows), jnp.int32),
        own_docs=VMEM((sections, z.batch_size * DOC_LEN, z.vector), BF16),
        table=VMEM((dp_size * z.doc_rows, z.vector), BF16),
        counts=VMEM((sections, z.batch_size * DOC_LEN, rows), BF16),
        pool=VMEM((z.pool, z.chunk, width), BF16),
        final_right=VMEM((z.total, z.vector), BF16),
        qkv=VMEM((z.total, 3 * H * DH), BF16),
        probs=VMEM((sections, H // 2, 2 * rows, rows), F32),
        bias_sc=VMEM((H // 2, 2, z.query_len, rows), F32),
        dbias=VMEM((H // 2, 2, z.query_len, rows), F32),
        fin_rx=VMEM((rows, width), BF16),
        unit_tx=VMEM((sections, rows, z.vector), BF16),
        unit_rx=VMEM((rows, z.vector), BF16),
        loss_tx=VMEM((sections, 8, rows), F32),
        loss_rx=VMEM((8, rows), F32),
        small_sem=dma((6,)),
        load_sem=dma((3,)),
        put_sem=dma((7,)),
        state_ss=dma((sections + 1,)),
        state_rs=dma((sections,)),
        grad_ss=dma((sections,)),
        grad_rs=dma((sections,)),
        meta_ss=dma((sections,)),
        meta_rs=dma((sections,)),
        idx_ss=dma,
        idx_rs=dma((sections,)),
        tab_ss=dma((dp_size,)),
        tab_rs=dma((dp_size,)),
        tabf_ss=dma((dp_size,)),
        lend_ss=dma((4, z.parts, LEND_CUTS)),
        lend_rs=dma((4, z.parts, LEND_CUTS)),
        fin_ss=dma((sections,)),
        fin_rs=dma,
        unit_ss=dma((sections,)),
        unit_rs=dma,
        loss_ss=dma((sections,)),
        loss_rs=dma,
    )
    factors = dict(left=((2, width, z.total), BF16), right=((3, z.total, ff), BF16))
    partials = dict(
        gain_grad=((1, width), F32),
        fgain_grad=((1, width), F32),
        tab_grad=((16, 32), F32),
        dproj=((width, z.vector), BF16 if z.summed else F32),
    )
    if z.summed:
        outputs |= dict(
            main_out=shape((1, share, ff), F32),
            side_out=shape((1, share, ff), F32),
            gain_out=shape((1, share), F32),
            table_out=shape((H, 32), F32),
            fgain_out=shape((width,), F32),
            proj_out=shape((width, z.vector), F32),
        )
        scratch |= {name: VMEM(*kind) for name, kind in (factors | partials).items()}
        scratch |= dict(
            gain_out_v=VMEM((1, share), F32),
            table_out_v=VMEM((H, 32), F32),
            fgain_out_v=VMEM((width,), F32),
            main_v=VMEM((share, ff), F32),
            side_v=VMEM((share, ff), F32),
            slab_sem=dma((2, z.per_slab)),
            mine=VMEM((2,) + piece, F32),
            up_mine=VMEM((2,) + piece, F32),
            core_tx=VMEM((4,) + piece, BF16),
            up_core_tx=VMEM((4,) + piece, BF16),
            up_tx=VMEM((4,) + piece, BF16),
            up_rx=VMEM((steps // 2,) + piece, BF16),
            gain_rx=VMEM((dp_size, 1, width), F32),
            tab_rx=VMEM((dp_size, 16, 32), F32),
            tab_tx=VMEM((16, 32), F32),
            tab_cx=VMEM(((sections + 1) // 2, 16, 32), F32),
            fgain_rx=VMEM((dp_size, 1, width), F32),
            fgain_tx=VMEM((1, width), F32),
            fgain_sum=VMEM((1, width), F32),
            proj_sum=VMEM((width, z.vector), BF16),
            proj_v=VMEM((width, z.vector), F32),
            proj_rx=VMEM((dp_size, share, z.vector), BF16),
            core_ss=dma((steps,)),
            core_rs=dma((steps,)),
            up_core_ss=dma((steps // 2,)),
            up_ss=dma((steps // 2,)),
            up_rs=dma((steps // 2,)),
            hand_rs=dma((3 * z.line - 2,)),
            home_ss=dma,
            home_rs=dma,
            line_ss=dma((steps,)),
            line_rs=dma((2, z.line - 1, units)),
            core_ready=pltpu.SemaphoreType.REGULAR,
            line_ready=pltpu.SemaphoreType.REGULAR,
            gain_ss=dma((dp_size,)),
            gain_rs=dma((dp_size,)),
            tabs_ss=dma((dp_size,)),
            tabs_rs=dma((dp_size,)),
            fg_ss=dma((dp_size,)),
            fg_rs=dma((dp_size,)),
            across_ss=dma((3, sections)),
            across_rs=dma((sections + 2,)),
            proj_ss=dma((dp_size,)),
            proj_rs=dma((dp_size,)),
            spread_ss=dma((dp_size,)),
            spread_rs=dma((dp_size,)),
        )
    else:
        outputs |= {name: shape(*kind) for name, kind in (factors | partials).items()}
    results = pl.pallas_call(
        functools.partial(relay_kernel, z, (*inputs, *outputs, *scratch)),
        out_shape=tuple(outputs.values()),
        in_specs=[spec for _, spec in inputs.values()],
        out_specs=tuple(vmem if name in factors or name in partials else anywhere for name in outputs),
        scratch_shapes=list(scratch.values()),
        compiler_params=pltpu.CompilerParams(
            collective_id=0, has_side_effects=True, vmem_limit_bytes=62 * 2**20
        ),
        name="relay",
    )(*[value for value, _ in inputs.values()])
    return types.SimpleNamespace(**dict(zip(outputs, results, strict=True)))


def deliver_kernel(count, *refs):
    for k in range(count):
        refs[count + 1 + k][...] = refs[k][...]
    losses, out = refs[count], refs[-1]
    out[...] = losses[0:1, : out.shape[0]].reshape(out.shape)


def deliver(values, losses, queries):
    count = len(values)
    vmem = pl.BlockSpec(memory_space=VMEM)
    return pl.pallas_call(
        functools.partial(deliver_kernel, count),
        out_shape=tuple(jax.ShapeDtypeStruct(v.shape, v.dtype) for v in values)
        + (jax.ShapeDtypeStruct((queries,), F32),),
        in_specs=[vmem] * (count + 1),
        out_specs=(vmem,) * (count + 1),
        name="deliver",
    )(*values, losses)


def sums_outside(z, out):
    head_width = H * DH
    section = lax.axis_index("section")
    is_attention = section % 2 == 0
    left, right = out.left, out.right
    second = jnp.where(is_attention, left[1], left[0])
    main_grad = jnp.concatenate(
        [nn(left[0], right[0, :, : 3 * head_width]), nn(second, right[0, :, 3 * head_width :])],
        axis=1,
    )
    up_grad = lax.ppermute(
        nn(left[0], right[2]).astype(BF16),
        "section",
        [(k, k - 1) for k in range(1, z.sections)],
    )
    side_grad = jnp.where(is_attention, up_grad.astype(F32), nn(left[1], right[1]))
    scatter = functools.partial(
        lax.psum_scatter, axis_name="dp", scatter_dimension=0, tiled=True
    )
    table, fgain, proj = lax.psum(
        (out.tab_grad[:H], out.fgain_grad[0], out.dproj), ("section", "dp")
    )
    return (
        scatter(main_grad)[None],
        scatter(side_grad)[None],
        scatter(out.gain_grad[0])[None],
        table.T,
        fgain,
        proj,
    )


def per_device(
    hidden_in,
    lengths,
    labels,
    chosen,
    slab_main,
    slab_side,
    section_gains,
    rel_bias,
    final_gain,
    out_proj,
    doc_vectors,
):
    batch_size, query_len, width = hidden_in.shape
    rows = batch_size * query_len
    retrieved = chosen.shape[2]
    z = Sizes(
        lax.axis_size("section"),
        lax.axis_size("dp"),
        batch_size,
        query_len,
        retrieved,
        width,
        slab_main.shape[2],
        out_proj.shape[1],
        doc_vectors.shape[0],
    )
    buckets = jnp.asarray(np.tile(bucket_table(query_len).T, (1, batch_size)))
    out = relay(
        z,
        hidden_in.reshape(rows, width),
        lengths,
        labels,
        chosen.reshape(rows, retrieved),
        slab_main,
        slab_side,
        section_gains,
        rel_bias.T,
        buckets,
        final_gain,
        out_proj,
        doc_vectors,
    )
    if not z.summed:
        return (out.units, out.loss[0, :batch_size], out.dx) + sums_outside(z, out)
    names = ("units", "dx", "main_out", "side_out", "gain_out", "table_out", "fgain_out", "proj_out")
    units, dx, main, side, gain, table, fgain, proj, losses = deliver(
        [getattr(out, n) for n in names], out.loss, batch_size
    )
    return units, losses, dx, main, side, gain, table.T, fgain, proj


def solution(mesh):
    both = ("section", "dp")
    in_specs = (
        P(both, None, None),
        P(both),
        P(both),
        P(both, None, None),
        P("section", None, None),
        P("section", None, None),
        P("section", None),
        P(),
        P(),
        P(),
        P("dp", None),
    )
    out_specs = (
        P(both, None, None),
        P(both),
        P(both, None, None),
        P("section", "dp", None),
        P("section", "dp", None),
        P("section", "dp"),
        P(),
        P(),
        P(),
    )
    return jax.shard_map(
        per_device, mesh=mesh, in_specs=in_specs, out_specs=out_specs, check_vma=False
    )
```

```python
import functools
import math
import types

import jax
import jax.numpy as jnp
import numpy as np
from jax import lax
from jax.experimental import pallas as pl
from jax.experimental.pallas import tpu as pltpu
from jax.sharding import PartitionSpec as P

H = 12
DH = 64
DOC_LEN = 128
EPS_NORM = 1e-06
MASK_FILL = -1000000000.0
HIGHEST = lax.Precision.HIGHEST
MESH = pl.DeviceIdType.MESH
F32 = jnp.float32
BF16 = jnp.bfloat16
VMEM = pltpu.VMEM
GELU_C = math.sqrt(2.0 / math.pi)
GELU_A = 0.044715
FF_STEP = 768
LEND_STEP = 128
LEND_CUTS = 2


def bucket_table(query_len):
    places = np.arange(query_len)
    relative = places[None, :] - places[:, None]
    distance = np.abs(relative)
    signed_part = np.where(relative > 0, 16, 0)
    far_bucket = 8 + np.floor(np.log(np.maximum(distance, 1) / 8.0) / np.log(16.0) * 8.0).astype(
        np.int64
    )
    far_bucket = np.minimum(far_bucket, 15)
    return (signed_part + np.where(distance < 8, distance, far_bucket)).astype(np.int32)


def nn(a, b):
    return jnp.dot(a, b, preferred_element_type=F32)


def nt(a, b):
    return lax.dot_general(a, b, (((1,), (1,)), ((), ())), preferred_element_type=F32)


def tn(a, b):
    return lax.dot_general(a, b, (((0,), (0,)), ((), ())), preferred_element_type=F32)


def rms_inverse(values):
    return lax.rsqrt(jnp.mean(values * values, axis=-1, keepdims=True) + EPS_NORM)


def rms_back(scaled, inverse, gain, grad):
    inner = grad * gain
    grad_values = inverse * (inner - scaled * jnp.mean(inner * scaled, axis=-1, keepdims=True))
    return grad_values, jnp.sum(grad * scaled, axis=0, keepdims=True)


def sum_order(line):
    orders = []
    for place in range(line):
        others = [j for j in range(line) if j != place]
        others.sort(key=lambda j: (-abs(j - place), min(j, line - 1 - j)))
        orders.append(others + [place])
    return orders


class Sizes:
    def __init__(self, sections, dp_size, batch_size, query_len, retrieved, width, ff, vector, doc_rows):
        self.sections = sections
        self.dp_size = dp_size
        self.batch_size = batch_size
        self.query_len = query_len
        self.retrieved = retrieved
        self.width = width
        self.ff = ff
        self.vector = vector
        self.doc_rows = doc_rows
        self.rows = batch_size * query_len
        self.total = sections * self.rows
        self.parts = ff // 4 // LEND_STEP
        self.share = width // dp_size
        self.summed = self.share % 16 == 0 and dp_size % 2 == 0
        self.line = dp_size // 2
        self.step_columns = H * DH
        self.per_slab = ff // self.step_columns
        self.units = 2 * self.per_slab
        self.steps = self.line * self.units
        self.chunk = self.share if self.summed else H * 8
        self.slab_chunks = ff // self.chunk
        self.windows = self.total // self.chunk
        self.handed = self.summed and sections == 4 and 3 * self.line - 2 <= 3 * self.windows
        arriving = self.steps + 2 * (self.line - 1) * self.units
        self.pool = max(3 * self.slab_chunks, arriving if self.summed else 0)


def relay_kernel(z, names, *refs):
    r = types.SimpleNamespace(**dict(zip(names, refs, strict=True)))
    s = lax.axis_index("section")
    d = lax.axis_index("dp")
    sections, dp_size, rows, width, ff = z.sections, z.dp_size, z.rows, z.width, z.ff
    batch_size, query_len, parts = z.batch_size, z.query_len, z.parts
    head_width = H * DH
    last = sections - 1
    after = lax.rem(s + 1, sections)
    before = lax.rem(s + sections - 1, sections)
    group = d - lax.rem(d, 4)
    place = lax.rem(d, 4)
    core_peer = group + place + 1 - 2 * lax.rem(place, 2)
    far_place = lax.rem(place + 2, 4)
    far_peer = group + far_place
    is_attention = lax.rem(s, 2) == 0
    is_ffn = jnp.logical_not(is_attention)

    def copy(src, dst, send_sem, recv_sem, section, dp):
        return pltpu.make_async_remote_copy(
            src_ref=src,
            dst_ref=dst,
            send_sem=send_sem,
            recv_sem=recv_sem,
            device_id=(section, dp),
            device_id_type=MESH,
        )

    def block(m):
        return pl.ds(pl.multiple_of(m * rows, rows), rows)

    def peers(body):
        def step(k, carry):
            body(lax.rem(d + k, dp_size))
            return carry

        lax.fori_loop(1, dp_size, step, 0)

    def other_sections(body):
        for k in range(1, sections):
            body(lax.rem(s + k, sections))

    def main_load():
        return pltpu.make_async_copy(r.main_hbm.at[0], r.main, r.load_sem.at[0])

    def side_load():
        return pltpu.make_async_copy(r.side_hbm.at[0], r.side, r.load_sem.at[1])

    small_loads = [
        pltpu.make_async_copy(getattr(r, name + "_hbm"), getattr(r, name), r.small_sem.at[k])
        for k, name in enumerate(("chosen", "bias", "buckets", "gain", "fgain", "proj"))
    ]
    for one in small_loads:
        one.start()

    def hid_load():
        return pltpu.make_async_copy(r.hid_hbm, r.xin.at[0], r.load_sem.at[2])

    def docs_load():
        return pltpu.make_async_copy(r.docs_hbm, r.table.at[table_rows(d), :], r.load_sem.at[2])

    def table_rows(owner):
        return pl.ds(pl.multiple_of(owner * z.doc_rows, z.doc_rows), z.doc_rows)

    @pl.when(s == 0)
    def _():
        hid_load().start()

    main_load().start()

    @pl.when(is_ffn)
    def _():
        side_load().start()

    @pl.when(s == last)
    def _():
        docs_load().start()

    barrier = pltpu.get_barrier_semaphore()
    other_sections(
        lambda to: pl.semaphore_signal(barrier, inc=1, device_id=(to, d), device_id_type=MESH)
    )
    peers(lambda to: pl.semaphore_signal(barrier, inc=1, device_id=(s, to), device_id_type=MESH))

    lane = lax.broadcasted_iota(jnp.int32, (1, rows), 1)
    token_query = lane // query_len
    token_slot = lax.rem(lane, query_len)
    length = jnp.zeros((1, rows), jnp.int32)
    for q in range(batch_size):
        length = jnp.where(token_query == q, r.lengths[q], length)
    live = jnp.where(token_slot < length, 1.0, 0.0)
    r.meta[...] = jnp.zeros_like(r.meta)
    r.meta[0:1, :] = live
    r.meta[1:2, :] = live / length.astype(F32)
    r.idx[:8, :] = jnp.zeros((8, rows), jnp.int32)
    for c in range(batch_size):
        r.idx[c : c + 1, :] = jnp.full((1, rows), r.labels[c], jnp.int32)
    for one in small_loads:
        one.wait()
    r.idx[8:, :] = r.chosen[...].T

    pl.semaphore_wait(barrier, sections - 1 + dp_size - 1)

    def lend_columns(quarter, part):
        start = quarter * (ff // 4) + part * LEND_STEP
        return pl.ds(pl.multiple_of(start, LEND_STEP), LEND_STEP)

    def lend_copy(part, half):
        columns = lend_columns(place, part)
        depth = slice(half * (width // LEND_CUTS), (half + 1) * (width // LEND_CUTS))
        return copy(
            r.side_hbm.at[0, depth, columns],
            r.lent.at[depth, columns],
            r.lend_ss.at[0, part, half],
            r.lend_rs.at[0, part, half],
            after,
            d,
        )

    def lend_forward(kind, quarter, part, half, peer):
        columns = lend_columns(quarter, part)
        depth = slice(half * (width // LEND_CUTS), (half + 1) * (width // LEND_CUTS))
        return copy(
            r.lent.at[depth, columns],
            r.lent.at[depth, columns],
            r.lend_ss.at[kind, part, half],
            r.lend_rs.at[kind, part, half],
            s,
            peer,
        )

    pieces = [(part, half) for part in range(parts) for half in range(LEND_CUTS)]

    def state_copy(m):
        return copy(r.xout.at[m], r.xin.at[m], r.state_ss.at[m], r.state_rs.at[m], after, d)

    def grad_copy(m):
        return copy(r.gout.at[m], r.gin.at[m], r.grad_ss.at[m], r.grad_rs.at[m], before, d)

    def meta_copy(to, slot):
        return copy(r.meta, r.meta_rx.at[slot], r.meta_ss.at[to], r.meta_rs.at[slot], to, d)

    def idx_copy(slot):
        return copy(r.idx, r.idx_rx.at[slot], r.idx_ss, r.idx_rs.at[slot], last, d)

    def hid_copy(slot):
        return copy(r.hid_hbm, r.xin.at[slot], r.state_ss.at[sections], r.state_rs.at[slot], 0, d)

    def unit_copy(m, to):
        return copy(r.unit_tx.at[m], r.unit_rx, r.unit_ss.at[m], r.unit_rs, to, d)

    def loss_copy(m, to):
        return copy(r.loss_tx.at[m], r.loss_rx, r.loss_ss.at[m], r.loss_rs, to, d)

    def fin_copy(m, to):
        return copy(r.gout.at[m], r.fin_rx, r.fin_ss.at[m], r.fin_rs, to, d)

    def table_copy(to, owner):
        return copy(
            r.docs_hbm, r.table.at[table_rows(owner), :], r.tab_ss.at[to], r.tab_rs.at[owner], s, to
        )

    def table_near(owner):
        return copy(
            r.docs_hbm,
            r.table.at[table_rows(owner), :],
            r.tab_ss.at[core_peer],
            r.tab_rs.at[owner],
            s,
            core_peer,
        )

    def table_forward(owner):
        rows = table_rows(owner)
        return copy(
            r.table.at[rows, :], r.table.at[rows, :], r.tabf_ss.at[owner], r.tab_rs.at[owner], s, core_peer
        )

    def far_owners(body):
        def step(k, carry):
            body(lax.rem(d + 2 * k, dp_size))
            return carry

        lax.fori_loop(1, dp_size // 2, step, 0)

    @pl.when(s != 0)
    def _():
        hid_copy(s).start()

    @pl.when(s == last)
    def _():
        table_near(d).start()
        far_owners(lambda to: table_copy(to, d).start())

    @pl.when(is_attention)
    def _():
        for part in range(parts):
            for half in range(LEND_CUTS):
                lend_copy(part, half).start()

    other_sections(lambda to: meta_copy(to, s).start())
    r.meta_rx[s] = r.meta[...]

    @pl.when(s != last)
    def _():
        idx_copy(s).start()

    r.gain_grad[...] = jnp.zeros_like(r.gain_grad)
    r.fgain_grad[...] = jnp.zeros_like(r.fgain_grad)

    if not z.summed:

        @pl.when(is_ffn)
        def _():
            r.tab_grad[...] = jnp.zeros_like(r.tab_grad)


    if not z.summed:

        @pl.when(s != last)
        def _():
            r.dproj[...] = jnp.zeros_like(r.dproj)

    r.dbias[...] = jnp.zeros_like(r.dbias)
    gain = r.gain[...]
    fgain = r.fgain[...].reshape(1, width)

    def wait_meta(m):
        @pl.when(m != s)
        def _():
            meta_copy(0, m).wait_recv()

    def load_state(m):
        states = r.xin[m].astype(F32)
        inverse = rms_inverse(states)
        return states, inverse, states * inverse

    low_half = lax.broadcasted_iota(jnp.int32, (1, 128), 1) < DH

    low_lanes = jnp.where(low_half, 1.0, 0.0).astype(BF16)
    high_lanes = jnp.where(low_half, 0.0, 1.0).astype(BF16)

    def split_heads(value):
        return jnp.concatenate([value * low_lanes, value * high_lanes], axis=0)

    def join_heads(value):
        return jnp.where(low_half, value[:rows], value[rows:]).astype(BF16)

    def attention_setup():
        buckets = r.buckets[...]
        for h in range(H):
            total = jnp.zeros(buckets.shape, F32)
            for b in range(32):
                total = jnp.where(buckets == b, r.bias[h : h + 1, b : b + 1], total)
            r.bias_sc[h // 2, h % 2] = total

    def attention_table():
        buckets = r.buckets[...]
        ones = jnp.ones((16, 128), BF16)
        head_row = lax.broadcasted_iota(jnp.int32, (16, 32), 0)

        def head(h, carry):
            grad = r.dbias[h // 2, lax.rem(h, 2)]
            rest = jnp.concatenate(
                [
                    jnp.sum(jnp.where(buckets == b, grad, 0.0), axis=0, keepdims=True)
                    for b in range(32)
                ],
                axis=0,
            )
            total = jnp.zeros((16, 32), F32)
            for _ in range(3):
                part = rest.astype(BF16)
                total = total + nt(ones, part)
                rest = rest - part.astype(F32)
            return carry + jnp.where(head_row == h, total, 0.0)

        r.tab_grad[...] = lax.fori_loop(0, H, head, jnp.zeros((16, 32), F32))

    def turn(source, slab, start):
        size = FF_STEP // z.chunk
        first = slab * z.slab_chunks + start // z.chunk
        r.pool[first : first + size] = source[:, start : start + FF_STEP].T.reshape(
            size, z.chunk, width
        )

    def turned(slab, start, stop):
        first = slab * z.slab_chunks
        return r.pool[first + start // z.chunk : first + stop // z.chunk].reshape(
            stop - start, width
        )

    def attention_forward(m):
        states, inverse, scaled = load_state(m)
        normed = scaled * gain
        r.left[0, :, block(m)] = normed.T.astype(BF16)
        normed_low = normed.astype(BF16)
        for start in range(0, 3 * head_width, head_width):
            r.qkv[block(m), start : start + head_width] = nn(
                normed_low, r.main[:, start : start + head_width]
            ).astype(BF16)
        live = jnp.broadcast_to(r.meta_rx[m, 0:1, :], (rows, rows)).T > 0.5
        row_query = lax.broadcasted_iota(jnp.int32, (rows, rows), 0) // query_len
        column_query = lax.broadcasted_iota(jnp.int32, (rows, rows), 1) // query_len
        keep = jnp.logical_and(row_query == column_query, live)
        for pair in range(H // 2):
            at = pair * 128
            query = r.qkv[block(m), at : at + 128]
            keys = r.qkv[block(m), head_width + at : head_width + at + 128]
            values = r.qkv[block(m), 2 * head_width + at : 2 * head_width + at + 128]
            raw = nt(split_heads(keys), query)
            biased = raw.reshape(2, batch_size, query_len, rows) + r.bias_sc[pair][:, None]
            scores = jnp.where(keep[None], biased.reshape(2, rows, rows), MASK_FILL)
            top = jnp.max(scores, axis=1, keepdims=True)
            grown = jnp.exp(scores - top)
            soft = grown * (1.0 / jnp.sum(grown, axis=1, keepdims=True))
            soft = soft.reshape(2 * rows, rows)
            r.probs[m, pair] = soft
            r.right[0, block(m), 3 * head_width + at : 3 * head_width + at + 128] = tn(
                soft.astype(BF16), split_heads(values)
            ).astype(BF16)
        context = r.right[0, block(m), 3 * head_width :]
        return states + nn(context, turned(0, 3 * head_width, ff))

    def attention_backward(m):
        states, inverse, scaled = load_state(m)
        grad_low = r.gin[m]
        grad = grad_low.astype(F32)
        r.left[1, :, block(m)] = grad.T.astype(BF16)
        grad_context = nn(grad_low, r.main[:, 3 * head_width :]).astype(BF16)
        for pair in range(H // 2):
            at = pair * 128
            query = r.qkv[block(m), at : at + 128]
            keys = r.qkv[block(m), head_width + at : head_width + at + 128]
            values = r.qkv[block(m), 2 * head_width + at : 2 * head_width + at + 128]
            grad_pair = grad_context[:, at : at + 128]
            soft = r.probs[m, pair]
            grad_soft = nt(split_heads(values), grad_pair)
            moved = (soft * grad_soft).reshape(2, rows, rows)
            grad_scores = moved - soft.reshape(2, rows, rows) * jnp.sum(
                moved, axis=1, keepdims=True
            )
            r.dbias[pair] += jnp.sum(
                grad_scores.reshape(2, batch_size, query_len, rows), axis=1
            )
            scores_low = grad_scores.reshape(2 * rows, rows).astype(BF16)
            found = (
                tn(scores_low, split_heads(keys)).astype(BF16),
                join_heads(nn(scores_low, query)),
                join_heads(nn(soft.astype(BF16), grad_pair)),
            )
            for third in range(3):
                start = third * head_width + at
                r.right[0, block(m), start : start + 128] = found[third]
        grad_normed = nn(r.right[0, block(m), : 3 * head_width], turned(0, 0, 3 * head_width))
        grad_states, grad_gain = rms_back(scaled, inverse, gain, grad_normed)
        r.gain_grad[...] += grad_gain
        return grad + grad_states

    def ffn_forward(m):
        states, inverse, scaled = load_state(m)
        normed = scaled * gain
        r.left[0, :, block(m)] = normed.T.astype(BF16)
        normed_low = normed.astype(BF16)
        outputs = states
        for start in range(0, ff, FF_STEP):
            columns = slice(start, start + FF_STEP)
            gate = nn(normed_low, r.main[:, columns])
            up = nn(normed_low, r.lent[:, columns])
            square = gate * gate
            bent = jnp.tanh(GELU_C * gate * (1.0 + GELU_A * square))
            half = 0.5 * (1.0 + bent)
            smooth = gate * half
            slope = half + 0.5 * gate * (1.0 - bent * bent) * (
                GELU_C * (1.0 + 3.0 * GELU_A * square)
            )
            hidden = (smooth * up).astype(BF16)
            r.right[1, block(m), columns] = hidden
            r.right[0, block(m), columns] = (slope * up).astype(BF16)
            r.right[2, block(m), columns] = smooth.astype(BF16)
            outputs = outputs + nn(hidden, turned(1, start, start + FF_STEP))
        return outputs

    def ffn_backward(m, grad):
        states, inverse, scaled = load_state(m)
        grad_low = grad.astype(BF16)
        r.left[1, :, block(m)] = grad.T.astype(BF16)
        grad_normed = jnp.zeros((rows, width), F32)
        for start in range(0, ff, FF_STEP):
            columns = slice(start, start + FF_STEP)
            grad_hidden = nn(grad_low, r.side[:, columns])
            grad_gate = (grad_hidden * r.right[0, block(m), columns].astype(F32)).astype(BF16)
            grad_up = (grad_hidden * r.right[2, block(m), columns].astype(F32)).astype(BF16)
            r.right[0, block(m), columns] = grad_gate
            r.right[2, block(m), columns] = grad_up
            grad_normed = (
                grad_normed
                + nn(grad_gate, turned(0, start, start + FF_STEP))
                + nn(grad_up, turned(2, start, start + FF_STEP))
            )
        grad_states, grad_gain = rms_back(scaled, inverse, gain, grad_normed)
        r.gain_grad[...] += grad_gain
        return grad + grad_states

    def count_hits(m):
        for c in range(batch_size):
            base = r.idx_rx[m, c : c + 1, :] * DOC_LEN
            numbers = lax.broadcasted_iota(jnp.int32, (DOC_LEN, rows), 0) + base
            total = jnp.zeros((DOC_LEN, rows), F32)
            for k in range(z.retrieved):
                total = total + jnp.where(r.idx_rx[m, 8 + k : 9 + k, :] == numbers, 1.0, 0.0)
            r.counts[m, c * DOC_LEN : (c + 1) * DOC_LEN, :] = total.astype(BF16)

    def pick_docs(m):
        for c in range(batch_size):
            label = r.idx_rx[m, c : c + 1, :]

            def pick(t, picked):
                here = r.table[pl.ds(pl.multiple_of(t * DOC_LEN, DOC_LEN), DOC_LEN), :].astype(F32)
                return jnp.where(label == t, here, picked)

            picked = lax.fori_loop(
                0, dp_size * z.doc_rows // DOC_LEN, pick, jnp.zeros((DOC_LEN, z.vector), F32)
            )
            r.own_docs[m, c * DOC_LEN : (c + 1) * DOC_LEN, :] = picked.astype(BF16)

    def loss_and_grad(m, unit):
        docs = r.own_docs[m]
        sims = nt(docs, unit)
        count = r.counts[m].astype(F32)
        imputed = jnp.sum(count * sims, axis=0, keepdims=True) / z.retrieved
        grown = count * jnp.exp(sims)
        imputed_mass = jnp.exp(imputed)
        mass = imputed_mass + jnp.concatenate(
            [
                jnp.sum(grown[c * DOC_LEN : (c + 1) * DOC_LEN], axis=0, keepdims=True)
                for c in range(batch_size)
            ],
            axis=0,
        )
        weighted = jnp.log(mass) * r.meta_rx[m, 1:2, :]
        candidate = lax.broadcasted_iota(jnp.int32, (batch_size, 1), 0)
        losses = jnp.zeros((1, rows), F32)
        grad_tokens = jnp.zeros((batch_size, rows), F32)
        for q in range(batch_size):
            own = token_query == q
            score = jnp.sum(jnp.where(own, weighted, 0.0), axis=1, keepdims=True)
            top = jnp.max(score, axis=0, keepdims=True)
            risen = jnp.exp(score - top)
            total = jnp.sum(risen, axis=0, keepdims=True)
            chosen_one = (candidate == q).astype(F32)
            loss = top + jnp.log(total) - jnp.sum(score * chosen_one, axis=0, keepdims=True)
            losses = losses + jnp.where(lane == q, loss, 0.0)
            grad_tokens = grad_tokens + jnp.where(own, risen / total - chosen_one, 0.0)
        grad_mass = grad_tokens * r.meta_rx[m, 1:2, :] / mass
        shared = jnp.sum(grad_mass, axis=0, keepdims=True) * imputed_mass / z.retrieved
        grad_sims = count * shared + jnp.concatenate(
            [
                grown[c * DOC_LEN : (c + 1) * DOC_LEN] * grad_mass[c : c + 1]
                for c in range(batch_size)
            ],
            axis=0,
        )
        high = grad_sims.astype(BF16)
        rest = (grad_sims - high.astype(F32)).astype(BF16)
        return losses, tn(high, docs) + tn(rest, docs)

    def finish_states(m, states):
        inverse = rms_inverse(states)
        scaled = states * inverse
        normed = (scaled * fgain).astype(BF16)
        projected = nn(normed, r.proj[...])
        size = lax.rsqrt(jnp.sum(projected * projected, axis=-1, keepdims=True) + EPS_NORM)
        exact = projected * size
        unit = exact.astype(BF16)
        losses, grad_unit = loss_and_grad(m, unit)
        r.unit_tx[m] = unit
        r.loss_tx[m] = jnp.broadcast_to(losses, (8, rows))

        @pl.when(m != last)
        def _():
            unit_copy(m, m).start()
            loss_copy(m, m).start()

        grad_projected = (
            size * (grad_unit - exact * jnp.sum(grad_unit * exact, axis=-1, keepdims=True))
        ).astype(BF16)
        r.xout[m] = normed
        r.final_right[block(m), :] = grad_projected
        grad_normed = nt(grad_projected, r.proj[...])
        grad_states, grad_gain = rms_back(scaled, inverse, fgain, grad_normed)
        r.fgain_grad[...] += grad_gain
        return grad_states

    def loop(body):
        def step(m, carry):
            body(m)
            return carry

        lax.fori_loop(0, sections, step, 0)

    def wait_state(m):
        @pl.when(jnp.logical_or(s != 0, m != 0))
        def _():
            state_copy(m).wait_recv()

    @pl.when(is_attention)
    def _():
        attention_setup()
        main_load().wait()
        for start in range(0, ff, FF_STEP):
            turn(r.main, 0, start)

        def forward(m):
            wait_meta(m)
            wait_state(m)

            @pl.when(jnp.logical_and(s == 0, m == 0))
            def _():
                hid_load().wait()

            r.xout[m] = attention_forward(m).astype(BF16)
            state_copy(m).start()

        loop(forward)

        def backward(m):
            grad_copy(m).wait_recv()
            r.gout[m] = attention_backward(m).astype(BF16)

            @pl.when(s != 0)
            def _():
                grad_copy(m).start()

            @pl.when(jnp.logical_and(s == 0, m != 0))
            def _():
                fin_copy(m, m).start()

        loop(backward)
        if not z.summed:
            attention_table()

    @pl.when(is_ffn)
    def _():
        turns = [(r.main, 0, start) for start in range(0, ff, FF_STEP)]
        turns += [(r.side, 1, start) for start in range(0, ff, FF_STEP)]
        main_load().wait()
        side_load().wait()
        def far_arrived(piece):
            lend_forward(2, far_place, *piece, far_peer).wait_recv()
            lend_forward(3, far_place, *piece, core_peer).start()

        lag = LEND_CUTS
        for k, piece in enumerate(pieces):
            lend_copy(*piece).wait_recv()
            lend_forward(2, place, *piece, far_peer).start()
            lend_forward(1, place, *piece, core_peer).start()
            if k >= lag:
                far_arrived(pieces[k - lag])
            for one in turns[k :: len(pieces)]:
                turn(*one)

        @pl.when(s == last)
        def _():
            r.idx_rx[last] = r.idx[...]

            def pass_on(owner):
                table_copy(owner, owner).wait_recv()
                table_forward(owner).start()

            far_owners(pass_on)

            def prepare(m):
                @pl.when(m != last)
                def _():
                    idx_copy(m).wait_recv()

                count_hits(m)

            loop(prepare)

        for piece in pieces[-lag:]:
            far_arrived(piece)
        for piece in pieces:
            lend_forward(1, place, *piece, core_peer).wait_recv()
            lend_forward(3, far_place, *piece, core_peer).wait_recv()

        def turn_lent():
            for start in range(0, ff, FF_STEP):
                turn(r.lent, 2, start)

        def lend_sent():
            for piece in pieces:
                lend_forward(1, place, *piece, core_peer).wait_send()
                lend_forward(2, place, *piece, far_peer).wait_send()
                lend_forward(3, far_place, *piece, core_peer).wait_send()

        @pl.when(s == last)
        def _():
            docs_load().wait()
            table_near(core_peer).wait_recv()

            def take(owner):
                table_forward(owner + core_peer - d).wait_recv()

            far_owners(take)
            loop(pick_docs)
            turn_lent()
            loop(wait_meta)
            lend_sent()

            def both(m):
                wait_state(m)
                states = ffn_forward(m)
                grad = finish_states(m, states)
                r.gout[m] = ffn_backward(m, grad).astype(BF16)
                grad_copy(m).start()

            loop(both)
            r.dproj[...] = tn(r.xout[...].reshape(z.total, width), r.final_right[...]).astype(
                r.dproj.dtype
            )

        @pl.when(s != last)
        def _():
            def forward(m):
                wait_state(m)
                r.xout[m] = ffn_forward(m).astype(BF16)
                state_copy(m).start()

            loop(forward)
            turn_lent()
            loop(wait_meta)
            lend_sent()

            def backward(m):
                grad_copy(m).wait_recv()
                r.gout[m] = ffn_backward(m, r.gin[m].astype(F32)).astype(BF16)
                grad_copy(m).start()

            loop(backward)

    def put(k, name):
        return pltpu.make_async_copy(getattr(r, name + "_v"), getattr(r, name), r.put_sem.at[k])

    homes = [put(k, name) for k, name in enumerate(("units", "loss", "dx"))]

    def come_home():
        @pl.when(s != 0)
        def _():
            fin_copy(0, s).wait_recv()
            r.dx_v[...] = r.fin_rx[...].astype(F32).reshape(batch_size, query_len, width)

        @pl.when(s == 0)
        def _():
            r.dx_v[...] = r.gout[0].astype(F32).reshape(batch_size, query_len, width)

        def write_own(unit, losses):
            r.units_v[...] = unit.reshape(batch_size, query_len, z.vector)
            r.loss_v[...] = losses

        @pl.when(s != last)
        def _():
            unit_copy(0, s).wait_recv()
            loss_copy(0, s).wait_recv()
            write_own(r.unit_rx[...], r.loss_rx[...])

        @pl.when(s == last)
        def _():
            write_own(r.unit_tx[last], r.loss_tx[last])

        for one in homes:
            one.start()
        sent()

    def sent():
        other_sections(lambda to: meta_copy(to, s).wait_send())

        @pl.when(s != 0)
        def _():
            hid_copy(s).wait_send()
            loop(lambda m: grad_copy(m).wait_send())

        @pl.when(s == 0)
        def _():
            for m in range(1, sections):
                fin_copy(m, m).wait_send()

        @pl.when(is_attention)
        def _():
            for piece in pieces:
                lend_copy(*piece).wait_send()

        @pl.when(s != last)
        def _():
            idx_copy(s).wait_send()
            loop(lambda m: state_copy(m).wait_send())

        @pl.when(s == last)
        def _():
            table_near(d).wait_send()
            far_owners(lambda to: table_copy(to, d).wait_send())
            far_owners(lambda owner: table_forward(owner).wait_send())
            for m in range(sections - 1):
                unit_copy(m, m).wait_send()
                loss_copy(m, m).wait_send()

    if z.summed:
        sum_gradients(
            z, r, s, d, copy, peers, other_sections, is_attention, attention_table, come_home
        )
    else:
        come_home()

    for one in homes:
        one.wait()


def sum_gradients(
    z, r, s, d, copy, peers, other_sections, is_attention, attention_table, come_home
):
    sections, dp_size, width, ff, share, line = z.sections, z.dp_size, z.width, z.ff, z.share, z.line
    step_columns, per_slab, units, steps = z.step_columns, z.per_slab, z.units, z.steps
    place = d // 2
    core = lax.rem(d, 2)
    peer = d + 1 - 2 * core
    last = sections - 1
    before = lax.rem(s + sections - 1, sections)
    is_ffn = jnp.logical_not(is_attention)
    orders = sum_order(line)

    def piece_rows(owner):
        return pl.ds(pl.multiple_of(owner * share, share), share)

    def gain_copy(to, slot):
        return copy(r.gain_grad, r.gain_rx.at[slot], r.gain_ss.at[to], r.gain_rs.at[slot], s, to)

    def table_copy(to, slot):
        return copy(r.tab_grad, r.tab_rx.at[slot], r.tabs_ss.at[to], r.tabs_rs.at[slot], s, to)

    def fgain_copy(to, slot):
        return copy(r.fgain_grad, r.fgain_rx.at[slot], r.fg_ss.at[to], r.fg_rs.at[slot], s, to)

    def proj_copy(to, slot):
        return copy(
            r.dproj.at[piece_rows(to), :],
            r.proj_rx.at[slot],
            r.proj_ss.at[to],
            r.proj_rs.at[slot],
            s,
            to,
        )

    def spread_copy(to, owner):
        rows = piece_rows(owner)
        return copy(
            r.proj_sum.at[rows, :],
            r.proj_sum.at[rows, :],
            r.spread_ss.at[to],
            r.spread_rs.at[owner],
            s,
            to,
        )

    def table_across(to, slot):
        return copy(r.tab_tx, r.tab_cx.at[slot], r.across_ss.at[0, to], r.across_rs.at[slot], to, d)

    def fgain_across(to):
        return copy(
            r.fgain_tx, r.fgain_sum, r.across_ss.at[1, to], r.across_rs.at[sections], to, d
        )

    def proj_across(to):
        return copy(
            r.proj_sum, r.proj_sum, r.across_ss.at[2, to], r.across_rs.at[sections + 1], to, d
        )

    small_puts = [
        pltpu.make_async_copy(source, target, r.put_sem.at[3 + k])
        for k, (source, target) in enumerate(
            (
                (r.gain_out_v, r.gain_out),
                (r.table_out_v, r.table_out),
                (r.fgain_out_v, r.fgain_out),
                (r.proj_v, r.proj_out),
            )
        )
    ]

    def slab_put(slab, column, columns):
        source, target = ((r.main_v, r.main_out), (r.side_v, r.side_out))[slab]
        return pltpu.make_async_copy(
            source.at[:, columns], target.at[0, :, columns], r.slab_sem.at[slab, column]
        )

    def total_of(ref, count):
        total = ref[0].astype(F32)
        for k in range(1, count):
            total = total + ref[k].astype(F32)
        return total

    def to_others(body):
        for to in range(sections):

            @pl.when(s != to)
            def _():
                body(to)

    def small_first():
        peers(lambda to: gain_copy(to, d).start())
        r.gain_rx[d] = r.gain_grad[...]

        @pl.when(is_attention)
        def _():
            attention_table()
            peers(lambda to: table_copy(to, d).start())
            r.tab_rx[d] = r.tab_grad[...]

    def proj_first():
        peers(lambda to: proj_copy(to, d).start())
        peers(lambda to: fgain_copy(to, d).start())
        r.proj_rx[d] = r.dproj[piece_rows(d), :]
        r.fgain_rx[d] = r.fgain_grad[...]

    def proj_second():
        peers(lambda owner: proj_copy(owner, owner).wait_recv())
        peers(lambda owner: fgain_copy(owner, owner).wait_recv())
        r.proj_sum[piece_rows(d), :] = total_of(r.proj_rx, dp_size).astype(BF16)
        r.fgain_tx[...] = total_of(r.fgain_rx, dp_size)
        r.fgain_sum[...] = r.fgain_tx[...]
        peers(lambda to: spread_copy(to, d).start())
        to_others(lambda to: fgain_across(to).start())

    def proj_third():
        peers(lambda owner: spread_copy(owner, owner).wait_recv())
        to_others(lambda to: proj_across(to).start())

    def small_second():
        peers(lambda owner: gain_copy(owner, owner).wait_recv())
        gain_sum = jnp.broadcast_to(total_of(r.gain_rx, dp_size), (8, width))
        r.gain_out_v[...] = pltpu.roll(gain_sum, width - d * share, 1)[0:1, :share]

        @pl.when(is_attention)
        def _():
            peers(lambda owner: table_copy(owner, owner).wait_recv())
            r.tab_tx[...] = total_of(r.tab_rx, dp_size)
            r.tab_cx[s // 2] = r.tab_tx[...]
            to_others(lambda to: table_across(to, s // 2).start())

    def small_last():
        for source in range(0, sections, 2):

            @pl.when(s != source)
            def _():
                table_across(source, source // 2).wait_recv()

        r.table_out_v[...] = total_of(r.tab_cx, (sections + 1) // 2)[:H]

        @pl.when(s != last)
        def _():
            fgain_across(last).wait_recv()
            proj_across(last).wait_recv()

        r.fgain_out_v[...] = r.fgain_sum[...].reshape(width)
        r.proj_v[...] = r.proj_sum[...].astype(F32)
        for one in small_puts:
            one.start()
        peers(lambda to: gain_copy(to, d).wait_send())

        @pl.when(is_attention)
        def _():
            peers(lambda to: table_copy(to, d).wait_send())
            to_others(lambda to: table_across(to, s // 2).wait_send())

        @pl.when(s == last)
        def _():
            peers(lambda to: proj_copy(to, d).wait_send())
            peers(lambda to: fgain_copy(to, d).wait_send())
            peers(lambda to: spread_copy(to, d).wait_send())
            to_others(lambda to: fgain_across(to).wait_send())
            to_others(lambda to: proj_across(to).wait_send())

    def target(i):
        found = jnp.int32(0)
        for k in range(line):
            found = jnp.where(place == k, orders[k][i], found)
        return found

    targets = [target(i) for i in range(line)]

    def target_of(i):
        j = targets[0]
        for k in range(1, line):
            j = jnp.where(i == k, targets[k], j)
        return j

    def parts_of(t):
        i, u = t // units, lax.rem(t, units)
        j = target_of(i)
        slab, column = 1 - lax.rem(u, 2), u // 2
        columns = pl.ds(pl.multiple_of(column * step_columns, step_columns), step_columns)
        return j, u, slab, column, columns

    def core_copy(t):
        return copy(
            r.core_tx.at[lax.rem(t, 4)], r.pool.at[t], r.core_ss.at[t], r.core_rs.at[t], s, peer
        )

    def up_core_copy(k):
        return copy(
            r.up_core_tx.at[lax.rem(k, 4)], r.up_rx.at[k], r.up_core_ss.at[k], r.up_rs.at[k], s, peer
        )

    def up_copy(k):
        return copy(
            r.up_tx.at[lax.rem(k, 4)], r.up_rx.at[k], r.up_ss.at[k], r.up_rs.at[k], before, d
        )

    hand_column = per_slab - 1
    hand_columns = slice(hand_column * step_columns, ff)

    def window(n):
        row = pl.ds(pl.multiple_of(lax.rem(n, z.windows) * share, share), share)
        column = pl.ds(pl.multiple_of(n // z.windows * step_columns, step_columns), step_columns)
        return r.qkv.at[row, column]

    def hand_copy(k):
        i = k // per_slab
        return copy(r.up_tx.at[lax.rem(k, 4)], window(i), r.up_ss.at[k], r.hand_rs.at[i], last, d)

    def hand_line(i, way, j, to):
        slot = way * (line - 1) + j - 1 + way
        return copy(
            line_view(steps - units + i),
            window(line + slot),
            r.line_ss.at[steps - units + i],
            r.hand_rs.at[line + slot],
            s,
            to * 2 + core,
        )

    def hand_home():
        return copy(
            r.up_mine.at[0], r.side_v.at[:, hand_columns], r.home_ss, r.home_rs, 0, d
        )

    def extra(i):
        j = target_of(i)
        total = r.up_mine.at[0]
        hand_copy(i * per_slab).wait_recv()
        total[...] = window(i)[...].astype(F32)
        way = jnp.where(j < place, 1, 0)

        @pl.when(jnp.logical_and(place > 0, j >= place))
        def _():
            hand_line(i, 0, j, place).wait_recv()
            total[...] += window(line + j - 1)[...].astype(F32)

        @pl.when(jnp.logical_and(place < line - 1, j <= place))
        def _():
            hand_line(i, 1, j, place).wait_recv()
            total[...] += window(line + line - 1 + j)[...].astype(F32)

        @pl.when(j == place)
        def _():
            hand_home().start()

        @pl.when(j != place)
        def _():
            line_view(steps - units + i)[...] = total[...].astype(BF16)
            hand_line(i, way, j, place + 1 - 2 * way).start()

    def line_view(t):
        row = pl.ds(pl.multiple_of(lax.rem(t, dp_size) * share, share), share)
        column = pl.ds(pl.multiple_of(t // dp_size * step_columns, step_columns), step_columns)
        return r.lent.at[row, column]

    def line_slot(way, j, u):
        return steps + (way * (line - 1) + j - 1 + way) * units + u

    def line_copy(t, way, j, u, to):
        slot = j - 1 + way
        return copy(
            line_view(t),
            r.pool.at[line_slot(way, j, u)],
            r.line_ss.at[t],
            r.line_rs.at[way, slot, u],
            s,
            to * 2 + core,
        )

    def theirs(j):
        return pl.ds(pl.multiple_of((j * 2 + 1 - core) * share, share), share)

    def ours(j):
        return pl.ds(pl.multiple_of((j * 2 + core) * share, share), share)

    def begin(t):
        j, u, slab, column, columns = parts_of(t)
        mixed = jnp.logical_and(is_attention, column == per_slab - 1)
        which = jnp.where(jnp.logical_or(slab == 1, mixed), 1, 0)

        @pl.when(jnp.logical_or(is_ffn, slab == 0))
        def _():
            right = r.right[slab, :, columns]

            @pl.when(t >= 4)
            def _():
                core_copy(t - 4).wait_send()

            r.core_tx[lax.rem(t, 4)] = nn(r.left[which, theirs(j), :], right).astype(BF16)
            core_copy(t).start()
            r.mine[lax.rem(t, 2)] = nn(r.left[which, ours(j), :], right)

    def up_parts(k):
        i, column = k // per_slab, lax.rem(k, per_slab)
        columns = pl.ds(pl.multiple_of(column * step_columns, step_columns), step_columns)
        return target_of(i), columns

    def begin_up(k):
        j, columns = up_parts(k)
        right = r.right[2, :, columns]

        @pl.when(k >= 4)
        def _():
            up_core_copy(k - 4).wait_send()

        r.up_core_tx[lax.rem(k, 4)] = nn(r.left[0, theirs(j), :], right).astype(BF16)
        up_core_copy(k).start()
        r.up_mine[lax.rem(k, 2)] = nn(r.left[0, ours(j), :], right)

    def finish_up(k):
        up_core_copy(k).wait_recv()

        @pl.when(k >= 4)
        def _():
            up_copy(k - 4).wait_send()

        r.up_tx[lax.rem(k, 4)] = (r.up_mine[lax.rem(k, 2)] + r.up_rx[k].astype(F32)).astype(BF16)
        if z.handed:
            handed = jnp.logical_and(s == 1, lax.rem(k, per_slab) == hand_column)

            @pl.when(handed)
            def _():
                hand_copy(k).start()

            @pl.when(jnp.logical_not(handed))
            def _():
                up_copy(k).start()
        else:
            up_copy(k).start()

    def gone(t):
        return jnp.logical_and(s == 0, lax.rem(t, units) == units - 2) if z.handed else False

    def finish(t):
        @pl.when(jnp.logical_not(gone(t)))
        def _():
            finish_here(t)

    def finish_here(t):
        j, u, slab, column, columns = parts_of(t)
        k = t // 2
        total = r.mine.at[lax.rem(t, 2)]

        @pl.when(jnp.logical_or(is_ffn, slab == 0))
        def _():
            core_copy(t).wait_recv()
            total[...] += r.pool[t].astype(F32)

        @pl.when(jnp.logical_and(is_attention, slab == 1))
        def _():
            up_copy(k).wait_recv()
            total[...] = r.up_rx[k].astype(F32)

        way = jnp.where(j < place, 1, 0)

        @pl.when(jnp.logical_and(place > 0, j >= place))
        def _():
            line_copy(t, 0, j, u, place).wait_recv()
            total[...] += r.pool[line_slot(0, j, u)].astype(F32)

        @pl.when(jnp.logical_and(place < line - 1, j <= place))
        def _():
            line_copy(t, 1, j, u, place).wait_recv()
            total[...] += r.pool[line_slot(1, j, u)].astype(F32)

        @pl.when(jnp.logical_and(j == place, slab == 0))
        def _():
            r.main_v[:, columns] = total[...]
            slab_put(0, column, columns).start()

        @pl.when(jnp.logical_and(j == place, slab == 1))
        def _():
            r.side_v[:, columns] = total[...]
            slab_put(1, column, columns).start()

        @pl.when(j != place)
        def _():
            line_view(t)[...] = total[...].astype(BF16)
            line_copy(t, way, j, u, place + 1 - 2 * way).start()

    pl.semaphore_signal(r.core_ready, inc=1, device_id=(s, peer), device_id_type=MESH)

    @pl.when(place > 0)
    def _():
        pl.semaphore_signal(r.line_ready, inc=1, device_id=(s, d - 2), device_id_type=MESH)

    @pl.when(place < line - 1)
    def _():
        pl.semaphore_signal(r.line_ready, inc=1, device_id=(s, d + 2), device_id_type=MESH)

    @pl.when(s == last)
    def _():
        proj_first()

    ups = steps // 2
    pl.semaphore_wait(r.core_ready, 1)
    begin(jnp.int32(0))

    @pl.when(is_ffn)
    def _():
        begin_up(jnp.int32(0))

    neighbours = jnp.where(place > 0, 1, 0) + jnp.where(place < line - 1, 1, 0)
    pl.semaphore_wait(r.line_ready, neighbours)

    def step(t, carry):
        @pl.when(t < steps)
        def _():
            begin(t)

        @pl.when(jnp.logical_and(is_ffn, t < ups))
        def _():
            begin_up(t)

        finish(t - 1)

        @pl.when(jnp.logical_and(is_ffn, t <= ups))
        def _():
            finish_up(t - 1)

        if z.handed:

            @pl.when(jnp.logical_and(s == last, jnp.logical_and(t >= 2 * units, t < 2 * units + line)))
            def _():
                extra(t - 2 * units)

        @pl.when(jnp.logical_and(s == last, t == 2))
        def _():
            proj_second()

        @pl.when(t == 4)
        def _():
            small_first()

        @pl.when(jnp.logical_and(s == last, t == 6))
        def _():
            proj_third()

        @pl.when(t == units + 4)
        def _():
            small_second()

        @pl.when(t == steps - units)
        def _():
            come_home()

        @pl.when(t > steps - units)
        def _():
            first = (t - 1 - (steps - units)) * (line - 1)
            for k in range(line - 1):

                @pl.when(jnp.logical_not(gone(first + k)))
                def _():
                    line_copy(first + k, 0, 1, 0, place).wait_send()

        @pl.when(t == steps - 2)
        def _():
            small_last()

        return carry

    lax.fori_loop(1, steps + 1, step, 0)
    if z.handed:

        @pl.when(s == 0)
        def _():
            hand_home().wait_recv()
            slab_put(1, hand_column, hand_columns).start()

        @pl.when(s == last)
        def _():
            hand_home().wait_send()
            for i in range(line - 1):
                hand_line(i, 0, 1, place).wait_send()

    for slab in range(2):
        for column in range(per_slab):
            slab_put(
                slab, column, slice(column * step_columns, (column + 1) * step_columns)
            ).wait()
    for one in small_puts:
        one.wait()

    def drain_core(t, carry):
        slab = 1 - lax.rem(t, 2)

        @pl.when(jnp.logical_or(is_ffn, slab == 0))
        def _():
            core_copy(t).wait_send()

        return carry

    lax.fori_loop(steps - 4, steps, drain_core, 0)

    @pl.when(is_ffn)
    def _():
        for k in range(steps // 2 - 4, steps // 2):
            up_core_copy(k).wait_send()
            up_copy(k).wait_send()


def relay(z, hid, lengths, labels, chosen, main, side, gain, bias, buckets, fgain, proj, docs):
    dma = pltpu.SemaphoreType.DMA
    shape = jax.ShapeDtypeStruct
    sections, rows, width, ff, dp_size = z.sections, z.rows, z.width, z.ff, z.dp_size
    share, steps, units = z.share, z.steps, z.units
    piece = (share, z.step_columns)
    vmem = pl.BlockSpec(memory_space=VMEM)
    smem = pl.BlockSpec(memory_space=pltpu.SMEM)
    anywhere = pl.BlockSpec(memory_space=pl.ANY)
    inputs = dict(
        hid_hbm=(hid, anywhere),
        lengths=(lengths, smem),
        labels=(labels, smem),
        chosen_hbm=(chosen, anywhere),
        main_hbm=(main, anywhere),
        side_hbm=(side, anywhere),
        gain_hbm=(gain, anywhere),
        bias_hbm=(bias, anywhere),
        buckets_hbm=(buckets, anywhere),
        fgain_hbm=(fgain, anywhere),
        proj_hbm=(proj, anywhere),
        docs_hbm=(docs, anywhere),
    )
    outputs = dict(
        units=shape((z.batch_size, z.query_len, z.vector), BF16),
        loss=shape((8, rows), F32),
        dx=shape((z.batch_size, z.query_len, width), F32),
    )
    def like(value):
        return VMEM(value.shape, value.dtype)

    scratch = {name + "_v": like(value) for name, value in outputs.items()}
    scratch |= dict(
        chosen=like(chosen),
        bias=like(bias),
        buckets=like(buckets),
        gain=like(gain),
        fgain=like(fgain),
        proj=like(proj),
        main=VMEM((width, ff), BF16),
        side=VMEM((width, ff), BF16),
        lent=VMEM((width, ff), BF16),
        xin=VMEM((sections, rows, width), BF16),
        xout=VMEM((sections, rows, width), BF16),
        gin=VMEM((sections, rows, width), BF16),
        gout=VMEM((sections, rows, width), BF16),
        meta=VMEM((8, rows), F32),
        meta_rx=VMEM((sections, 8, rows), F32),
        idx=VMEM((8 + z.retrieved, rows), jnp.int32),
        idx_rx=VMEM((sections, 8 + z.retrieved, rows), jnp.int32),
        own_docs=VMEM((sections, z.batch_size * DOC_LEN, z.vector), BF16),
        table=VMEM((dp_size * z.doc_rows, z.vector), BF16),
        counts=VMEM((sections, z.batch_size * DOC_LEN, rows), BF16),
        pool=VMEM((z.pool, z.chunk, width), BF16),
        final_right=VMEM((z.total, z.vector), BF16),
        qkv=VMEM((z.total, 3 * H * DH), BF16),
        probs=VMEM((sections, H // 2, 2 * rows, rows), F32),
        bias_sc=VMEM((H // 2, 2, z.query_len, rows), F32),
        dbias=VMEM((H // 2, 2, z.query_len, rows), F32),
        fin_rx=VMEM((rows, width), BF16),
        unit_tx=VMEM((sections, rows, z.vector), BF16),
        unit_rx=VMEM((rows, z.vector), BF16),
        loss_tx=VMEM((sections, 8, rows), F32),
        loss_rx=VMEM((8, rows), F32),
        small_sem=dma((6,)),
        load_sem=dma((3,)),
        put_sem=dma((7,)),
        state_ss=dma((sections + 1,)),
        state_rs=dma((sections,)),
        grad_ss=dma((sections,)),
        grad_rs=dma((sections,)),
        meta_ss=dma((sections,)),
        meta_rs=dma((sections,)),
        idx_ss=dma,
        idx_rs=dma((sections,)),
        tab_ss=dma((dp_size,)),
        tab_rs=dma((dp_size,)),
        tabf_ss=dma((dp_size,)),
        lend_ss=dma((4, z.parts, LEND_CUTS)),
        lend_rs=dma((4, z.parts, LEND_CUTS)),
        fin_ss=dma((sections,)),
        fin_rs=dma,
        unit_ss=dma((sections,)),
        unit_rs=dma,
        loss_ss=dma((sections,)),
        loss_rs=dma,
    )
    factors = dict(left=((2, width, z.total), BF16), right=((3, z.total, ff), BF16))
    partials = dict(
        gain_grad=((1, width), F32),
        fgain_grad=((1, width), F32),
        tab_grad=((16, 32), F32),
        dproj=((width, z.vector), BF16 if z.summed else F32),
    )
    if z.summed:
        outputs |= dict(
            main_out=shape((1, share, ff), F32),
            side_out=shape((1, share, ff), F32),
            gain_out=shape((1, share), F32),
            table_out=shape((H, 32), F32),
            fgain_out=shape((width,), F32),
            proj_out=shape((width, z.vector), F32),
        )
        scratch |= {name: VMEM(*kind) for name, kind in (factors | partials).items()}
        scratch |= dict(
            gain_out_v=VMEM((1, share), F32),
            table_out_v=VMEM((H, 32), F32),
            fgain_out_v=VMEM((width,), F32),
            main_v=VMEM((share, ff), F32),
            side_v=VMEM((share, ff), F32),
            slab_sem=dma((2, z.per_slab)),
            mine=VMEM((2,) + piece, F32),
            up_mine=VMEM((2,) + piece, F32),
            core_tx=VMEM((4,) + piece, BF16),
            up_core_tx=VMEM((4,) + piece, BF16),
            up_tx=VMEM((4,) + piece, BF16),
            up_rx=VMEM((steps // 2,) + piece, BF16),
            gain_rx=VMEM((dp_size, 1, width), F32),
            tab_rx=VMEM((dp_size, 16, 32), F32),
            tab_tx=VMEM((16, 32), F32),
            tab_cx=VMEM(((sections + 1) // 2, 16, 32), F32),
            fgain_rx=VMEM((dp_size, 1, width), F32),
            fgain_tx=VMEM((1, width), F32),
            fgain_sum=VMEM((1, width), F32),
            proj_sum=VMEM((width, z.vector), BF16),
            proj_v=VMEM((width, z.vector), F32),
            proj_rx=VMEM((dp_size, share, z.vector), BF16),
            core_ss=dma((steps,)),
            core_rs=dma((steps,)),
            up_core_ss=dma((steps // 2,)),
            up_ss=dma((steps // 2,)),
            up_rs=dma((steps // 2,)),
            hand_rs=dma((3 * z.line - 2,)),
            home_ss=dma,
            home_rs=dma,
            line_ss=dma((steps,)),
            line_rs=dma((2, z.line - 1, units)),
            core_ready=pltpu.SemaphoreType.REGULAR,
            line_ready=pltpu.SemaphoreType.REGULAR,
            gain_ss=dma((dp_size,)),
            gain_rs=dma((dp_size,)),
            tabs_ss=dma((dp_size,)),
            tabs_rs=dma((dp_size,)),
            fg_ss=dma((dp_size,)),
            fg_rs=dma((dp_size,)),
            across_ss=dma((3, sections)),
            across_rs=dma((sections + 2,)),
            proj_ss=dma((dp_size,)),
            proj_rs=dma((dp_size,)),
            spread_ss=dma((dp_size,)),
            spread_rs=dma((dp_size,)),
        )
    else:
        outputs |= {name: shape(*kind) for name, kind in (factors | partials).items()}
    results = pl.pallas_call(
        functools.partial(relay_kernel, z, (*inputs, *outputs, *scratch)),
        out_shape=tuple(outputs.values()),
        in_specs=[spec for _, spec in inputs.values()],
        out_specs=tuple(vmem if name in factors or name in partials else anywhere for name in outputs),
        scratch_shapes=list(scratch.values()),
        compiler_params=pltpu.CompilerParams(
            collective_id=0, has_side_effects=True, vmem_limit_bytes=62 * 2**20
        ),
        name="relay",
    )(*[value for value, _ in inputs.values()])
    return types.SimpleNamespace(**dict(zip(outputs, results, strict=True)))


def deliver_kernel(count, *refs):
    for k in range(count):
        refs[count + 1 + k][...] = refs[k][...]
    losses, out = refs[count], refs[-1]
    out[...] = losses[0:1, : out.shape[0]].reshape(out.shape)


def deliver(values, losses, queries):
    count = len(values)
    vmem = pl.BlockSpec(memory_space=VMEM)
    return pl.pallas_call(
        functools.partial(deliver_kernel, count),
        out_shape=tuple(jax.ShapeDtypeStruct(v.shape, v.dtype) for v in values)
        + (jax.ShapeDtypeStruct((queries,), F32),),
        in_specs=[vmem] * (count + 1),
        out_specs=(vmem,) * (count + 1),
        name="deliver",
    )(*values, losses)


def sums_outside(z, out):
    head_width = H * DH
    section = lax.axis_index("section")
    is_attention = section % 2 == 0
    left, right = out.left, out.right
    second = jnp.where(is_attention, left[1], left[0])
    main_grad = jnp.concatenate(
        [nn(left[0], right[0, :, : 3 * head_width]), nn(second, right[0, :, 3 * head_width :])],
        axis=1,
    )
    up_grad = lax.ppermute(
        nn(left[0], right[2]).astype(BF16),
        "section",
        [(k, k - 1) for k in range(1, z.sections)],
    )
    side_grad = jnp.where(is_attention, up_grad.astype(F32), nn(left[1], right[1]))
    scatter = functools.partial(
        lax.psum_scatter, axis_name="dp", scatter_dimension=0, tiled=True
    )
    table, fgain, proj = lax.psum(
        (out.tab_grad[:H], out.fgain_grad[0], out.dproj), ("section", "dp")
    )
    return (
        scatter(main_grad)[None],
        scatter(side_grad)[None],
        scatter(out.gain_grad[0])[None],
        table.T,
        fgain,
        proj,
    )


def per_device(
    hidden_in,
    lengths,
    labels,
    chosen,
    slab_main,
    slab_side,
    section_gains,
    rel_bias,
    final_gain,
    out_proj,
    doc_vectors,
):
    batch_size, query_len, width = hidden_in.shape
    rows = batch_size * query_len
    retrieved = chosen.shape[2]
    z = Sizes(
        lax.axis_size("section"),
        lax.axis_size("dp"),
        batch_size,
        query_len,
        retrieved,
        width,
        slab_main.shape[2],
        out_proj.shape[1],
        doc_vectors.shape[0],
    )
    buckets = jnp.asarray(np.tile(bucket_table(query_len).T, (1, batch_size)))
    out = relay(
        z,
        hidden_in.reshape(rows, width),
        lengths,
        labels,
        chosen.reshape(rows, retrieved),
        slab_main,
        slab_side,
        section_gains,
        rel_bias.T,
        buckets,
        final_gain,
        out_proj,
        doc_vectors,
    )
    if not z.summed:
        return (out.units, out.loss[0, :batch_size], out.dx) + sums_outside(z, out)
    names = ("units", "dx", "main_out", "side_out", "gain_out", "table_out", "fgain_out", "proj_out")
    units, dx, main, side, gain, table, fgain, proj, losses = deliver(
        [getattr(out, n) for n in names], out.loss, batch_size
    )
    return units, losses, dx, main, side, gain, table.T, fgain, proj


def solution(mesh):
    both = ("section", "dp")
    in_specs = (
        P(both, None, None),
        P(both),
        P(both),
        P(both, None, None),
        P("section", None, None),
        P("section", None, None),
        P("section", None),
        P(),
        P(),
        P(),
        P("dp", None),
    )
    out_specs = (
        P(both, None, None),
        P(both),
        P(both, None, None),
        P("section", "dp", None),
        P("section", "dp", None),
        P("section", "dp"),
        P(),
        P(),
        P(),
    )
    return jax.shard_map(
        per_device, mesh=mesh, in_specs=in_specs, out_specs=out_specs, check_vma=False
    )
```
